128 devices in a mesh: row: 8 (over y_lo, z), col: 16 (over x, y_hi, core).
Axes of the slice: x: 4, y: 4 (y_hi: 2, y_lo: 2; y = y_hi * 2 + y_lo), z: 4, core: 2. Of those that a mesh axis runs over, the one named last changes fastest.
Arguments:
- image_embeds: float32 [16384, 1280], P(('row', 'col')), may hold values from -100 to 100
- text_embeds: float32 [16384, 1280], P(('col', 'row')), may hold values from -100 to 100
Outputs:
- image_grad: float32 [16384, 1280], P(('row', 'col'))
- text_grad: float32 [16384, 1280], P(('col', 'row'))
- loss: float32 [], replicated
The draws below stay inside these ranges and needn't reach their ends.
All inputs are finite; a program needn't handle non-finite values.
Results may differ from the reference program's by a relative error of at most 0.0076.
Values may be sent and summed in bfloat16 or wider, within the bound.
No kernel may reach another device: no remote copies, remote signals or barrier semaphores. Data moves between devices by JAX's collectives and lax.ppermute only.
A program may use at most 128 MiB of HBM per device.

```python
import jax
import jax.numpy as jnp
from jax import lax

EMBED = 1280
BATCH = 16384


def pair_fields(key, ramp_low, ramp_high, spread, planted):
    keys = jax.random.split(key, 7)
    common = jax.random.normal(keys[0], (BATCH, EMBED), jnp.float32)
    image_noise = jax.random.normal(keys[1], (BATCH, EMBED), jnp.float32)
    text_noise = jax.random.normal(keys[2], (BATCH, EMBED), jnp.float32)
    image_scale = jnp.exp(jax.random.uniform(keys[4], (BATCH, 1), jnp.float32, 0.0, jnp.log(spread)))
    text_scale = jnp.exp(jax.random.uniform(keys[5], (BATCH, 1), jnp.float32, 0.0, jnp.log(spread)))
    jitter = jax.random.uniform(keys[6], (BATCH, 1), jnp.float32, 0.7, 1.3)
    row_ids = jnp.arange(BATCH, dtype=jnp.int32)
    position = row_ids.astype(jnp.float32)[:, None] / BATCH
    mixing = (ramp_low + (ramp_high - ramp_low) * position) * jitter
    image_raw = mixing * common + image_noise
    text_raw = mixing * common + text_noise
    marked = (row_ids % 64 == 0)[:, None] & (planted > 0.5)
    strength = (row_ids // 64 % 3).astype(jnp.float32)[:, None] * 0.05
    moved = jnp.roll(text_raw, -(BATCH // 2), axis=0)
    image_raw = jnp.where(marked, moved + strength * image_noise, image_raw)
    follower = ((row_ids - 1 - BATCH // 2) % BATCH % 64 == 0)[:, None] & (planted > 0.5)
    text_raw = jnp.where(follower, jnp.roll(text_raw, 1, axis=0) + 0.15 * text_noise, text_raw)
    image_out = jnp.clip(image_raw * image_scale, -100.0, 100.0)
    text_out = jnp.clip(text_raw * text_scale, -100.0, 100.0)
    return (image_out, text_out)


def draw_image_embeds(key, part):
    fields = pair_fields(key, 0.15, 1.0, 10.0, 0.0)
    return fields[0]


def draw_text_embeds(key, part):
    fields = pair_fields(key, 0.15, 1.0, 10.0, 0.0)
    return fields[1]


def setup_inputs(seed: int = 0) -> dict:
    splits = jax.random.split(jax.random.key(seed), 3)
    image_embeds = draw_image_embeds(jax.random.fold_in(splits[2], 71), 0)
    text_embeds = draw_text_embeds(jax.random.fold_in(splits[2], 71), 0)
    return dict(image_embeds=image_embeds, text_embeds=text_embeds)


LOGIT_SCALE = 100.0

def unit_rows(values):
    norms = jnp.sqrt(lax.optimization_barrier(jnp.sum(values * values, axis=1, keepdims=True)) + 1e-06)
    return (values / norms, norms)

def reference(image_embeds, text_embeds):
    image_unit, image_norm = unit_rows(image_embeds)
    text_unit, text_norm = unit_rows(text_embeds)
    image_bf = image_unit.astype(jnp.bfloat16)
    text_bf = text_unit.astype(jnp.bfloat16)
    block_rows = math_gcd(BATCH, 1024)
    blocks = BATCH // block_rows
    image_blocks = image_bf.reshape(blocks, block_rows, EMBED)
    starts = jnp.arange(blocks, dtype=jnp.int32) * block_rows
    column_ids = jnp.arange(BATCH, dtype=jnp.int32)

    def forward(carried, inputs):
        rows_bf, anchor = inputs
        scores = LOGIT_SCALE * jnp.dot(rows_bf, text_bf.T, preferred_element_type=jnp.float32)
        row_peak = lax.optimization_barrier(jnp.max(scores, axis=1))
        row_lse = row_peak + jnp.log(lax.optimization_barrier(jnp.sum(jnp.exp(scores - row_peak[:, None]), axis=1)))
        col_peak, col_total, diag_sum = carried
        new_peak = jnp.maximum(col_peak, lax.optimization_barrier(jnp.max(scores, axis=0)))
        col_total = col_total * jnp.exp(col_peak - new_peak) + lax.optimization_barrier(jnp.sum(jnp.exp(scores - new_peak[None, :]), axis=0))
        row_ids = anchor + jnp.arange(block_rows, dtype=jnp.int32)
        matched = row_ids[:, None] == column_ids[None, :]
        diag_sum = diag_sum + jnp.sum(jnp.where(matched, scores, jnp.zeros_like(scores)))
        return ((new_peak, col_total, diag_sum), row_lse)
    initial = (jnp.full((BATCH,), -jnp.inf, jnp.float32), jnp.zeros((BATCH,), jnp.float32), jnp.zeros((), jnp.float32))
    (col_peak, col_total, diag_sum), row_lse = lax.scan(forward, initial, (image_blocks, starts))
    col_lse = col_peak + jnp.log(col_total)
    loss = (jnp.sum(row_lse) + jnp.sum(col_lse) - 2.0 * diag_sum) / (2.0 * BATCH)

    def backward(text_dir, inputs):
        rows_bf, anchor, lse_rows = inputs
        scores = LOGIT_SCALE * jnp.dot(rows_bf, text_bf.T, preferred_element_type=jnp.float32)
        row_ids = anchor + jnp.arange(block_rows, dtype=jnp.int32)
        matched = (row_ids[:, None] == column_ids[None, :]).astype(jnp.float32)
        weights = ((jnp.exp(scores - lse_rows[:, None]) + jnp.exp(scores - col_lse[None, :]) - 2.0 * matched) * 0.5).astype(jnp.bfloat16)
        image_dir = jnp.dot(weights, text_bf, preferred_element_type=jnp.float32)
        text_dir = text_dir + jnp.dot(weights.T, rows_bf, preferred_element_type=jnp.float32)
        return (text_dir, image_dir)
    text_dir, image_dir = lax.scan(backward, jnp.zeros((BATCH, EMBED), jnp.float32), (image_blocks, starts, row_lse))
    image_dir = image_dir.reshape(BATCH, EMBED)
    image_grad = (image_dir - image_unit * lax.optimization_barrier(jnp.sum(image_unit * image_dir, axis=1, keepdims=True))) / image_norm
    text_grad = (text_dir - text_unit * lax.optimization_barrier(jnp.sum(text_unit * text_dir, axis=1, keepdims=True))) / text_norm
    return (image_grad, text_grad, loss)

def math_gcd(first, second):
    while second:
        first, second = (second, first % second)
    return first
```

```python
import functools
import math

import jax
import jax.numpy as jnp
from jax import lax
from jax.experimental import pallas as pl
from jax.experimental.pallas import tpu as pltpu
from jax.sharding import PartitionSpec as P

PIECE = 128
WIDTH = 1280
XS, YS, KS, ZS = 4, 2, 2, 4
IMG = XS * YS * KS
TXT = ZS * YS

SHIFT = 22.0
LIFT = 70.0
FLOOR = math.exp(-62.0)
LOG2E = math.log2(math.e)

ANY = pl.BlockSpec(memory_space=pl.ANY)
VM = pl.BlockSpec(memory_space=pltpu.VMEM)
SM = pl.BlockSpec(memory_space=pltpu.SMEM)
PARAMS = pltpu.CompilerParams(vmem_limit_bytes=48 * 1024 * 1024)
F32, BF = jnp.float32, jnp.bfloat16
NT = (((1,), (1,)), ((), ()))
NN = (((1,), (0,)), ((), ()))
TN = (((0,), (0,)), ((), ()))


def dot(a, b, dims):
    return lax.dot_general(a, b, dims, preferred_element_type=F32)


def col_index(x, y, k):
    return (x * YS + y) * KS + k


def col_perm(dx, dy, dk):
    return [
        (col_index(x, y, k), col_index((x + dx) % XS, y ^ dy, k ^ dk))
        for x in range(XS)
        for y in range(YS)
        for k in range(KS)
    ]


def row_perm(dz, dy):
    return [(y * ZS + z, (y ^ dy) * ZS + (z + dz) % ZS) for y in range(YS) for z in range(ZS)]


def send_col(value, dx=0, dy=0, dk=0):
    return lax.ppermute(value, "col", col_perm(dx, dy, dk))


def send_row(value, dz=0, dy=0):
    return lax.ppermute(value, "row", row_perm(dz, dy))


def sum_col(value):
    value = value + send_col(value, dk=1)
    value = value + send_col(value, dx=1) + send_col(value, dx=2) + send_col(value, dx=3)
    return value + send_col(value, dy=1)


def sum_row(value):
    value = value + send_row(value, dz=1) + send_row(value, dz=2) + send_row(value, dz=3)
    return value + send_row(value, dy=1)


def cost(flops, bytes_accessed):
    return pl.CostEstimate(flops=flops, bytes_accessed=bytes_accessed, transcendentals=0)


def unit_kernel(image_ref, text_ref, image_out, text_out):
    for src, dst in ((image_ref, image_out), (text_ref, text_out)):
        x = src[...]
        dst[...] = (x / jnp.sqrt(jnp.sum(x * x, axis=1, keepdims=True) + 1e-06)).astype(BF)


def unit_pair(image, text):
    shape = jax.ShapeDtypeStruct((PIECE, WIDTH), BF)
    return pl.pallas_call(
        unit_kernel, out_shape=(shape, shape), in_specs=[VM, VM], out_specs=(VM, VM),
        compiler_params=PARAMS, name="unit_rows",
    )(image, text)


def forward_kernel(ids, *refs):
    img_in, txt_in = refs[:IMG], refs[IMG:IMG + TXT]
    h_own, h_oth, rs_out, cs_out, dg_out = refs[IMG + TXT:IMG + TXT + 5]
    img, txt, half, cacc, img_sem, txt_sem, out_sem = refs[IMG + TXT + 5:]
    txt_cp = [
        pltpu.make_async_copy(txt_in[q], txt.at[pl.ds(q * PIECE, PIECE)], txt_sem.at[q])
        for q in range(TXT)
    ]
    img_cp = [pltpu.make_async_copy(img_in[p], img.at[p], img_sem.at[p]) for p in range(IMG)]
    img_cp[0].start()
    img_cp[1].start()
    for c in txt_cp:
        c.start()
    for c in img_cp[2:]:
        c.start()
    cacc[...] = jnp.zeros_like(cacc)
    dg_out[...] = jnp.zeros_like(dg_out)
    for c in txt_cp:
        c.wait()
    eye = (
        lax.broadcasted_iota(jnp.int32, (PIECE, PIECE), 0)
        == lax.broadcasted_iota(jnp.int32, (PIECE, PIECE), 1)
    )

    @pl.loop(0, IMG // 2)
    def _(i):
        rows = []
        for u in range(2):
            p = 2 * i + u
            pltpu.make_async_copy(img.at[p], img.at[p], img_sem.at[p]).wait()
        block = img[pl.ds(2 * i, 2)].reshape(2 * PIECE, WIDTH)
        racc = [jnp.zeros((2 * PIECE, PIECE), F32) for _ in range(2)]
        for n in range(4):
            cols = pl.ds(n * 256, 256)
            d = dot(block, txt[cols, :], NT)
            h = jnp.exp2(d * (50.0 * LOG2E) - (0.5 * SHIFT * LOG2E))
            half[pl.ds(2 * i, 2), :, cols] = h.reshape(2, PIECE, 256)
            g = h * math.exp(0.5 * (SHIFT + LIFT))
            for t, v in enumerate((h * h, g * g)):
                racc[t] += v[:, :PIECE] + v[:, PIECE:]
                cacc[t, :, cols] += jnp.sum(v.reshape(32, 8, 256), axis=0)
        for u in range(2):
            p = 2 * i + u
            at = pl.ds(ids[p], 1)
            for t in range(2):
                part = racc[t][u * PIECE:(u + 1) * PIECE]
                rs_out[t, at, :] = jnp.sum(part.T, axis=0, keepdims=True)

            @pl.when(ids[IMG + TXT + p] >= 0)
            def _():
                q = ids[IMG + TXT + p]
                other = txt[pl.ds(pl.multiple_of(q * PIECE, PIECE), PIECE), :]
                s = 100.0 * dot(img[p], other, NT)
                dg_out[...] += jnp.sum(jnp.where(eye, s, 0.0).reshape(16, 8, PIECE), axis=0)

        @pl.when(i < IMG // 4)
        def _():
            pltpu.make_async_copy(half.at[pl.ds(2 * i, 2)], h_own.at[pl.ds(2 * i, 2)], out_sem).start()

        @pl.when(i >= IMG // 4)
        def _():
            j = 2 * i - IMG // 2
            pltpu.make_async_copy(half.at[pl.ds(2 * i, 2)], h_oth.at[pl.ds(j, 2)], out_sem).start()

    for t in range(2):
        total = jnp.sum(cacc[t], axis=0, keepdims=True)
        for q in range(TXT):
            cs_out[t, pl.ds(ids[IMG + q], 1), :] = total[:, q * PIECE:(q + 1) * PIECE]
    pltpu.make_async_copy(half, half, out_sem).wait()


def forward(ids, img, txt):
    half = jax.ShapeDtypeStruct((IMG // 2, PIECE, TXT * PIECE), F32)
    return pl.pallas_call(
        forward_kernel,
        out_shape=(
            half, half,
            jax.ShapeDtypeStruct((2, IMG, PIECE), F32),
            jax.ShapeDtypeStruct((2, TXT, PIECE), F32),
            jax.ShapeDtypeStruct((8, PIECE), F32),
        ),
        in_specs=[SM] + [ANY] * (IMG + TXT),
        out_specs=(ANY, ANY, VM, VM, VM),
        scratch_shapes=[
            pltpu.VMEM((IMG, PIECE, WIDTH), BF),
            pltpu.VMEM((TXT * PIECE, WIDTH), BF),
            pltpu.VMEM((IMG, PIECE, TXT * PIECE), F32),
            pltpu.VMEM((2, 8, TXT * PIECE), F32),
            pltpu.SemaphoreType.DMA((IMG,)),
            pltpu.SemaphoreType.DMA((TXT,)),
            pltpu.SemaphoreType.DMA,
        ],
        compiler_params=PARAMS,
        cost_estimate=cost(2 * 2048 * 1024 * 1280, 16 << 20),
        name="pair_scores",
    )(ids, *img, *txt)


def lse_of(sums):
    return jnp.where(sums[0] >= FLOOR, SHIFT + jnp.log(sums[0]), jnp.log(sums[1]) - LIFT)


def half_kernel(base, ids, rs, cs, h_in, *refs):
    txt_in = refs[:TXT]
    w_out, p_out = refs[TXT:TXT + 2]
    txt, half, a_s, b_s, h_sem, txt_sem = refs[TXT + 2:]
    n_p = IMG // 2
    h_cp = [pltpu.make_async_copy(h_in.at[p], half.at[p], h_sem.at[p]) for p in range(n_p)]
    txt_cp = [
        pltpu.make_async_copy(txt_in[q], txt.at[pl.ds(q * PIECE, PIECE)], txt_sem.at[q])
        for q in range(TXT)
    ]
    for c in h_cp[:2] + txt_cp + h_cp[2:]:
        c.start()
    scale = math.sqrt(0.5)
    a_s[...] = scale * jnp.exp(0.5 * (SHIFT - lse_of(rs[...])))
    b_s[...] = scale * jnp.exp(0.5 * (SHIFT - lse_of(cs[...])))
    b = [b_s[pl.ds(ids[IMG + q], 1), :] for q in range(TXT)]
    for c in txt_cp:
        c.wait()

    def weights(p):
        a = jnp.broadcast_to(a_s[pl.ds(ids[base + p], 1), :], (PIECE, PIECE)).T
        for q in range(TXT):
            h = half[p, :, q * PIECE:(q + 1) * PIECE]
            u, v = h * a, h * b[q]
            w_out[pl.ds(p * PIECE, PIECE), q * PIECE:(q + 1) * PIECE] = (u * u + v * v).astype(BF)
        match = ids[IMG + TXT + base + p]

        @pl.when(match >= 0)
        def _():
            cols = pl.ds(pl.multiple_of(match * PIECE, PIECE), PIECE)
            h = half[p, :, cols]
            bm = b_s[pl.ds(ids[IMG + match], 1), :]
            u, v = h * a, h * bm
            eye = (
                lax.broadcasted_iota(jnp.int32, (PIECE, PIECE), 0)
                == lax.broadcasted_iota(jnp.int32, (PIECE, PIECE), 1)
            ).astype(F32)
            w_out[pl.ds(p * PIECE, PIECE), cols] = (u * u + v * v - eye).astype(BF)

    @pl.loop(0, n_p // 2)
    def _(i):
        for u in range(2):
            p = 2 * i + u
            pltpu.make_async_copy(half.at[p], half.at[p], h_sem.at[p]).wait()
            weights(p)
        rows = pl.ds(i * 256, 256)
        for n in range(5):
            cols = slice(n * 256, n * 256 + 256)
            p_out[rows, cols] = dot(w_out[rows, :], txt[:, cols], NN).astype(p_out.dtype)


def half_products(base, ids, rs, cs, h, txt, dtype):
    rows = IMG // 2 * PIECE
    return pl.pallas_call(
        functools.partial(half_kernel, base),
        out_shape=(
            jax.ShapeDtypeStruct((rows, TXT * PIECE), BF),
            jax.ShapeDtypeStruct((rows, WIDTH), dtype),
        ),
        in_specs=[SM, VM, VM] + [ANY] * (1 + TXT),
        out_specs=(VM, VM),
        scratch_shapes=[
            pltpu.VMEM((TXT * PIECE, WIDTH), BF),
            pltpu.VMEM((IMG // 2, PIECE, TXT * PIECE), F32),
            pltpu.VMEM((IMG, PIECE), F32),
            pltpu.VMEM((TXT, PIECE), F32),
            pltpu.SemaphoreType.DMA((IMG // 2,)),
            pltpu.SemaphoreType.DMA((TXT,)),
        ],
        compiler_params=PARAMS,
        cost_estimate=cost(2 * 1024 * 1024 * 1280, 8 << 20),
        name="image_products",
    )(ids, rs, cs, h, *txt)


def text_kernel(w_own, w_oth, *refs):
    img_in = refs[:IMG]
    outs = refs[IMG:IMG + TXT]
    img, wo, wt, img_sem, w_sem = refs[IMG + TXT:]
    half = IMG // 2 * PIECE
    w_cp = [
        pltpu.make_async_copy(w_own, wo, w_sem.at[0]),
        pltpu.make_async_copy(w_oth, wt, w_sem.at[1]),
    ]
    img_cp = [
        pltpu.make_async_copy(img_in[p], img.at[pl.ds(p * PIECE, PIECE)], img_sem.at[p])
        for p in range(IMG)
    ]
    w_cp[1].start()
    for c in img_cp[IMG // 2:]:
        c.start()
    w_cp[0].start()
    for c in img_cp[:IMG // 2]:
        c.start()
    for c in w_cp + img_cp:
        c.wait()
    for z in (2, 1, 3, 0):
        for n in range(5):
            cols = slice(n * 256, n * 256 + 256)
            lanes = slice(z * 256, z * 256 + 256)
            d = dot(wt[:, lanes], img[half:, cols], TN) + dot(wo[:, lanes], img[:half, cols], TN)
            for y in range(YS):
                out = outs[z * YS + y]
                out[:, cols] = d[y * PIECE:(y + 1) * PIECE].astype(out.dtype)


def text_products(w_own, w_oth, img):
    return pl.pallas_call(
        text_kernel,
        out_shape=tuple(
            jax.ShapeDtypeStruct((PIECE, WIDTH), F32 if q < YS else BF) for q in range(TXT)
        ),
        in_specs=[ANY] * (2 + IMG),
        out_specs=(VM,) * TXT,
        scratch_shapes=[
            pltpu.VMEM((IMG * PIECE, WIDTH), BF),
            pltpu.VMEM((IMG // 2 * PIECE, TXT * PIECE), BF),
            pltpu.VMEM((IMG // 2 * PIECE, TXT * PIECE), BF),
            pltpu.SemaphoreType.DMA((IMG,)),
            pltpu.SemaphoreType.DMA((2,)),
        ],
        compiler_params=PARAMS,
        cost_estimate=cost(2 * 2048 * 1024 * 1280, 12 << 20),
        name="text_products",
    )(w_own, w_oth, *img)


def grad_kernel(values_ref, *refs):
    out = refs[-1]
    total = refs[0][...].astype(F32)
    for r in refs[1:-1]:
        total = total + r[...].astype(F32)
    x = values_ref[...]
    norm = jnp.sqrt(jnp.sum(x * x, axis=1, keepdims=True) + 1e-06)
    unit = x / norm
    out[...] = (total - unit * jnp.sum(unit * total, axis=1, keepdims=True)) / norm


def grad_rows(values, parts):
    return pl.pallas_call(
        grad_kernel,
        out_shape=jax.ShapeDtypeStruct((PIECE, WIDTH), F32),
        in_specs=[VM] * (1 + len(parts)),
        out_specs=VM,
        compiler_params=PARAMS,
        name="grad_rows",
    )(values, *parts)


def gather_ring(own, flip, step):
    other = flip(own)
    left0, right0 = step(own, 1), step(own, 3)
    left1, right1 = step(other, 1), step(other, 3)
    far0, far1 = step(left0, 1), step(right1, 3)
    return [own, other, right0, right1, far0, far1, left0, left1]


def scatter_ring(parts, flip, step):
    (own, other, near0, near1, far0, far1, back0, back1) = parts
    through0, through1 = step(far0, 1), step(far1, 3)
    add = lambda a, b: (a.astype(F32) + b.astype(F32)).astype(BF)
    right1, left0 = step(near1, 1), step(back0, 3)
    right0 = step(add(near0, through0), 1)
    left1 = step(add(back1, through1), 3)
    back = flip((other + right1.astype(F32) + left1.astype(F32)).astype(BF))
    return [own, right0, left0, back]


def per_device(image_embeds, text_embeds):
    row, col = lax.axis_index("row"), lax.axis_index("col")
    x, y, k = col // 4, col // 2 % 2, col % 2
    yl, z = row // 4, row % 4
    img_ids = [
        col_index((x + dx) % XS, y ^ dy, k ^ dk)
        for dk in range(KS) for dx in range(XS) for dy in range(YS)
    ]
    txt_ids = [(yl ^ dy) * ZS + (z + dz) % ZS for dz in range(ZS) for dy in range(YS)]
    match = []
    for c in img_ids:
        t = c % TXT
        q = ((t % ZS - z) % ZS) * YS + ((t // ZS) ^ yl)
        match.append(jnp.where(2 * row + c // TXT == col, q, -1))
    ids = jnp.stack(img_ids + txt_ids + match).astype(jnp.int32)

    image_own, text_own = unit_pair(image_embeds, text_embeds)
    txt = gather_ring(
        text_own, lambda v: send_row(v, dy=1), lambda v, d: send_row(v, dz=d)
    )
    img = gather_ring(
        image_own, lambda v: send_col(v, dy=1), lambda v, d: send_col(v, dx=d)
    )
    img = img + [send_col(v, dk=1) for v in img]

    h_own, h_oth, rs, cs, dg = forward(ids, img, txt)
    rs, cs = sum_col(rs), sum_row(cs)

    w_oth, p_oth = half_products(IMG // 2, ids, rs, cs, h_oth, txt, BF)
    far = {d: send_col(p_oth[d * 256:(d + 1) * 256], dk=1) for d in (2, 1, 3, 0)}
    w_own, p_own = half_products(0, ids, rs, cs, h_own, txt, F32)
    t_parts = text_products(w_own, w_oth, img)

    parts = []
    for d in range(XS):
        both = p_own[d * 256:(d + 1) * 256] + far[d].astype(F32)
        for dy in range(YS):
            part = both[dy * PIECE:(dy + 1) * PIECE]
            parts.append(part if d == 0 else part.astype(BF))
    i_sum = scatter_ring(parts, lambda v: send_col(v, dy=1), lambda v, d: send_col(v, dx=d))
    t_sum = scatter_ring(
        list(t_parts), lambda v: send_row(v, dy=1), lambda v, d: send_row(v, dz=d)
    )
    image_grad = grad_rows(image_embeds, i_sum)
    text_grad = grad_rows(text_embeds, t_sum)

    own = jnp.sum(lse_of(rs)) / IMG + jnp.sum(lse_of(cs)) / TXT - 2.0 * jnp.sum(dg)
    total = sum_row(sum_col(jnp.full((8, PIECE), own, F32)))
    batch = TXT * IMG * PIECE
    loss = total[0, 0] / (2.0 * batch)
    return (image_grad, text_grad, loss)


def solution(mesh):
    return jax.shard_map(
        per_device,
        mesh=mesh,
        in_specs=(P(("row", "col"), None), P(("col", "row"), None)),
        out_specs=(P(("row", "col"), None), P(("col", "row"), None), P()),
        check_vma=False,
    )
```

```python
import functools
import math

import jax
import jax.numpy as jnp
import numpy as np
from jax import lax
from jax.experimental import pallas as pl
from jax.experimental.pallas import tpu as pltpu
from jax.sharding import PartitionSpec as P

PIECE = 128
PART = 2 * PIECE
WIDTH = 1280
RING = 4
PARTS = 2 * RING
ROWS, COLS = 8, 16
IMG = PARTS * PART
TXT = PARTS * PIECE
CORE, TXT_AT, MATCH_AT = 40, 32, 16

SHIFT = 22.0
LIFT = 70.0
FLOOR = math.exp(-62.0)
LOG2E = math.log2(math.e)

VM = pl.BlockSpec(memory_space=pltpu.VMEM)
SM = pl.BlockSpec(memory_space=pltpu.SMEM)
PARAMS = pltpu.CompilerParams(vmem_limit_bytes=20 * 1024 * 1024)
F32, BF = jnp.float32, jnp.bfloat16
NT = (((1,), (1,)), ((), ()))
NN = (((1,), (0,)), ((), ()))
AXES = ("row", "col")


def dot(a, b, dims):
    return lax.dot_general(a, b, dims, preferred_element_type=F32)


def device(yl, z, x, yh, k):
    return (yl * 4 + z) * COLS + (x * 2 + yh) * 2 + k


def places():
    return [
        (yl, z, x, yh, k)
        for yl in range(2) for z in range(RING) for x in range(RING) for yh in range(2) for k in range(2)
    ]


def ring(value, d):
    return lax.ppermute(value, AXES, [
        (device(yl, z, x, yh, k),
         device(yl, (z + d * k) % RING, (x + d * (1 - k)) % RING, yh, k))
        for yl, z, x, yh, k in places()
    ])


def flip(value):
    return lax.ppermute(value, AXES, [
        (device(yl, z, x, yh, k), device(yl ^ k, z, x, yh ^ (1 - k), k))
        for yl, z, x, yh, k in places()
    ])


def swap(value):
    return lax.ppermute(value, AXES, [
        (device(yl, z, x, yh, k), device(yl, z, x, yh, 1 - k)) for yl, z, x, yh, k in places()
    ])


def device_table():
    table = np.zeros((ROWS * COLS, 41), np.int32)
    for yl, z, x, yh, k in places():
        col, row = (x * 2 + yh) * 2 + k, yl * 4 + z
        parts = [(d, y) for d in range(RING) for y in range(2)]
        img = [((x + d) % RING * 2 + (yh ^ y)) * 2 + h for d, y in parts for h in range(2)]
        txt = [(yl ^ y) * 4 + (z + d) % RING for d, y in parts]
        match = [txt.index(c % ROWS) if 2 * row + c // ROWS == col else -1 for c in img]
        table[device(yl, z, x, yh, k)] = img + match + txt + [k]
    return table


def cost(flops, bytes_accessed):
    return pl.CostEstimate(flops=flops, bytes_accessed=bytes_accessed, transcendentals=0)


def diagonal():
    shape = (PIECE, PIECE)
    return lax.broadcasted_iota(jnp.int32, shape, 0) == lax.broadcasted_iota(jnp.int32, shape, 1)


def unit_kernel(image_ref, text_ref, keep_ref, send_ref):
    core = lax.axis_index("col") % 2

    def unit(src):
        x = src[...]
        return (x / jnp.sqrt(jnp.sum(x * x, axis=1, keepdims=True) + 1e-06)).astype(BF)

    image, text = unit(image_ref), unit(text_ref)

    @pl.when(core == 0)
    def _():
        keep_ref[...] = image
        send_ref[...] = text

    @pl.when(core == 1)
    def _():
        keep_ref[...] = text
        send_ref[...] = image


def unit_pair(image, text):
    shape = jax.ShapeDtypeStruct((PIECE, WIDTH), BF)
    return pl.pallas_call(
        unit_kernel, out_shape=(shape, shape), in_specs=[VM, VM], out_specs=(VM, VM),
        compiler_params=PARAMS, name="unit_rows",
    )(image, text)


def forward_kernel(ids, *refs):
    here, there = refs[:PARTS], refs[PARTS:2 * PARTS]
    h_out, img, txt, keep, send = refs[2 * PARTS:2 * PARTS + 5]
    even, odd, racc, cacc, rs, cs, dg = refs[2 * PARTS + 5:]
    core = ids[CORE]

    @pl.when(core == 0)
    def _():
        for m in range(PARTS):
            img[m * PART:(m + 1) * PART, :] = here[m][...]
            txt[m * PIECE:(m + 1) * PIECE, :] = there[m][:PIECE, :]

    @pl.when(core == 1)
    def _():
        for m in range(PARTS):
            img[m * PART:(m + 1) * PART, :] = there[m][...]
            txt[m * PIECE:(m + 1) * PIECE, :] = here[m][PIECE:, :]

    for ref in (racc, cacc, rs, cs, dg, keep, send):
        ref[...] = jnp.zeros_like(ref)
    held = (even, odd)
    half_rows = IMG // 2
    tiles = [(n, u) for n in range(TXT // 256) for u in range(2)]

    def epilogue(t):
        n, u = tiles[t]
        cols = slice(n * 256, n * 256 + 256)
        total = jnp.zeros((8, 256), F32)
        for p in range(half_rows // PIECE):
            d = held[t % 2][p * PIECE:(p + 1) * PIECE, :]
            h = jnp.exp2(d * (50.0 * LOG2E) - (0.5 * SHIFT * LOG2E))
            at = u * half_rows + p * PIECE
            h_out[at:at + PIECE, cols] = h
            q = h * h
            racc[at:at + PIECE, :] += q[:, :PIECE] + q[:, PIECE:]
            total += jnp.sum(q.reshape(16, 8, 256), axis=0)
        cacc[:, cols] += total

    for t, (n, u) in enumerate(tiles):
        held[t % 2][...] = dot(
            img[u * half_rows:(u + 1) * half_rows, :], txt[n * 256:n * 256 + 256, :], NT
        )
        if t:
            epilogue(t - 1)
    epilogue(len(tiles) - 1)

    lowest = jnp.full((1, PIECE), jnp.inf, F32)
    for p in range(COLS):
        part = jnp.sum(racc[p * PIECE:(p + 1) * PIECE, :].T, axis=0, keepdims=True)
        rs[0, pl.ds(ids[p], 1), :] = part
        lowest = jnp.minimum(lowest, part)
    total = jnp.sum(cacc[...], axis=0, keepdims=True)
    for m in range(PARTS):
        part = total[:, m * PIECE:(m + 1) * PIECE]
        cs[0, pl.ds(ids[TXT_AT + m], 1), :] = part
        lowest = jnp.minimum(lowest, part)

    @pl.when(jnp.min(lowest) < FLOOR)
    def _():
        for p in range(COLS):
            rows = pl.ds(p * PIECE, PIECE)
            part = jnp.zeros((PIECE, PIECE), F32)
            for m in range(PARTS):
                g = h_out[rows, m * PIECE:(m + 1) * PIECE] * math.exp(0.5 * (SHIFT + LIFT))
                part += g * g
                cs[1, pl.ds(ids[TXT_AT + m], 1), :] += jnp.sum(g * g, axis=0, keepdims=True)
            rs[1, pl.ds(ids[p], 1), :] = jnp.sum(part.T, axis=0, keepdims=True)

    for p in range(COLS):
        match = ids[MATCH_AT + p]

        @pl.when(match >= 0)
        def _():
            other = txt[pl.ds(pl.multiple_of(match * PIECE, PIECE), PIECE), :]
            s = 100.0 * dot(img[p * PIECE:(p + 1) * PIECE, :], other, NT)
            dg[...] += jnp.sum(jnp.where(diagonal(), s, 0.0).reshape(16, 8, PIECE), axis=0)

    @pl.when(core == 0)
    def _():
        keep[0:2] = rs[...]
        keep[2, 0:8] = dg[...]
        send[0:2, 0:8] = cs[...]

    @pl.when(core == 1)
    def _():
        send[0:2] = rs[...]
        send[2, 0:8] = dg[...]
        keep[0:2, 8:16] = cs[...]


def forward(ids, here, there):
    sums = jax.ShapeDtypeStruct((3, COLS, PIECE), F32)
    return pl.pallas_call(
        forward_kernel,
        out_shape=(
            jax.ShapeDtypeStruct((IMG, TXT), F32),
            jax.ShapeDtypeStruct((IMG, WIDTH), BF),
            jax.ShapeDtypeStruct((TXT, WIDTH), BF),
            sums, sums,
        ),
        in_specs=[SM] + [VM] * (2 * PARTS),
        out_specs=(VM,) * 5,
        scratch_shapes=[
            pltpu.VMEM((IMG // 2, 256), F32),
            pltpu.VMEM((IMG // 2, 256), F32),
            pltpu.VMEM((IMG, PIECE), F32),
            pltpu.VMEM((8, TXT), F32),
            pltpu.VMEM((2, COLS, PIECE), F32),
            pltpu.VMEM((2, ROWS, PIECE), F32),
            pltpu.VMEM((8, PIECE), F32),
        ],
        compiler_params=PARAMS,
        cost_estimate=cost(2 * IMG * TXT * WIDTH, 30 << 20),
        name="pair_scores",
    )(ids, *here, *there)


def lse_of(sums):
    return jnp.where(sums[0] >= FLOOR, SHIFT + jnp.log(sums[0]), jnp.log(sums[1]) - LIFT)


def product_kernel(first, ids, own, far, half, img, txt, *refs):
    outs = refs[:PARTS]
    w, a_s, b_s = refs[PARTS:]
    core = ids[CORE]
    scale = math.sqrt(0.5)
    rows_at_core0 = core == 0
    factors = [scale * jnp.exp(0.5 * (SHIFT - lse_of(v))) for v in (own, far)]
    a_s[...] = jnp.where(rows_at_core0, factors[0], factors[1])
    b_s[...] = jnp.where(rows_at_core0, factors[1][:8], factors[0][8:])
    half_pieces = COLS // 2

    def weights(turned):
        @pl.loop(0, half_pieces)
        def _(i):
            at = pl.ds(pl.multiple_of(i * PIECE, PIECE), PIECE)
            for u in range(2):
                p = u * half_pieces + i
                rows = pl.ds(pl.multiple_of(p * PIECE, PIECE), PIECE)
                a = jnp.broadcast_to(a_s[pl.ds(ids[p], 1), :], (PIECE, PIECE)).T

                def put(cols, value):
                    if turned:
                        w[u, cols, at] = value.T.astype(BF)
                    else:
                        w[u, at, cols] = value.astype(BF)

                for m in range(PARTS):
                    cols = slice(m * PIECE, (m + 1) * PIECE)
                    h = half[rows, cols]
                    v, t = h * a, h * b_s[pl.ds(ids[TXT_AT + m], 1), :]
                    put(cols, v * v + t * t)
                match = ids[MATCH_AT + p]

                @pl.when(match >= 0)
                def _():
                    cols = pl.ds(pl.multiple_of(match * PIECE, PIECE), PIECE)
                    h = half[rows, cols]
                    v, t = h * a, h * b_s[pl.ds(ids[TXT_AT + match], 1), :]
                    put(cols, v * v + t * t - diagonal().astype(F32))

    def image_side():
        weights(False)
        for n in range(WIDTH // 256):
            cols = slice(n * 256, n * 256 + 256)
            for u in range(2):
                d = dot(w[u], txt[:, cols], NN)
                for i in range(PARTS // 2):
                    out = outs[u * PARTS // 2 + i]
                    out[:, cols] = d[i * PART:(i + 1) * PART].astype(out.dtype)

    def text_side(at, pad):
        weights(True)
        for out in outs:
            out[pad:pad + PIECE, :] = jnp.zeros((PIECE, WIDTH), out.dtype)
        for n in range(WIDTH // 256):
            cols = slice(n * 256, n * 256 + 256)
            d = dot(w[0], img[:IMG // 2, cols], NN) + dot(w[1], img[IMG // 2:, cols], NN)
            for m, out in enumerate(outs):
                out[at:at + PIECE, cols] = d[m * PIECE:(m + 1) * PIECE].astype(out.dtype)

    pl.when(core == (1 if first else 0))(image_side)
    if first:
        pl.when(core == 0)(lambda: text_side(0, PIECE))
    else:
        pl.when(core == 1)(lambda: text_side(PIECE, 0))


def products(first, ids, own, far, half, img, txt):
    return pl.pallas_call(
        functools.partial(product_kernel, first),
        out_shape=tuple(
            jax.ShapeDtypeStruct((PART, WIDTH), F32 if m == 0 and not first else BF)
            for m in range(PARTS)
        ),
        in_specs=[SM] + [VM] * 5,
        out_specs=(VM,) * PARTS,
        scratch_shapes=[
            pltpu.VMEM((2, IMG // 2, TXT), BF),
            pltpu.VMEM((COLS, PIECE), F32),
            pltpu.VMEM((ROWS, PIECE), F32),
        ],
        compiler_params=PARAMS,
        cost_estimate=cost(2 * IMG * TXT * WIDTH, 24 << 20),
        name="products_sent" if first else "products_kept",
    )(ids, own, far, half, img, txt)


def sum_kernel(own, kept, sent, *refs):
    parts, (keep, send) = refs[:-2], refs[-2:]
    core = lax.axis_index("col") % 2
    total = own[...] + kept[...].astype(F32) + sent[...].astype(F32)
    for r in parts:
        total = total + r[...].astype(F32)

    @pl.when(core == 0)
    def _():
        keep[...] = total[:PIECE]
        send[...] = total[PIECE:]

    @pl.when(core == 1)
    def _():
        keep[...] = total[PIECE:]
        send[...] = total[:PIECE]


def grad_kernel(image, text, keep, got, image_out, text_out):
    core = lax.axis_index("col") % 2

    def grad(values, total, out):
        x = values[...]
        norm = jnp.sqrt(jnp.sum(x * x, axis=1, keepdims=True) + 1e-06)
        unit = x / norm
        g = total[...]
        out[...] = (g - unit * jnp.sum(unit * g, axis=1, keepdims=True)) / norm

    @pl.when(core == 0)
    def _():
        grad(image, keep, image_out)
        grad(text, got, text_out)

    @pl.when(core == 1)
    def _():
        grad(image, got, image_out)
        grad(text, keep, text_out)


def per_device(image_embeds, text_embeds):
    here = lax.axis_index("row") * COLS + lax.axis_index("col")
    ids = lax.dynamic_index_in_dim(jnp.asarray(device_table()), here, keepdims=False)
    first = lax.axis_index("col") % 2 == 0

    keep, send = unit_pair(image_embeds, text_embeds)
    got = swap(send)
    own = jnp.concatenate([jnp.where(first, keep, got), jnp.where(first, got, keep)])

    other = flip(own)
    left0, right0 = ring(own, 1), ring(own, 3)
    left1, right1 = ring(other, 1), ring(other, 3)
    far0, far1 = ring(left0, 1), ring(right1, 3)
    mine = [own, other, right0, right1, far0, far1, left0, left1]
    theirs = [swap(v) for v in mine]

    half, img, txt, keep, send = forward(ids, mine, theirs)
    sums = keep + swap(send)
    sums = sums + ring(sums, 1) + ring(sums, 2) + ring(sums, 3)
    sums = sums + flip(sums)
    theirs = swap(sums)

    sent = [swap(v) for v in products(True, ids, sums, theirs, half, img, txt)]
    kept = products(False, ids, sums, theirs, half, img, txt)

    add = lambda *v: functools.reduce(lambda a, b: a + b, [u.astype(F32) for u in v]).astype(BF)
    through0, through1 = ring(add(kept[4], sent[4]), 1), ring(add(kept[5], sent[5]), 3)
    right1, left0 = ring(add(kept[3], sent[3]), 1), ring(add(kept[6], sent[6]), 3)
    right0 = ring(add(kept[2], sent[2], through0), 1)
    left1 = ring(add(kept[7], sent[7], through1), 3)
    lse = lse_of(theirs).reshape(2, 8, PIECE).sum(0)
    lse = jnp.where(first, lse, lse - 2.0 * theirs[2, :8])
    lse = lse + ring(lse, 1) + ring(lse, 2) + ring(lse, 3)
    last, lse = lax.optimization_barrier((add(kept[1], sent[1], right1, left1), lse))
    back, there = flip(last), flip(lse)
    shape = jax.ShapeDtypeStruct((PIECE, WIDTH), F32)
    keep, send = pl.pallas_call(
        sum_kernel, out_shape=(shape, shape), in_specs=[VM] * 5, out_specs=(VM, VM),
        compiler_params=PARAMS, name="own_sums",
    )(kept[0], sent[0], right0, left0, back)
    send, lse = lax.optimization_barrier((send, lse + there))
    got, there = swap(send), swap(lse)
    image_grad, text_grad = pl.pallas_call(
        grad_kernel, out_shape=(shape, shape), in_specs=[VM] * 4, out_specs=(VM, VM),
        compiler_params=PARAMS, name="grad_rows",
    )(image_embeds, text_embeds, keep, got)
    loss = jnp.sum(lse + there) / (2.0 * ROWS * COLS * PIECE)
    return (image_grad, text_grad, loss)


def solution(mesh):
    return jax.shard_map(
        per_device,
        mesh=mesh,
        in_specs=(P(("row", "col"), None), P(("col", "row"), None)),
        out_specs=(P(("row", "col"), None), P(("col", "row"), None), P()),
        check_vma=False,
    )
```

```python
import functools
import math

import jax
import jax.numpy as jnp
import numpy as np
from jax import lax
from jax.experimental import pallas as pl
from jax.experimental.pallas import tpu as pltpu
from jax.sharding import PartitionSpec as P

PIECE = 128
PART = 2 * PIECE
WIDTH = 1280
RING = 4
PART_AT = ((2, 0), (2, 1), (1, 1), (3, 0), (1, 0), (3, 1), (0, 1), (0, 0))
PARTS = len(PART_AT)
ROWS, COLS = 8, 16
IMG = PARTS * PART
TXT = PARTS * PIECE
CORE, TXT_AT, MATCH_AT = 40, 32, 16

SHIFT = 22.0
LIFT = 70.0
FLOOR = math.exp(-62.0)
LOG2E = math.log2(math.e)

VM = pl.BlockSpec(memory_space=pltpu.VMEM)
SM = pl.BlockSpec(memory_space=pltpu.SMEM)
PARAMS = pltpu.CompilerParams(vmem_limit_bytes=20 * 1024 * 1024)
F32, BF = jnp.float32, jnp.bfloat16
NT = (((1,), (1,)), ((), ()))
NN = (((1,), (0,)), ((), ()))
TN = (((0,), (0,)), ((), ()))
AXES = ("row", "col")


def dot(a, b, dims):
    return lax.dot_general(a, b, dims, preferred_element_type=F32)


def device(yl, z, x, yh, k):
    return (yl * 4 + z) * COLS + (x * 2 + yh) * 2 + k


def places():
    return [
        (yl, z, x, yh, k)
        for yl in range(2) for z in range(RING) for x in range(RING) for yh in range(2) for k in range(2)
    ]


def ring(value, d):
    return lax.ppermute(value, AXES, [
        (device(yl, z, x, yh, k),
         device(yl, (z + d * k) % RING, (x + d * (1 - k)) % RING, yh, k))
        for yl, z, x, yh, k in places()
    ])


def neighbour(y, k):
    return y ^ 1 if k == 0 else (y + (1 if y % 2 else 3)) % RING


def flip(value):
    pairs = []
    for yl, z, x, yh, k in places():
        y = neighbour(yh * 2 + yl, k)
        pairs.append((device(yl, z, x, yh, k), device(y % 2, z, x, y // 2, k)))
    return lax.ppermute(value, AXES, pairs)


def swap(value):
    return lax.ppermute(value, AXES, [
        (device(yl, z, x, yh, k), device(yl, z, x, yh, 1 - k)) for yl, z, x, yh, k in places()
    ])


def device_table():
    table = np.zeros((ROWS * COLS, 41), np.int32)
    for yl, z, x, yh, k in places():
        y = yh * 2 + yl
        img, match, txt, owned = [], [], [], []
        for d, side in PART_AT:
            zt, yt = (z + d) % RING, neighbour(y, 1) if side else y
            txt.append(zt * 2 + (yt + 1) % 2)
            owner = device(yt % 2, zt, x, yt // 2, k)
            owned.append(owner % COLS * ROWS + owner // COLS)
        for d, side in PART_AT:
            xi, yi = (x + d) % RING, neighbour(y, 0) if side else y
            for h in range(2):
                img.append((xi * 2 + yi % 2) * 2 + h)
                piece = device(yi % 2, z, xi, yi // 2, h)
                match.append(owned.index(piece) if piece in owned else -1)
        table[device(yl, z, x, yh, k)] = img + match + txt + [k]
    return table


def cost(flops, bytes_accessed):
    return pl.CostEstimate(flops=flops, bytes_accessed=bytes_accessed, transcendentals=0)


def diagonal():
    shape = (PIECE, PIECE)
    return lax.broadcasted_iota(jnp.int32, shape, 0) == lax.broadcasted_iota(jnp.int32, shape, 1)


def unit_kernel(image_hbm, text_hbm, keep_ref, send_ref, image, text, sems):
    copies = []
    for i, (src, dst) in enumerate(((image_hbm, image), (text_hbm, text))):
        for j in range(4):
            rows = pl.ds(j * 32, 32)
            copies.append(pltpu.make_async_copy(src.at[rows], dst.at[rows], sems.at[i * 4 + j]))
    for c in copies:
        c.start()
    core = lax.axis_index("col") % 2

    def unit(src, done):
        for c in done:
            c.wait()
        x = src[...]
        return (x / jnp.sqrt(jnp.sum(x * x, axis=1, keepdims=True) + 1e-06)).astype(BF)

    image_unit, text_unit = unit(image, copies[:4]), unit(text, copies[4:])

    @pl.when(core == 0)
    def _():
        keep_ref[...] = image_unit
        send_ref[...] = text_unit

    @pl.when(core == 1)
    def _():
        keep_ref[...] = text_unit
        send_ref[...] = image_unit


def unit_pair(image, text):
    shape = jax.ShapeDtypeStruct((PIECE, WIDTH), BF)
    hbm = pl.BlockSpec(memory_space=pltpu.HBM)
    return pl.pallas_call(
        unit_kernel, out_shape=(shape, shape), in_specs=[hbm, hbm], out_specs=(VM, VM),
        scratch_shapes=[
            pltpu.VMEM((PIECE, WIDTH), F32), pltpu.VMEM((PIECE, WIDTH), F32),
            pltpu.SemaphoreType.DMA((8,)),
        ],
        compiler_params=PARAMS, name="unit_rows",
    )(image, text)


def forward_kernel(ids, *refs):
    here, there = refs[:PARTS], refs[PARTS:2 * PARTS]
    h_out, img, txt, keep, send = refs[2 * PARTS:2 * PARTS + 5]
    even, odd, racc, cacc, rs, cs, dg = refs[2 * PARTS + 5:]
    core = ids[CORE]

    @pl.when(core == 0)
    def _():
        for m in range(PARTS):
            img[m * PART:(m + 1) * PART, :] = here[m][...]
            txt[m * PIECE:(m + 1) * PIECE, :] = there[m][:PIECE, :]

    @pl.when(core == 1)
    def _():
        for m in range(PARTS):
            img[m * PART:(m + 1) * PART, :] = there[m][...]
            txt[m * PIECE:(m + 1) * PIECE, :] = here[m][PIECE:, :]

    for ref in (racc, cacc, rs, cs, dg, keep, send):
        ref[...] = jnp.zeros_like(ref)
    held = (even, odd)
    half_rows = IMG // 2
    tiles = [(n, u) for n in range(TXT // 256) for u in range(2)]

    def epilogue(t):
        n, u = tiles[t]
        cols = slice(n * 256, n * 256 + 256)
        total = jnp.zeros((8, 256), F32)
        for p in range(half_rows // PIECE):
            d = held[t % 2][p * PIECE:(p + 1) * PIECE, :]
            h = jnp.exp2(d * (50.0 * LOG2E) - (0.5 * SHIFT * LOG2E))
            at = u * half_rows + p * PIECE
            h_out[at:at + PIECE, cols] = h
            q = h * h
            racc[at:at + PIECE, :] += q[:, :PIECE] + q[:, PIECE:]
            total += jnp.sum(q.reshape(16, 8, 256), axis=0)
        cacc[:, cols] += total

    for t, (n, u) in enumerate(tiles):
        held[t % 2][...] = dot(
            img[u * half_rows:(u + 1) * half_rows, :], txt[n * 256:n * 256 + 256, :], NT
        )
        if t:
            epilogue(t - 1)
    epilogue(len(tiles) - 1)

    lowest = jnp.full((1, PIECE), jnp.inf, F32)
    for p in range(COLS):
        part = jnp.sum(racc[p * PIECE:(p + 1) * PIECE, :].T, axis=0, keepdims=True)
        rs[0, pl.ds(ids[p], 1), :] = part
        lowest = jnp.minimum(lowest, part)
    total = jnp.sum(cacc[...], axis=0, keepdims=True)
    for m in range(PARTS):
        part = total[:, m * PIECE:(m + 1) * PIECE]
        cs[0, pl.ds(ids[TXT_AT + m], 1), :] = part
        lowest = jnp.minimum(lowest, part)

    @pl.when(jnp.min(lowest) < FLOOR)
    def _():
        for p in range(COLS):
            rows = pl.ds(p * PIECE, PIECE)
            part = jnp.zeros((PIECE, PIECE), F32)
            for m in range(PARTS):
                g = h_out[rows, m * PIECE:(m + 1) * PIECE] * math.exp(0.5 * (SHIFT + LIFT))
                part += g * g
                cs[1, pl.ds(ids[TXT_AT + m], 1), :] += jnp.sum(g * g, axis=0, keepdims=True)
            rs[1, pl.ds(ids[p], 1), :] = jnp.sum(part.T, axis=0, keepdims=True)

    for p in range(COLS):
        match = ids[MATCH_AT + p]

        @pl.when(match >= 0)
        def _():
            other = txt[pl.ds(pl.multiple_of(match * PIECE, PIECE), PIECE), :]
            s = 100.0 * dot(img[p * PIECE:(p + 1) * PIECE, :], other, NT)
            dg[...] += jnp.sum(jnp.where(diagonal(), s, 0.0).reshape(16, 8, PIECE), axis=0)

    @pl.when(core == 0)
    def _():
        keep[0:2] = rs[...]
        keep[2, 0:8] = dg[...]
        send[0:2, 0:8] = cs[...]

    @pl.when(core == 1)
    def _():
        send[0:2] = rs[...]
        send[2, 0:8] = dg[...]
        keep[0:2, 8:16] = cs[...]


def forward(ids, here, there):
    sums = jax.ShapeDtypeStruct((3, COLS, PIECE), F32)
    return pl.pallas_call(
        forward_kernel,
        out_shape=(
            jax.ShapeDtypeStruct((IMG, TXT), F32),
            jax.ShapeDtypeStruct((IMG, WIDTH), BF),
            jax.ShapeDtypeStruct((TXT, WIDTH), BF),
            sums, sums,
        ),
        in_specs=[SM] + [VM] * (2 * PARTS),
        out_specs=(VM,) * 5,
        scratch_shapes=[
            pltpu.VMEM((IMG // 2, 256), F32),
            pltpu.VMEM((IMG // 2, 256), F32),
            pltpu.VMEM((IMG, PIECE), F32),
            pltpu.VMEM((8, TXT), F32),
            pltpu.VMEM((2, COLS, PIECE), F32),
            pltpu.VMEM((2, ROWS, PIECE), F32),
            pltpu.VMEM((8, PIECE), F32),
        ],
        compiler_params=PARAMS,
        cost_estimate=cost(2 * IMG * TXT * WIDTH, 30 << 20),
        name="pair_scores",
    )(ids, *here, *there)


def lse_of(sums):
    return jnp.where(sums[0] >= FLOOR, SHIFT + jnp.log(sums[0]), jnp.log(sums[1]) - LIFT)


def weights_kernel(ids, own, far, half, w, a_s, b_s):
    scale = math.sqrt(0.5)
    core0 = ids[CORE] == 0
    factors = [scale * jnp.exp(0.5 * (SHIFT - lse_of(v))) for v in (own, far)]
    a_s[...] = jnp.where(core0, factors[0], factors[1])
    b_s[...] = jnp.where(core0, factors[1][:8], factors[0][8:])
    b = [b_s[pl.ds(ids[TXT_AT + m], 1), :] for m in range(PARTS)]

    @pl.loop(0, COLS)
    def _(p):
        rows = pl.ds(pl.multiple_of(p * PIECE, PIECE), PIECE)
        a = jnp.broadcast_to(a_s[pl.ds(ids[p], 1), :], (PIECE, PIECE)).T
        for m in range(PARTS):
            cols = slice(m * PIECE, (m + 1) * PIECE)
            h = half[rows, cols]
            v, t = h * a, h * b[m]
            w[rows, cols] = (v * v + t * t).astype(BF)
        match = ids[MATCH_AT + p]

        @pl.when(match >= 0)
        def _():
            cols = pl.ds(pl.multiple_of(match * PIECE, PIECE), PIECE)
            h = half[rows, cols]
            v, t = h * a, h * b_s[pl.ds(ids[TXT_AT + match], 1), :]
            w[rows, cols] = (v * v + t * t - diagonal().astype(F32)).astype(BF)


def product_kernel(start, end, kept_here, core, w, img, txt, out):
    def image_side():
        out[...] = dot(w[start * PART:end * PART, :], txt[...], NN).astype(BF)

    def text_side():
        at, pad = (PIECE, 0) if kept_here else (0, PIECE)
        d = dot(w[:, start * PIECE:end * PIECE], img[...], TN).astype(BF)
        for i in range(end - start):
            out[i * PART + at:i * PART + at + PIECE, :] = d[i * PIECE:(i + 1) * PIECE]
            out[i * PART + pad:i * PART + pad + PIECE, :] = jnp.zeros((PIECE, WIDTH), BF)

    pl.when(core == (0 if kept_here else 1))(image_side)
    pl.when(core == (1 if kept_here else 0))(text_side)


def first_products(end, ids, own, far, half, img, txt):
    def kernel(ids, own, far, half, img, txt, w, out, a_s, b_s):
        weights_kernel(ids, own, far, half, w, a_s, b_s)
        product_kernel(0, end, False, ids[CORE], w, img, txt, out)

    return pl.pallas_call(
        kernel,
        out_shape=(
            jax.ShapeDtypeStruct((IMG, TXT), BF),
            jax.ShapeDtypeStruct((end * PART, WIDTH), BF),
        ),
        in_specs=[SM] + [VM] * 5,
        out_specs=(VM, VM),
        scratch_shapes=[pltpu.VMEM((COLS, PIECE), F32), pltpu.VMEM((ROWS, PIECE), F32)],
        compiler_params=PARAMS,
        cost_estimate=cost(5 * 10**10, 1),
        name="weights_products",
    )(ids, own, far, half, img, txt)


def products(start, end, kept_here, ids, w, img, txt):
    def kernel(ids, w, img, txt, out):
        product_kernel(start, end, kept_here, ids[CORE], w, img, txt, out)

    return pl.pallas_call(
        kernel,
        out_shape=jax.ShapeDtypeStruct(((end - start) * PART, WIDTH), BF),
        in_specs=[SM] + [VM] * 3,
        out_specs=VM,
        compiler_params=PARAMS,
        cost_estimate=cost(5 * 10**10, 1),
        name="products_kept" if kept_here else "products_sent",
    )(ids, w, img, txt)


def sum_kernel(own, kept, sent, *refs):
    parts, (keep, send) = refs[:-2], refs[-2:]
    core = lax.axis_index("col") % 2
    total = own[...].astype(F32) + kept[...].astype(F32) + sent[...].astype(F32)
    for r in parts:
        total = total + r[...].astype(F32)

    @pl.when(core == 0)
    def _():
        keep[...] = total[:PIECE]
        send[...] = total[PIECE:]

    @pl.when(core == 1)
    def _():
        keep[...] = total[PIECE:]
        send[...] = total[:PIECE]


def grad_kernel(image, text, keep, got, image_out, text_out):
    core = lax.axis_index("col") % 2

    def grad(values, total, out):
        x = values[...]
        norm = jnp.sqrt(jnp.sum(x * x, axis=1, keepdims=True) + 1e-06)
        unit = x / norm
        g = total[...]
        out[...] = (g - unit * jnp.sum(unit * g, axis=1, keepdims=True)) / norm

    @pl.when(core == 0)
    def _():
        grad(image, keep, image_out)
        grad(text, got, text_out)

    @pl.when(core == 1)
    def _():
        grad(image, got, image_out)
        grad(text, keep, text_out)


def per_device(image_embeds, text_embeds):
    here = lax.axis_index("row") * COLS + lax.axis_index("col")
    ids = lax.dynamic_index_in_dim(jnp.asarray(device_table()), here, keepdims=False)
    first = lax.axis_index("col") % 2 == 0

    keep, send = unit_pair(image_embeds, text_embeds)
    got = swap(send)
    own = jnp.concatenate([jnp.where(first, keep, got), jnp.where(first, got, keep)])

    other = flip(own)
    left0, right0 = ring(own, 1), ring(own, 3)
    left1, right1 = ring(other, 1), ring(other, 3)
    far0, far1 = ring(left0, 1), ring(right1, 3)
    mine = [far0, far1, right1, left0, right0, left1, other, own]
    theirs = [swap(v) for v in mine]

    half, img, txt, keep, send = forward(ids, mine, theirs)
    sums = keep + swap(send)
    sums = sums + ring(sums, 1) + ring(sums, 2) + ring(sums, 3)
    sums = sums + flip(sums)
    theirs = swap(sums)

    def add(*v):
        return functools.reduce(lambda a, b: a + b, [u.astype(F32) for u in v]).astype(BF)

    def part(value, i):
        return value[i * PART:(i + 1) * PART]

    weights, sent = first_products(2, ids, sums, theirs, half, img, txt)
    lse = lse_of(theirs).reshape(2, 8, PIECE).sum(0)
    lse = jnp.where(first, lse, lse - 2.0 * theirs[2, :8])
    sent, lse = lax.optimization_barrier((sent, lse))
    sent = swap(sent)
    lse = lse + ring(lse, 1) + ring(lse, 2) + ring(lse, 3)
    kept = products(0, 2, True, ids, weights, img, txt)
    far0, far1 = add(part(kept, 0), part(sent, 0)), add(part(kept, 1), part(sent, 1))
    weights, far0, far1, lse = lax.optimization_barrier((weights, far0, far1, lse))
    through0, through1 = ring(far0, 1), ring(far1, 3)

    sent = swap(products(2, 4, False, ids, weights, img, txt))
    kept = products(2, 4, True, ids, weights, img, txt)
    near, back = add(part(kept, 0), part(sent, 0)), add(part(kept, 1), part(sent, 1))
    weights, near, back = lax.optimization_barrier((weights, near, back))
    right1 = ring(near, 1)

    sent = swap(products(4, 6, False, ids, weights, img, txt))
    kept = products(4, 6, True, ids, weights, img, txt)
    near = add(part(kept, 0), part(sent, 0), through0)
    back1 = add(part(kept, 1), part(sent, 1), through1)
    weights, near, back, back1 = lax.optimization_barrier((weights, near, back, back1))
    left1, right0, left0 = ring(back1, 3), ring(near, 1), ring(back, 3)

    sent = swap(products(6, 8, False, ids, weights, img, txt))
    kept = products(6, 8, True, ids, weights, img, txt)
    last = add(part(kept, 0), part(sent, 0), right1, left1)
    back, there = flip(last), flip(lse)
    shape = jax.ShapeDtypeStruct((PIECE, WIDTH), F32)
    keep, send = pl.pallas_call(
        sum_kernel, out_shape=(shape, shape), in_specs=[VM] * 5, out_specs=(VM, VM),
        compiler_params=PARAMS, name="own_sums",
    )(part(kept, 1), part(sent, 1), right0, left0, back)
    send, lse = lax.optimization_barrier((send, lse + there))
    got, there = swap(send), swap(lse)
    image_grad, text_grad = pl.pallas_call(
        grad_kernel, out_shape=(shape, shape), in_specs=[VM] * 4, out_specs=(VM, VM),
        compiler_params=PARAMS, name="grad_rows",
    )(image_embeds, text_embeds, keep, got)
    loss = jnp.sum(lse + there) / (2.0 * ROWS * COLS * PIECE)
    return (image_grad, text_grad, loss)


def solution(mesh):
    return jax.shard_map(
        per_device,
        mesh=mesh,
        in_specs=(P(("row", "col"), None), P(("col", "row"), None)),
        out_specs=(P(("row", "col"), None), P(("col", "row"), None), P()),
        check_vma=False,
    )
```

```python
import functools
import math

import jax
import jax.numpy as jnp
import numpy as np
from jax import lax
from jax.experimental import pallas as pl
from jax.experimental.pallas import tpu as pltpu
from jax.sharding import PartitionSpec as P

PIECE = 128
PART = 2 * PIECE
WIDTH = 1280
RING = 4
PART_AT = ((2, 0), (2, 1), (1, 1), (3, 0), (1, 0), (3, 1), (0, 1), (0, 0))
PARTS = len(PART_AT)
FAR = 2
ROWS, COLS = 8, 16
IMG = PARTS * PART
TXT = PARTS * PIECE
FAR_IMG, FAR_TXT = FAR * PART, FAR * PIECE
NEAR_IMG, NEAR_TXT = IMG - FAR_IMG, TXT - FAR_TXT
CORE, TXT_AT, MATCH_AT = 40, 32, 16
PRODUCT_FLOPS = 50000000000

SHIFT = 22.0
LIFT = 70.0
FLOOR = math.exp(-62.0)
LOG2E = math.log2(math.e)

VM = pl.BlockSpec(memory_space=pltpu.VMEM)
SM = pl.BlockSpec(memory_space=pltpu.SMEM)
PARAMS = pltpu.CompilerParams(vmem_limit_bytes=20 * 1024 * 1024)
F32, BF = jnp.float32, jnp.bfloat16
NT = (((1,), (1,)), ((), ()))
NN = (((1,), (0,)), ((), ()))
TN = (((0,), (0,)), ((), ()))
AXES = ("row", "col")


def dot(a, b, dims):
    return lax.dot_general(a, b, dims, preferred_element_type=F32)


def device(yl, z, x, yh, k):
    return (yl * 4 + z) * COLS + (x * 2 + yh) * 2 + k


def places():
    return [
        (yl, z, x, yh, k)
        for yl in range(2) for z in range(RING) for x in range(RING) for yh in range(2) for k in range(2)
    ]


def ring(value, d):
    return lax.ppermute(value, AXES, [
        (device(yl, z, x, yh, k),
         device(yl, (z + d * k) % RING, (x + d * (1 - k)) % RING, yh, k))
        for yl, z, x, yh, k in places()
    ])


def neighbour(y, k):
    return y ^ 1 if k == 0 else (y + (1 if y % 2 else 3)) % RING


def flip(value):
    pairs = []
    for yl, z, x, yh, k in places():
        y = neighbour(yh * 2 + yl, k)
        pairs.append((device(yl, z, x, yh, k), device(y % 2, z, x, y // 2, k)))
    return lax.ppermute(value, AXES, pairs)


def swap(value):
    return lax.ppermute(value, AXES, [
        (device(yl, z, x, yh, k), device(yl, z, x, yh, 1 - k)) for yl, z, x, yh, k in places()
    ])


def device_table():
    table = np.zeros((ROWS * COLS, 41), np.int32)
    for yl, z, x, yh, k in places():
        y = yh * 2 + yl
        img, match, txt, owned = [], [], [], []
        for d, side in PART_AT:
            zt, yt = (z + d) % RING, neighbour(y, 1) if side else y
            txt.append(zt * 2 + (yt + 1) % 2)
            owner = device(yt % 2, zt, x, yt // 2, k)
            owned.append(owner % COLS * ROWS + owner // COLS)
        for d, side in PART_AT:
            xi, yi = (x + d) % RING, neighbour(y, 0) if side else y
            for h in range(2):
                img.append((xi * 2 + yi % 2) * 2 + h)
                piece = device(yi % 2, z, xi, yi // 2, h)
                match.append(owned.index(piece) if piece in owned else -1)
        table[device(yl, z, x, yh, k)] = img + match + txt + [k]
    return table


def cost(flops, bytes_accessed):
    return pl.CostEstimate(flops=flops, bytes_accessed=bytes_accessed, transcendentals=0)


def diagonal():
    shape = (PIECE, PIECE)
    return lax.broadcasted_iota(jnp.int32, shape, 0) == lax.broadcasted_iota(jnp.int32, shape, 1)


def unit_kernel(image_ref, text_ref, keep_ref, send_ref):
    core = lax.axis_index("col") % 2

    def unit(src):
        x = src[...]
        return (x / jnp.sqrt(jnp.sum(x * x, axis=1, keepdims=True) + 1e-06)).astype(BF)

    image, text = unit(image_ref), unit(text_ref)

    @pl.when(core == 0)
    def _():
        keep_ref[...] = image
        send_ref[...] = text

    @pl.when(core == 1)
    def _():
        keep_ref[...] = text
        send_ref[...] = image


def unit_pair(image, text):
    shape = jax.ShapeDtypeStruct((PIECE, WIDTH), BF)
    return pl.pallas_call(
        unit_kernel, out_shape=(shape, shape), in_specs=[VM, VM], out_specs=(VM, VM),
        compiler_params=PARAMS, name="unit_rows",
    )(image, text)


def place_parts(core, here, there, img, txt):
    @pl.when(core == 0)
    def _():
        for m, (mine, other) in enumerate(zip(here, there)):
            img[m * PART:(m + 1) * PART, :] = mine[...]
            txt[m * PIECE:(m + 1) * PIECE, :] = other[:PIECE, :]

    @pl.when(core == 1)
    def _():
        for m, (mine, other) in enumerate(zip(here, there)):
            img[m * PART:(m + 1) * PART, :] = other[...]
            txt[m * PIECE:(m + 1) * PIECE, :] = mine[PIECE:, :]


def score_tiles(tiles, img, txt, held, racc, cacc):
    def epilogue(t):
        row, rows, col, h_out, h_row, h_col = tiles[t]
        cols = slice(col, col + 256)
        total = jnp.zeros((8, 256), F32)
        for p in range(0, rows, PIECE):
            d = held[t % 2][p:p + PIECE, :]
            h = jnp.exp2(d * (50.0 * LOG2E) - (0.5 * SHIFT * LOG2E))
            h_out[h_row + p:h_row + p + PIECE, h_col:h_col + 256] = h
            q = h * h
            racc[row + p:row + p + PIECE, :] += q[:, :PIECE] + q[:, PIECE:]
            total += jnp.sum(q.reshape(16, 8, 256), axis=0)
        cacc[:, cols] += total

    for t, (row, rows, col, *_) in enumerate(tiles):
        held[t % 2][:rows, :] = dot(img[row:row + rows, :], txt[col:col + 256, :], NT)
        if t:
            epilogue(t - 1)
    epilogue(len(tiles) - 1)


def near_kernel(ids, *refs):
    count = PARTS - FAR
    here, there = refs[:count], refs[count:2 * count]
    h_out, img, txt, racc, cacc, even, odd = refs[2 * count:]
    place_parts(ids[CORE], here, there, img, txt)
    racc[...] = jnp.zeros_like(racc)
    cacc[...] = jnp.zeros_like(cacc)
    half = NEAR_IMG // 2
    tiles = [(r, half, c, h_out, r, c) for c in range(0, NEAR_TXT, 256) for r in (0, half)]
    score_tiles(tiles, img, txt, (even, odd), racc, cacc)


def near_scores(ids, here, there):
    return pl.pallas_call(
        near_kernel,
        out_shape=(
            jax.ShapeDtypeStruct((NEAR_IMG, NEAR_TXT), F32),
            jax.ShapeDtypeStruct((NEAR_IMG, WIDTH), BF),
            jax.ShapeDtypeStruct((NEAR_TXT, WIDTH), BF),
            jax.ShapeDtypeStruct((NEAR_IMG, PIECE), F32),
            jax.ShapeDtypeStruct((8, NEAR_TXT), F32),
        ),
        in_specs=[SM] + [VM] * (2 * len(here)),
        out_specs=(VM,) * 5,
        scratch_shapes=[pltpu.VMEM((NEAR_IMG // 2, 256), F32)] * 2,
        compiler_params=PARAMS,
        cost_estimate=cost(2 * NEAR_IMG * NEAR_TXT * WIDTH, 16 << 20),
        name="near_scores",
    )(ids, *here, *there)


def far_kernel(ids, here0, here1, there0, there1, near, near_img, near_txt, near_racc, near_cacc,
               h_rows, h_cols, img, txt, keep, send, even, odd, racc, cacc, rs, cs, dg):
    core = ids[CORE]
    place_parts(core, (here0, here1), (there0, there1), img, txt)
    img[FAR_IMG:, :] = near_img[...]
    txt[FAR_TXT:, :] = near_txt[...]
    racc[:FAR_IMG, :] = jnp.zeros((FAR_IMG, PIECE), F32)
    racc[FAR_IMG:, :] = near_racc[...]
    cacc[:, :FAR_TXT] = jnp.zeros((8, FAR_TXT), F32)
    cacc[:, FAR_TXT:] = near_cacc[...]
    for ref in (rs, cs, dg, keep, send):
        ref[...] = jnp.zeros_like(ref)
    half = NEAR_IMG // 2
    tiles = [(FAR_IMG + r, half, 0, h_cols, r, 0) for r in (0, half)]
    tiles += [(0, FAR_IMG, c, h_rows, 0, c) for c in range(0, TXT, 256)]
    score_tiles(tiles, img, txt, (even, odd), racc, cacc)

    lowest = jnp.full((1, PIECE), jnp.inf, F32)
    for p in range(COLS):
        part = jnp.sum(racc[p * PIECE:(p + 1) * PIECE, :].T, axis=0, keepdims=True)
        rs[0, pl.ds(ids[p], 1), :] = part
        lowest = jnp.minimum(lowest, part)
    total = jnp.sum(cacc[...], axis=0, keepdims=True)
    for m in range(PARTS):
        part = total[:, m * PIECE:(m + 1) * PIECE]
        cs[0, pl.ds(ids[TXT_AT + m], 1), :] = part
        lowest = jnp.minimum(lowest, part)

    def half_of(p, m):
        at = p * PIECE if p < 2 * FAR else (p - 2 * FAR) * PIECE
        if p < 2 * FAR:
            return h_rows[at:at + PIECE, m * PIECE:(m + 1) * PIECE]
        if m < FAR:
            return h_cols[at:at + PIECE, m * PIECE:(m + 1) * PIECE]
        return near[at:at + PIECE, (m - FAR) * PIECE:(m - FAR + 1) * PIECE]

    @pl.when(jnp.min(lowest) < FLOOR)
    def _():
        for p in range(COLS):
            part = jnp.zeros((PIECE, PIECE), F32)
            for m in range(PARTS):
                g = half_of(p, m) * math.exp(0.5 * (SHIFT + LIFT))
                part += g * g
                cs[1, pl.ds(ids[TXT_AT + m], 1), :] += jnp.sum(g * g, axis=0, keepdims=True)
            rs[1, pl.ds(ids[p], 1), :] = jnp.sum(part.T, axis=0, keepdims=True)

    for p in range(COLS):
        match = ids[MATCH_AT + p]

        @pl.when(match >= 0)
        def _():
            other = txt[pl.ds(pl.multiple_of(match * PIECE, PIECE), PIECE), :]
            s = 100.0 * dot(img[p * PIECE:(p + 1) * PIECE, :], other, NT)
            dg[...] += jnp.sum(jnp.where(diagonal(), s, 0.0).reshape(16, 8, PIECE), axis=0)

    @pl.when(core == 0)
    def _():
        keep[0:2] = rs[...]
        keep[2, 0:8] = dg[...]
        send[0:2, 0:8] = cs[...]

    @pl.when(core == 1)
    def _():
        send[0:2] = rs[...]
        send[2, 0:8] = dg[...]
        keep[0:2, 8:16] = cs[...]


def far_scores(ids, here, there, near):
    sums = jax.ShapeDtypeStruct((3, COLS, PIECE), F32)
    return pl.pallas_call(
        far_kernel,
        out_shape=(
            jax.ShapeDtypeStruct((FAR_IMG, TXT), F32),
            jax.ShapeDtypeStruct((NEAR_IMG, FAR_TXT), F32),
            jax.ShapeDtypeStruct((IMG, WIDTH), BF),
            jax.ShapeDtypeStruct((TXT, WIDTH), BF),
            sums, sums,
        ),
        in_specs=[SM] + [VM] * 9,
        out_specs=(VM,) * 6,
        scratch_shapes=[
            pltpu.VMEM((NEAR_IMG // 2, 256), F32),
            pltpu.VMEM((NEAR_IMG // 2, 256), F32),
            pltpu.VMEM((IMG, PIECE), F32),
            pltpu.VMEM((8, TXT), F32),
            pltpu.VMEM((2, COLS, PIECE), F32),
            pltpu.VMEM((2, ROWS, PIECE), F32),
            pltpu.VMEM((8, PIECE), F32),
        ],
        compiler_params=PARAMS,
        cost_estimate=cost(2 * (IMG * TXT - NEAR_IMG * NEAR_TXT) * WIDTH, 16 << 20),
        name="far_scores",
    )(ids, *here, *there, *near)


def lse_of(sums):
    return jnp.where(sums[0] >= FLOOR, SHIFT + jnp.log(sums[0]), jnp.log(sums[1]) - LIFT)


def row_col_factors(core, own, far, a_s, b_s):
    scale = math.sqrt(0.5)
    factors = [scale * jnp.exp(0.5 * (SHIFT - lse_of(v))) for v in (own, far)]
    a_s[...] = jnp.where(core == 0, factors[0], factors[1])
    b_s[...] = jnp.where(core == 0, factors[1][:8], factors[0][8:])


def weights_block(ids, half, w, a_s, b_s, p0, p1, m0, m1):
    b = [b_s[pl.ds(ids[TXT_AT + m], 1), :] for m in range(m0, m1)]

    @pl.loop(p0, p1)
    def _(p):
        rows = pl.ds(pl.multiple_of((p - p0) * PIECE, PIECE), PIECE)
        a = jnp.broadcast_to(a_s[pl.ds(ids[p], 1), :], (PIECE, PIECE)).T
        for m in range(m1 - m0):
            cols = slice(m * PIECE, (m + 1) * PIECE)
            h = half[rows, cols]
            v, t = h * a, h * b[m]
            w[rows, cols] = (v * v + t * t).astype(BF)
        match = ids[MATCH_AT + p]

        @pl.when((match >= m0) & (match < m1))
        def _():
            cols = pl.ds(pl.multiple_of((match - m0) * PIECE, PIECE), PIECE)
            h = half[rows, cols]
            v, t = h * a, h * b_s[pl.ds(ids[TXT_AT + match], 1), :]
            w[rows, cols] = (v * v + t * t - diagonal().astype(F32)).astype(BF)


def product_kernel(start, end, kept_here, core, w_rows, w_cols, w_near, img, txt, out):
    first, last = start - FAR, end - FAR

    def image_side():
        if start < FAR:
            d = dot(w_rows[start * PART:end * PART, :], txt[...], NN)
        else:
            rows = slice(first * PART, last * PART)
            d = dot(w_cols[rows, :], txt[:FAR_TXT, :], NN)
            d = d + dot(w_near[rows, :], txt[FAR_TXT:, :], NN)
        out[...] = d.astype(BF)

    def text_side():
        at, pad = (PIECE, 0) if kept_here else (0, PIECE)
        d = dot(w_rows[:, start * PIECE:end * PIECE], img[:FAR_IMG, :], TN)
        if start < FAR:
            d = d + dot(w_cols[:, start * PIECE:end * PIECE], img[FAR_IMG:, :], TN)
        else:
            d = d + dot(w_near[:, first * PIECE:last * PIECE], img[FAR_IMG:, :], TN)
        d = d.astype(BF)
        for i in range(end - start):
            out[i * PART + at:i * PART + at + PIECE, :] = d[i * PIECE:(i + 1) * PIECE]
            out[i * PART + pad:i * PART + pad + PIECE, :] = jnp.zeros((PIECE, WIDTH), BF)

    pl.when(core == (0 if kept_here else 1))(image_side)
    pl.when(core == (1 if kept_here else 0))(text_side)


FACTORS = [pltpu.VMEM((COLS, PIECE), F32), pltpu.VMEM((ROWS, PIECE), F32)]


def far_products(ids, own, far, h_rows, h_cols, img, txt):
    def kernel(ids, own, far, h_rows, h_cols, img, txt, w_rows, w_cols, out, a_s, b_s):
        row_col_factors(ids[CORE], own, far, a_s, b_s)
        weights_block(ids, h_rows, w_rows, a_s, b_s, 0, 2 * FAR, 0, PARTS)
        weights_block(ids, h_cols, w_cols, a_s, b_s, 2 * FAR, COLS, 0, FAR)
        product_kernel(0, FAR, False, ids[CORE], w_rows, w_cols, None, img, txt, out)

    return pl.pallas_call(
        kernel,
        out_shape=(
            jax.ShapeDtypeStruct((FAR_IMG, TXT), BF),
            jax.ShapeDtypeStruct((NEAR_IMG, FAR_TXT), BF),
            jax.ShapeDtypeStruct((FAR * PART, WIDTH), BF),
        ),
        in_specs=[SM] + [VM] * 6,
        out_specs=(VM,) * 3,
        scratch_shapes=FACTORS,
        compiler_params=PARAMS,
        cost_estimate=cost(PRODUCT_FLOPS, 1),
        name="far_products",
    )(ids, own, far, h_rows, h_cols, img, txt)


def near_products(end, token, ids, own, far, near, w_rows, w_cols, img, txt):
    def kernel(token, ids, own, far, near, w_rows, w_cols, img, txt, w_near, out, a_s, b_s):
        row_col_factors(ids[CORE], own, far, a_s, b_s)
        weights_block(ids, near, w_near, a_s, b_s, 2 * FAR, COLS, FAR, PARTS)
        product_kernel(FAR, end, False, ids[CORE], w_rows, w_cols, w_near, img, txt, out)

    return pl.pallas_call(
        kernel,
        out_shape=(
            jax.ShapeDtypeStruct((NEAR_IMG, NEAR_TXT), BF),
            jax.ShapeDtypeStruct(((end - FAR) * PART, WIDTH), BF),
        ),
        in_specs=[VM, SM] + [VM] * 7,
        out_specs=(VM, VM),
        scratch_shapes=FACTORS,
        compiler_params=PARAMS,
        cost_estimate=cost(PRODUCT_FLOPS, 1),
        name="near_products",
    )(token, ids, own, far, near, w_rows, w_cols, img, txt)


def products(start, end, kept_here, tokens, ids, w, img, txt):
    def kernel(ids, img, txt, *refs):
        w_near = refs[2] if len(w) == 3 else None
        product_kernel(
            start, end, kept_here, ids[CORE], refs[0], refs[1], w_near, img, txt, refs[-1]
        )

    return pl.pallas_call(
        kernel,
        out_shape=jax.ShapeDtypeStruct(((end - start) * PART, WIDTH), BF),
        in_specs=[SM] + [VM] * (2 + len(w) + len(tokens)),
        out_specs=VM,
        compiler_params=PARAMS,
        cost_estimate=cost(PRODUCT_FLOPS, 1),
        name="products_kept" if kept_here else "products_sent",
    )(ids, img, txt, *w, *tokens)


def sum_kernel(own, kept, sent, *refs):
    parts, (keep, send) = refs[:-2], refs[-2:]
    core = lax.axis_index("col") % 2
    total = own[...].astype(F32) + kept[...].astype(F32) + sent[...].astype(F32)
    for r in parts:
        total = total + r[...].astype(F32)

    @pl.when(core == 0)
    def _():
        keep[...] = total[:PIECE]
        send[...] = total[PIECE:].astype(BF)

    @pl.when(core == 1)
    def _():
        keep[...] = total[PIECE:]
        send[...] = total[:PIECE].astype(BF)


def grad_kernel(image, text, keep, got, image_out, text_out):
    core = lax.axis_index("col") % 2

    def grad(values, total, out):
        x = values[...]
        norm = jnp.sqrt(jnp.sum(x * x, axis=1, keepdims=True) + 1e-06)
        unit = x / norm
        g = total[...].astype(F32)
        out[...] = (g - unit * jnp.sum(unit * g, axis=1, keepdims=True)) / norm

    @pl.when(core == 0)
    def _():
        grad(image, keep, image_out)
        grad(text, got, text_out)

    @pl.when(core == 1)
    def _():
        grad(image, got, image_out)
        grad(text, keep, text_out)


def per_device(image_embeds, text_embeds):
    here = lax.axis_index("row") * COLS + lax.axis_index("col")
    ids = lax.dynamic_index_in_dim(jnp.asarray(device_table()), here, keepdims=False)
    first = lax.axis_index("col") % 2 == 0

    keep, send = unit_pair(image_embeds, text_embeds)
    got = swap(send)
    own = jnp.concatenate([jnp.where(first, keep, got), jnp.where(first, got, keep)])

    other = flip(own)
    left0, right0 = ring(own, 1), ring(own, 3)
    left1, right1 = ring(other, 1), ring(other, 3)
    far0, far1 = ring(left0, 1), ring(right1, 3)
    mine = [far0, far1, right1, left0, right0, left1, other, own]
    late, _ = lax.optimization_barrier((own, left0))
    theirs = [swap(v) for v in mine[FAR:-1]] + [swap(late)]
    near = near_scores(ids, mine[FAR:], theirs)
    far0, far1, *near = lax.optimization_barrier((far0, far1, *near))
    h_rows, h_cols, img, txt, keep, send = far_scores(
        ids, (far0, far1), (swap(far0), swap(far1)), near
    )
    sums = keep + swap(send)
    sums = sums + ring(sums, 1) + ring(sums, 2) + ring(sums, 3)
    sums = sums + flip(sums)
    theirs = swap(sums)

    def add(*v):
        return functools.reduce(lambda a, b: a + b, [u.astype(F32) for u in v]).astype(BF)

    def part(value, i):
        return value[i * PART:(i + 1) * PART]

    def mark(done):
        return swap(done[:16, :PIECE])

    w_rows, w_cols, sent = far_products(ids, sums, theirs, h_rows, h_cols, img, txt)
    sent = swap(sent)
    kept = products(0, FAR, True, (), ids, (w_rows, w_cols), img, txt)
    far0, far1 = add(part(kept, 0), part(sent, 0)), add(part(kept, 1), part(sent, 1))
    through0, through1 = ring(far0, 1), ring(far1, 3)

    w_near, sent = near_products(6, mark(far0), ids, sums, theirs, near[0], w_rows, w_cols, img, txt)
    sent = swap(sent)
    kept = products(FAR, 4, True, (), ids, (w_rows, w_cols, w_near), img, txt)
    right1 = ring(add(part(kept, 0), part(sent, 0)), 1)
    back = add(part(kept, 1), part(sent, 1))
    kept = products(4, 6, True, (through0, through1), ids, (w_rows, w_cols, w_near), img, txt)
    back1 = add(part(kept, 1), part(sent, 3), through1)
    left1 = ring(back1, 3)
    right0 = ring(add(part(kept, 0), part(sent, 2), through0), 1)
    left0 = ring(back, 3)

    w, token = (w_rows, w_cols, w_near), mark(back1)
    sent = swap(products(6, 8, False, (token,), ids, w, img, txt))
    kept = products(6, 8, True, (token,), ids, w, img, txt)
    lse = lse_of(theirs).reshape(2, 8, PIECE).sum(0)
    lse = jnp.where(first, lse, lse - 2.0 * theirs[2, :8])
    kept, lse = lax.optimization_barrier((kept, lse))
    lse = lse + ring(lse, 1) + ring(lse, 2) + ring(lse, 3)
    last = add(part(kept, 0), part(sent, 0), right1, left1)
    back, there = flip(last), flip(lse)
    shape = jax.ShapeDtypeStruct((PIECE, WIDTH), F32)
    keep, send = pl.pallas_call(
        sum_kernel, out_shape=(shape, jax.ShapeDtypeStruct((PIECE, WIDTH), BF)), in_specs=[VM] * 5, out_specs=(VM, VM),
        compiler_params=PARAMS, name="own_sums",
    )(part(kept, 1), part(sent, 1), right0, left0, back)
    send, lse = lax.optimization_barrier((send, lse + there))
    got, there = swap(send), swap(lse)
    image_grad, text_grad = pl.pallas_call(
        grad_kernel, out_shape=(shape, shape), in_specs=[VM] * 4, out_specs=(VM, VM),
        compiler_params=PARAMS, name="grad_rows",
    )(image_embeds, text_embeds, keep, got)
    loss = jnp.sum(lse + there) / (2.0 * ROWS * COLS * PIECE)
    return (image_grad, text_grad, loss)


def solution(mesh):
    return jax.shard_map(
        per_device,
        mesh=mesh,
        in_specs=(P(("row", "col"), None), P(("col", "row"), None)),
        out_specs=(P(("row", "col"), None), P(("col", "row"), None), P()),
        check_vma=False,
    )
```

```python
import functools
import math

import jax
import jax.numpy as jnp
import numpy as np
from jax import lax
from jax.experimental import pallas as pl
from jax.experimental.pallas import tpu as pltpu
from jax.sharding import PartitionSpec as P

PIECE = 128
PART = 2 * PIECE
WIDTH = 1280
RING = 4
PART_AT = ((2, 0), (2, 1), (1, 1), (3, 1), (0, 1), (0, 0), (1, 0), (3, 0))
PARTS = len(PART_AT)
FAR = 2
ROWS, COLS = 8, 16
IMG = PARTS * PART
TXT = PARTS * PIECE
FAR_IMG, FAR_TXT = FAR * PART, FAR * PIECE
NEAR_IMG, NEAR_TXT = IMG - FAR_IMG, TXT - FAR_TXT
CORE, TXT_AT, MATCH_AT = 40, 32, 16
PRODUCT_FLOPS = 5 * 10**10

SHIFT = 22.0
LIFT = 70.0
FLOOR = math.exp(-62.0)
LOG2E = math.log2(math.e)

VM = pl.BlockSpec(memory_space=pltpu.VMEM)
SM = pl.BlockSpec(memory_space=pltpu.SMEM)
PARAMS = pltpu.CompilerParams(vmem_limit_bytes=8 * 1024 * 1024)
F32, BF = jnp.float32, jnp.bfloat16
NT = (((1,), (1,)), ((), ()))
NN = (((1,), (0,)), ((), ()))
TN = (((0,), (0,)), ((), ()))
AXES = ("row", "col")


def dot(a, b, dims):
    return lax.dot_general(a, b, dims, preferred_element_type=F32)


def device(yl, z, x, yh, k):
    return (yl * 4 + z) * COLS + (x * 2 + yh) * 2 + k


def places():
    return [
        (yl, z, x, yh, k)
        for yl in range(2) for z in range(RING) for x in range(RING) for yh in range(2) for k in range(2)
    ]


def neighbour(y, k):
    return y ^ 1 if k == 0 else (y + (1 if y % 2 else 3)) % RING


def group(value, d, side):
    pairs = []
    for yl, z, x, yh, k in places():
        y = yh * 2 + yl
        y = neighbour(y, k) if side else y
        target = device(y % 2, (z + d * k) % RING, (x + d * (1 - k)) % RING, y // 2, k)
        pairs.append((device(yl, z, x, yh, k), target))
    return lax.ppermute(value, AXES, pairs)


def ring(value, d):
    return group(value, d, 0)


def flip(value):
    return group(value, 0, 1)


def group_sum(value):
    others = ((2, 1), (1, 1), (3, 1), (2, 0), (1, 0), (3, 0), (0, 1))
    return functools.reduce(lambda a, b: a + b, [group(value, *at) for at in others], value)


def swap(value):
    return lax.ppermute(value, AXES, [
        (device(yl, z, x, yh, k), device(yl, z, x, yh, 1 - k)) for yl, z, x, yh, k in places()
    ])


def device_table():
    table = np.zeros((ROWS * COLS, 41), np.int32)
    for yl, z, x, yh, k in places():
        y = yh * 2 + yl
        img, match, txt, owned = [], [], [], []
        for d, side in PART_AT:
            zt, yt = (z + d) % RING, neighbour(y, 1) if side else y
            txt.append(zt * 2 + (yt + 1) % 2)
            owner = device(yt % 2, zt, x, yt // 2, k)
            owned.append(owner % COLS * ROWS + owner // COLS)
        for d, side in PART_AT:
            xi, yi = (x + d) % RING, neighbour(y, 0) if side else y
            for h in range(2):
                img.append((xi * 2 + yi % 2) * 2 + h)
                piece = device(yi % 2, z, xi, yi // 2, h)
                match.append(owned.index(piece) if piece in owned else -1)
        table[device(yl, z, x, yh, k)] = img + match + txt + [k]
    return table


def cost(flops, bytes_accessed):
    return pl.CostEstimate(flops=flops, bytes_accessed=bytes_accessed, transcendentals=0)


def diagonal():
    shape = (PIECE, PIECE)
    return lax.broadcasted_iota(jnp.int32, shape, 0) == lax.broadcasted_iota(jnp.int32, shape, 1)


def unit_kernel(image_ref, text_ref, keep_ref, send_ref):
    core = lax.axis_index("col") % 2

    def unit(src):
        x = src[...]
        return (x / jnp.sqrt(jnp.sum(x * x, axis=1, keepdims=True) + 1e-06)).astype(BF)

    image, text = unit(image_ref), unit(text_ref)

    @pl.when(core == 0)
    def _():
        keep_ref[...] = image
        send_ref[...] = text

    @pl.when(core == 1)
    def _():
        keep_ref[...] = text
        send_ref[...] = image


def unit_pair(image, text):
    shape = jax.ShapeDtypeStruct((PIECE, WIDTH), BF)
    return pl.pallas_call(
        unit_kernel, out_shape=(shape, shape), in_specs=[VM, VM], out_specs=(VM, VM),
        compiler_params=PARAMS, name="unit_rows",
    )(image, text)


def place_parts(core, here, there, img, txt):
    @pl.when(core == 0)
    def _():
        for m, (mine, other) in enumerate(zip(here, there)):
            img[m * PART:(m + 1) * PART, :] = mine[...]
            txt[m * PIECE:(m + 1) * PIECE, :] = other[:PIECE, :]

    @pl.when(core == 1)
    def _():
        for m, (mine, other) in enumerate(zip(here, there)):
            img[m * PART:(m + 1) * PART, :] = other[...]
            txt[m * PIECE:(m + 1) * PIECE, :] = mine[PIECE:, :]


def score_tiles(tiles, img, txt, held, racc, cacc):
    def epilogue(t):
        row, rows, col, h_out, h_row, h_col = tiles[t]
        cols = slice(col, col + 256)
        total = jnp.zeros((8, 256), F32)
        for p in range(0, rows, PIECE):
            d = held[t % 2][p:p + PIECE, :]
            h = jnp.exp2(d * (50.0 * LOG2E) - (0.5 * SHIFT * LOG2E))
            h_out[h_row + p:h_row + p + PIECE, h_col:h_col + 256] = h
            q = h * h
            racc[row + p:row + p + PIECE, :] += q[:, :PIECE] + q[:, PIECE:]
            total += jnp.sum(q.reshape(16, 8, 256), axis=0)
        cacc[:, cols] += total

    for t, (row, rows, col, *_) in enumerate(tiles):
        held[t % 2][:rows, :] = dot(img[row:row + rows, :], txt[col:col + 256, :], NT)
        if t:
            epilogue(t - 1)
    epilogue(len(tiles) - 1)


def near_kernel(ids, *refs):
    count = PARTS - FAR
    here, there = refs[:count], refs[count:2 * count]
    h_out, img, txt, racc, cacc, even, odd = refs[2 * count:]
    place_parts(ids[CORE], here, there, img, txt)
    racc[...] = jnp.zeros_like(racc)
    cacc[...] = jnp.zeros_like(cacc)
    half = NEAR_IMG // 2
    tiles = [(r, half, c, h_out, r, c) for c in range(0, NEAR_TXT, 256) for r in (0, half)]
    score_tiles(tiles, img, txt, (even, odd), racc, cacc)


def near_scores(ids, here, there):
    return pl.pallas_call(
        near_kernel,
        out_shape=(
            jax.ShapeDtypeStruct((NEAR_IMG, NEAR_TXT), F32),
            jax.ShapeDtypeStruct((NEAR_IMG, WIDTH), BF),
            jax.ShapeDtypeStruct((NEAR_TXT, WIDTH), BF),
            jax.ShapeDtypeStruct((NEAR_IMG, PIECE), F32),
            jax.ShapeDtypeStruct((8, NEAR_TXT), F32),
        ),
        in_specs=[SM] + [VM] * (2 * len(here)),
        out_specs=(VM,) * 5,
        scratch_shapes=[pltpu.VMEM((NEAR_IMG // 2, 256), F32)] * 2,
        compiler_params=PARAMS,
        cost_estimate=cost(2 * NEAR_IMG * NEAR_TXT * WIDTH, 16 << 20),
        name="near_scores",
    )(ids, *here, *there)


def far_kernel(ids, here0, here1, there0, there1, near, near_img, near_txt, near_racc, near_cacc,
               h_rows, h_cols, img, txt, keep, send, even, odd, racc, cacc, rs, cs, dg):
    core = ids[CORE]
    place_parts(core, (here0, here1), (there0, there1), img, txt)
    img[FAR_IMG:, :] = near_img[...]
    txt[FAR_TXT:, :] = near_txt[...]
    racc[:FAR_IMG, :] = jnp.zeros((FAR_IMG, PIECE), F32)
    racc[FAR_IMG:, :] = near_racc[...]
    cacc[:, :FAR_TXT] = jnp.zeros((8, FAR_TXT), F32)
    cacc[:, FAR_TXT:] = near_cacc[...]
    for ref in (rs, cs, dg, keep, send):
        ref[...] = jnp.zeros_like(ref)
    half = NEAR_IMG // 2
    tiles = [(FAR_IMG + r, half, 0, h_cols, r, 0) for r in (0, half)]
    tiles += [(0, FAR_IMG, c, h_rows, 0, c) for c in range(0, TXT, 256)]
    score_tiles(tiles, img, txt, (even, odd), racc, cacc)

    lowest = jnp.full((1, PIECE), jnp.inf, F32)
    for p in range(COLS):
        part = jnp.sum(racc[p * PIECE:(p + 1) * PIECE, :].T, axis=0, keepdims=True)
        rs[0, pl.ds(ids[p], 1), :] = part
        lowest = jnp.minimum(lowest, part)
    total = jnp.sum(cacc[...], axis=0, keepdims=True)
    for m in range(PARTS):
        part = total[:, m * PIECE:(m + 1) * PIECE]
        cs[0, pl.ds(ids[TXT_AT + m], 1), :] = part
        lowest = jnp.minimum(lowest, part)

    def half_of(p, m):
        at = p * PIECE if p < 2 * FAR else (p - 2 * FAR) * PIECE
        if p < 2 * FAR:
            return h_rows[at:at + PIECE, m * PIECE:(m + 1) * PIECE]
        if m < FAR:
            return h_cols[at:at + PIECE, m * PIECE:(m + 1) * PIECE]
        return near[at:at + PIECE, (m - FAR) * PIECE:(m - FAR + 1) * PIECE]

    @pl.when(jnp.min(lowest) < FLOOR)
    def _():
        for p in range(COLS):
            part = jnp.zeros((PIECE, PIECE), F32)
            for m in range(PARTS):
                g = half_of(p, m) * math.exp(0.5 * (SHIFT + LIFT))
                part += g * g
                cs[1, pl.ds(ids[TXT_AT + m], 1), :] += jnp.sum(g * g, axis=0, keepdims=True)
            rs[1, pl.ds(ids[p], 1), :] = jnp.sum(part.T, axis=0, keepdims=True)

    for p in range(COLS):
        match = ids[MATCH_AT + p]

        @pl.when(match >= 0)
        def _():
            other = txt[pl.ds(pl.multiple_of(match * PIECE, PIECE), PIECE), :]
            s = 100.0 * dot(img[p * PIECE:(p + 1) * PIECE, :], other, NT)
            dg[...] += jnp.sum(jnp.where(diagonal(), s, 0.0).reshape(16, 8, PIECE), axis=0)

    @pl.when(core == 0)
    def _():
        keep[0:2] = rs[...]
        keep[2, 0:8] = dg[...]
        send[0:2, 0:8] = cs[...]

    @pl.when(core == 1)
    def _():
        send[0:2] = rs[...]
        send[2, 0:8] = dg[...]
        keep[0:2, 8:16] = cs[...]


def far_scores(ids, here, there, near):
    sums = jax.ShapeDtypeStruct((3, COLS, PIECE), F32)
    return pl.pallas_call(
        far_kernel,
        out_shape=(
            jax.ShapeDtypeStruct((FAR_IMG, TXT), F32),
            jax.ShapeDtypeStruct((NEAR_IMG, FAR_TXT), F32),
            jax.ShapeDtypeStruct((IMG, WIDTH), BF),
            jax.ShapeDtypeStruct((TXT, WIDTH), BF),
            sums, sums,
        ),
        in_specs=[SM] + [VM] * 9,
        out_specs=(VM,) * 6,
        scratch_shapes=[
            pltpu.VMEM((NEAR_IMG // 2, 256), F32),
            pltpu.VMEM((NEAR_IMG // 2, 256), F32),
            pltpu.VMEM((IMG, PIECE), F32),
            pltpu.VMEM((8, TXT), F32),
            pltpu.VMEM((2, COLS, PIECE), F32),
            pltpu.VMEM((2, ROWS, PIECE), F32),
            pltpu.VMEM((8, PIECE), F32),
        ],
        compiler_params=PARAMS,
        cost_estimate=cost(2 * (IMG * TXT - NEAR_IMG * NEAR_TXT) * WIDTH, 16 << 20),
        name="far_scores",
    )(ids, *here, *there, *near)


def lse_of(sums):
    return jnp.where(sums[0] >= FLOOR, SHIFT + jnp.log(sums[0]), jnp.log(sums[1]) - LIFT)


def row_col_factors(core, own, far, a_s, b_s):
    scale = math.sqrt(0.5)
    factors = [scale * jnp.exp(0.5 * (SHIFT - lse_of(v))) for v in (own, far)]
    a_s[...] = jnp.where(core == 0, factors[0], factors[1])
    b_s[...] = jnp.where(core == 0, factors[1][:8], factors[0][8:])


def weights_block(ids, half, w, a_s, b_s, p0, p1, m0, m1):
    b = [b_s[pl.ds(ids[TXT_AT + m], 1), :] for m in range(m0, m1)]

    @pl.loop(p0, p1)
    def _(p):
        rows = pl.ds(pl.multiple_of((p - p0) * PIECE, PIECE), PIECE)
        a = jnp.broadcast_to(a_s[pl.ds(ids[p], 1), :], (PIECE, PIECE)).T
        for m in range(m1 - m0):
            cols = slice(m * PIECE, (m + 1) * PIECE)
            h = half[rows, cols]
            v, t = h * a, h * b[m]
            w[rows, cols] = (v * v + t * t).astype(BF)
        match = ids[MATCH_AT + p]

        @pl.when((match >= m0) & (match < m1))
        def _():
            cols = pl.ds(pl.multiple_of((match - m0) * PIECE, PIECE), PIECE)
            h = half[rows, cols]
            v, t = h * a, h * b_s[pl.ds(ids[TXT_AT + match], 1), :]
            w[rows, cols] = (v * v + t * t - diagonal().astype(F32)).astype(BF)


def product_kernel(start, end, kept_here, core, w_rows, w_cols, w_near, img, txt, out):
    first, last = start - FAR, end - FAR

    def image_side():
        if start < FAR:
            d = dot(w_rows[start * PART:end * PART, :], txt[...], NN)
        else:
            rows = slice(first * PART, last * PART)
            d = dot(w_cols[rows, :], txt[:FAR_TXT, :], NN)
            d = d + dot(w_near[rows, :], txt[FAR_TXT:, :], NN)
        out[...] = d.astype(BF)

    def text_side():
        at, pad = (PIECE, 0) if kept_here else (0, PIECE)
        d = dot(w_rows[:, start * PIECE:end * PIECE], img[:FAR_IMG, :], TN)
        if start < FAR:
            d = d + dot(w_cols[:, start * PIECE:end * PIECE], img[FAR_IMG:, :], TN)
        else:
            d = d + dot(w_near[:, first * PIECE:last * PIECE], img[FAR_IMG:, :], TN)
        d = d.astype(BF)
        for i in range(end - start):
            out[i * PART + at:i * PART + at + PIECE, :] = d[i * PIECE:(i + 1) * PIECE]
            out[i * PART + pad:i * PART + pad + PIECE, :] = jnp.zeros((PIECE, WIDTH), BF)

    pl.when(core == (0 if kept_here else 1))(image_side)
    pl.when(core == (1 if kept_here else 0))(text_side)


FACTORS = [pltpu.VMEM((COLS, PIECE), F32), pltpu.VMEM((ROWS, PIECE), F32)]


def far_products(ids, own, far, h_rows, h_cols, img, txt):
    def kernel(ids, own, far, h_rows, h_cols, img, txt, w_rows, w_cols, out, a_s, b_s):
        row_col_factors(ids[CORE], own, far, a_s, b_s)
        weights_block(ids, h_rows, w_rows, a_s, b_s, 0, 2 * FAR, 0, PARTS)
        weights_block(ids, h_cols, w_cols, a_s, b_s, 2 * FAR, COLS, 0, FAR)
        product_kernel(0, FAR, False, ids[CORE], w_rows, w_cols, None, img, txt, out)

    return pl.pallas_call(
        kernel,
        out_shape=(
            jax.ShapeDtypeStruct((FAR_IMG, TXT), BF),
            jax.ShapeDtypeStruct((NEAR_IMG, FAR_TXT), BF),
            jax.ShapeDtypeStruct((FAR * PART, WIDTH), BF),
        ),
        in_specs=[SM] + [VM] * 6,
        out_specs=(VM,) * 3,
        scratch_shapes=FACTORS,
        compiler_params=PARAMS,
        cost_estimate=cost(PRODUCT_FLOPS, 1),
        name="far_products",
    )(ids, own, far, h_rows, h_cols, img, txt)


def near_products(end, token, ids, own, far, near, w_rows, w_cols, img, txt):
    def kernel(token, ids, own, far, near, w_rows, w_cols, img, txt, w_near, out, a_s, b_s):
        row_col_factors(ids[CORE], own, far, a_s, b_s)
        weights_block(ids, near, w_near, a_s, b_s, 2 * FAR, COLS, FAR, PARTS)
        product_kernel(FAR, end, False, ids[CORE], w_rows, w_cols, w_near, img, txt, out)

    return pl.pallas_call(
        kernel,
        out_shape=(
            jax.ShapeDtypeStruct((NEAR_IMG, NEAR_TXT), BF),
            jax.ShapeDtypeStruct(((end - FAR) * PART, WIDTH), BF),
        ),
        in_specs=[VM, SM] + [VM] * 7,
        out_specs=(VM, VM),
        scratch_shapes=FACTORS,
        compiler_params=PARAMS,
        cost_estimate=cost(PRODUCT_FLOPS, 1),
        name="near_products",
    )(token, ids, own, far, near, w_rows, w_cols, img, txt)


def products(start, end, kept_here, tokens, ids, w, img, txt):
    def kernel(ids, img, txt, *refs):
        w_near = refs[2] if len(w) == 3 else None
        product_kernel(
            start, end, kept_here, ids[CORE], refs[0], refs[1], w_near, img, txt, refs[-1]
        )

    return pl.pallas_call(
        kernel,
        out_shape=jax.ShapeDtypeStruct(((end - start) * PART, WIDTH), BF),
        in_specs=[SM] + [VM] * (2 + len(w) + len(tokens)),
        out_specs=VM,
        compiler_params=PARAMS,
        cost_estimate=cost(PRODUCT_FLOPS, 1),
        name="products_kept" if kept_here else "products_sent",
    )(ids, img, txt, *w, *tokens)


def pack(value):
    pieces = []
    for _ in range(2):
        pieces.append(lax.reduce_precision(value, exponent_bits=8, mantissa_bits=7))
        value = value - pieces[-1]
    rows = jnp.concatenate([v.astype(BF) for v in (*pieces, value)], axis=1)
    return jnp.pad(rows, ((0, 8), (0, WIDTH - 3 * PIECE)))


def unpack(rows):
    return sum(rows[:8, i * PIECE:(i + 1) * PIECE].astype(F32) for i in range(3))


def with_tail(part, tail):
    return jnp.concatenate([part, tail])


def sum_kernel(own, kept, sent, *refs):
    parts, (keep, send) = refs[:-2], refs[-2:]
    core = lax.axis_index("col") % 2
    total = own[...].astype(F32) + kept[...].astype(F32) + sent[...].astype(F32)
    for r in parts:
        total = total + r[:PART, :].astype(F32)

    @pl.when(core == 0)
    def _():
        keep[...] = total[:PIECE]
        send[...] = total[PIECE:].astype(BF)

    @pl.when(core == 1)
    def _():
        keep[...] = total[PIECE:]
        send[...] = total[:PIECE].astype(BF)


def grad_kernel(image, text, keep, got, image_out, text_out):
    core = lax.axis_index("col") % 2

    def grad(values, total, out):
        x = values[...]
        norm = jnp.sqrt(jnp.sum(x * x, axis=1, keepdims=True) + 1e-06)
        unit = x / norm
        g = total[...].astype(F32)
        out[...] = (g - unit * jnp.sum(unit * g, axis=1, keepdims=True)) / norm

    @pl.when(core == 0)
    def _():
        grad(image, keep, image_out)
        grad(text, got, text_out)

    @pl.when(core == 1)
    def _():
        grad(image, got, image_out)
        grad(text, keep, text_out)


def per_device(image_embeds, text_embeds):
    here = lax.axis_index("row") * COLS + lax.axis_index("col")
    ids = lax.dynamic_index_in_dim(jnp.asarray(device_table()), here, keepdims=False)
    first = lax.axis_index("col") % 2 == 0

    keep, send = unit_pair(image_embeds, text_embeds)
    got = swap(send)
    own = jnp.concatenate([jnp.where(first, keep, got), jnp.where(first, got, keep)])

    other = flip(own)
    left0, right0 = ring(own, 1), ring(own, 3)
    left1, right1 = ring(other, 1), ring(other, 3)
    far0, far1 = ring(left0, 1), ring(right1, 3)
    mine = [far0, far1, right1, left1, other, own, right0, left0]
    late, _ = lax.optimization_barrier((own, left0))
    theirs = [swap(late if v is own else v) for v in mine[FAR:]]
    near = near_scores(ids, mine[FAR:], theirs)
    far0, far1, *near = lax.optimization_barrier((far0, far1, *near))
    h_rows, h_cols, img, txt, keep, send = far_scores(
        ids, (far0, far1), (swap(far0), swap(far1)), near
    )
    sums = keep + swap(send)
    sums = group_sum(sums)
    theirs = swap(sums)

    def add(*v):
        return functools.reduce(lambda a, b: a + b, [u.astype(F32) for u in v]).astype(BF)

    def part(value, i):
        return value[i * PART:(i + 1) * PART]

    def mark(done):
        return swap(done[:16, :PIECE])

    w_rows, w_cols, sent = far_products(ids, sums, theirs, h_rows, h_cols, img, txt)
    sent = swap(sent)
    kept = products(0, FAR, True, (), ids, (w_rows, w_cols), img, txt)
    lse = lse_of(theirs).reshape(2, 8, PIECE).sum(0)
    lse = jnp.where(first, lse, lse - 2.0 * theirs[2, :8])
    tail = pack(lse)
    far0 = with_tail(add(part(kept, 0), part(sent, 0)), tail)
    far1 = with_tail(add(part(kept, 1), part(sent, 1)), tail)
    through0, through1 = ring(far0, 1), ring(far1, 3)

    w_near, sent = near_products(4, mark(far0), ids, sums, theirs, near[0], w_rows, w_cols, img, txt)
    sent = swap(sent)
    w = (w_rows, w_cols, w_near)
    kept = products(FAR, 4, True, (through0, through1), ids, w, img, txt)
    near1 = with_tail(add(part(kept, 0), part(sent, 0)), through0[PART:])
    back1 = add(part(kept, 1), part(sent, 1), part(through1, 0))
    right1, left1 = ring(near1, 1), ring(back1, 3)

    token = mark(back1)
    sent = swap(products(4, 8, False, (token,), ids, w, img, txt))
    kept = products(4, 8, True, (token,), ids, w, img, txt)
    right0 = ring(add(part(kept, 2), part(sent, 2), part(through0, 0)), 1)
    left0 = ring(add(part(kept, 3), part(sent, 3)), 3)
    lse = lse + unpack(through0[PART:]) + unpack(through1[PART:]) + unpack(right1[PART:])
    last = add(part(kept, 0), part(sent, 0), part(right1, 0), left1)
    back = flip(with_tail(last, pack(lse)))
    lse = lse + unpack(back[PART:])
    shape = jax.ShapeDtypeStruct((PIECE, WIDTH), F32)
    keep, send = pl.pallas_call(
        sum_kernel, out_shape=(shape, jax.ShapeDtypeStruct((PIECE, WIDTH), BF)), in_specs=[VM] * 5, out_specs=(VM, VM),
        compiler_params=PARAMS, name="own_sums",
    )(part(kept, 1), part(sent, 1), right0, left0, back)
    got, there = swap(send), swap(lse)
    image_grad, text_grad = pl.pallas_call(
        grad_kernel, out_shape=(shape, shape), in_specs=[VM] * 4, out_specs=(VM, VM),
        compiler_params=PARAMS, name="grad_rows",
    )(image_embeds, text_embeds, keep, got)
    loss = jnp.sum(lse + there) / (2.0 * ROWS * COLS * PIECE)
    return (image_grad, text_grad, loss)


def solution(mesh):
    return jax.shard_map(
        per_device,
        mesh=mesh,
        in_specs=(P(("row", "col"), None), P(("col", "row"), None)),
        out_specs=(P(("row", "col"), None), P(("col", "row"), None), P()),
        check_vma=False,
    )
```

```python
import functools
import math

import jax
import jax.numpy as jnp
import numpy as np
from jax import lax
from jax.experimental import pallas as pl
from jax.experimental.pallas import tpu as pltpu
from jax.sharding import PartitionSpec as P

PIECE = 128
PART = 2 * PIECE
WIDTH = 1280
RING = 4
PART_AT = ((2, 0), (2, 1), (1, 1), (3, 1), (0, 1), (0, 0), (1, 0), (3, 0))
PARTS = len(PART_AT)
FAR = 2
ROWS, COLS = 8, 16
IMG = PARTS * PART
TXT = PARTS * PIECE
FAR_IMG, FAR_TXT = FAR * PART, FAR * PIECE
NEAR_IMG, NEAR_TXT = IMG - FAR_IMG, TXT - FAR_TXT
CORE, TXT_AT, MATCH_AT = 40, 32, 16
PRODUCT_FLOPS = 5 * 10**10

SHIFT = 22.0
LIFT = 70.0
FLOOR = math.exp(-62.0)
LOG2E = math.log2(math.e)

VM = pl.BlockSpec(memory_space=pltpu.VMEM)
SM = pl.BlockSpec(memory_space=pltpu.SMEM)
PARAMS = pltpu.CompilerParams(vmem_limit_bytes=8 * 1024 * 1024)
F32, BF = jnp.float32, jnp.bfloat16
NT = (((1,), (1,)), ((), ()))
NN = (((1,), (0,)), ((), ()))
TN = (((0,), (0,)), ((), ()))
AXES = ("row", "col")


def dot(a, b, dims):
    return lax.dot_general(a, b, dims, preferred_element_type=F32)


def device(yl, z, x, yh, k):
    return (yl * 4 + z) * COLS + (x * 2 + yh) * 2 + k


def places():
    return [
        (yl, z, x, yh, k)
        for yl in range(2) for z in range(RING) for x in range(RING) for yh in range(2) for k in range(2)
    ]


def neighbour(y, k):
    return y ^ 1 if k == 0 else (y + (1 if y % 2 else 3)) % RING


def group(value, d, side):
    pairs = []
    for yl, z, x, yh, k in places():
        y = yh * 2 + yl
        y = neighbour(y, k) if side else y
        target = device(y % 2, (z + d * k) % RING, (x + d * (1 - k)) % RING, y // 2, k)
        pairs.append((device(yl, z, x, yh, k), target))
    return lax.ppermute(value, AXES, pairs)


def ring(value, d):
    return group(value, d, 0)


def flip(value):
    return group(value, 0, 1)


def group_sum(value):
    value = value + ring(value, 1) + ring(value, 2) + ring(value, 3)
    return value + flip(value)


def swap(value):
    return lax.ppermute(value, AXES, [
        (device(yl, z, x, yh, k), device(yl, z, x, yh, 1 - k)) for yl, z, x, yh, k in places()
    ])


def device_table():
    table = np.zeros((ROWS * COLS, 41), np.int32)
    for yl, z, x, yh, k in places():
        y = yh * 2 + yl
        img, match, txt, owned = [], [], [], []
        for d, side in PART_AT:
            zt, yt = (z + d) % RING, neighbour(y, 1) if side else y
            txt.append(zt * 2 + (yt + 1) % 2)
            owner = device(yt % 2, zt, x, yt // 2, k)
            owned.append(owner % COLS * ROWS + owner // COLS)
        for d, side in PART_AT:
            xi, yi = (x + d) % RING, neighbour(y, 0) if side else y
            for h in range(2):
                img.append((xi * 2 + yi % 2) * 2 + h)
                piece = device(yi % 2, z, xi, yi // 2, h)
                match.append(owned.index(piece) if piece in owned else -1)
        table[device(yl, z, x, yh, k)] = img + match + txt + [k]
    return table


def cost(flops, bytes_accessed):
    return pl.CostEstimate(flops=flops, bytes_accessed=bytes_accessed, transcendentals=0)


def diagonal():
    shape = (PIECE, PIECE)
    return lax.broadcasted_iota(jnp.int32, shape, 0) == lax.broadcasted_iota(jnp.int32, shape, 1)


def unit_kernel(ids, image_ref, text_ref, keep_ref, send_ref):
    core = ids[CORE]

    def unit(src):
        x = src[...]
        return (x / jnp.sqrt(jnp.sum(x * x, axis=1, keepdims=True) + 1e-06)).astype(BF)

    image, text = unit(image_ref), unit(text_ref)

    @pl.when(core == 0)
    def _():
        keep_ref[...] = image
        send_ref[...] = text

    @pl.when(core == 1)
    def _():
        keep_ref[...] = text
        send_ref[...] = image


def unit_pair(ids, image, text):
    shape = jax.ShapeDtypeStruct((PIECE, WIDTH), BF)
    return pl.pallas_call(
        unit_kernel, out_shape=(shape, shape), in_specs=[SM, VM, VM], out_specs=(VM, VM),
        compiler_params=PARAMS, name="unit_rows",
    )(ids, image, text)


def place_parts(core, here, there, img, txt):
    @pl.when(core == 0)
    def _():
        for m, (mine, other) in enumerate(zip(here, there)):
            img[m * PART:(m + 1) * PART, :] = mine[...]
            txt[m * PIECE:(m + 1) * PIECE, :] = other[:PIECE, :]

    @pl.when(core == 1)
    def _():
        for m, (mine, other) in enumerate(zip(here, there)):
            img[m * PART:(m + 1) * PART, :] = other[...]
            txt[m * PIECE:(m + 1) * PIECE, :] = mine[PIECE:, :]


def score_tiles(tiles, img, txt, held, racc, cacc):
    def epilogue(t):
        row, rows, col, h_out, h_row, h_col = tiles[t]
        cols = slice(col, col + 256)
        total = jnp.zeros((8, 256), F32)
        for p in range(0, rows, PIECE):
            d = held[t % 2][p:p + PIECE, :]
            h = jnp.exp2(d * (50.0 * LOG2E) - (0.5 * SHIFT * LOG2E))
            h_out[h_row + p:h_row + p + PIECE, h_col:h_col + 256] = h
            q = h * h
            racc[row + p:row + p + PIECE, :] += q[:, :PIECE] + q[:, PIECE:]
            total += jnp.sum(q.reshape(16, 8, 256), axis=0)
        cacc[:, cols] += total

    for t, (row, rows, col, *_) in enumerate(tiles):
        held[t % 2][:rows, :] = dot(img[row:row + rows, :], txt[col:col + 256, :], NT)
        if t:
            epilogue(t - 1)
    epilogue(len(tiles) - 1)


def near_kernel(ids, *refs):
    count = PARTS - FAR
    here, there = refs[:count], refs[count:2 * count]
    h_out, img, txt, racc, cacc, even, odd = refs[2 * count:]
    place_parts(ids[CORE], here, there, img, txt)
    racc[...] = jnp.zeros_like(racc)
    cacc[...] = jnp.zeros_like(cacc)
    half = NEAR_IMG // 2
    tiles = [(r, half, c, h_out, r, c) for c in range(0, NEAR_TXT, 256) for r in (0, half)]
    score_tiles(tiles, img, txt, (even, odd), racc, cacc)


def near_scores(ids, here, there):
    return pl.pallas_call(
        near_kernel,
        out_shape=(
            jax.ShapeDtypeStruct((NEAR_IMG, NEAR_TXT), F32),
            jax.ShapeDtypeStruct((NEAR_IMG, WIDTH), BF),
            jax.ShapeDtypeStruct((NEAR_TXT, WIDTH), BF),
            jax.ShapeDtypeStruct((NEAR_IMG, PIECE), F32),
            jax.ShapeDtypeStruct((8, NEAR_TXT), F32),
        ),
        in_specs=[SM] + [VM] * (2 * len(here)),
        out_specs=(VM,) * 5,
        scratch_shapes=[pltpu.VMEM((NEAR_IMG // 2, 256), F32)] * 2,
        compiler_params=PARAMS,
        cost_estimate=cost(2 * NEAR_IMG * NEAR_TXT * WIDTH, 16 << 20),
        name="near_scores",
    )(ids, *here, *there)


def far_kernel(ids, here0, here1, there0, there1, near, near_img, near_txt, near_racc, near_cacc,
               h_rows, h_cols, img, txt, keep, send, even, odd, racc, cacc, rs, cs, dg):
    core = ids[CORE]
    place_parts(core, (here0, here1), (there0, there1), img, txt)
    img[FAR_IMG:, :] = near_img[...]
    txt[FAR_TXT:, :] = near_txt[...]
    racc[:FAR_IMG, :] = jnp.zeros((FAR_IMG, PIECE), F32)
    racc[FAR_IMG:, :] = near_racc[...]
    cacc[:, :FAR_TXT] = jnp.zeros((8, FAR_TXT), F32)
    cacc[:, FAR_TXT:] = near_cacc[...]
    for ref in (rs, cs, dg, keep, send):
        ref[...] = jnp.zeros_like(ref)
    half = NEAR_IMG // 2
    tiles = [(FAR_IMG + r, half, 0, h_cols, r, 0) for r in (0, half)]
    tiles += [(0, FAR_IMG, c, h_rows, 0, c) for c in range(0, TXT, 256)]
    score_tiles(tiles, img, txt, (even, odd), racc, cacc)

    lowest = jnp.full((1, PIECE), jnp.inf, F32)
    for p in range(COLS):
        part = jnp.sum(racc[p * PIECE:(p + 1) * PIECE, :].T, axis=0, keepdims=True)
        rs[0, pl.ds(ids[p], 1), :] = part
        lowest = jnp.minimum(lowest, part)
    total = jnp.sum(cacc[...], axis=0, keepdims=True)
    for m in range(PARTS):
        part = total[:, m * PIECE:(m + 1) * PIECE]
        cs[0, pl.ds(ids[TXT_AT + m], 1), :] = part
        lowest = jnp.minimum(lowest, part)

    def half_of(p, m):
        at = p * PIECE if p < 2 * FAR else (p - 2 * FAR) * PIECE
        if p < 2 * FAR:
            return h_rows[at:at + PIECE, m * PIECE:(m + 1) * PIECE]
        if m < FAR:
            return h_cols[at:at + PIECE, m * PIECE:(m + 1) * PIECE]
        return near[at:at + PIECE, (m - FAR) * PIECE:(m - FAR + 1) * PIECE]

    @pl.when(jnp.min(lowest) < FLOOR)
    def _():
        for p in range(COLS):
            part = jnp.zeros((PIECE, PIECE), F32)
            for m in range(PARTS):
                g = half_of(p, m) * math.exp(0.5 * (SHIFT + LIFT))
                part += g * g
                cs[1, pl.ds(ids[TXT_AT + m], 1), :] += jnp.sum(g * g, axis=0, keepdims=True)
            rs[1, pl.ds(ids[p], 1), :] = jnp.sum(part.T, axis=0, keepdims=True)

    for p in range(COLS):
        match = ids[MATCH_AT + p]

        @pl.when(match >= 0)
        def _():
            other = txt[pl.ds(pl.multiple_of(match * PIECE, PIECE), PIECE), :]
            s = 100.0 * dot(img[p * PIECE:(p + 1) * PIECE, :], other, NT)
            dg[...] += jnp.sum(jnp.where(diagonal(), s, 0.0).reshape(16, 8, PIECE), axis=0)

    @pl.when(core == 0)
    def _():
        keep[0:2] = rs[...]
        keep[2, 0:8] = dg[...]
        send[0:2, 0:8] = cs[...]

    @pl.when(core == 1)
    def _():
        send[0:2] = rs[...]
        send[2, 0:8] = dg[...]
        keep[0:2, 8:16] = cs[...]


def far_scores(ids, here, there, near):
    sums = jax.ShapeDtypeStruct((3, COLS, PIECE), F32)
    return pl.pallas_call(
        far_kernel,
        out_shape=(
            jax.ShapeDtypeStruct((FAR_IMG, TXT), F32),
            jax.ShapeDtypeStruct((NEAR_IMG, FAR_TXT), F32),
            jax.ShapeDtypeStruct((IMG, WIDTH), BF),
            jax.ShapeDtypeStruct((TXT, WIDTH), BF),
            sums, sums,
        ),
        in_specs=[SM] + [VM] * 9,
        out_specs=(VM,) * 6,
        scratch_shapes=[
            pltpu.VMEM((NEAR_IMG // 2, 256), F32),
            pltpu.VMEM((NEAR_IMG // 2, 256), F32),
            pltpu.VMEM((IMG, PIECE), F32),
            pltpu.VMEM((8, TXT), F32),
            pltpu.VMEM((2, COLS, PIECE), F32),
            pltpu.VMEM((2, ROWS, PIECE), F32),
            pltpu.VMEM((8, PIECE), F32),
        ],
        compiler_params=PARAMS,
        cost_estimate=cost(2 * (IMG * TXT - NEAR_IMG * NEAR_TXT) * WIDTH, 16 << 20),
        name="far_scores",
    )(ids, *here, *there, *near)


def lse_of(sums):
    return jnp.where(sums[0] >= FLOOR, SHIFT + jnp.log(sums[0]), jnp.log(sums[1]) - LIFT)


def row_col_factors(core, own, far, a_s, b_s):
    scale = math.sqrt(0.5)
    factors = [scale * jnp.exp(0.5 * (SHIFT - lse_of(v))) for v in (own, far)]
    a_s[...] = jnp.where(core == 0, factors[0], factors[1])
    b_s[...] = jnp.where(core == 0, factors[1][:8], factors[0][8:])


def weights_block(ids, half, w, a_s, b_s, p0, p1, m0, m1):
    b = [b_s[pl.ds(ids[TXT_AT + m], 1), :] for m in range(m0, m1)]

    @pl.loop(p0, p1)
    def _(p):
        rows = pl.ds(pl.multiple_of((p - p0) * PIECE, PIECE), PIECE)
        a = jnp.broadcast_to(a_s[pl.ds(ids[p], 1), :], (PIECE, PIECE)).T
        for m in range(m1 - m0):
            cols = slice(m * PIECE, (m + 1) * PIECE)
            h = half[rows, cols]
            v, t = h * a, h * b[m]
            w[rows, cols] = (v * v + t * t).astype(BF)
        match = ids[MATCH_AT + p]

        @pl.when((match >= m0) & (match < m1))
        def _():
            cols = pl.ds(pl.multiple_of((match - m0) * PIECE, PIECE), PIECE)
            h = half[rows, cols]
            v, t = h * a, h * b_s[pl.ds(ids[TXT_AT + match], 1), :]
            w[rows, cols] = (v * v + t * t - diagonal().astype(F32)).astype(BF)


def product_kernel(start, end, kept_here, core, w_rows, w_cols, w_near, img, txt, out):
    first, last = start - FAR, end - FAR

    def image_side():
        if start < FAR:
            d = dot(w_rows[start * PART:end * PART, :], txt[...], NN)
        else:
            rows = slice(first * PART, last * PART)
            d = dot(w_cols[rows, :], txt[:FAR_TXT, :], NN)
            d = d + dot(w_near[rows, :], txt[FAR_TXT:, :], NN)
        out[...] = d.astype(BF)

    def text_side():
        at, pad = (PIECE, 0) if kept_here else (0, PIECE)
        d = dot(w_rows[:, start * PIECE:end * PIECE], img[:FAR_IMG, :], TN)
        if start < FAR:
            d = d + dot(w_cols[:, start * PIECE:end * PIECE], img[FAR_IMG:, :], TN)
        else:
            d = d + dot(w_near[:, first * PIECE:last * PIECE], img[FAR_IMG:, :], TN)
        d = d.astype(BF)
        for i in range(end - start):
            out[i * PART + at:i * PART + at + PIECE, :] = d[i * PIECE:(i + 1) * PIECE]
            out[i * PART + pad:i * PART + pad + PIECE, :] = jnp.zeros((PIECE, WIDTH), BF)

    pl.when(core == (0 if kept_here else 1))(image_side)
    pl.when(core == (1 if kept_here else 0))(text_side)


FACTORS = [pltpu.VMEM((COLS, PIECE), F32), pltpu.VMEM((ROWS, PIECE), F32)]


def far_products(ids, own, far, h_rows, h_cols, img, txt):
    def kernel(ids, own, far, h_rows, h_cols, img, txt, w_rows, w_cols, out, a_s, b_s):
        row_col_factors(ids[CORE], own, far, a_s, b_s)
        weights_block(ids, h_rows, w_rows, a_s, b_s, 0, 2 * FAR, 0, PARTS)
        weights_block(ids, h_cols, w_cols, a_s, b_s, 2 * FAR, COLS, 0, FAR)
        product_kernel(0, FAR, False, ids[CORE], w_rows, w_cols, None, img, txt, out)

    return pl.pallas_call(
        kernel,
        out_shape=(
            jax.ShapeDtypeStruct((FAR_IMG, TXT), BF),
            jax.ShapeDtypeStruct((NEAR_IMG, FAR_TXT), BF),
            jax.ShapeDtypeStruct((FAR * PART, WIDTH), BF),
        ),
        in_specs=[SM] + [VM] * 6,
        out_specs=(VM,) * 3,
        scratch_shapes=FACTORS,
        compiler_params=PARAMS,
        cost_estimate=cost(PRODUCT_FLOPS, 1),
        name="far_products",
    )(ids, own, far, h_rows, h_cols, img, txt)


def near_products(end, token, ids, own, far, near, w_rows, w_cols, img, txt):
    def kernel(token, ids, own, far, near, w_rows, w_cols, img, txt, w_near, out, a_s, b_s):
        row_col_factors(ids[CORE], own, far, a_s, b_s)
        weights_block(ids, near, w_near, a_s, b_s, 2 * FAR, COLS, FAR, PARTS)
        product_kernel(FAR, end, False, ids[CORE], w_rows, w_cols, w_near, img, txt, out)

    return pl.pallas_call(
        kernel,
        out_shape=(
            jax.ShapeDtypeStruct((NEAR_IMG, NEAR_TXT), BF),
            jax.ShapeDtypeStruct(((end - FAR) * PART, WIDTH), BF),
        ),
        in_specs=[VM, SM] + [VM] * 7,
        out_specs=(VM, VM),
        scratch_shapes=FACTORS,
        compiler_params=PARAMS,
        cost_estimate=cost(PRODUCT_FLOPS, 1),
        name="near_products",
    )(token, ids, own, far, near, w_rows, w_cols, img, txt)


def products(start, end, kept_here, tokens, ids, w, img, txt, flops=PRODUCT_FLOPS):
    def kernel(ids, img, txt, *refs):
        w_near = refs[2] if len(w) == 3 else None
        product_kernel(
            start, end, kept_here, ids[CORE], refs[0], refs[1], w_near, img, txt, refs[-1]
        )

    return pl.pallas_call(
        kernel,
        out_shape=jax.ShapeDtypeStruct(((end - start) * PART, WIDTH), BF),
        in_specs=[SM] + [VM] * (2 + len(w) + len(tokens)),
        out_specs=VM,
        compiler_params=PARAMS,
        cost_estimate=cost(flops, 1),
        name="products_kept" if kept_here else "products_sent",
    )(ids, img, txt, *w, *tokens)


def pack(value):
    pieces = []
    for _ in range(2):
        pieces.append(lax.reduce_precision(value, exponent_bits=8, mantissa_bits=7))
        value = value - pieces[-1]
    rows = jnp.concatenate([v.astype(BF) for v in (*pieces, value)], axis=1)
    return jnp.pad(rows, ((0, 8), (0, WIDTH - 3 * PIECE)))


def unpack(rows):
    return sum(rows[:8, i * PIECE:(i + 1) * PIECE].astype(F32) for i in range(3))


def with_tail(part, tail):
    return jnp.concatenate([part, tail])


def sum_kernel(own, kept, sent, *refs):
    parts, (keep, send) = refs[:-2], refs[-2:]
    core = lax.axis_index("col") % 2
    total = own[...].astype(F32) + kept[...].astype(F32) + sent[...].astype(F32)
    for r in parts:
        total = total + r[:PART, :].astype(F32)

    @pl.when(core == 0)
    def _():
        keep[...] = total[:PIECE]
        send[...] = total[PIECE:].astype(BF)

    @pl.when(core == 1)
    def _():
        keep[...] = total[PIECE:]
        send[...] = total[:PIECE].astype(BF)


def grad_kernel(image, text, keep, got, image_out, text_out):
    core = lax.axis_index("col") % 2

    def grad(values, total, out):
        x = values[...]
        norm = jnp.sqrt(jnp.sum(x * x, axis=1, keepdims=True) + 1e-06)
        unit = x / norm
        g = total[...].astype(F32)
        out[...] = (g - unit * jnp.sum(unit * g, axis=1, keepdims=True)) / norm

    @pl.when(core == 0)
    def _():
        grad(image, keep, image_out)
        grad(text, got, text_out)

    @pl.when(core == 1)
    def _():
        grad(image, got, image_out)
        grad(text, keep, text_out)


def per_device(image_embeds, text_embeds):
    here = lax.axis_index("row") * COLS + lax.axis_index("col")
    ids = lax.dynamic_index_in_dim(jnp.asarray(device_table()), here, keepdims=False)
    first = lax.axis_index("col") % 2 == 0

    keep, send = unit_pair(ids, image_embeds, text_embeds)
    got = swap(send)
    own = jnp.concatenate([jnp.where(first, keep, got), jnp.where(first, got, keep)])

    other = flip(own)
    left0, right0 = ring(own, 1), ring(own, 3)
    left1, right1 = ring(other, 1), ring(other, 3)
    far0, far1 = ring(left0, 1), ring(right1, 3)
    mine = [far0, far1, right1, left1, other, own, right0, left0]
    late, _ = lax.optimization_barrier((own, left0))
    theirs = [swap(late if v is own else v) for v in mine[FAR:]]
    near = near_scores(ids, mine[FAR:], theirs)
    far0, far1, *near = lax.optimization_barrier((far0, far1, *near))
    h_rows, h_cols, img, txt, keep, send = far_scores(
        ids, (far0, far1), (swap(far0), swap(far1)), near
    )
    sums = keep + swap(send)
    sums = group_sum(sums)
    theirs = swap(sums)

    def add(*v):
        return functools.reduce(lambda a, b: a + b, [u.astype(F32) for u in v]).astype(BF)

    def part(value, i):
        return value[i * PART:(i + 1) * PART]

    def mark(done):
        return swap(done[:16, :PIECE])

    w_rows, w_cols, sent = far_products(ids, sums, theirs, h_rows, h_cols, img, txt)
    sent = swap(sent)
    kept = products(0, FAR, True, (), ids, (w_rows, w_cols), img, txt)
    lse = lse_of(theirs).reshape(2, 8, PIECE).sum(0)
    lse = jnp.where(first, lse, lse - 2.0 * theirs[2, :8])
    tail = pack(lse)
    far0 = with_tail(add(part(kept, 0), part(sent, 0)), tail)
    far1 = with_tail(add(part(kept, 1), part(sent, 1)), tail)
    through0, through1 = ring(far0, 1), ring(far1, 3)

    w_near, sent = near_products(4, mark(far0), ids, sums, theirs, near[0], w_rows, w_cols, img, txt)
    w = (w_rows, w_cols, w_near)
    sent_on = products(4, 8, False, (), ids, w, img, txt)
    sent = swap(sent)
    kept = products(FAR, 4, True, (through0, through1, sent_on), ids, w, img, txt)
    sent_on = swap(sent_on)
    near1 = with_tail(add(part(kept, 0), part(sent, 0)), through0[PART:])
    back1 = add(part(kept, 1), part(sent, 1), part(through1, 0))
    right1, left1 = ring(near1, 1), ring(back1, 3)

    kept = products(4, 8, True, (mark(back1),), ids, w, img, txt)
    right0 = ring(add(part(kept, 2), part(sent_on, 2), part(through0, 0)), 1)
    left0 = ring(add(part(kept, 3), part(sent_on, 3)), 3)

    lse = lse + unpack(through0[PART:]) + unpack(through1[PART:]) + unpack(right1[PART:])
    last = add(part(kept, 0), part(sent_on, 0), part(right1, 0), left1)
    back = flip(with_tail(last, pack(lse)))
    lse = lse + unpack(back[PART:])
    shape = jax.ShapeDtypeStruct((PIECE, WIDTH), F32)
    keep, send = pl.pallas_call(
        sum_kernel, out_shape=(shape, jax.ShapeDtypeStruct((PIECE, WIDTH), BF)), in_specs=[VM] * 5, out_specs=(VM, VM),
        compiler_params=PARAMS, name="own_sums",
    )(part(kept, 1), part(sent_on, 1), right0, left0, back)
    got, there = swap(send), swap(lse)
    image_grad, text_grad = pl.pallas_call(
        grad_kernel, out_shape=(shape, shape), in_specs=[VM] * 4, out_specs=(VM, VM),
        compiler_params=PARAMS, name="grad_rows",
    )(image_embeds, text_embeds, keep, got)
    loss = jnp.sum(lse + there) / (2.0 * ROWS * COLS * PIECE)
    return (image_grad, text_grad, loss)


def solution(mesh):
    return jax.shard_map(
        per_device,
        mesh=mesh,
        in_specs=(P(("row", "col"), None), P(("col", "row"), None)),
        out_specs=(P(("row", "col"), None), P(("col", "row"), None), P()),
        check_vma=False,
    )
```

```python
import functools
import math

import jax
import jax.numpy as jnp
import numpy as np
from jax import lax
from jax.experimental import pallas as pl
from jax.experimental.pallas import tpu as pltpu
from jax.sharding import PartitionSpec as P

PIECE = 128
PART = 2 * PIECE
WIDTH = 1280
RING = 4
PART_AT = ((2, 0), (2, 1), (1, 1), (3, 1), (0, 1), (0, 0), (1, 0), (3, 0))
PARTS = len(PART_AT)
FAR = 2
ROWS, COLS = 8, 16
IMG = PARTS * PART
TXT = PARTS * PIECE
FAR_IMG, FAR_TXT = FAR * PART, FAR * PIECE
NEAR_IMG, NEAR_TXT = IMG - FAR_IMG, TXT - FAR_TXT
CORE, TXT_AT, MATCH_AT = 40, 32, 16
TAIL = 16
PRODUCT_FLOPS = 5 * 10**10

SHIFT = 22.0
LIFT = 70.0
FLOOR = math.exp(-62.0)
LOG2E = math.log2(math.e)

VM = pl.BlockSpec(memory_space=pltpu.VMEM)
SM = pl.BlockSpec(memory_space=pltpu.SMEM)
PARAMS = pltpu.CompilerParams(vmem_limit_bytes=8 * 1024 * 1024)
F32, BF = jnp.float32, jnp.bfloat16
NT = (((1,), (1,)), ((), ()))
NN = (((1,), (0,)), ((), ()))
TN = (((0,), (0,)), ((), ()))
AXES = ("row", "col")


def dot(a, b, dims):
    return lax.dot_general(a, b, dims, preferred_element_type=F32)


def device(yl, z, x, yh, k):
    return (yl * 4 + z) * COLS + (x * 2 + yh) * 2 + k


def places():
    return [
        (yl, z, x, yh, k)
        for yl in range(2) for z in range(RING) for x in range(RING) for yh in range(2) for k in range(2)
    ]


def neighbour(y, k):
    return y ^ 1 if k == 0 else (y + (1 if y % 2 else 3)) % RING


def group(value, d, side):
    pairs = []
    for yl, z, x, yh, k in places():
        y = yh * 2 + yl
        y = neighbour(y, k) if side else y
        target = device(y % 2, (z + d * k) % RING, (x + d * (1 - k)) % RING, y // 2, k)
        pairs.append((device(yl, z, x, yh, k), target))
    return lax.ppermute(value, AXES, pairs)


def ring(value, d):
    return group(value, d, 0)


def flip(value):
    return group(value, 0, 1)


def group_sum(value):
    value = value + ring(value, 1) + ring(value, 2) + ring(value, 3)
    return value + flip(value)


def swap(value):
    return lax.ppermute(value, AXES, [
        (device(yl, z, x, yh, k), device(yl, z, x, yh, 1 - k)) for yl, z, x, yh, k in places()
    ])


def device_table():
    table = np.zeros((ROWS * COLS, 41), np.int32)
    for yl, z, x, yh, k in places():
        y = yh * 2 + yl
        img, match, txt, owned = [], [], [], []
        for d, side in PART_AT:
            zt, yt = (z + d) % RING, neighbour(y, 1) if side else y
            txt.append(zt * 2 + (yt + 1) % 2)
            owner = device(yt % 2, zt, x, yt // 2, k)
            owned.append(owner % COLS * ROWS + owner // COLS)
        for d, side in PART_AT:
            xi, yi = (x + d) % RING, neighbour(y, 0) if side else y
            for h in range(2):
                img.append((xi * 2 + yi % 2) * 2 + h)
                piece = device(yi % 2, z, xi, yi // 2, h)
                match.append(owned.index(piece) if piece in owned else -1)
        table[device(yl, z, x, yh, k)] = img + match + txt + [k]
    return table


def cost(flops, bytes_accessed):
    return pl.CostEstimate(flops=flops, bytes_accessed=bytes_accessed, transcendentals=0)


def diagonal():
    shape = (PIECE, PIECE)
    return lax.broadcasted_iota(jnp.int32, shape, 0) == lax.broadcasted_iota(jnp.int32, shape, 1)


def unit_kernel(image_ref, text_ref, keep_ref, send_ref):
    core = lax.axis_index("col") % 2

    def unit(src):
        x = src[...]
        return (x / jnp.sqrt(jnp.sum(x * x, axis=1, keepdims=True) + 1e-06)).astype(BF)

    image, text = unit(image_ref), unit(text_ref)

    @pl.when(core == 0)
    def _():
        keep_ref[...] = image
        send_ref[...] = text

    @pl.when(core == 1)
    def _():
        keep_ref[...] = text
        send_ref[...] = image


def unit_pair(image, text):
    shape = jax.ShapeDtypeStruct((PIECE, WIDTH), BF)
    return pl.pallas_call(
        unit_kernel, out_shape=(shape, shape), in_specs=[VM, VM], out_specs=(VM, VM),
        compiler_params=PARAMS, name="unit_rows",
    )(image, text)


def place_parts(core, here, there, img, txt):
    @pl.when(core == 0)
    def _():
        for m, (mine, other) in enumerate(zip(here, there)):
            img[m * PART:(m + 1) * PART, :] = mine[...]
            txt[m * PIECE:(m + 1) * PIECE, :] = other[:PIECE, :]

    @pl.when(core == 1)
    def _():
        for m, (mine, other) in enumerate(zip(here, there)):
            img[m * PART:(m + 1) * PART, :] = other[...]
            txt[m * PIECE:(m + 1) * PIECE, :] = mine[PIECE:, :]


def score_tiles(tiles, img, txt, held, racc, cacc):
    def epilogue(t):
        row, rows, col, h_out, h_row, h_col = tiles[t]
        cols = slice(col, col + 256)
        total = jnp.zeros((8, 256), F32)
        for p in range(0, rows, PIECE):
            d = held[t % 2][p:p + PIECE, :]
            h = jnp.exp2(d * (50.0 * LOG2E) - (0.5 * SHIFT * LOG2E))
            h_out[h_row + p:h_row + p + PIECE, h_col:h_col + 256] = h
            q = h * h
            racc[row + p:row + p + PIECE, :] += q[:, :PIECE] + q[:, PIECE:]
            total += jnp.sum(q.reshape(16, 8, 256), axis=0)
        cacc[:, cols] += total

    for t, (row, rows, col, *_) in enumerate(tiles):
        held[t % 2][:rows, :] = dot(img[row:row + rows, :], txt[col:col + 256, :], NT)
        if t:
            epilogue(t - 1)
    epilogue(len(tiles) - 1)


def near_kernel(ids, *refs):
    count = PARTS - FAR
    here, there = refs[:count], refs[count:2 * count]
    h_out, img, txt, racc, cacc, even, odd = refs[2 * count:]
    place_parts(ids[CORE], here, there, img, txt)
    racc[...] = jnp.zeros_like(racc)
    cacc[...] = jnp.zeros_like(cacc)
    half = NEAR_IMG // 2
    tiles = [(r, half, c, h_out, r, c) for c in range(0, NEAR_TXT, 256) for r in (0, half)]
    score_tiles(tiles, img, txt, (even, odd), racc, cacc)


def near_scores(ids, here, there):
    return list(pl.pallas_call(
        near_kernel,
        out_shape=(
            jax.ShapeDtypeStruct((NEAR_IMG, NEAR_TXT), F32),
            jax.ShapeDtypeStruct((NEAR_IMG, WIDTH), BF),
            jax.ShapeDtypeStruct((NEAR_TXT, WIDTH), BF),
            jax.ShapeDtypeStruct((NEAR_IMG, PIECE), F32),
            jax.ShapeDtypeStruct((8, NEAR_TXT), F32),
        ),
        in_specs=[SM] + [VM] * (2 * len(here)),
        out_specs=(VM,) * 5,
        scratch_shapes=[pltpu.VMEM((NEAR_IMG // 2, 256), F32)] * 2,
        compiler_params=PARAMS,
        cost_estimate=cost(1, 1),
        name="near_scores",
    )(ids, *here, *there))


def far_kernel(ids, here0, here1, there0, there1, near, near_img, near_txt, near_racc, near_cacc,
               h_rows, h_cols, img, txt, keep, send, even, odd, racc, cacc, rs, cs, dg):
    core = ids[CORE]
    place_parts(core, (here0, here1), (there0, there1), img, txt)
    img[FAR_IMG:, :] = near_img[...]
    txt[FAR_TXT:, :] = near_txt[...]
    racc[:FAR_IMG, :] = jnp.zeros((FAR_IMG, PIECE), F32)
    racc[FAR_IMG:, :] = near_racc[...]
    cacc[:, :FAR_TXT] = jnp.zeros((8, FAR_TXT), F32)
    cacc[:, FAR_TXT:] = near_cacc[...]
    for ref in (rs, cs, dg, keep, send):
        ref[...] = jnp.zeros_like(ref)
    half = NEAR_IMG // 2
    tiles = [(FAR_IMG + r, half, 0, h_cols, r, 0) for r in (0, half)]
    tiles += [(0, FAR_IMG, c, h_rows, 0, c) for c in range(0, TXT, 256)]
    score_tiles(tiles, img, txt, (even, odd), racc, cacc)

    lowest = jnp.full((1, PIECE), jnp.inf, F32)
    for p in range(COLS):
        part = jnp.sum(racc[p * PIECE:(p + 1) * PIECE, :].T, axis=0, keepdims=True)
        rs[0, pl.ds(ids[p], 1), :] = part
        lowest = jnp.minimum(lowest, part)
    total = jnp.sum(cacc[...], axis=0, keepdims=True)
    for m in range(PARTS):
        part = total[:, m * PIECE:(m + 1) * PIECE]
        cs[0, pl.ds(ids[TXT_AT + m], 1), :] = part
        lowest = jnp.minimum(lowest, part)

    def half_of(p, m):
        at = p * PIECE if p < 2 * FAR else (p - 2 * FAR) * PIECE
        if p < 2 * FAR:
            return h_rows[at:at + PIECE, m * PIECE:(m + 1) * PIECE]
        if m < FAR:
            return h_cols[at:at + PIECE, m * PIECE:(m + 1) * PIECE]
        return near[at:at + PIECE, (m - FAR) * PIECE:(m - FAR + 1) * PIECE]

    @pl.when(jnp.min(lowest) < FLOOR)
    def _():
        for p in range(COLS):
            part = jnp.zeros((PIECE, PIECE), F32)
            for m in range(PARTS):
                g = half_of(p, m) * math.exp(0.5 * (SHIFT + LIFT))
                part += g * g
                cs[1, pl.ds(ids[TXT_AT + m], 1), :] += jnp.sum(g * g, axis=0, keepdims=True)
            rs[1, pl.ds(ids[p], 1), :] = jnp.sum(part.T, axis=0, keepdims=True)

    for p in range(COLS):
        match = ids[MATCH_AT + p]

        @pl.when(match >= 0)
        def _():
            other = txt[pl.ds(pl.multiple_of(match * PIECE, PIECE), PIECE), :]
            s = 100.0 * dot(img[p * PIECE:(p + 1) * PIECE, :], other, NT)
            dg[...] += jnp.sum(jnp.where(diagonal(), s, 0.0).reshape(16, 8, PIECE), axis=0)

    @pl.when(core == 0)
    def _():
        keep[0:2] = rs[...]
        keep[2, 0:8] = dg[...]
        send[0:2, 0:8] = cs[...]

    @pl.when(core == 1)
    def _():
        send[0:2] = rs[...]
        send[2, 0:8] = dg[...]
        keep[0:2, 8:16] = cs[...]


def far_scores(ids, here, there, near):
    sums = jax.ShapeDtypeStruct((3, COLS, PIECE), F32)
    return pl.pallas_call(
        far_kernel,
        out_shape=(
            jax.ShapeDtypeStruct((FAR_IMG, TXT), F32),
            jax.ShapeDtypeStruct((NEAR_IMG, FAR_TXT), F32),
            jax.ShapeDtypeStruct((IMG, WIDTH), BF),
            jax.ShapeDtypeStruct((TXT, WIDTH), BF),
            sums, sums,
        ),
        in_specs=[SM] + [VM] * 9,
        out_specs=(VM,) * 6,
        scratch_shapes=[
            pltpu.VMEM((NEAR_IMG // 2, 256), F32),
            pltpu.VMEM((NEAR_IMG // 2, 256), F32),
            pltpu.VMEM((IMG, PIECE), F32),
            pltpu.VMEM((8, TXT), F32),
            pltpu.VMEM((2, COLS, PIECE), F32),
            pltpu.VMEM((2, ROWS, PIECE), F32),
            pltpu.VMEM((8, PIECE), F32),
        ],
        compiler_params=PARAMS,
        cost_estimate=cost(2 * (IMG * TXT - NEAR_IMG * NEAR_TXT) * WIDTH, 16 << 20),
        name="far_scores",
    )(ids, *here, *there, *near)


def lse_of(sums):
    return jnp.where(sums[0] >= FLOOR, SHIFT + jnp.log(sums[0]), jnp.log(sums[1]) - LIFT)


def row_col_factors(core, own, far, a_s, b_s):
    scale = math.sqrt(0.5)
    factors = [scale * jnp.exp(0.5 * (SHIFT - lse_of(v))) for v in (own, far)]
    a_s[...] = jnp.where(core == 0, factors[0], factors[1])
    b_s[...] = jnp.where(core == 0, factors[1][:8], factors[0][8:])


def weights_block(ids, half, w, a_s, b_s, p0, p1, m0, m1):
    b = [b_s[pl.ds(ids[TXT_AT + m], 1), :] for m in range(m0, m1)]

    @pl.loop(p0, p1)
    def _(p):
        rows = pl.ds(pl.multiple_of((p - p0) * PIECE, PIECE), PIECE)
        a = jnp.broadcast_to(a_s[pl.ds(ids[p], 1), :], (PIECE, PIECE)).T
        for m in range(m1 - m0):
            cols = slice(m * PIECE, (m + 1) * PIECE)
            h = half[rows, cols]
            v, t = h * a, h * b[m]
            w[rows, cols] = (v * v + t * t).astype(BF)
        match = ids[MATCH_AT + p]

        @pl.when((match >= m0) & (match < m1))
        def _():
            cols = pl.ds(pl.multiple_of((match - m0) * PIECE, PIECE), PIECE)
            h = half[rows, cols]
            v, t = h * a, h * b_s[pl.ds(ids[TXT_AT + match], 1), :]
            w[rows, cols] = (v * v + t * t - diagonal().astype(F32)).astype(BF)


def product_kernel(start, end, kept_here, core, w_rows, w_cols, w_near, img, txt, out):
    first, last = start - FAR, end - FAR

    def image_side():
        if start < FAR:
            d = dot(w_rows[start * PART:end * PART, :], txt[...], NN)
        else:
            rows = slice(first * PART, last * PART)
            d = dot(w_cols[rows, :], txt[:FAR_TXT, :], NN)
            d = d + dot(w_near[rows, :], txt[FAR_TXT:, :], NN)
        out[...] = d.astype(BF)

    def text_side():
        at, pad = (PIECE, 0) if kept_here else (0, PIECE)
        d = dot(w_rows[:, start * PIECE:end * PIECE], img[:FAR_IMG, :], TN)
        if start < FAR:
            d = d + dot(w_cols[:, start * PIECE:end * PIECE], img[FAR_IMG:, :], TN)
        else:
            d = d + dot(w_near[:, first * PIECE:last * PIECE], img[FAR_IMG:, :], TN)
        d = d.astype(BF)
        for i in range(end - start):
            out[i * PART + at:i * PART + at + PIECE, :] = d[i * PIECE:(i + 1) * PIECE]
            out[i * PART + pad:i * PART + pad + PIECE, :] = jnp.zeros((PIECE, WIDTH), BF)

    pl.when(core == (0 if kept_here else 1))(image_side)
    pl.when(core == (1 if kept_here else 0))(text_side)


FACTORS = [pltpu.VMEM((COLS, PIECE), F32), pltpu.VMEM((ROWS, PIECE), F32)]


def far_products(ids, own, far, h_rows, h_cols, img, txt):
    def kernel(ids, own, far, h_rows, h_cols, img, txt, w_rows, w_cols, out, a_s, b_s):
        row_col_factors(ids[CORE], own, far, a_s, b_s)
        weights_block(ids, h_rows, w_rows, a_s, b_s, 0, 2 * FAR, 0, PARTS)
        weights_block(ids, h_cols, w_cols, a_s, b_s, 2 * FAR, COLS, 0, FAR)
        product_kernel(0, FAR, False, ids[CORE], w_rows, w_cols, None, img, txt, out)

    return pl.pallas_call(
        kernel,
        out_shape=(
            jax.ShapeDtypeStruct((FAR_IMG, TXT), BF),
            jax.ShapeDtypeStruct((NEAR_IMG, FAR_TXT), BF),
            jax.ShapeDtypeStruct((FAR * PART, WIDTH), BF),
        ),
        in_specs=[SM] + [VM] * 6,
        out_specs=(VM,) * 3,
        scratch_shapes=FACTORS,
        compiler_params=PARAMS,
        cost_estimate=cost(PRODUCT_FLOPS, 1),
        name="far_products",
    )(ids, own, far, h_rows, h_cols, img, txt)


def near_products(end, token, ids, own, far, near, w_rows, w_cols, img, txt):
    def kernel(token, ids, own, far, near, w_rows, w_cols, img, txt, w_near, out, a_s, b_s):
        row_col_factors(ids[CORE], own, far, a_s, b_s)
        weights_block(ids, near, w_near, a_s, b_s, 2 * FAR, COLS, FAR, PARTS)
        product_kernel(FAR, end, False, ids[CORE], w_rows, w_cols, w_near, img, txt, out)

    return pl.pallas_call(
        kernel,
        out_shape=(
            jax.ShapeDtypeStruct((NEAR_IMG, NEAR_TXT), BF),
            jax.ShapeDtypeStruct(((end - FAR) * PART, WIDTH), BF),
        ),
        in_specs=[VM, SM] + [VM] * 7,
        out_specs=(VM, VM),
        scratch_shapes=FACTORS,
        compiler_params=PARAMS,
        cost_estimate=cost(PRODUCT_FLOPS, 1),
        name="near_products",
    )(token, ids, own, far, near, w_rows, w_cols, img, txt)


def products(start, end, kept_here, tokens, ids, w, img, txt, flops=PRODUCT_FLOPS):
    def kernel(ids, img, txt, *refs):
        w_near = refs[2] if len(w) == 3 else None
        product_kernel(
            start, end, kept_here, ids[CORE], refs[0], refs[1], w_near, img, txt, refs[-1]
        )

    return pl.pallas_call(
        kernel,
        out_shape=jax.ShapeDtypeStruct(((end - start) * PART, WIDTH), BF),
        in_specs=[SM] + [VM] * (2 + len(w) + len(tokens)),
        out_specs=VM,
        compiler_params=PARAMS,
        cost_estimate=cost(flops, 1),
        name="products_kept" if kept_here else "products_sent",
    )(ids, img, txt, *w, *tokens)


def pack(value):
    pieces = []
    for _ in range(2):
        pieces.append(lax.reduce_precision(value, exponent_bits=8, mantissa_bits=7))
        value = value - pieces[-1]
    rows = jnp.concatenate([v.astype(BF) for v in (*pieces, value)], axis=1)
    return jnp.pad(rows, ((0, 8), (0, WIDTH - 3 * PIECE)))


def unpack(rows):
    return sum(rows[:8, i * PIECE:(i + 1) * PIECE].astype(F32) for i in range(3))


def with_tail(part, tail):
    return jnp.concatenate([part, tail])


def sum_kernel(ids, own, sent, right, left, back, lse, keep, send, lse_out):
    core = ids[CORE]
    total = own[...].astype(F32) + sent[...].astype(F32) + right[...].astype(F32)
    total = total + left[...].astype(F32) + back[:PART, :].astype(F32)
    terms = lse[...]
    for i in range(3):
        terms = terms + back[PART:, i * PIECE:(i + 1) * PIECE].astype(F32)[:8]
    lse_out[...] = terms
    send[PIECE:, :] = jnp.zeros((TAIL, WIDTH), BF)
    pad = jnp.zeros((TAIL - 8, PIECE), F32)
    for i in range(3):
        piece = terms.astype(BF).astype(F32)
        send[PIECE:, i * PIECE:(i + 1) * PIECE] = jnp.concatenate([piece, pad]).astype(BF)
        terms = terms - piece

    @pl.when(core == 0)
    def _():
        keep[...] = total[:PIECE]
        send[:PIECE, :] = total[PIECE:].astype(BF)

    @pl.when(core == 1)
    def _():
        keep[...] = total[PIECE:]
        send[:PIECE, :] = total[:PIECE].astype(BF)


def grad_kernel(ids, image, text, keep, got, lse, image_out, text_out, loss_out):
    core = ids[CORE]

    def grad(values, total, out):
        x = values[...]
        norm = jnp.sqrt(jnp.sum(x * x, axis=1, keepdims=True) + 1e-06)
        unit = x / norm
        g = total[:PIECE, :].astype(F32)
        out[...] = (g - unit * jnp.sum(unit * g, axis=1, keepdims=True)) / norm

    @pl.when(core == 0)
    def _():
        grad(image, keep, image_out)
        grad(text, got, text_out)

    @pl.when(core == 1)
    def _():
        grad(image, got, image_out)
        grad(text, keep, text_out)

    terms = lse[...]
    for i in range(3):
        terms = terms + got[PIECE:, i * PIECE:(i + 1) * PIECE].astype(F32)[:8]
    total = jnp.sum(jnp.sum(terms, axis=0, keepdims=True), axis=1, keepdims=True)
    loss_out[...] = total * (1.0 / (2.0 * ROWS * COLS * PIECE))


def per_device(image_embeds, text_embeds):
    here = lax.axis_index("row") * COLS + lax.axis_index("col")
    first = lax.axis_index("col") % 2 == 0

    keep, send = unit_pair(image_embeds, text_embeds)
    got = swap(send)
    here, keep = lax.optimization_barrier((here, keep))
    ids = lax.dynamic_index_in_dim(jnp.asarray(device_table()), here, keepdims=False)
    own = jnp.concatenate([jnp.where(first, keep, got), jnp.where(first, got, keep)])
    own, ids = lax.optimization_barrier((own, ids))

    other = flip(own)
    left0, right0 = ring(own, 1), ring(own, 3)
    left1, right1 = ring(other, 1), ring(other, 3)
    across = swap(other)
    from_left, across = lax.optimization_barrier((left0, across))
    far0, far1 = ring(from_left, 1), ring(right1, 3)
    mine = [right1, left1, other, own, right0, left0]
    late, _ = lax.optimization_barrier((own, other))
    theirs = [swap(right1), swap(left1), across, swap(late), swap(right0), swap(left0)]
    near = near_scores(ids, mine, theirs)
    far0, far1, near[0] = lax.optimization_barrier((far0, far1, near[0]))
    h_rows, h_cols, img, txt, keep, send = far_scores(
        ids, (far0, far1), (swap(far0), swap(far1)), near
    )
    sums = keep + swap(send)
    sums = group_sum(sums)
    theirs = swap(sums)

    def add(*v):
        return functools.reduce(lambda a, b: a + b, [u.astype(F32) for u in v]).astype(BF)

    def part(value, i):
        return value[i * PART:(i + 1) * PART]

    def mark(done):
        return swap(done[:16, :PIECE])

    w_rows, w_cols, sent = far_products(ids, sums, theirs, h_rows, h_cols, img, txt)
    sent = swap(sent)
    kept = products(0, FAR, True, (), ids, (w_rows, w_cols), img, txt)
    lse = lse_of(theirs).reshape(2, 8, PIECE).sum(0)
    lse = jnp.where(first, lse, lse - 2.0 * theirs[2, :8])
    tail = pack(lse)
    far0 = with_tail(add(part(kept, 0), part(sent, 0)), tail)
    far1 = with_tail(add(part(kept, 1), part(sent, 1)), tail)
    through0, through1 = ring(far0, 1), ring(far1, 3)

    w_near, sent = near_products(4, mark(far0), ids, sums, theirs, near[0], w_rows, w_cols, img, txt)
    w = (w_rows, w_cols, w_near)
    sent_on = products(4, 8, False, (), ids, w, img, txt)
    sent = swap(sent)
    kept = products(FAR, 4, True, (through0, through1, sent_on), ids, w, img, txt)
    sent_on = swap(sent_on)
    near1 = with_tail(add(part(kept, 0), part(sent, 0)), through0[PART:])
    back1 = add(part(kept, 1), part(sent, 1), part(through1, 0))
    right1, left1 = ring(near1, 1), ring(back1, 3)

    kept = products(6, 8, True, (mark(back1),), ids, w, img, txt)
    near0 = add(part(kept, 0), part(sent_on, 2), part(through0, 0))
    right0, left0 = ring(near0, 1), ring(add(part(kept, 1), part(sent_on, 3)), 3)
    kept = products(4, 6, True, (mark(near0),), ids, w, img, txt)

    lse = lse + unpack(through0[PART:]) + unpack(through1[PART:]) + unpack(right1[PART:])
    last = add(part(kept, 0), part(sent_on, 0), part(right1, 0), left1)
    back = flip(with_tail(last, pack(lse)))
    shape = jax.ShapeDtypeStruct((PIECE, WIDTH), F32)
    lane = jax.ShapeDtypeStruct((8, PIECE), F32)
    keep, send, lse = pl.pallas_call(
        sum_kernel,
        out_shape=(shape, jax.ShapeDtypeStruct((PIECE + TAIL, WIDTH), BF), lane),
        in_specs=[SM] + [VM] * 6, out_specs=(VM, VM, VM),
        compiler_params=PARAMS, name="own_sums",
    )(ids, part(kept, 1), part(sent_on, 1), right0, left0, back, lse)
    image_grad, text_grad, loss = pl.pallas_call(
        grad_kernel,
        out_shape=(shape, shape, jax.ShapeDtypeStruct((1, 1), F32)),
        in_specs=[SM] + [VM] * 5, out_specs=(VM, VM, VM),
        compiler_params=PARAMS, name="grad_rows",
    )(ids, image_embeds, text_embeds, keep, swap(send), lse)
    loss = loss[0, 0]
    return (image_grad, text_grad, loss)


def solution(mesh):
    return jax.shard_map(
        per_device,
        mesh=mesh,
        in_specs=(P(("row", "col"), None), P(("col", "row"), None)),
        out_specs=(P(("row", "col"), None), P(("col", "row"), None), P()),
        check_vma=False,
    )
```

```python
import functools
import math

import jax
import jax.numpy as jnp
import numpy as np
from jax import lax
from jax.experimental import pallas as pl
from jax.experimental.pallas import tpu as pltpu
from jax.sharding import PartitionSpec as P

PIECE = 128
PART = 2 * PIECE
WIDTH = 1280
RING = 4
PART_AT = ((2, 0), (2, 1), (1, 1), (3, 1), (0, 1), (0, 0), (1, 0), (3, 0))
PARTS = len(PART_AT)
FAR = 2
ROWS, COLS = 8, 16
IMG = PARTS * PART
TXT = PARTS * PIECE
FAR_IMG, FAR_TXT = FAR * PART, FAR * PIECE
NEAR_IMG, NEAR_TXT = IMG - FAR_IMG, TXT - FAR_TXT
CORE, TXT_AT, MATCH_AT = 40, 32, 16
TAIL = 16
PRODUCT_FLOPS = 5 * 10**10

SHIFT = 22.0
LIFT = 70.0
FLOOR = math.exp(-62.0)
LOG2E = math.log2(math.e)

VM = pl.BlockSpec(memory_space=pltpu.VMEM)
SM = pl.BlockSpec(memory_space=pltpu.SMEM)
PARAMS = pltpu.CompilerParams(vmem_limit_bytes=8 * 1024 * 1024)
F32, BF = jnp.float32, jnp.bfloat16
NT = (((1,), (1,)), ((), ()))
NN = (((1,), (0,)), ((), ()))
TN = (((0,), (0,)), ((), ()))
AXES = ("row", "col")


def dot(a, b, dims):
    return lax.dot_general(a, b, dims, preferred_element_type=F32)


def device(yl, z, x, yh, k):
    return (yl * 4 + z) * COLS + (x * 2 + yh) * 2 + k


def places():
    return [
        (yl, z, x, yh, k)
        for yl in range(2) for z in range(RING) for x in range(RING) for yh in range(2) for k in range(2)
    ]


def neighbour(y, k):
    return y ^ 1 if k == 0 else (y + (1 if y % 2 else 3)) % RING


def group(value, d, side):
    pairs = []
    for yl, z, x, yh, k in places():
        y = yh * 2 + yl
        y = neighbour(y, k) if side else y
        target = device(y % 2, (z + d * k) % RING, (x + d * (1 - k)) % RING, y // 2, k)
        pairs.append((device(yl, z, x, yh, k), target))
    return lax.ppermute(value, AXES, pairs)


def ring(value, d):
    return group(value, d, 0)


def flip(value):
    return group(value, 0, 1)


def group_sum(value):
    value = value + ring(value, 1) + ring(value, 2) + ring(value, 3)
    return value + flip(value)


def swap(value):
    return lax.ppermute(value, AXES, [
        (device(yl, z, x, yh, k), device(yl, z, x, yh, 1 - k)) for yl, z, x, yh, k in places()
    ])


def device_table():
    table = np.zeros((ROWS * COLS, 41), np.int32)
    for yl, z, x, yh, k in places():
        y = yh * 2 + yl
        img, match, txt, owned = [], [], [], []
        for d, side in PART_AT:
            zt, yt = (z + d) % RING, neighbour(y, 1) if side else y
            txt.append(zt * 2 + (yt + 1) % 2)
            owner = device(yt % 2, zt, x, yt // 2, k)
            owned.append(owner % COLS * ROWS + owner // COLS)
        for d, side in PART_AT:
            xi, yi = (x + d) % RING, neighbour(y, 0) if side else y
            for h in range(2):
                img.append((xi * 2 + yi % 2) * 2 + h)
                piece = device(yi % 2, z, xi, yi // 2, h)
                match.append(owned.index(piece) if piece in owned else -1)
        table[device(yl, z, x, yh, k)] = img + match + txt + [k]
    return table


def cost(flops, bytes_accessed):
    return pl.CostEstimate(flops=flops, bytes_accessed=bytes_accessed, transcendentals=0)


def diagonal():
    shape = (PIECE, PIECE)
    return lax.broadcasted_iota(jnp.int32, shape, 0) == lax.broadcasted_iota(jnp.int32, shape, 1)


def unit_kernel(image_ref, text_ref, keep_ref, send_ref):
    core = lax.axis_index("col") % 2

    def unit(src):
        x = src[...]
        return (x / jnp.sqrt(jnp.sum(x * x, axis=1, keepdims=True) + 1e-06)).astype(BF)

    image, text = unit(image_ref), unit(text_ref)

    @pl.when(core == 0)
    def _():
        keep_ref[...] = image
        send_ref[...] = text

    @pl.when(core == 1)
    def _():
        keep_ref[...] = text
        send_ref[...] = image


def unit_pair(image, text):
    shape = jax.ShapeDtypeStruct((PIECE, WIDTH), BF)
    return pl.pallas_call(
        unit_kernel, out_shape=(shape, shape), in_specs=[VM, VM], out_specs=(VM, VM),
        compiler_params=PARAMS, name="unit_rows",
    )(image, text)


def place_parts(core, here, there, img, txt):
    @pl.when(core == 0)
    def _():
        for m, (mine, other) in enumerate(zip(here, there)):
            img[m * PART:(m + 1) * PART, :] = mine[...]
            txt[m * PIECE:(m + 1) * PIECE, :] = other[:PIECE, :]

    @pl.when(core == 1)
    def _():
        for m, (mine, other) in enumerate(zip(here, there)):
            img[m * PART:(m + 1) * PART, :] = other[...]
            txt[m * PIECE:(m + 1) * PIECE, :] = mine[PIECE:, :]


def score_tiles(tiles, img, txt, held, racc, cacc):
    def epilogue(t):
        row, rows, col, h_out, h_row, h_col = tiles[t]
        cols = slice(col, col + 256)
        total = jnp.zeros((8, 256), F32)
        for p in range(0, rows, PIECE):
            d = held[t % 2][p:p + PIECE, :]
            h = jnp.exp2(d * (50.0 * LOG2E) - (0.5 * SHIFT * LOG2E))
            h_out[h_row + p:h_row + p + PIECE, h_col:h_col + 256] = h
            q = h * h
            racc[row + p:row + p + PIECE, :] += q[:, :PIECE] + q[:, PIECE:]
            total += jnp.sum(q.reshape(16, 8, 256), axis=0)
        cacc[:, cols] += total

    for t, (row, rows, col, *_) in enumerate(tiles):
        held[t % 2][:rows, :] = dot(img[row:row + rows, :], txt[col:col + 256, :], NT)
        if t:
            epilogue(t - 1)
    epilogue(len(tiles) - 1)


def near_kernel(ids, *refs):
    count = PARTS - FAR
    here, there = refs[:count], refs[count:2 * count]
    h_out, img, txt, racc, cacc, even, odd = refs[2 * count:]
    place_parts(ids[CORE], here, there, img, txt)
    racc[...] = jnp.zeros_like(racc)
    cacc[...] = jnp.zeros_like(cacc)
    half = NEAR_IMG // 2
    tiles = [(r, half, c, h_out, r, c) for c in range(0, NEAR_TXT, 256) for r in (0, half)]
    score_tiles(tiles, img, txt, (even, odd), racc, cacc)


def near_scores(ids, here, there):
    return list(pl.pallas_call(
        near_kernel,
        out_shape=(
            jax.ShapeDtypeStruct((NEAR_IMG, NEAR_TXT), F32),
            jax.ShapeDtypeStruct((NEAR_IMG, WIDTH), BF),
            jax.ShapeDtypeStruct((NEAR_TXT, WIDTH), BF),
            jax.ShapeDtypeStruct((NEAR_IMG, PIECE), F32),
            jax.ShapeDtypeStruct((8, NEAR_TXT), F32),
        ),
        in_specs=[SM] + [VM] * (2 * len(here)),
        out_specs=(VM,) * 5,
        scratch_shapes=[pltpu.VMEM((NEAR_IMG // 2, 256), F32)] * 2,
        compiler_params=PARAMS,
        cost_estimate=cost(1, 1),
        name="near_scores",
    )(ids, *here, *there))


def far_kernel(ids, *refs):
    here, there = refs[:2 * FAR], refs[2 * FAR:4 * FAR]
    near, near_img, near_txt, near_racc, near_cacc = refs[4 * FAR:4 * FAR + 5]
    h_rows, h_cols, img, txt, keep, send = refs[4 * FAR + 5:4 * FAR + 11]
    even, odd, racc, cacc, rs, cs, dg = refs[4 * FAR + 11:]
    core = ids[CORE]

    @pl.when(core == 0)
    def _():
        for i, mine in enumerate(here):
            img[i * PIECE:(i + 1) * PIECE, :] = mine[...]
        for i in range(FAR):
            txt[i * PIECE:(i + 1) * PIECE, :] = there[2 * i][...]

    @pl.when(core == 1)
    def _():
        for i, other in enumerate(there):
            img[i * PIECE:(i + 1) * PIECE, :] = other[...]
        for i in range(FAR):
            txt[i * PIECE:(i + 1) * PIECE, :] = here[2 * i + 1][...]

    img[FAR_IMG:, :] = near_img[...]
    txt[FAR_TXT:, :] = near_txt[...]
    racc[:FAR_IMG, :] = jnp.zeros((FAR_IMG, PIECE), F32)
    racc[FAR_IMG:, :] = near_racc[...]
    cacc[:, :FAR_TXT] = jnp.zeros((8, FAR_TXT), F32)
    cacc[:, FAR_TXT:] = near_cacc[...]
    for ref in (rs, cs, dg, keep, send):
        ref[...] = jnp.zeros_like(ref)
    half = NEAR_IMG // 2
    tiles = [(FAR_IMG + r, half, 0, h_cols, r, 0) for r in (0, half)]
    tiles += [(0, FAR_IMG, c, h_rows, 0, c) for c in range(0, TXT, 256)]
    score_tiles(tiles, img, txt, (even, odd), racc, cacc)

    lowest = jnp.full((1, PIECE), jnp.inf, F32)
    for p in range(COLS):
        part = jnp.sum(racc[p * PIECE:(p + 1) * PIECE, :].T, axis=0, keepdims=True)
        rs[0, pl.ds(ids[p], 1), :] = part
        lowest = jnp.minimum(lowest, part)
    total = jnp.sum(cacc[...], axis=0, keepdims=True)
    for m in range(PARTS):
        part = total[:, m * PIECE:(m + 1) * PIECE]
        cs[0, pl.ds(ids[TXT_AT + m], 1), :] = part
        lowest = jnp.minimum(lowest, part)

    def half_of(p, m):
        at = p * PIECE if p < 2 * FAR else (p - 2 * FAR) * PIECE
        if p < 2 * FAR:
            return h_rows[at:at + PIECE, m * PIECE:(m + 1) * PIECE]
        if m < FAR:
            return h_cols[at:at + PIECE, m * PIECE:(m + 1) * PIECE]
        return near[at:at + PIECE, (m - FAR) * PIECE:(m - FAR + 1) * PIECE]

    @pl.when(jnp.min(lowest) < FLOOR)
    def _():
        for p in range(COLS):
            part = jnp.zeros((PIECE, PIECE), F32)
            for m in range(PARTS):
                g = half_of(p, m) * math.exp(0.5 * (SHIFT + LIFT))
                part += g * g
                cs[1, pl.ds(ids[TXT_AT + m], 1), :] += jnp.sum(g * g, axis=0, keepdims=True)
            rs[1, pl.ds(ids[p], 1), :] = jnp.sum(part.T, axis=0, keepdims=True)

    for p in range(COLS):
        match = ids[MATCH_AT + p]

        @pl.when(match >= 0)
        def _():
            other = txt[pl.ds(pl.multiple_of(match * PIECE, PIECE), PIECE), :]
            s = 100.0 * dot(img[p * PIECE:(p + 1) * PIECE, :], other, NT)
            dg[...] += jnp.sum(jnp.where(diagonal(), s, 0.0).reshape(16, 8, PIECE), axis=0)

    @pl.when(core == 0)
    def _():
        keep[0:2] = rs[...]
        keep[2, 0:8] = dg[...]
        send[0:2, 0:8] = cs[...]

    @pl.when(core == 1)
    def _():
        send[0:2] = rs[...]
        send[2, 0:8] = dg[...]
        keep[0:2, 8:16] = cs[...]


def far_scores(ids, here, there, near):
    sums = jax.ShapeDtypeStruct((3, COLS, PIECE), F32)
    return pl.pallas_call(
        far_kernel,
        out_shape=(
            jax.ShapeDtypeStruct((FAR_IMG, TXT), F32),
            jax.ShapeDtypeStruct((NEAR_IMG, FAR_TXT), F32),
            jax.ShapeDtypeStruct((IMG, WIDTH), BF),
            jax.ShapeDtypeStruct((TXT, WIDTH), BF),
            sums, sums,
        ),
        in_specs=[SM] + [VM] * (4 * FAR + 5),
        out_specs=(VM,) * 6,
        scratch_shapes=[
            pltpu.VMEM((NEAR_IMG // 2, 256), F32),
            pltpu.VMEM((NEAR_IMG // 2, 256), F32),
            pltpu.VMEM((IMG, PIECE), F32),
            pltpu.VMEM((8, TXT), F32),
            pltpu.VMEM((2, COLS, PIECE), F32),
            pltpu.VMEM((2, ROWS, PIECE), F32),
            pltpu.VMEM((8, PIECE), F32),
        ],
        compiler_params=PARAMS,
        cost_estimate=cost(2 * (IMG * TXT - NEAR_IMG * NEAR_TXT) * WIDTH, 16 << 20),
        name="far_scores",
    )(ids, *here, *there, *near)


def lse_of(sums):
    return jnp.where(sums[0] >= FLOOR, SHIFT + jnp.log(sums[0]), jnp.log(sums[1]) - LIFT)


def row_col_factors(core, own, far, a_s, b_s):
    scale = math.sqrt(0.5)
    factors = [scale * jnp.exp(0.5 * (SHIFT - lse_of(v))) for v in (own, far)]
    a_s[...] = jnp.where(core == 0, factors[0], factors[1])
    b_s[...] = jnp.where(core == 0, factors[1][:8], factors[0][8:])


def weights_block(ids, half, w, a_s, b_s, p0, p1, m0, m1):
    b = [b_s[pl.ds(ids[TXT_AT + m], 1), :] for m in range(m0, m1)]

    @pl.loop(p0, p1)
    def _(p):
        rows = pl.ds(pl.multiple_of((p - p0) * PIECE, PIECE), PIECE)
        a = jnp.broadcast_to(a_s[pl.ds(ids[p], 1), :], (PIECE, PIECE)).T
        for m in range(m1 - m0):
            cols = slice(m * PIECE, (m + 1) * PIECE)
            h = half[rows, cols]
            v, t = h * a, h * b[m]
            w[rows, cols] = (v * v + t * t).astype(BF)
        match = ids[MATCH_AT + p]

        @pl.when((match >= m0) & (match < m1))
        def _():
            cols = pl.ds(pl.multiple_of((match - m0) * PIECE, PIECE), PIECE)
            h = half[rows, cols]
            v, t = h * a, h * b_s[pl.ds(ids[TXT_AT + match], 1), :]
            w[rows, cols] = (v * v + t * t - diagonal().astype(F32)).astype(BF)


def product_kernel(start, end, kept_here, core, w_rows, w_cols, w_near, img, txt, out):
    first, last = start - FAR, end - FAR

    def image_side():
        if start < FAR:
            d = dot(w_rows[start * PART:end * PART, :], txt[...], NN)
        else:
            rows = slice(first * PART, last * PART)
            d = dot(w_cols[rows, :], txt[:FAR_TXT, :], NN)
            d = d + dot(w_near[rows, :], txt[FAR_TXT:, :], NN)
        out[...] = d.astype(BF)

    def text_side():
        at, pad = (PIECE, 0) if kept_here else (0, PIECE)
        d = dot(w_rows[:, start * PIECE:end * PIECE], img[:FAR_IMG, :], TN)
        if start < FAR:
            d = d + dot(w_cols[:, start * PIECE:end * PIECE], img[FAR_IMG:, :], TN)
        else:
            d = d + dot(w_near[:, first * PIECE:last * PIECE], img[FAR_IMG:, :], TN)
        d = d.astype(BF)
        for i in range(end - start):
            out[i * PART + at:i * PART + at + PIECE, :] = d[i * PIECE:(i + 1) * PIECE]
            out[i * PART + pad:i * PART + pad + PIECE, :] = jnp.zeros((PIECE, WIDTH), BF)

    pl.when(core == (0 if kept_here else 1))(image_side)
    pl.when(core == (1 if kept_here else 0))(text_side)


FACTORS = [pltpu.VMEM((COLS, PIECE), F32), pltpu.VMEM((ROWS, PIECE), F32)]


def far_products(ids, own, far, h_rows, h_cols, img, txt):
    def kernel(ids, own, far, h_rows, h_cols, img, txt, w_rows, w_cols, out, a_s, b_s):
        row_col_factors(ids[CORE], own, far, a_s, b_s)
        weights_block(ids, h_rows, w_rows, a_s, b_s, 0, 2 * FAR, 0, PARTS)
        weights_block(ids, h_cols, w_cols, a_s, b_s, 2 * FAR, COLS, 0, FAR)
        product_kernel(0, FAR, False, ids[CORE], w_rows, w_cols, None, img, txt, out)

    return pl.pallas_call(
        kernel,
        out_shape=(
            jax.ShapeDtypeStruct((FAR_IMG, TXT), BF),
            jax.ShapeDtypeStruct((NEAR_IMG, FAR_TXT), BF),
            jax.ShapeDtypeStruct((FAR * PART, WIDTH), BF),
        ),
        in_specs=[SM] + [VM] * 6,
        out_specs=(VM,) * 3,
        scratch_shapes=FACTORS,
        compiler_params=PARAMS,
        cost_estimate=cost(PRODUCT_FLOPS, 1),
        name="far_products",
    )(ids, own, far, h_rows, h_cols, img, txt)


def near_products(end, token, ids, own, far, near, w_rows, w_cols, img, txt):
    def kernel(token, ids, own, far, near, w_rows, w_cols, img, txt, w_near, out, a_s, b_s):
        row_col_factors(ids[CORE], own, far, a_s, b_s)
        weights_block(ids, near, w_near, a_s, b_s, 2 * FAR, COLS, FAR, PARTS)
        product_kernel(FAR, end, False, ids[CORE], w_rows, w_cols, w_near, img, txt, out)

    return pl.pallas_call(
        kernel,
        out_shape=(
            jax.ShapeDtypeStruct((NEAR_IMG, NEAR_TXT), BF),
            jax.ShapeDtypeStruct(((end - FAR) * PART, WIDTH), BF),
        ),
        in_specs=[VM, SM] + [VM] * 7,
        out_specs=(VM, VM),
        scratch_shapes=FACTORS,
        compiler_params=PARAMS,
        cost_estimate=cost(PRODUCT_FLOPS, 1),
        name="near_products",
    )(token, ids, own, far, near, w_rows, w_cols, img, txt)


def products(start, end, kept_here, tokens, ids, w, img, txt, flops=PRODUCT_FLOPS):
    def kernel(ids, img, txt, *refs):
        w_near = refs[2] if len(w) == 3 else None
        product_kernel(
            start, end, kept_here, ids[CORE], refs[0], refs[1], w_near, img, txt, refs[-1]
        )

    return pl.pallas_call(
        kernel,
        out_shape=jax.ShapeDtypeStruct(((end - start) * PART, WIDTH), BF),
        in_specs=[SM] + [VM] * (2 + len(w) + len(tokens)),
        out_specs=VM,
        compiler_params=PARAMS,
        cost_estimate=cost(flops, 1),
        name="products_kept" if kept_here else "products_sent",
    )(ids, img, txt, *w, *tokens)


def pack(value):
    pieces = []
    for _ in range(2):
        pieces.append(lax.reduce_precision(value, exponent_bits=8, mantissa_bits=7))
        value = value - pieces[-1]
    rows = jnp.concatenate([v.astype(BF) for v in (*pieces, value)], axis=1)
    return jnp.pad(rows, ((0, 8), (0, WIDTH - 3 * PIECE)))


def with_tail(part, tail):
    return jnp.concatenate([part, tail])


def read_tail(ref, at):
    rows = ref[at:at + TAIL, :3 * PIECE].astype(F32)[:8]
    return sum(rows[:, i * PIECE:(i + 1) * PIECE] for i in range(3))


def write_tail(ref, at, terms):
    ref[at:at + TAIL, :] = jnp.zeros((TAIL, WIDTH), BF)
    pad = jnp.zeros((TAIL - 8, PIECE), F32)
    for i in range(3):
        piece = terms.astype(BF).astype(F32)
        ref[at:at + TAIL, i * PIECE:(i + 1) * PIECE] = jnp.concatenate([piece, pad]).astype(BF)
        terms = terms - piece


def across_kernel(kept, sent, right, left, through0, through1, lse, first, second, lse_out):
    total = kept[:PART, :].astype(F32) + sent[:PART, :].astype(F32)
    total = (total + right[:PART, :].astype(F32) + left[...].astype(F32)).astype(BF)
    first[...] = total[:PIECE]
    second[:PIECE, :] = total[PIECE:]
    terms = lse[...]
    for ref in (through0, through1, right):
        terms = terms + read_tail(ref, PART)
    lse_out[...] = terms
    write_tail(second, PIECE, terms)


def sum_kernel(ids, kept, sent, right, left, back0, back1, lse, keep, send, lse_out):
    core = ids[CORE]
    total = kept[PART:2 * PART, :].astype(F32) + sent[PART:2 * PART, :].astype(F32)
    total = total + right[...].astype(F32) + left[...].astype(F32)
    back = (back0[...].astype(F32), back1[:PIECE, :].astype(F32))
    terms = lse[...] + read_tail(back1, PIECE)
    lse_out[...] = terms
    write_tail(send, PIECE, terms)

    @pl.when(core == 0)
    def _():
        keep[...] = total[:PIECE] + back[0]
        send[:PIECE, :] = (total[PIECE:] + back[1]).astype(BF)

    @pl.when(core == 1)
    def _():
        keep[...] = total[PIECE:] + back[1]
        send[:PIECE, :] = (total[:PIECE] + back[0]).astype(BF)


def grad_kernel(ids, image, text, keep, got, lse, image_out, text_out, loss_out):
    core = ids[CORE]

    def grad(values, total, out):
        x = values[...]
        norm = jnp.sqrt(jnp.sum(x * x, axis=1, keepdims=True) + 1e-06)
        unit = x / norm
        g = total[:PIECE, :].astype(F32)
        out[...] = (g - unit * jnp.sum(unit * g, axis=1, keepdims=True)) / norm

    @pl.when(core == 0)
    def _():
        grad(image, keep, image_out)
        grad(text, got, text_out)

    @pl.when(core == 1)
    def _():
        grad(image, got, image_out)
        grad(text, keep, text_out)

    terms = lse[...] + read_tail(got, PIECE)
    total = jnp.sum(jnp.sum(terms, axis=0, keepdims=True), axis=1, keepdims=True)
    loss_out[...] = total * (1.0 / (2.0 * ROWS * COLS * PIECE))


def per_device(image_embeds, text_embeds):
    here = lax.axis_index("row") * COLS + lax.axis_index("col")
    first = lax.axis_index("col") % 2 == 0

    keep, send = unit_pair(image_embeds, text_embeds)
    got = swap(send)
    here, keep = lax.optimization_barrier((here, keep))
    ids = lax.dynamic_index_in_dim(jnp.asarray(device_table()), here, keepdims=False)
    own = jnp.concatenate([jnp.where(first, keep, got), jnp.where(first, got, keep)])
    own, ids = lax.optimization_barrier((own, ids))

    other = flip(own)
    left0, right0 = ring(own, 1), ring(own, 3)
    left1, right1 = ring(other, 1), ring(other, 3)
    across = swap(other)
    from_left, from_right, across = lax.optimization_barrier((left0, right0, across))
    far = [ring(from_left[:PIECE], 1), ring(from_right[PIECE:], 3)]
    far += [ring(left1[:PIECE], 1), ring(right1[PIECE:], 3)]
    mine = [right1, left1, other, own, right0, left0]
    late, _ = lax.optimization_barrier((own, other))
    next0, next1, far[0], far[1] = lax.optimization_barrier((right0, left0, far[0], far[1]))
    theirs = [swap(right1), swap(left1), across, swap(late), swap(next0), swap(next1)]
    near = near_scores(ids, mine, theirs)
    *far, near[0] = lax.optimization_barrier((*far, near[0]))
    h_rows, h_cols, img, txt, keep, send = far_scores(ids, far, [swap(v) for v in far], near)
    sums = keep + swap(send)
    sums = group_sum(sums)
    theirs = swap(sums)

    def add(*v):
        return functools.reduce(lambda a, b: a + b, [u.astype(F32) for u in v]).astype(BF)

    def part(value, i):
        return value[i * PART:(i + 1) * PART]

    def mark(done):
        return swap(done[:16, :PIECE])

    w_rows, w_cols, sent = far_products(ids, sums, theirs, h_rows, h_cols, img, txt)
    sent = swap(sent)
    kept = products(0, FAR, True, (), ids, (w_rows, w_cols), img, txt)
    lse = lse_of(theirs).reshape(2, 8, PIECE).sum(0)
    lse = jnp.where(first, lse, lse - 2.0 * theirs[2, :8])
    tail = pack(lse)
    far0 = with_tail(add(part(kept, 0), part(sent, 0)), tail)
    far1 = with_tail(add(part(kept, 1), part(sent, 1)), tail)
    through0, through1 = ring(far0, 1), ring(far1, 3)

    w_near, sent = near_products(4, mark(far0), ids, sums, theirs, near[0], w_rows, w_cols, img, txt)
    w = (w_rows, w_cols, w_near)
    sent_on = products(4, 8, False, (), ids, w, img, txt)
    sent = swap(sent)
    kept = products(FAR, 4, True, (through0, through1, sent_on), ids, w, img, txt)
    sent_on = swap(sent_on)
    near1 = with_tail(add(part(kept, 0), part(sent, 0)), through0[PART:])
    back1 = add(part(kept, 1), part(sent, 1), part(through1, 0))
    right1, left1 = ring(near1, 1), ring(back1, 3)

    kept = products(4, 8, True, (mark(back1),), ids, w, img, txt)
    near0 = add(part(kept, 2), part(sent_on, 2), part(through0, 0))
    back0 = add(part(kept, 3), part(sent_on, 3))
    near0, back0, kept, sent_on = lax.optimization_barrier((near0, back0, kept, sent_on))
    right0, left0 = ring(near0, 1), ring(back0, 3)
    shape = jax.ShapeDtypeStruct((PIECE, WIDTH), F32)
    lane = jax.ShapeDtypeStruct((8, PIECE), F32)
    last0, last1, lse = pl.pallas_call(
        across_kernel,
        out_shape=(
            jax.ShapeDtypeStruct((PIECE, WIDTH), BF),
            jax.ShapeDtypeStruct((PIECE + TAIL, WIDTH), BF),
            lane,
        ),
        in_specs=[VM] * 7, out_specs=(VM, VM, VM),
        compiler_params=PARAMS, name="across_sums",
    )(kept, sent_on, right1, left1, through0, through1, lse)
    backs = flip(last0), flip(last1)
    keep, send, lse = pl.pallas_call(
        sum_kernel,
        out_shape=(shape, jax.ShapeDtypeStruct((PIECE + TAIL, WIDTH), BF), lane),
        in_specs=[SM] + [VM] * 7, out_specs=(VM, VM, VM),
        compiler_params=PARAMS, name="own_sums",
    )(ids, kept, sent_on, right0, left0, *backs, lse)
    image_grad, text_grad, loss = pl.pallas_call(
        grad_kernel,
        out_shape=(shape, shape, jax.ShapeDtypeStruct((1, 1), F32)),
        in_specs=[SM] + [VM] * 5, out_specs=(VM, VM, VM),
        compiler_params=PARAMS, name="grad_rows",
    )(ids, image_embeds, text_embeds, keep, swap(send), lse)
    loss = loss[0, 0]
    return (image_grad, text_grad, loss)


def solution(mesh):
    return jax.shard_map(
        per_device,
        mesh=mesh,
        in_specs=(P(("row", "col"), None), P(("col", "row"), None)),
        out_specs=(P(("row", "col"), None), P(("col", "row"), None), P()),
        check_vma=False,
    )
```

```python
import functools
import math

import jax
import jax.numpy as jnp
import numpy as np
from jax import lax
from jax.experimental import pallas as pl
from jax.experimental.pallas import tpu as pltpu
from jax.sharding import PartitionSpec as P

PIECE = 128
PART = 2 * PIECE
WIDTH = 1280
RING = 4
PART_AT = ((2, 0), (2, 1), (1, 1), (3, 1), (0, 1), (0, 0), (1, 0), (3, 0))
PARTS = len(PART_AT)
FAR = 2
ROWS, COLS = 8, 16
IMG = PARTS * PART
TXT = PARTS * PIECE
FAR_IMG, FAR_TXT = FAR * PART, FAR * PIECE
NEAR_IMG, NEAR_TXT = IMG - FAR_IMG, TXT - FAR_TXT
CORE, TXT_AT, MATCH_AT = 40, 32, 16
TAIL = 16
PRODUCT_FLOPS = 5 * 10**10

SHIFT = 22.0
LIFT = 70.0
FLOOR = math.exp(-62.0)
LOG2E = math.log2(math.e)

VM = pl.BlockSpec(memory_space=pltpu.VMEM)
SM = pl.BlockSpec(memory_space=pltpu.SMEM)
PARAMS = pltpu.CompilerParams(vmem_limit_bytes=8 * 1024 * 1024)
F32, BF = jnp.float32, jnp.bfloat16
NT = (((1,), (1,)), ((), ()))
NN = (((1,), (0,)), ((), ()))
TN = (((0,), (0,)), ((), ()))
AXES = ("row", "col")


def dot(a, b, dims):
    return lax.dot_general(a, b, dims, preferred_element_type=F32)


def device(yl, z, x, yh, k):
    return (yl * 4 + z) * COLS + (x * 2 + yh) * 2 + k


def places():
    return [
        (yl, z, x, yh, k)
        for yl in range(2) for z in range(RING) for x in range(RING) for yh in range(2) for k in range(2)
    ]


def neighbour(y, k):
    return y ^ 1 if k == 0 else (y + (1 if y % 2 else 3)) % RING


def group(value, d, side):
    pairs = []
    for yl, z, x, yh, k in places():
        y = yh * 2 + yl
        y = neighbour(y, k) if side else y
        target = device(y % 2, (z + d * k) % RING, (x + d * (1 - k)) % RING, y // 2, k)
        pairs.append((device(yl, z, x, yh, k), target))
    return lax.ppermute(value, AXES, pairs)


def ring(value, d):
    return group(value, d, 0)


def flip(value):
    return group(value, 0, 1)


def group_sum(value):
    value = value + ring(value, 1) + ring(value, 2) + ring(value, 3)
    return value + flip(value)


def swap(value):
    return lax.ppermute(value, AXES, [
        (device(yl, z, x, yh, k), device(yl, z, x, yh, 1 - k)) for yl, z, x, yh, k in places()
    ])


def device_table():
    table = np.zeros((ROWS * COLS, 41), np.int32)
    for yl, z, x, yh, k in places():
        y = yh * 2 + yl
        img, match, txt, owned = [], [], [], []
        for d, side in PART_AT:
            zt, yt = (z + d) % RING, neighbour(y, 1) if side else y
            txt.append(zt * 2 + (yt + 1) % 2)
            owner = device(yt % 2, zt, x, yt // 2, k)
            owned.append(owner % COLS * ROWS + owner // COLS)
        for d, side in PART_AT:
            xi, yi = (x + d) % RING, neighbour(y, 0) if side else y
            for h in range(2):
                img.append((xi * 2 + yi % 2) * 2 + h)
                piece = device(yi % 2, z, xi, yi // 2, h)
                match.append(owned.index(piece) if piece in owned else -1)
        table[device(yl, z, x, yh, k)] = img + match + txt + [k]
    return table


def cost(flops, bytes_accessed):
    return pl.CostEstimate(flops=flops, bytes_accessed=bytes_accessed, transcendentals=0)


def diagonal():
    shape = (PIECE, PIECE)
    return lax.broadcasted_iota(jnp.int32, shape, 0) == lax.broadcasted_iota(jnp.int32, shape, 1)


def unit_kernel(image_ref, text_ref, keep_ref, send_ref):
    core = lax.axis_index("col") % 2

    def unit(src):
        x = src[...]
        return (x / jnp.sqrt(jnp.sum(x * x, axis=1, keepdims=True) + 1e-06)).astype(BF)

    image, text = unit(image_ref), unit(text_ref)

    @pl.when(core == 0)
    def _():
        keep_ref[...] = image
        send_ref[...] = text

    @pl.when(core == 1)
    def _():
        keep_ref[...] = text
        send_ref[...] = image


def unit_pair(image, text):
    shape = jax.ShapeDtypeStruct((PIECE, WIDTH), BF)
    return pl.pallas_call(
        unit_kernel, out_shape=(shape, shape), in_specs=[VM, VM], out_specs=(VM, VM),
        compiler_params=PARAMS, name="unit_rows",
    )(image, text)


def place_parts(core, here, there, img, txt):
    @pl.when(core == 0)
    def _():
        for m, (mine, other) in enumerate(zip(here, there)):
            img[m * PART:(m + 1) * PART, :] = mine[...]
            txt[m * PIECE:(m + 1) * PIECE, :] = other[:PIECE, :]

    @pl.when(core == 1)
    def _():
        for m, (mine, other) in enumerate(zip(here, there)):
            img[m * PART:(m + 1) * PART, :] = other[...]
            txt[m * PIECE:(m + 1) * PIECE, :] = mine[PIECE:, :]


def score_tiles(tiles, img, txt, held, racc, cacc):
    def epilogue(t):
        row, rows, col, h_out, h_row, h_col = tiles[t]
        cols = slice(col, col + 256)
        total = jnp.zeros((8, 256), F32)
        for p in range(0, rows, PIECE):
            d = held[t % 2][p:p + PIECE, :]
            h = jnp.exp2(d * (50.0 * LOG2E) - (0.5 * SHIFT * LOG2E))
            h_out[h_row + p:h_row + p + PIECE, h_col:h_col + 256] = h
            q = h * h
            racc[row + p:row + p + PIECE, :] += q[:, :PIECE] + q[:, PIECE:]
            total += jnp.sum(q.reshape(16, 8, 256), axis=0)
        cacc[:, cols] += total

    for t, (row, rows, col, *_) in enumerate(tiles):
        held[t % 2][:rows, :] = dot(img[row:row + rows, :], txt[col:col + 256, :], NT)
        if t:
            epilogue(t - 1)
    epilogue(len(tiles) - 1)


def near_kernel(ids, *refs):
    count = PARTS - FAR
    here, there = refs[:count], refs[count:2 * count]
    h_out, img, txt, racc, cacc, even, odd = refs[2 * count:]
    place_parts(ids[CORE], here, there, img, txt)
    racc[...] = jnp.zeros_like(racc)
    cacc[...] = jnp.zeros_like(cacc)
    half = NEAR_IMG // 2
    tiles = [(r, half, c, h_out, r, c) for c in range(0, NEAR_TXT, 256) for r in (0, half)]
    score_tiles(tiles, img, txt, (even, odd), racc, cacc)


def near_scores(ids, here, there):
    return list(pl.pallas_call(
        near_kernel,
        out_shape=(
            jax.ShapeDtypeStruct((NEAR_IMG, NEAR_TXT), F32),
            jax.ShapeDtypeStruct((NEAR_IMG, WIDTH), BF),
            jax.ShapeDtypeStruct((NEAR_TXT, WIDTH), BF),
            jax.ShapeDtypeStruct((NEAR_IMG, PIECE), F32),
            jax.ShapeDtypeStruct((8, NEAR_TXT), F32),
        ),
        in_specs=[SM] + [VM] * (2 * len(here)),
        out_specs=(VM,) * 5,
        scratch_shapes=[pltpu.VMEM((NEAR_IMG // 2, 256), F32)] * 2,
        compiler_params=PARAMS,
        cost_estimate=cost(1, 1),
        name="near_scores",
    )(ids, *here, *there))


def far_kernel(ids, *refs):
    here, there = refs[:2 * FAR], refs[2 * FAR:4 * FAR]
    near, near_img, near_txt, near_racc, near_cacc = refs[4 * FAR:4 * FAR + 5]
    h_rows, h_cols, img, txt, keep, send = refs[4 * FAR + 5:4 * FAR + 11]
    even, odd, racc, cacc, rs, cs, dg = refs[4 * FAR + 11:]
    core = ids[CORE]

    @pl.when(core == 0)
    def _():
        for i, mine in enumerate(here):
            img[i * PIECE:(i + 1) * PIECE, :] = mine[...]
        for i in range(FAR):
            txt[i * PIECE:(i + 1) * PIECE, :] = there[2 * i][...]

    @pl.when(core == 1)
    def _():
        for i, other in enumerate(there):
            img[i * PIECE:(i + 1) * PIECE, :] = other[...]
        for i in range(FAR):
            txt[i * PIECE:(i + 1) * PIECE, :] = here[2 * i + 1][...]

    img[FAR_IMG:, :] = near_img[...]
    txt[FAR_TXT:, :] = near_txt[...]
    racc[:FAR_IMG, :] = jnp.zeros((FAR_IMG, PIECE), F32)
    racc[FAR_IMG:, :] = near_racc[...]
    cacc[:, :FAR_TXT] = jnp.zeros((8, FAR_TXT), F32)
    cacc[:, FAR_TXT:] = near_cacc[...]
    for ref in (rs, cs, dg, keep, send):
        ref[...] = jnp.zeros_like(ref)
    half = NEAR_IMG // 2
    tiles = [(FAR_IMG + r, half, 0, h_cols, r, 0) for r in (0, half)]
    tiles += [(0, FAR_IMG, c, h_rows, 0, c) for c in range(0, TXT, 256)]
    score_tiles(tiles, img, txt, (even, odd), racc, cacc)

    lowest = jnp.full((1, PIECE), jnp.inf, F32)
    for p in range(COLS):
        part = jnp.sum(racc[p * PIECE:(p + 1) * PIECE, :].T, axis=0, keepdims=True)
        rs[0, pl.ds(ids[p], 1), :] = part
        lowest = jnp.minimum(lowest, part)
    total = jnp.sum(cacc[...], axis=0, keepdims=True)
    for m in range(PARTS):
        part = total[:, m * PIECE:(m + 1) * PIECE]
        cs[0, pl.ds(ids[TXT_AT + m], 1), :] = part
        lowest = jnp.minimum(lowest, part)

    def half_of(p, m):
        at = p * PIECE if p < 2 * FAR else (p - 2 * FAR) * PIECE
        if p < 2 * FAR:
            return h_rows[at:at + PIECE, m * PIECE:(m + 1) * PIECE]
        if m < FAR:
            return h_cols[at:at + PIECE, m * PIECE:(m + 1) * PIECE]
        return near[at:at + PIECE, (m - FAR) * PIECE:(m - FAR + 1) * PIECE]

    @pl.when(jnp.min(lowest) < FLOOR)
    def _():
        for p in range(COLS):
            part = jnp.zeros((PIECE, PIECE), F32)
            for m in range(PARTS):
                g = half_of(p, m) * math.exp(0.5 * (SHIFT + LIFT))
                part += g * g
                cs[1, pl.ds(ids[TXT_AT + m], 1), :] += jnp.sum(g * g, axis=0, keepdims=True)
            rs[1, pl.ds(ids[p], 1), :] = jnp.sum(part.T, axis=0, keepdims=True)

    for p in range(COLS):
        match = ids[MATCH_AT + p]

        @pl.when(match >= 0)
        def _():
            other = txt[pl.ds(pl.multiple_of(match * PIECE, PIECE), PIECE), :]
            s = 100.0 * dot(img[p * PIECE:(p + 1) * PIECE, :], other, NT)
            dg[...] += jnp.sum(jnp.where(diagonal(), s, 0.0).reshape(16, 8, PIECE), axis=0)

    @pl.when(core == 0)
    def _():
        keep[0:2] = rs[...]
        keep[2, 0:8] = dg[...]
        send[0:2, 0:8] = cs[...]

    @pl.when(core == 1)
    def _():
        send[0:2] = rs[...]
        send[2, 0:8] = dg[...]
        keep[0:2, 8:16] = cs[...]


def far_scores(ids, here, there, near):
    sums = jax.ShapeDtypeStruct((3, COLS, PIECE), F32)
    return pl.pallas_call(
        far_kernel,
        out_shape=(
            jax.ShapeDtypeStruct((FAR_IMG, TXT), F32),
            jax.ShapeDtypeStruct((NEAR_IMG, FAR_TXT), F32),
            jax.ShapeDtypeStruct((IMG, WIDTH), BF),
            jax.ShapeDtypeStruct((TXT, WIDTH), BF),
            sums, sums,
        ),
        in_specs=[SM] + [VM] * (4 * FAR + 5),
        out_specs=(VM,) * 6,
        scratch_shapes=[
            pltpu.VMEM((NEAR_IMG // 2, 256), F32),
            pltpu.VMEM((NEAR_IMG // 2, 256), F32),
            pltpu.VMEM((IMG, PIECE), F32),
            pltpu.VMEM((8, TXT), F32),
            pltpu.VMEM((2, COLS, PIECE), F32),
            pltpu.VMEM((2, ROWS, PIECE), F32),
            pltpu.VMEM((8, PIECE), F32),
        ],
        compiler_params=PARAMS,
        cost_estimate=cost(2 * (IMG * TXT - NEAR_IMG * NEAR_TXT) * WIDTH, 16 << 20),
        name="far_scores",
    )(ids, *here, *there, *near)


def lse_of(sums):
    return jnp.where(sums[0] >= FLOOR, SHIFT + jnp.log(sums[0]), jnp.log(sums[1]) - LIFT)


def row_col_factors(core, own, far, a_s, b_s):
    scale = math.sqrt(0.5)
    factors = [scale * jnp.exp(0.5 * (SHIFT - lse_of(v))) for v in (own, far)]
    a_s[...] = jnp.where(core == 0, factors[0], factors[1])
    b_s[...] = jnp.where(core == 0, factors[1][:8], factors[0][8:])


def weights_block(ids, half, w, a_s, b_s, p0, p1, m0, m1):
    b = [b_s[pl.ds(ids[TXT_AT + m], 1), :] for m in range(m0, m1)]

    @pl.loop(p0, p1)
    def _(p):
        rows = pl.ds(pl.multiple_of((p - p0) * PIECE, PIECE), PIECE)
        a = jnp.broadcast_to(a_s[pl.ds(ids[p], 1), :], (PIECE, PIECE)).T
        for m in range(m1 - m0):
            cols = slice(m * PIECE, (m + 1) * PIECE)
            h = half[rows, cols]
            v, t = h * a, h * b[m]
            w[rows, cols] = (v * v + t * t).astype(BF)
        match = ids[MATCH_AT + p]

        @pl.when((match >= m0) & (match < m1))
        def _():
            cols = pl.ds(pl.multiple_of((match - m0) * PIECE, PIECE), PIECE)
            h = half[rows, cols]
            v, t = h * a, h * b_s[pl.ds(ids[TXT_AT + match], 1), :]
            w[rows, cols] = (v * v + t * t - diagonal().astype(F32)).astype(BF)


def product_kernel(start, end, kept_here, core, w_rows, w_cols, w_near, img, txt, out):
    first, last = start - FAR, end - FAR

    def image_side():
        if start < FAR:
            d = dot(w_rows[start * PART:end * PART, :], txt[...], NN)
        else:
            rows = slice(first * PART, last * PART)
            d = dot(w_cols[rows, :], txt[:FAR_TXT, :], NN)
            d = d + dot(w_near[rows, :], txt[FAR_TXT:, :], NN)
        out[...] = d.astype(BF)

    def text_side():
        at, pad = (PIECE, 0) if kept_here else (0, PIECE)
        d = dot(w_rows[:, start * PIECE:end * PIECE], img[:FAR_IMG, :], TN)
        if start < FAR:
            d = d + dot(w_cols[:, start * PIECE:end * PIECE], img[FAR_IMG:, :], TN)
        else:
            d = d + dot(w_near[:, first * PIECE:last * PIECE], img[FAR_IMG:, :], TN)
        d = d.astype(BF)
        for i in range(end - start):
            out[i * PART + at:i * PART + at + PIECE, :] = d[i * PIECE:(i + 1) * PIECE]
            out[i * PART + pad:i * PART + pad + PIECE, :] = jnp.zeros((PIECE, WIDTH), BF)

    pl.when(core == (0 if kept_here else 1))(image_side)
    pl.when(core == (1 if kept_here else 0))(text_side)


FACTORS = [pltpu.VMEM((COLS, PIECE), F32), pltpu.VMEM((ROWS, PIECE), F32)]


def far_products(ids, own, far, h_rows, h_cols, img, txt):
    def kernel(ids, own, far, h_rows, h_cols, img, txt, w_rows, w_cols, out, a_s, b_s):
        row_col_factors(ids[CORE], own, far, a_s, b_s)
        weights_block(ids, h_rows, w_rows, a_s, b_s, 0, 2 * FAR, 0, PARTS)
        weights_block(ids, h_cols, w_cols, a_s, b_s, 2 * FAR, COLS, 0, FAR)
        product_kernel(0, FAR, False, ids[CORE], w_rows, w_cols, None, img, txt, out)

    return pl.pallas_call(
        kernel,
        out_shape=(
            jax.ShapeDtypeStruct((FAR_IMG, TXT), BF),
            jax.ShapeDtypeStruct((NEAR_IMG, FAR_TXT), BF),
            jax.ShapeDtypeStruct((FAR * PART, WIDTH), BF),
        ),
        in_specs=[SM] + [VM] * 6,
        out_specs=(VM,) * 3,
        scratch_shapes=FACTORS,
        compiler_params=PARAMS,
        cost_estimate=cost(PRODUCT_FLOPS, 1),
        name="far_products",
    )(ids, own, far, h_rows, h_cols, img, txt)


def near_products(token, ids, own, far, near, w_rows, w_cols, img, txt):
    def kernel(token, ids, own, far, near, w_rows, w_cols, img, txt, w_near, s0, s1, out, a_s, b_s,
               sent):
        row_col_factors(ids[CORE], own, far, a_s, b_s)
        weights_block(ids, near, w_near, a_s, b_s, 2 * FAR, COLS, FAR, PARTS)
        args = (ids[CORE], w_rows, w_cols, w_near, img, txt)
        product_kernel(FAR, FAR + 2, False, *args, sent)
        s0[...] = sent[:PART, :]
        s1[...] = sent[PART:, :]
        product_kernel(FAR, FAR + 2, True, *args, out)

    part = jax.ShapeDtypeStruct((PART, WIDTH), BF)
    return pl.pallas_call(
        kernel,
        out_shape=(
            jax.ShapeDtypeStruct((NEAR_IMG, NEAR_TXT), BF),
            part, part,
            jax.ShapeDtypeStruct((2 * PART, WIDTH), BF),
        ),
        in_specs=[VM, SM] + [VM] * 7,
        out_specs=(VM,) * 4,
        scratch_shapes=[*FACTORS, pltpu.VMEM((2 * PART, WIDTH), BF)],
        compiler_params=PARAMS,
        cost_estimate=cost(PRODUCT_FLOPS, 1),
        name="near_products",
    )(token, ids, own, far, near, w_rows, w_cols, img, txt)


def products(start, end, kept_here, tokens, ids, w, img, txt, flops=PRODUCT_FLOPS):
    def kernel(ids, img, txt, *refs):
        w_near = refs[2] if len(w) == 3 else None
        product_kernel(
            start, end, kept_here, ids[CORE], refs[0], refs[1], w_near, img, txt, refs[-1]
        )

    return pl.pallas_call(
        kernel,
        out_shape=jax.ShapeDtypeStruct(((end - start) * PART, WIDTH), BF),
        in_specs=[SM] + [VM] * (2 + len(w) + len(tokens)),
        out_specs=VM,
        compiler_params=PARAMS,
        cost_estimate=cost(flops, 1),
        name="products_kept" if kept_here else "products_sent",
    )(ids, img, txt, *w, *tokens)


def read_tail(ref, at):
    rows = ref[at:at + TAIL, :3 * PIECE].astype(F32)[:8]
    return sum(rows[:, i * PIECE:(i + 1) * PIECE] for i in range(3))


def write_tail(ref, at, terms):
    ref[at:at + TAIL, :] = jnp.zeros((TAIL, WIDTH), BF)
    pad = jnp.zeros((TAIL - 8, PIECE), F32)
    for i in range(3):
        piece = terms.astype(BF).astype(F32)
        ref[at:at + TAIL, i * PIECE:(i + 1) * PIECE] = jnp.concatenate([piece, pad]).astype(BF)
        terms = terms - piece


def far_sum_kernel(ids, kept, sent, sums, far0, far1, lse_out):
    terms = lse_of(sums[...])
    terms = terms[:8] + terms[8:]
    terms = terms - jnp.where(ids[CORE] == 0, 0.0, 2.0) * sums[2, :8]
    lse_out[...] = terms
    for i, far in enumerate((far0, far1)):
        rows = slice(i * PART, (i + 1) * PART)
        far[:PART, :] = (kept[rows, :].astype(F32) + sent[rows, :].astype(F32)).astype(BF)
        write_tail(far, PART, terms)


def near_sum_kernel(kept, sent0, sent1, through0, through1, token, near, back):
    near[:PART, :] = (kept[:PART, :].astype(F32) + sent0[...].astype(F32)).astype(BF)
    near[PART:, :] = through0[PART:, :]
    total = kept[PART:, :].astype(F32) + sent1[...].astype(F32)
    back[...] = (total + through1[:PART, :].astype(F32)).astype(BF)


def across_kernel(kept, sent, right, left, through0, through1, lse, first, second, lse_out):
    total = kept[:PART, :].astype(F32) + sent[:PART, :].astype(F32)
    total = (total + right[:PART, :].astype(F32) + left[...].astype(F32)).astype(BF)
    first[...] = total[:PIECE]
    second[:PIECE, :] = total[PIECE:]
    terms = lse[...]
    for ref in (through0, through1, right):
        terms = terms + read_tail(ref, PART)
    lse_out[...] = terms
    write_tail(second, PIECE, terms)


def sum_kernel(ids, kept, sent, right, left, back0, back1, lse, keep, send, lse_out):
    core = ids[CORE]
    total = kept[PART:2 * PART, :].astype(F32) + sent[PART:2 * PART, :].astype(F32)
    total = total + right[...].astype(F32) + left[...].astype(F32)
    back = (back0[...].astype(F32), back1[:PIECE, :].astype(F32))
    terms = lse[...] + read_tail(back1, PIECE)
    lse_out[...] = terms
    write_tail(send, PIECE, terms)

    @pl.when(core == 0)
    def _():
        keep[...] = total[:PIECE] + back[0]
        send[:PIECE, :] = (total[PIECE:] + back[1]).astype(BF)

    @pl.when(core == 1)
    def _():
        keep[...] = total[PIECE:] + back[1]
        send[:PIECE, :] = (total[:PIECE] + back[0]).astype(BF)


def grad_kernel(ids, image, text, keep, got, lse, image_out, text_out, loss_out):
    core = ids[CORE]

    def grad(values, total, out):
        x = values[...]
        norm = jnp.sqrt(jnp.sum(x * x, axis=1, keepdims=True) + 1e-06)
        unit = x / norm
        g = total[:PIECE, :].astype(F32)
        out[...] = (g - unit * jnp.sum(unit * g, axis=1, keepdims=True)) / norm

    @pl.when(core == 0)
    def _():
        grad(image, keep, image_out)
        grad(text, got, text_out)

    @pl.when(core == 1)
    def _():
        grad(image, got, image_out)
        grad(text, keep, text_out)

    terms = lse[...] + read_tail(got, PIECE)
    total = jnp.sum(jnp.sum(terms, axis=0, keepdims=True), axis=1, keepdims=True)
    loss_out[...] = total * (1.0 / (2.0 * ROWS * COLS * PIECE))


def per_device(image_embeds, text_embeds):
    here = lax.axis_index("row") * COLS + lax.axis_index("col")
    first = lax.axis_index("col") % 2 == 0

    keep, send = unit_pair(image_embeds, text_embeds)
    got = swap(send)
    here, keep = lax.optimization_barrier((here, keep))
    ids = lax.dynamic_index_in_dim(jnp.asarray(device_table()), here, keepdims=False)
    own = jnp.concatenate([jnp.where(first, keep, got), jnp.where(first, got, keep)])
    own, ids = lax.optimization_barrier((own, ids))

    other = flip(own)
    left0, right0 = ring(own, 1), ring(own, 3)
    left1, right1 = ring(other, 1), ring(other, 3)
    across = swap(other)
    from_left, from_right, across = lax.optimization_barrier((left0, right0, across))
    far = [ring(from_left[:PIECE], 1), ring(from_right[PIECE:], 3)]
    far += [ring(left1[:PIECE], 1), ring(right1[PIECE:], 3)]
    mine = [right1, left1, other, own, right0, left0]
    late, _ = lax.optimization_barrier((own, other))
    next0, next1, far[0], far[1] = lax.optimization_barrier((right0, left0, far[0], far[1]))
    theirs = [swap(right1), swap(left1), across, swap(late), swap(next0), swap(next1)]
    near = near_scores(ids, mine, theirs)
    *far, near[0] = lax.optimization_barrier((*far, near[0]))
    h_rows, h_cols, img, txt, keep, send = far_scores(ids, far, [swap(v) for v in far], near)
    sums = keep + swap(send)
    sums = group_sum(sums)
    theirs = swap(sums)

    def add(*v):
        return functools.reduce(lambda a, b: a + b, [u.astype(F32) for u in v]).astype(BF)

    def part(value, i):
        return value[i * PART:(i + 1) * PART]

    def mark(done):
        return swap(done[:16, :PIECE])

    w_rows, w_cols, sent = far_products(ids, sums, theirs, h_rows, h_cols, img, txt)
    sent = swap(sent)
    kept = products(0, FAR, True, (), ids, (w_rows, w_cols), img, txt)
    tailed = jax.ShapeDtypeStruct((PART + TAIL, WIDTH), BF)
    lane = jax.ShapeDtypeStruct((8, PIECE), F32)
    far0, far1, lse = pl.pallas_call(
        far_sum_kernel, out_shape=(tailed, tailed, lane), in_specs=[SM] + [VM] * 3,
        out_specs=(VM,) * 3, compiler_params=PARAMS, name="far_sums",
    )(ids, kept, sent, theirs)
    through0, through1 = ring(far0, 1), ring(far1, 3)

    w_near, s0, s1, kept = near_products(
        mark(far0), ids, sums, theirs, near[0], w_rows, w_cols, img, txt
    )
    w = (w_rows, w_cols, w_near)
    sent_on = products(4, 8, False, (), ids, w, img, txt, 1)
    near1, back1 = pl.pallas_call(
        near_sum_kernel, out_shape=(tailed, jax.ShapeDtypeStruct((PART, WIDTH), BF)),
        in_specs=[VM] * 6, out_specs=(VM, VM), compiler_params=PARAMS, name="near_sums",
    )(kept, swap(s0), swap(s1), through0, through1, sent_on)
    sent_on = swap(sent_on)
    right1, left1 = ring(near1, 1), ring(back1, 3)

    kept = products(4, 8, True, (mark(back1),), ids, w, img, txt)
    near0 = add(part(kept, 2), part(sent_on, 2), part(through0, 0))
    back0 = add(part(kept, 3), part(sent_on, 3))
    near0, back0, kept, sent_on = lax.optimization_barrier((near0, back0, kept, sent_on))
    right0, left0 = ring(near0, 1), ring(back0, 3)
    shape = jax.ShapeDtypeStruct((PIECE, WIDTH), F32)
    last0, last1, lse = pl.pallas_call(
        across_kernel,
        out_shape=(
            jax.ShapeDtypeStruct((PIECE, WIDTH), BF),
            jax.ShapeDtypeStruct((PIECE + TAIL, WIDTH), BF),
            lane,
        ),
        in_specs=[VM] * 7, out_specs=(VM, VM, VM),
        compiler_params=PARAMS, name="across_sums",
    )(kept, sent_on, right1, left1, through0, through1, lse)
    backs = flip(last0), flip(last1)
    keep, send, lse = pl.pallas_call(
        sum_kernel,
        out_shape=(shape, jax.ShapeDtypeStruct((PIECE + TAIL, WIDTH), BF), lane),
        in_specs=[SM] + [VM] * 7, out_specs=(VM, VM, VM),
        compiler_params=PARAMS, name="own_sums",
    )(ids, kept, sent_on, right0, left0, *backs, lse)
    image_grad, text_grad, loss = pl.pallas_call(
        grad_kernel,
        out_shape=(shape, shape, jax.ShapeDtypeStruct((1, 1), F32)),
        in_specs=[SM] + [VM] * 5, out_specs=(VM, VM, VM),
        compiler_params=PARAMS, name="grad_rows",
    )(ids, image_embeds, text_embeds, keep, swap(send), lse)
    loss = loss[0, 0]
    return (image_grad, text_grad, loss)


def solution(mesh):
    return jax.shard_map(
        per_device,
        mesh=mesh,
        in_specs=(P(("row", "col"), None), P(("col", "row"), None)),
        out_specs=(P(("row", "col"), None), P(("col", "row"), None), P()),
        check_vma=False,
    )
```

```python
import functools
import math

import jax
import jax.numpy as jnp
import numpy as np
from jax import lax
from jax.experimental import pallas as pl
from jax.experimental.pallas import tpu as pltpu
from jax.sharding import PartitionSpec as P

PIECE = 128
PART = 2 * PIECE
WIDTH = 1280
RING = 4
PART_AT = ((2, 0), (2, 1), (1, 1), (3, 1), (0, 1), (0, 0), (1, 0), (3, 0))
PARTS = len(PART_AT)
FAR = 2
ROWS, COLS = 8, 16
IMG = PARTS * PART
TXT = PARTS * PIECE
FAR_IMG, FAR_TXT = FAR * PART, FAR * PIECE
NEAR_IMG, NEAR_TXT = IMG - FAR_IMG, TXT - FAR_TXT
CORE, TXT_AT, MATCH_AT = 40, 32, 16
TAIL = 16
PRODUCT_FLOPS = 5 * 10**10

SHIFT = 22.0
LIFT = 70.0
FLOOR = math.exp(-62.0)
LOG2E = math.log2(math.e)

VM = pl.BlockSpec(memory_space=pltpu.VMEM)
SM = pl.BlockSpec(memory_space=pltpu.SMEM)
PARAMS = pltpu.CompilerParams(vmem_limit_bytes=8 * 1024 * 1024)
F32, BF = jnp.float32, jnp.bfloat16
NT = (((1,), (1,)), ((), ()))
NN = (((1,), (0,)), ((), ()))
TN = (((0,), (0,)), ((), ()))
AXES = ("row", "col")


def dot(a, b, dims):
    return lax.dot_general(a, b, dims, preferred_element_type=F32)


def device(yl, z, x, yh, k):
    return (yl * 4 + z) * COLS + (x * 2 + yh) * 2 + k


def places():
    return [
        (yl, z, x, yh, k)
        for yl in range(2) for z in range(RING) for x in range(RING) for yh in range(2) for k in range(2)
    ]


def neighbour(y, k):
    return y ^ 1 if k == 0 else (y + (1 if y % 2 else 3)) % RING


def group(value, d, side):
    pairs = []
    for yl, z, x, yh, k in places():
        y = yh * 2 + yl
        y = neighbour(y, k) if side else y
        target = device(y % 2, (z + d * k) % RING, (x + d * (1 - k)) % RING, y // 2, k)
        pairs.append((device(yl, z, x, yh, k), target))
    return lax.ppermute(value, AXES, pairs)


def ring(value, d):
    return group(value, d, 0)


def flip(value):
    return group(value, 0, 1)


def group_sum(value):
    value = value + ring(value, 1) + ring(value, 2) + ring(value, 3)
    return value + flip(value)


def swap(value):
    return lax.ppermute(value, AXES, [
        (device(yl, z, x, yh, k), device(yl, z, x, yh, 1 - k)) for yl, z, x, yh, k in places()
    ])


def device_table():
    table = np.zeros((ROWS * COLS, 41), np.int32)
    for yl, z, x, yh, k in places():
        y = yh * 2 + yl
        img, match, txt, owned = [], [], [], []
        for d, side in PART_AT:
            zt, yt = (z + d) % RING, neighbour(y, 1) if side else y
            txt.append(zt * 2 + (yt + 1) % 2)
            owner = device(yt % 2, zt, x, yt // 2, k)
            owned.append(owner % COLS * ROWS + owner // COLS)
        for d, side in PART_AT:
            xi, yi = (x + d) % RING, neighbour(y, 0) if side else y
            for h in range(2):
                img.append((xi * 2 + yi % 2) * 2 + h)
                piece = device(yi % 2, z, xi, yi // 2, h)
                match.append(owned.index(piece) if piece in owned else -1)
        table[device(yl, z, x, yh, k)] = img + match + txt + [k]
    return table


def cost(flops, bytes_accessed):
    return pl.CostEstimate(flops=flops, bytes_accessed=bytes_accessed, transcendentals=0)


def diagonal():
    shape = (PIECE, PIECE)
    return lax.broadcasted_iota(jnp.int32, shape, 0) == lax.broadcasted_iota(jnp.int32, shape, 1)


def unit_kernel(image_ref, text_ref, keep_ref, send_ref):
    core = lax.axis_index("col") % 2

    def unit(src):
        x = src[...]
        return (x / jnp.sqrt(jnp.sum(x * x, axis=1, keepdims=True) + 1e-06)).astype(BF)

    image, text = unit(image_ref), unit(text_ref)

    @pl.when(core == 0)
    def _():
        keep_ref[...] = image
        send_ref[...] = text

    @pl.when(core == 1)
    def _():
        keep_ref[...] = text
        send_ref[...] = image


def unit_pair(image, text):
    shape = jax.ShapeDtypeStruct((PIECE, WIDTH), BF)
    return pl.pallas_call(
        unit_kernel, out_shape=(shape, shape), in_specs=[VM, VM], out_specs=(VM, VM),
        compiler_params=PARAMS, name="unit_rows",
    )(image, text)


def place_parts(core, here, there, img, txt):
    @pl.when(core == 0)
    def _():
        for m, (mine, other) in enumerate(zip(here, there)):
            img[m * PART:(m + 1) * PART, :] = mine[...]
            txt[m * PIECE:(m + 1) * PIECE, :] = other[:PIECE, :]

    @pl.when(core == 1)
    def _():
        for m, (mine, other) in enumerate(zip(here, there)):
            img[m * PART:(m + 1) * PART, :] = other[...]
            txt[m * PIECE:(m + 1) * PIECE, :] = mine[PIECE:, :]


def score_tiles(tiles, img, txt, held, racc, cacc):
    def epilogue(t):
        row, rows, col, h_out, h_row, h_col = tiles[t]
        cols = slice(col, col + 256)
        total = jnp.zeros((8, 256), F32)
        for p in range(0, rows, PIECE):
            d = held[t % 2][p:p + PIECE, :]
            h = jnp.exp2(d * (50.0 * LOG2E) - (0.5 * SHIFT * LOG2E))
            h_out[h_row + p:h_row + p + PIECE, h_col:h_col + 256] = h
            q = h * h
            racc[row + p:row + p + PIECE, :] += q[:, :PIECE] + q[:, PIECE:]
            total += jnp.sum(q.reshape(16, 8, 256), axis=0)
        cacc[:, cols] += total

    for t, (row, rows, col, *_) in enumerate(tiles):
        held[t % 2][:rows, :] = dot(img[row:row + rows, :], txt[col:col + 256, :], NT)
        if t:
            epilogue(t - 1)
    epilogue(len(tiles) - 1)


def near_kernel(ids, *refs):
    count = PARTS - FAR
    here, there = refs[:count], refs[count:2 * count]
    h_out, img, txt, racc, cacc, even, odd = refs[2 * count:]
    place_parts(ids[CORE], here, there, img, txt)
    racc[...] = jnp.zeros_like(racc)
    cacc[...] = jnp.zeros_like(cacc)
    half = NEAR_IMG // 2
    tiles = [(r, half, c, h_out, r, c) for c in range(0, NEAR_TXT, 256) for r in (0, half)]
    score_tiles(tiles, img, txt, (even, odd), racc, cacc)


def near_scores(ids, here, there):
    return list(pl.pallas_call(
        near_kernel,
        out_shape=(
            jax.ShapeDtypeStruct((NEAR_IMG, NEAR_TXT), F32),
            jax.ShapeDtypeStruct((NEAR_IMG, WIDTH), BF),
            jax.ShapeDtypeStruct((NEAR_TXT, WIDTH), BF),
            jax.ShapeDtypeStruct((NEAR_IMG, PIECE), F32),
            jax.ShapeDtypeStruct((8, NEAR_TXT), F32),
        ),
        in_specs=[SM] + [VM] * (2 * len(here)),
        out_specs=(VM,) * 5,
        scratch_shapes=[pltpu.VMEM((NEAR_IMG // 2, 256), F32)] * 2,
        compiler_params=PARAMS,
        cost_estimate=cost(1, 1),
        name="near_scores",
    )(ids, *here, *there))


def far_kernel(ids, left, right, there_left, there_right, near, near_img, near_txt, near_racc,
               near_cacc, h_rows, h_cols, img, txt, keep, send, even, odd, racc, cacc, rs, cs, dg):
    core = ids[CORE]

    def place(halves, text):
        for i in range(FAR):
            for k, half in enumerate(halves):
                at = i * PART + k * PIECE
                img[at:at + PIECE, :] = half[i * PIECE:(i + 1) * PIECE, :]
        txt[:FAR_TXT, :] = text[...]

    pl.when(core == 0)(lambda: place((left, right), there_left))
    pl.when(core == 1)(lambda: place((there_left, there_right), right))
    img[FAR_IMG:, :] = near_img[...]
    txt[FAR_TXT:, :] = near_txt[...]
    racc[:FAR_IMG, :] = jnp.zeros((FAR_IMG, PIECE), F32)
    racc[FAR_IMG:, :] = near_racc[...]
    cacc[:, :FAR_TXT] = jnp.zeros((8, FAR_TXT), F32)
    cacc[:, FAR_TXT:] = near_cacc[...]
    for ref in (rs, cs, dg, keep, send):
        ref[...] = jnp.zeros_like(ref)
    half = NEAR_IMG // 2
    tiles = [(FAR_IMG + r, half, 0, h_cols, r, 0) for r in (0, half)]
    tiles += [(0, FAR_IMG, c, h_rows, 0, c) for c in range(0, TXT, 256)]
    score_tiles(tiles, img, txt, (even, odd), racc, cacc)

    lowest = jnp.full((1, PIECE), jnp.inf, F32)
    for p in range(COLS):
        part = jnp.sum(racc[p * PIECE:(p + 1) * PIECE, :].T, axis=0, keepdims=True)
        rs[0, pl.ds(ids[p], 1), :] = part
        lowest = jnp.minimum(lowest, part)
    total = jnp.sum(cacc[...], axis=0, keepdims=True)
    for m in range(PARTS):
        part = total[:, m * PIECE:(m + 1) * PIECE]
        cs[0, pl.ds(ids[TXT_AT + m], 1), :] = part
        lowest = jnp.minimum(lowest, part)

    def half_of(p, m):
        at = p * PIECE if p < 2 * FAR else (p - 2 * FAR) * PIECE
        if p < 2 * FAR:
            return h_rows[at:at + PIECE, m * PIECE:(m + 1) * PIECE]
        if m < FAR:
            return h_cols[at:at + PIECE, m * PIECE:(m + 1) * PIECE]
        return near[at:at + PIECE, (m - FAR) * PIECE:(m - FAR + 1) * PIECE]

    @pl.when(jnp.min(lowest) < FLOOR)
    def _():
        for p in range(COLS):
            part = jnp.zeros((PIECE, PIECE), F32)
            for m in range(PARTS):
                g = half_of(p, m) * math.exp(0.5 * (SHIFT + LIFT))
                part += g * g
                cs[1, pl.ds(ids[TXT_AT + m], 1), :] += jnp.sum(g * g, axis=0, keepdims=True)
            rs[1, pl.ds(ids[p], 1), :] = jnp.sum(part.T, axis=0, keepdims=True)

    for p in range(COLS):
        match = ids[MATCH_AT + p]

        @pl.when(match >= 0)
        def _():
            other = txt[pl.ds(pl.multiple_of(match * PIECE, PIECE), PIECE), :]
            s = 100.0 * dot(img[p * PIECE:(p + 1) * PIECE, :], other, NT)
            dg[...] += jnp.sum(jnp.where(diagonal(), s, 0.0).reshape(16, 8, PIECE), axis=0)

    @pl.when(core == 0)
    def _():
        keep[0:2] = rs[...]
        keep[2, 0:8] = dg[...]
        send[0:2, 0:8] = cs[...]

    @pl.when(core == 1)
    def _():
        send[0:2] = rs[...]
        send[2, 0:8] = dg[...]
        keep[0:2, 8:16] = cs[...]


def far_scores(ids, here, there, near):
    sums = jax.ShapeDtypeStruct((3, COLS, PIECE), F32)
    return pl.pallas_call(
        far_kernel,
        out_shape=(
            jax.ShapeDtypeStruct((FAR_IMG, TXT), F32),
            jax.ShapeDtypeStruct((NEAR_IMG, FAR_TXT), F32),
            jax.ShapeDtypeStruct((IMG, WIDTH), BF),
            jax.ShapeDtypeStruct((TXT, WIDTH), BF),
            sums, sums,
        ),
        in_specs=[SM] + [VM] * 9,
        out_specs=(VM,) * 6,
        scratch_shapes=[
            pltpu.VMEM((NEAR_IMG // 2, 256), F32),
            pltpu.VMEM((NEAR_IMG // 2, 256), F32),
            pltpu.VMEM((IMG, PIECE), F32),
            pltpu.VMEM((8, TXT), F32),
            pltpu.VMEM((2, COLS, PIECE), F32),
            pltpu.VMEM((2, ROWS, PIECE), F32),
            pltpu.VMEM((8, PIECE), F32),
        ],
        compiler_params=PARAMS,
        cost_estimate=cost(2 * (IMG * TXT - NEAR_IMG * NEAR_TXT) * WIDTH, 16 << 20),
        name="far_scores",
    )(ids, *here, *there, *near)


def lse_of(sums):
    return jnp.where(sums[0] >= FLOOR, SHIFT + jnp.log(sums[0]), jnp.log(sums[1]) - LIFT)


def row_col_factors(core, own, far, a_s, b_s):
    scale = math.sqrt(0.5)
    factors = [scale * jnp.exp(0.5 * (SHIFT - lse_of(v))) for v in (own, far)]
    a_s[...] = jnp.where(core == 0, factors[0], factors[1])
    b_s[...] = jnp.where(core == 0, factors[1][:8], factors[0][8:])


def weights_block(ids, half, w, a_s, b_s, p0, p1, m0, m1):
    b = [b_s[pl.ds(ids[TXT_AT + m], 1), :] for m in range(m0, m1)]

    @pl.loop(p0, p1)
    def _(p):
        rows = pl.ds(pl.multiple_of((p - p0) * PIECE, PIECE), PIECE)
        a = jnp.broadcast_to(a_s[pl.ds(ids[p], 1), :], (PIECE, PIECE)).T
        for m in range(m1 - m0):
            cols = slice(m * PIECE, (m + 1) * PIECE)
            h = half[rows, cols]
            v, t = h * a, h * b[m]
            w[rows, cols] = (v * v + t * t).astype(BF)
        match = ids[MATCH_AT + p]

        @pl.when((match >= m0) & (match < m1))
        def _():
            cols = pl.ds(pl.multiple_of((match - m0) * PIECE, PIECE), PIECE)
            h = half[rows, cols]
            v, t = h * a, h * b_s[pl.ds(ids[TXT_AT + match], 1), :]
            w[rows, cols] = (v * v + t * t - diagonal().astype(F32)).astype(BF)


def product_kernel(start, end, kept_here, core, w_rows, w_cols, w_near, img, txt, out):
    first, last = start - FAR, end - FAR

    def image_side():
        if start < FAR:
            d = dot(w_rows[start * PART:end * PART, :], txt[...], NN)
        else:
            rows = slice(first * PART, last * PART)
            d = dot(w_cols[rows, :], txt[:FAR_TXT, :], NN)
            d = d + dot(w_near[rows, :], txt[FAR_TXT:, :], NN)
        out[...] = d.astype(BF)

    def text_side():
        at, pad = (PIECE, 0) if kept_here else (0, PIECE)
        d = dot(w_rows[:, start * PIECE:end * PIECE], img[:FAR_IMG, :], TN)
        if start < FAR:
            d = d + dot(w_cols[:, start * PIECE:end * PIECE], img[FAR_IMG:, :], TN)
        else:
            d = d + dot(w_near[:, first * PIECE:last * PIECE], img[FAR_IMG:, :], TN)
        d = d.astype(BF)
        for i in range(end - start):
            out[i * PART + at:i * PART + at + PIECE, :] = d[i * PIECE:(i + 1) * PIECE]
            out[i * PART + pad:i * PART + pad + PIECE, :] = jnp.zeros((PIECE, WIDTH), BF)

    pl.when(core == (0 if kept_here else 1))(image_side)
    pl.when(core == (1 if kept_here else 0))(text_side)


FACTORS = [pltpu.VMEM((COLS, PIECE), F32), pltpu.VMEM((ROWS, PIECE), F32)]


def far_products(ids, own, far, h_rows, h_cols, img, txt):
    def kernel(ids, own, far, h_rows, h_cols, img, txt, w_rows, w_cols, out, a_s, b_s):
        row_col_factors(ids[CORE], own, far, a_s, b_s)
        weights_block(ids, h_rows, w_rows, a_s, b_s, 0, 2 * FAR, 0, PARTS)
        weights_block(ids, h_cols, w_cols, a_s, b_s, 2 * FAR, COLS, 0, FAR)
        product_kernel(0, FAR, False, ids[CORE], w_rows, w_cols, None, img, txt, out)

    return pl.pallas_call(
        kernel,
        out_shape=(
            jax.ShapeDtypeStruct((FAR_IMG, TXT), BF),
            jax.ShapeDtypeStruct((NEAR_IMG, FAR_TXT), BF),
            jax.ShapeDtypeStruct((FAR * PART, WIDTH), BF),
        ),
        in_specs=[SM] + [VM] * 6,
        out_specs=(VM,) * 3,
        scratch_shapes=FACTORS,
        compiler_params=PARAMS,
        cost_estimate=cost(PRODUCT_FLOPS, 1),
        name="far_products",
    )(ids, own, far, h_rows, h_cols, img, txt)


def near_products(token, ids, own, far, near, w_rows, w_cols, img, txt):
    def kernel(token, ids, own, far, near, w_rows, w_cols, img, txt, w_near, s0, s1, out, a_s, b_s,
               sent):
        row_col_factors(ids[CORE], own, far, a_s, b_s)
        weights_block(ids, near, w_near, a_s, b_s, 2 * FAR, COLS, FAR, PARTS)
        args = (ids[CORE], w_rows, w_cols, w_near, img, txt)
        product_kernel(FAR, FAR + 2, False, *args, sent)
        s0[...] = sent[:PART, :]
        s1[...] = sent[PART:, :]
        product_kernel(FAR, FAR + 2, True, *args, out)

    part = jax.ShapeDtypeStruct((PART, WIDTH), BF)
    return pl.pallas_call(
        kernel,
        out_shape=(
            jax.ShapeDtypeStruct((NEAR_IMG, NEAR_TXT), BF),
            part, part,
            jax.ShapeDtypeStruct((2 * PART, WIDTH), BF),
        ),
        in_specs=[VM, SM] + [VM] * 7,
        out_specs=(VM,) * 4,
        scratch_shapes=[*FACTORS, pltpu.VMEM((2 * PART, WIDTH), BF)],
        compiler_params=PARAMS,
        cost_estimate=cost(PRODUCT_FLOPS, 1),
        name="near_products",
    )(token, ids, own, far, near, w_rows, w_cols, img, txt)


def products(start, end, kept_here, tokens, ids, w, img, txt, flops=PRODUCT_FLOPS):
    def kernel(ids, img, txt, *refs):
        w_near = refs[2] if len(w) == 3 else None
        product_kernel(
            start, end, kept_here, ids[CORE], refs[0], refs[1], w_near, img, txt, refs[-1]
        )

    return pl.pallas_call(
        kernel,
        out_shape=jax.ShapeDtypeStruct(((end - start) * PART, WIDTH), BF),
        in_specs=[SM] + [VM] * (2 + len(w) + len(tokens)),
        out_specs=VM,
        compiler_params=PARAMS,
        cost_estimate=cost(flops, 1),
        name="products_kept" if kept_here else "products_sent",
    )(ids, img, txt, *w, *tokens)


def read_tail(ref, at):
    rows = ref[at:at + TAIL, :3 * PIECE].astype(F32)[:8]
    return sum(rows[:, i * PIECE:(i + 1) * PIECE] for i in range(3))


def write_tail(ref, at, terms):
    ref[at:at + TAIL, :] = jnp.zeros((TAIL, WIDTH), BF)
    pad = jnp.zeros((TAIL - 8, PIECE), F32)
    for i in range(3):
        piece = terms.astype(BF).astype(F32)
        ref[at:at + TAIL, i * PIECE:(i + 1) * PIECE] = jnp.concatenate([piece, pad]).astype(BF)
        terms = terms - piece


def far_sum_kernel(ids, kept, sent, sums, far0, far1, lse_out):
    terms = lse_of(sums[...])
    terms = terms[:8] + terms[8:]
    terms = terms - jnp.where(ids[CORE] == 0, 0.0, 2.0) * sums[2, :8]
    lse_out[...] = terms
    for i, far in enumerate((far0, far1)):
        rows = slice(i * PART, (i + 1) * PART)
        far[:PART, :] = (kept[rows, :].astype(F32) + sent[rows, :].astype(F32)).astype(BF)
        write_tail(far, PART, terms)


def near_sum_kernel(kept, sent0, sent1, through0, through1, token, near, back):
    near[:PART, :] = (kept[:PART, :].astype(F32) + sent0[...].astype(F32)).astype(BF)
    near[PART:, :] = through0[PART:, :]
    total = kept[PART:, :].astype(F32) + sent1[...].astype(F32)
    back[...] = (total + through1[:PART, :].astype(F32)).astype(BF)


def across_kernel(kept, sent, right, left, through0, through1, lse, out, lse_out):
    total = kept[:PART, :].astype(F32) + sent[:PART, :].astype(F32)
    out[:PART, :] = (total + right[:PART, :].astype(F32) + left[...].astype(F32)).astype(BF)
    terms = lse[...]
    for ref in (through0, through1, right):
        terms = terms + read_tail(ref, PART)
    lse_out[...] = terms
    write_tail(out, PART, terms)


def sum_kernel(ids, kept, sent, right, left, back, lse, keep, send, lse_out):
    core = ids[CORE]
    total = kept[PART:2 * PART, :].astype(F32) + sent[PART:2 * PART, :].astype(F32)
    total = total + right[...].astype(F32) + left[...].astype(F32) + back[:PART, :].astype(F32)
    terms = lse[...] + read_tail(back, PART)
    lse_out[...] = terms
    write_tail(send, PIECE, terms)

    @pl.when(core == 0)
    def _():
        keep[...] = total[:PIECE]
        send[:PIECE, :] = total[PIECE:].astype(BF)

    @pl.when(core == 1)
    def _():
        keep[...] = total[PIECE:]
        send[:PIECE, :] = total[:PIECE].astype(BF)


def grad_kernel(ids, image, text, keep, got, lse, image_out, text_out, loss_out):
    core = ids[CORE]

    def grad(values, total, out):
        x = values[...]
        norm = jnp.sqrt(jnp.sum(x * x, axis=1, keepdims=True) + 1e-06)
        unit = x / norm
        g = total[:PIECE, :].astype(F32)
        out[...] = (g - unit * jnp.sum(unit * g, axis=1, keepdims=True)) / norm

    @pl.when(core == 0)
    def _():
        grad(image, keep, image_out)
        grad(text, got, text_out)

    @pl.when(core == 1)
    def _():
        grad(image, got, image_out)
        grad(text, keep, text_out)

    terms = lse[...] + read_tail(got, PIECE)
    total = jnp.sum(jnp.sum(terms, axis=0, keepdims=True), axis=1, keepdims=True)
    loss_out[...] = total * (1.0 / (2.0 * ROWS * COLS * PIECE))


def per_device(image_embeds, text_embeds):
    here = lax.axis_index("row") * COLS + lax.axis_index("col")
    first = lax.axis_index("col") % 2 == 0

    keep, send = unit_pair(image_embeds, text_embeds)
    got = swap(send)
    here, keep = lax.optimization_barrier((here, keep))
    ids = lax.dynamic_index_in_dim(jnp.asarray(device_table()), here, keepdims=False)
    own = jnp.concatenate([jnp.where(first, keep, got), jnp.where(first, got, keep)])
    own, ids = lax.optimization_barrier((own, ids))

    other = flip(own)
    left0, right0 = ring(own, 1), ring(own, 3)
    left1, right1 = ring(other, 1), ring(other, 3)
    far_left = ring(jnp.concatenate([left0[:PIECE], left1[:PIECE]]), 1)
    far_right = ring(jnp.concatenate([right0[PIECE:], right1[PIECE:]]), 3)
    mine = [right1, left1, other, own, right0, left0]
    late, _ = lax.optimization_barrier((own, other))
    theirs = [swap(late if v is own else v) for v in mine]
    near = near_scores(ids, mine, theirs)
    far_left, far_right, near[0] = lax.optimization_barrier((far_left, far_right, near[0]))
    h_rows, h_cols, img, txt, keep, send = far_scores(
        ids, (far_left, far_right), (swap(far_left), swap(far_right)), near
    )
    sums = keep + swap(send)
    sums = group_sum(sums)
    theirs = swap(sums)

    def add(*v):
        return functools.reduce(lambda a, b: a + b, [u.astype(F32) for u in v]).astype(BF)

    def part(value, i):
        return value[i * PART:(i + 1) * PART]

    def mark(done):
        return swap(done[:16, :PIECE])

    w_rows, w_cols, sent = far_products(ids, sums, theirs, h_rows, h_cols, img, txt)
    sent = swap(sent)
    kept = products(0, FAR, True, (), ids, (w_rows, w_cols), img, txt)
    tailed = jax.ShapeDtypeStruct((PART + TAIL, WIDTH), BF)
    lane = jax.ShapeDtypeStruct((8, PIECE), F32)
    far0, far1, lse = pl.pallas_call(
        far_sum_kernel, out_shape=(tailed, tailed, lane), in_specs=[SM] + [VM] * 3,
        out_specs=(VM,) * 3, compiler_params=PARAMS, name="far_sums",
    )(ids, kept, sent, theirs)
    through0, through1 = ring(far0, 1), ring(far1, 3)

    w_near, s0, s1, kept = near_products(
        mark(far0), ids, sums, theirs, near[0], w_rows, w_cols, img, txt
    )
    w = (w_rows, w_cols, w_near)
    sent_on = products(4, 8, False, (), ids, w, img, txt, 1)
    near1, back1 = pl.pallas_call(
        near_sum_kernel, out_shape=(tailed, jax.ShapeDtypeStruct((PART, WIDTH), BF)),
        in_specs=[VM] * 6, out_specs=(VM, VM), compiler_params=PARAMS, name="near_sums",
    )(kept, swap(s0), swap(s1), through0, through1, sent_on)
    sent_on = swap(sent_on)
    right1, left1 = ring(near1, 1), ring(back1, 3)

    kept = products(4, 8, True, (mark(back1),), ids, w, img, txt)
    near0 = add(part(kept, 2), part(sent_on, 2), part(through0, 0))
    back0 = add(part(kept, 3), part(sent_on, 3))
    near0, back0, kept, sent_on = lax.optimization_barrier((near0, back0, kept, sent_on))
    right0, left0 = ring(near0, 1), ring(back0, 3)
    shape = jax.ShapeDtypeStruct((PIECE, WIDTH), F32)
    last, lse = pl.pallas_call(
        across_kernel, out_shape=(tailed, lane), in_specs=[VM] * 7, out_specs=(VM, VM),
        compiler_params=PARAMS, name="across_sums",
    )(kept, sent_on, right1, left1, through0, through1, lse)
    back = flip(last)
    keep, send, lse = pl.pallas_call(
        sum_kernel,
        out_shape=(shape, jax.ShapeDtypeStruct((PIECE + TAIL, WIDTH), BF), lane),
        in_specs=[SM] + [VM] * 6, out_specs=(VM, VM, VM),
        compiler_params=PARAMS, name="own_sums",
    )(ids, kept, sent_on, right0, left0, back, lse)
    image_grad, text_grad, loss = pl.pallas_call(
        grad_kernel,
        out_shape=(shape, shape, jax.ShapeDtypeStruct((1, 1), F32)),
        in_specs=[SM] + [VM] * 5, out_specs=(VM, VM, VM),
        compiler_params=PARAMS, name="grad_rows",
    )(ids, image_embeds, text_embeds, keep, swap(send), lse)
    loss = loss[0, 0]
    return (image_grad, text_grad, loss)


def solution(mesh):
    return jax.shard_map(
        per_device,
        mesh=mesh,
        in_specs=(P(("row", "col"), None), P(("col", "row"), None)),
        out_specs=(P(("row", "col"), None), P(("col", "row"), None), P()),
        check_vma=False,
    )
```

```python
import functools
import math

import jax
import jax.numpy as jnp
import numpy as np
from jax import lax
from jax.experimental import pallas as pl
from jax.experimental.pallas import tpu as pltpu
from jax.sharding import PartitionSpec as P

PIECE = 128
PART = 2 * PIECE
WIDTH = 1280
RING = 4
PART_AT = ((2, 0), (2, 1), (1, 1), (3, 1), (0, 1), (0, 0), (1, 0), (3, 0))
PARTS = len(PART_AT)
FAR = 2
ROWS, COLS = 8, 16
IMG = PARTS * PART
TXT = PARTS * PIECE
FAR_IMG, FAR_TXT = FAR * PART, FAR * PIECE
NEAR_IMG, NEAR_TXT = IMG - FAR_IMG, TXT - FAR_TXT
CORE, TXT_AT, MATCH_AT = 40, 32, 16
TAIL = 16
PRODUCT_FLOPS = 5 * 10**10

SHIFT = 22.0
LIFT = 70.0
FLOOR = math.exp(-62.0)
LOG2E = math.log2(math.e)

VM = pl.BlockSpec(memory_space=pltpu.VMEM)
SM = pl.BlockSpec(memory_space=pltpu.SMEM)
PARAMS = pltpu.CompilerParams(vmem_limit_bytes=8 * 1024 * 1024)
F32, BF = jnp.float32, jnp.bfloat16
NT = (((1,), (1,)), ((), ()))
NN = (((1,), (0,)), ((), ()))
TN = (((0,), (0,)), ((), ()))
AXES = ("row", "col")


def dot(a, b, dims):
    return lax.dot_general(a, b, dims, preferred_element_type=F32)


def device(yl, z, x, yh, k):
    return (yl * 4 + z) * COLS + (x * 2 + yh) * 2 + k


def places():
    return [
        (yl, z, x, yh, k)
        for yl in range(2) for z in range(RING) for x in range(RING) for yh in range(2) for k in range(2)
    ]


def neighbour(y, k):
    return y ^ 1 if k == 0 else (y + (1 if y % 2 else 3)) % RING


def group(value, d, side):
    pairs = []
    for yl, z, x, yh, k in places():
        y = yh * 2 + yl
        y = neighbour(y, k) if side else y
        target = device(y % 2, (z + d * k) % RING, (x + d * (1 - k)) % RING, y // 2, k)
        pairs.append((device(yl, z, x, yh, k), target))
    return lax.ppermute(value, AXES, pairs)


def ring(value, d):
    return group(value, d, 0)


def flip(value):
    return group(value, 0, 1)


def group_sum(value):
    value = value + ring(value, 1) + ring(value, 2) + ring(value, 3)
    return value + flip(value)


def swap(value):
    return lax.ppermute(value, AXES, [
        (device(yl, z, x, yh, k), device(yl, z, x, yh, 1 - k)) for yl, z, x, yh, k in places()
    ])


def device_table():
    table = np.zeros((ROWS * COLS, 41), np.int32)
    for yl, z, x, yh, k in places():
        y = yh * 2 + yl
        img, match, txt, owned = [], [], [], []
        for d, side in PART_AT:
            zt, yt = (z + d) % RING, neighbour(y, 1) if side else y
            txt.append(zt * 2 + (yt + 1) % 2)
            owner = device(yt % 2, zt, x, yt // 2, k)
            owned.append(owner % COLS * ROWS + owner // COLS)
        for d, side in PART_AT:
            xi, yi = (x + d) % RING, neighbour(y, 0) if side else y
            for h in range(2):
                img.append((xi * 2 + yi % 2) * 2 + h)
                piece = device(yi % 2, z, xi, yi // 2, h)
                match.append(owned.index(piece) if piece in owned else -1)
        table[device(yl, z, x, yh, k)] = img + match + txt + [k]
    return table


def cost(flops, bytes_accessed):
    return pl.CostEstimate(flops=flops, bytes_accessed=bytes_accessed, transcendentals=0)


def diagonal():
    shape = (PIECE, PIECE)
    return lax.broadcasted_iota(jnp.int32, shape, 0) == lax.broadcasted_iota(jnp.int32, shape, 1)


def unit_kernel(image_ref, text_ref, keep_ref, send_ref):
    core = lax.axis_index("col") % 2

    def unit(src):
        x = src[...]
        return (x / jnp.sqrt(jnp.sum(x * x, axis=1, keepdims=True) + 1e-06)).astype(BF)

    image, text = unit(image_ref), unit(text_ref)

    @pl.when(core == 0)
    def _():
        keep_ref[...] = image
        send_ref[...] = text

    @pl.when(core == 1)
    def _():
        keep_ref[...] = text
        send_ref[...] = image


def unit_pair(image, text):
    shape = jax.ShapeDtypeStruct((PIECE, WIDTH), BF)
    return pl.pallas_call(
        unit_kernel, out_shape=(shape, shape), in_specs=[VM, VM], out_specs=(VM, VM),
        compiler_params=PARAMS, name="unit_rows",
    )(image, text)


def place_parts(core, here, there, img, txt):
    @pl.when(core == 0)
    def _():
        for m, (mine, other) in enumerate(zip(here, there)):
            img[m * PART:(m + 1) * PART, :] = mine[...]
            txt[m * PIECE:(m + 1) * PIECE, :] = other[:PIECE, :]

    @pl.when(core == 1)
    def _():
        for m, (mine, other) in enumerate(zip(here, there)):
            img[m * PART:(m + 1) * PART, :] = other[...]
            txt[m * PIECE:(m + 1) * PIECE, :] = mine[PIECE:, :]


def score_tiles(tiles, img, txt, held, racc, cacc):
    def epilogue(t):
        row, rows, col, h_out, h_row, h_col = tiles[t]
        cols = slice(col, col + 256)
        total = jnp.zeros((8, 256), F32)
        for p in range(0, rows, PIECE):
            d = held[t % 2][p:p + PIECE, :]
            h = jnp.exp2(d * (50.0 * LOG2E) - (0.5 * SHIFT * LOG2E))
            h_out[h_row + p:h_row + p + PIECE, h_col:h_col + 256] = h
            q = h * h
            racc[row + p:row + p + PIECE, :] += q[:, :PIECE] + q[:, PIECE:]
            total += jnp.sum(q.reshape(16, 8, 256), axis=0)
        cacc[:, cols] += total

    for t, (row, rows, col, *_) in enumerate(tiles):
        held[t % 2][:rows, :] = dot(img[row:row + rows, :], txt[col:col + 256, :], NT)
        if t:
            epilogue(t - 1)
    epilogue(len(tiles) - 1)


def near_kernel(ids, *refs):
    count = PARTS - FAR
    here, there = refs[:count], refs[count:2 * count]
    h_out, img, txt, racc, cacc, even, odd = refs[2 * count:]
    place_parts(ids[CORE], here, there, img, txt)
    racc[...] = jnp.zeros_like(racc)
    cacc[...] = jnp.zeros_like(cacc)
    half = NEAR_IMG // 2
    tiles = [(r, half, c, h_out, r, c) for c in range(0, NEAR_TXT, 256) for r in (0, half)]
    score_tiles(tiles, img, txt, (even, odd), racc, cacc)


def near_scores(ids, here, there):
    return list(pl.pallas_call(
        near_kernel,
        out_shape=(
            jax.ShapeDtypeStruct((NEAR_IMG, NEAR_TXT), F32),
            jax.ShapeDtypeStruct((NEAR_IMG, WIDTH), BF),
            jax.ShapeDtypeStruct((NEAR_TXT, WIDTH), BF),
            jax.ShapeDtypeStruct((NEAR_IMG, PIECE), F32),
            jax.ShapeDtypeStruct((8, NEAR_TXT), F32),
        ),
        in_specs=[SM] + [VM] * (2 * len(here)),
        out_specs=(VM,) * 5,
        scratch_shapes=[pltpu.VMEM((NEAR_IMG // 2, 256), F32)] * 2,
        compiler_params=PARAMS,
        cost_estimate=cost(1, 1),
        name="near_scores",
    )(ids, *here, *there))


def far_kernel(ids, left, right, there_left, there_right, near, near_img, near_txt, near_racc,
               near_cacc, h_rows, h_cols, img, txt, keep, send, even, odd, racc, cacc, rs, cs, dg):
    core = ids[CORE]

    def place(halves, text):
        for i in range(FAR):
            for k, half in enumerate(halves):
                at = i * PART + k * PIECE
                img[at:at + PIECE, :] = half[i * PIECE:(i + 1) * PIECE, :]
        txt[:FAR_TXT, :] = text[...]

    pl.when(core == 0)(lambda: place((left, right), there_left))
    pl.when(core == 1)(lambda: place((there_left, there_right), right))
    img[FAR_IMG:, :] = near_img[...]
    txt[FAR_TXT:, :] = near_txt[...]
    racc[:FAR_IMG, :] = jnp.zeros((FAR_IMG, PIECE), F32)
    racc[FAR_IMG:, :] = near_racc[...]
    cacc[:, :FAR_TXT] = jnp.zeros((8, FAR_TXT), F32)
    cacc[:, FAR_TXT:] = near_cacc[...]
    for ref in (rs, cs, dg, keep, send):
        ref[...] = jnp.zeros_like(ref)
    half = NEAR_IMG // 2
    tiles = [(FAR_IMG + r, half, 0, h_cols, r, 0) for r in (0, half)]
    tiles += [(0, FAR_IMG, c, h_rows, 0, c) for c in range(0, TXT, 256)]
    score_tiles(tiles, img, txt, (even, odd), racc, cacc)

    lowest = jnp.full((1, PIECE), jnp.inf, F32)
    for p in range(COLS):
        part = jnp.sum(racc[p * PIECE:(p + 1) * PIECE, :].T, axis=0, keepdims=True)
        rs[0, pl.ds(ids[p], 1), :] = part
        lowest = jnp.minimum(lowest, part)
    total = jnp.sum(cacc[...], axis=0, keepdims=True)
    for m in range(PARTS):
        part = total[:, m * PIECE:(m + 1) * PIECE]
        cs[0, pl.ds(ids[TXT_AT + m], 1), :] = part
        lowest = jnp.minimum(lowest, part)

    def half_of(p, m):
        at = p * PIECE if p < 2 * FAR else (p - 2 * FAR) * PIECE
        if p < 2 * FAR:
            return h_rows[at:at + PIECE, m * PIECE:(m + 1) * PIECE]
        if m < FAR:
            return h_cols[at:at + PIECE, m * PIECE:(m + 1) * PIECE]
        return near[at:at + PIECE, (m - FAR) * PIECE:(m - FAR + 1) * PIECE]

    @pl.when(jnp.min(lowest) < FLOOR)
    def _():
        for p in range(COLS):
            part = jnp.zeros((PIECE, PIECE), F32)
            for m in range(PARTS):
                g = half_of(p, m) * math.exp(0.5 * (SHIFT + LIFT))
                part += g * g
                cs[1, pl.ds(ids[TXT_AT + m], 1), :] += jnp.sum(g * g, axis=0, keepdims=True)
            rs[1, pl.ds(ids[p], 1), :] = jnp.sum(part.T, axis=0, keepdims=True)

    for p in range(COLS):
        match = ids[MATCH_AT + p]

        @pl.when(match >= 0)
        def _():
            other = txt[pl.ds(pl.multiple_of(match * PIECE, PIECE), PIECE), :]
            s = 100.0 * dot(img[p * PIECE:(p + 1) * PIECE, :], other, NT)
            dg[...] += jnp.sum(jnp.where(diagonal(), s, 0.0).reshape(16, 8, PIECE), axis=0)

    @pl.when(core == 0)
    def _():
        keep[0:2] = rs[...]
        keep[2, 0:8] = dg[...]
        send[0:2, 0:8] = cs[...]

    @pl.when(core == 1)
    def _():
        send[0:2] = rs[...]
        send[2, 0:8] = dg[...]
        keep[0:2, 8:16] = cs[...]


def far_scores(ids, here, there, near):
    sums = jax.ShapeDtypeStruct((3, COLS, PIECE), F32)
    return pl.pallas_call(
        far_kernel,
        out_shape=(
            jax.ShapeDtypeStruct((FAR_IMG, TXT), F32),
            jax.ShapeDtypeStruct((NEAR_IMG, FAR_TXT), F32),
            jax.ShapeDtypeStruct((IMG, WIDTH), BF),
            jax.ShapeDtypeStruct((TXT, WIDTH), BF),
            sums, sums,
        ),
        in_specs=[SM] + [VM] * 9,
        out_specs=(VM,) * 6,
        scratch_shapes=[
            pltpu.VMEM((NEAR_IMG // 2, 256), F32),
            pltpu.VMEM((NEAR_IMG // 2, 256), F32),
            pltpu.VMEM((IMG, PIECE), F32),
            pltpu.VMEM((8, TXT), F32),
            pltpu.VMEM((2, COLS, PIECE), F32),
            pltpu.VMEM((2, ROWS, PIECE), F32),
            pltpu.VMEM((8, PIECE), F32),
        ],
        compiler_params=PARAMS,
        cost_estimate=cost(2 * (IMG * TXT - NEAR_IMG * NEAR_TXT) * WIDTH, 16 << 20),
        name="far_scores",
    )(ids, *here, *there, *near)


def lse_of(sums):
    return jnp.where(sums[0] >= FLOOR, SHIFT + jnp.log(sums[0]), jnp.log(sums[1]) - LIFT)


def row_col_factors(core, own, far, a_s, b_s):
    scale = math.sqrt(0.5)
    factors = [scale * jnp.exp(0.5 * (SHIFT - lse_of(v))) for v in (own, far)]
    a_s[...] = jnp.where(core == 0, factors[0], factors[1])
    b_s[...] = jnp.where(core == 0, factors[1][:8], factors[0][8:])


def weights_block(ids, half, w, row, col, a_s, b_s, p0, p1, m0, m1):
    b = [b_s[pl.ds(ids[TXT_AT + m], 1), :] for m in range(m0, m1)]

    @pl.loop(p0, p1)
    def _(p):
        rows = pl.ds(pl.multiple_of((p - p0) * PIECE, PIECE), PIECE)
        to = pl.ds(pl.multiple_of((p - p0) * PIECE + row, PIECE), PIECE)
        a = jnp.broadcast_to(a_s[pl.ds(ids[p], 1), :], (PIECE, PIECE)).T
        for m in range(m1 - m0):
            h = half[rows, m * PIECE:(m + 1) * PIECE]
            v, t = h * a, h * b[m]
            w[to, col + m * PIECE:col + (m + 1) * PIECE] = (v * v + t * t).astype(BF)
        match = ids[MATCH_AT + p]

        @pl.when((match >= m0) & (match < m1))
        def _():
            at = pl.multiple_of((match - m0) * PIECE, PIECE)
            h = half[rows, pl.ds(at, PIECE)]
            v, t = h * a, h * b_s[pl.ds(ids[TXT_AT + match], 1), :]
            cols = pl.ds(pl.multiple_of(at + col, PIECE), PIECE)
            w[to, cols] = (v * v + t * t - diagonal().astype(F32)).astype(BF)


def product_kernel(kept_here, core, w_rows, w_lanes, img, txt, out):
    def image_side():
        w, where = w_rows
        for n in range(WIDTH // 256):
            cols = slice(n * 256, n * 256 + 256)
            out[:, cols] = dot(w[where, :], txt[:, cols], NN).astype(BF)

    def text_side():
        at, pad = (PIECE, 0) if kept_here else (0, PIECE)
        w, where = w_lanes
        d = dot(w[:, where], img[...], TN).astype(BF)
        for i in range(d.shape[0] // PIECE):
            out[i * PART + at:i * PART + at + PIECE, :] = d[i * PIECE:(i + 1) * PIECE]
            out[i * PART + pad:i * PART + pad + PIECE, :] = jnp.zeros((PIECE, WIDTH), BF)

    pl.when(core == (0 if kept_here else 1))(image_side)
    pl.when(core == (1 if kept_here else 0))(text_side)


def parts_of(w, start, end):
    return (w, slice(start * PART, end * PART)), (w, slice(start * PIECE, end * PIECE))


FACTORS = [pltpu.VMEM((COLS, PIECE), F32), pltpu.VMEM((ROWS, PIECE), F32)]


def far_products(ids, own, far, h_rows, h_cols, img, txt):
    def kernel(ids, own, far, h_rows, h_cols, img, txt, w_rows, w_lanes, out, a_s, b_s):
        row_col_factors(ids[CORE], own, far, a_s, b_s)
        weights_block(ids, h_rows, w_rows, 0, 0, a_s, b_s, 0, 2 * FAR, 0, PARTS)
        weights_block(ids, h_cols, w_lanes, FAR_IMG, 0, a_s, b_s, 2 * FAR, COLS, 0, FAR)
        w_lanes[:FAR_IMG, :] = w_rows[:, :FAR_TXT]
        product_kernel(
            False, ids[CORE], (w_rows, slice(None)), (w_lanes, slice(None)), img, txt, out
        )

    return pl.pallas_call(
        kernel,
        out_shape=(
            jax.ShapeDtypeStruct((FAR_IMG, TXT), BF),
            jax.ShapeDtypeStruct((IMG, FAR_TXT), BF),
            jax.ShapeDtypeStruct((FAR * PART, WIDTH), BF),
        ),
        in_specs=[SM] + [VM] * 6,
        out_specs=(VM,) * 3,
        scratch_shapes=FACTORS,
        compiler_params=PARAMS,
        cost_estimate=cost(PRODUCT_FLOPS, 1),
        name="far_products",
    )(ids, own, far, h_rows, h_cols, img, txt)


def near_products(token, ids, own, far, near, w_rows, w_lanes, img, txt):
    def kernel(token, ids, own, far, near, w_rows, w_lanes, img, txt, w, s0, s1, out, a_s, b_s,
               sent):
        row_col_factors(ids[CORE], own, far, a_s, b_s)
        w[:FAR_IMG, :] = w_rows[...]
        w[FAR_IMG:, :FAR_TXT] = w_lanes[FAR_IMG:, :]
        weights_block(ids, near, w, FAR_IMG, FAR_TXT, a_s, b_s, 2 * FAR, COLS, FAR, PARTS)
        parts = parts_of(w, FAR, FAR + 2)
        product_kernel(False, ids[CORE], *parts, img, txt, sent)
        s0[...] = sent[:PART, :]
        s1[...] = sent[PART:, :]
        product_kernel(True, ids[CORE], *parts, img, txt, out)

    part = jax.ShapeDtypeStruct((PART, WIDTH), BF)
    return pl.pallas_call(
        kernel,
        out_shape=(
            jax.ShapeDtypeStruct((IMG, TXT), BF),
            part, part,
            jax.ShapeDtypeStruct((2 * PART, WIDTH), BF),
        ),
        in_specs=[VM, SM] + [VM] * 7,
        out_specs=(VM,) * 4,
        scratch_shapes=[*FACTORS, pltpu.VMEM((2 * PART, WIDTH), BF)],
        compiler_params=PARAMS,
        cost_estimate=cost(PRODUCT_FLOPS, 1),
        name="near_products",
    )(token, ids, own, far, near, w_rows, w_lanes, img, txt)


def kept_far(ids, w_rows, w_lanes, img, txt):
    def kernel(ids, w_rows, w_lanes, img, txt, out):
        product_kernel(
            True, ids[CORE], (w_rows, slice(None)), (w_lanes, slice(None)), img, txt, out
        )

    return pl.pallas_call(
        kernel,
        out_shape=jax.ShapeDtypeStruct((FAR * PART, WIDTH), BF),
        in_specs=[SM] + [VM] * 4,
        out_specs=VM,
        compiler_params=PARAMS,
        cost_estimate=cost(PRODUCT_FLOPS, 1),
        name="far_kept",
    )(ids, w_rows, w_lanes, img, txt)


def products(start, end, kept_here, tokens, ids, w, img, txt, flops=PRODUCT_FLOPS):
    def kernel(ids, img, txt, w, *refs):
        product_kernel(kept_here, ids[CORE], *parts_of(w, start, end), img, txt, refs[-1])

    return pl.pallas_call(
        kernel,
        out_shape=jax.ShapeDtypeStruct(((end - start) * PART, WIDTH), BF),
        in_specs=[SM] + [VM] * (3 + len(tokens)),
        out_specs=VM,
        compiler_params=PARAMS,
        cost_estimate=cost(flops, 1),
        name="products_kept" if kept_here else "products_sent",
    )(ids, img, txt, w, *tokens)


def read_tail(ref, at):
    rows = ref[at:at + TAIL, :3 * PIECE].astype(F32)[:8]
    return sum(rows[:, i * PIECE:(i + 1) * PIECE] for i in range(3))


def write_tail(ref, at, terms):
    ref[at:at + TAIL, :] = jnp.zeros((TAIL, WIDTH), BF)
    pad = jnp.zeros((TAIL - 8, PIECE), F32)
    for i in range(3):
        piece = terms.astype(BF).astype(F32)
        ref[at:at + TAIL, i * PIECE:(i + 1) * PIECE] = jnp.concatenate([piece, pad]).astype(BF)
        terms = terms - piece


def far_sum_kernel(ids, kept, sent, sums, far0, far1, lse_out):
    terms = lse_of(sums[...])
    terms = terms[:8] + terms[8:]
    terms = terms - jnp.where(ids[CORE] == 0, 0.0, 2.0) * sums[2, :8]
    lse_out[...] = terms
    for i, far in enumerate((far0, far1)):
        rows = slice(i * PART, (i + 1) * PART)
        far[:PART, :] = (kept[rows, :].astype(F32) + sent[rows, :].astype(F32)).astype(BF)
        write_tail(far, PART, terms)


def near_sum_kernel(kept, sent0, sent1, through0, through1, token, near, back):
    near[:PART, :] = (kept[:PART, :].astype(F32) + sent0[...].astype(F32)).astype(BF)
    near[PART:, :] = through0[PART:, :]
    total = kept[PART:, :].astype(F32) + sent1[...].astype(F32)
    back[...] = (total + through1[:PART, :].astype(F32)).astype(BF)


def across_kernel(kept, sent, right, left, through0, through1, lse, first, second, lse_out):
    total = kept[:PART, :].astype(F32) + sent[:PART, :].astype(F32)
    total = (total + right[:PART, :].astype(F32) + left[...].astype(F32)).astype(BF)
    first[...] = total[:PIECE]
    second[:PIECE, :] = total[PIECE:]
    terms = lse[...]
    for ref in (through0, through1, right):
        terms = terms + read_tail(ref, PART)
    lse_out[...] = terms
    write_tail(second, PIECE, terms)


def sum_kernel(ids, kept, sent, right, left, back0, back1, lse, keep, send, lse_out):
    core = ids[CORE]
    total = kept[PART:2 * PART, :].astype(F32) + sent[PART:2 * PART, :].astype(F32)
    total = total + right[...].astype(F32) + left[...].astype(F32)
    back = (back0[...].astype(F32), back1[:PIECE, :].astype(F32))
    terms = lse[...] + read_tail(back1, PIECE)
    lse_out[...] = terms
    write_tail(send, PIECE, terms)

    @pl.when(core == 0)
    def _():
        keep[...] = total[:PIECE] + back[0]
        send[:PIECE, :] = (total[PIECE:] + back[1]).astype(BF)

    @pl.when(core == 1)
    def _():
        keep[...] = total[PIECE:] + back[1]
        send[:PIECE, :] = (total[:PIECE] + back[0]).astype(BF)


def grad_kernel(ids, image, text, keep, got, lse, image_out, text_out, loss_out):
    core = ids[CORE]

    def grad(values, total, out):
        x = values[...]
        norm = jnp.sqrt(jnp.sum(x * x, axis=1, keepdims=True) + 1e-06)
        unit = x / norm
        g = total[:PIECE, :].astype(F32)
        out[...] = (g - unit * jnp.sum(unit * g, axis=1, keepdims=True)) / norm

    @pl.when(core == 0)
    def _():
        grad(image, keep, image_out)
        grad(text, got, text_out)

    @pl.when(core == 1)
    def _():
        grad(image, got, image_out)
        grad(text, keep, text_out)

    terms = lse[...] + read_tail(got, PIECE)
    total = jnp.sum(jnp.sum(terms, axis=0, keepdims=True), axis=1, keepdims=True)
    loss_out[...] = total * (1.0 / (2.0 * ROWS * COLS * PIECE))


def per_device(image_embeds, text_embeds):
    here = lax.axis_index("row") * COLS + lax.axis_index("col")
    first = lax.axis_index("col") % 2 == 0

    keep, send = unit_pair(image_embeds, text_embeds)
    got = swap(send)
    here, keep = lax.optimization_barrier((here, keep))
    ids = lax.dynamic_index_in_dim(jnp.asarray(device_table()), here, keepdims=False)
    own = jnp.concatenate([jnp.where(first, keep, got), jnp.where(first, got, keep)])
    own, ids = lax.optimization_barrier((own, ids))

    other = flip(own)
    left0, right0 = ring(own, 1), ring(own, 3)
    left1, right1 = ring(other, 1), ring(other, 3)
    far_left = ring(jnp.concatenate([left0[:PIECE], left1[:PIECE]]), 1)
    far_right = ring(jnp.concatenate([right0[PIECE:], right1[PIECE:]]), 3)
    mine = [right1, left1, other, own, right0, left0]
    late, _ = lax.optimization_barrier((own, other))
    theirs = [swap(late if v is own else v) for v in mine]
    near = near_scores(ids, mine, theirs)
    far_left, far_right, near[0] = lax.optimization_barrier((far_left, far_right, near[0]))
    h_rows, h_cols, img, txt, keep, send = far_scores(
        ids, (far_left, far_right), (swap(far_left), swap(far_right)), near
    )
    sums = keep + swap(send)
    sums = group_sum(sums)
    theirs = swap(sums)

    def add(*v):
        return functools.reduce(lambda a, b: a + b, [u.astype(F32) for u in v]).astype(BF)

    def part(value, i):
        return value[i * PART:(i + 1) * PART]

    def mark(done):
        return swap(done[:16, :PIECE])

    w_rows, w_lanes, sent = far_products(ids, sums, theirs, h_rows, h_cols, img, txt)
    sent = swap(sent)
    kept = kept_far(ids, w_rows, w_lanes, img, txt)
    tailed = jax.ShapeDtypeStruct((PART + TAIL, WIDTH), BF)
    lane = jax.ShapeDtypeStruct((8, PIECE), F32)
    far0, far1, lse = pl.pallas_call(
        far_sum_kernel, out_shape=(tailed, tailed, lane), in_specs=[SM] + [VM] * 3,
        out_specs=(VM,) * 3, compiler_params=PARAMS, name="far_sums",
    )(ids, kept, sent, theirs)
    through0, through1 = ring(far0, 1), ring(far1, 3)

    w, s0, s1, kept = near_products(
        mark(far0), ids, sums, theirs, near[0], w_rows, w_lanes, img, txt
    )
    sent_on = products(4, 8, False, (), ids, w, img, txt, 1)
    near1, back1 = pl.pallas_call(
        near_sum_kernel, out_shape=(tailed, jax.ShapeDtypeStruct((PART, WIDTH), BF)),
        in_specs=[VM] * 6, out_specs=(VM, VM), compiler_params=PARAMS, name="near_sums",
    )(kept, swap(s0), swap(s1), through0, through1, sent_on)
    sent_on = swap(sent_on)
    right1, left1 = ring(near1, 1), ring(back1, 3)

    kept = products(4, 8, True, (mark(back1),), ids, w, img, txt)
    near0 = add(part(kept, 2), part(sent_on, 2), part(through0, 0))
    back0 = add(part(kept, 3), part(sent_on, 3))
    near0, back0, kept, sent_on = lax.optimization_barrier((near0, back0, kept, sent_on))
    right0, left0 = ring(near0, 1), ring(back0, 3)
    shape = jax.ShapeDtypeStruct((PIECE, WIDTH), F32)
    last0, last1, lse = pl.pallas_call(
        across_kernel,
        out_shape=(
            jax.ShapeDtypeStruct((PIECE, WIDTH), BF),
            jax.ShapeDtypeStruct((PIECE + TAIL, WIDTH), BF),
            lane,
        ),
        in_specs=[VM] * 7, out_specs=(VM, VM, VM),
        compiler_params=PARAMS, name="across_sums",
    )(kept, sent_on, right1, left1, through0, through1, lse)
    backs = flip(last0), flip(last1)
    keep, send, lse = pl.pallas_call(
        sum_kernel,
        out_shape=(shape, jax.ShapeDtypeStruct((PIECE + TAIL, WIDTH), BF), lane),
        in_specs=[SM] + [VM] * 7, out_specs=(VM, VM, VM),
        compiler_params=PARAMS, name="own_sums",
    )(ids, kept, sent_on, right0, left0, *backs, lse)
    image_grad, text_grad, loss = pl.pallas_call(
        grad_kernel,
        out_shape=(shape, shape, jax.ShapeDtypeStruct((1, 1), F32)),
        in_specs=[SM] + [VM] * 5, out_specs=(VM, VM, VM),
        compiler_params=PARAMS, name="grad_rows",
    )(ids, image_embeds, text_embeds, keep, swap(send), lse)
    loss = loss[0, 0]
    return (image_grad, text_grad, loss)


def solution(mesh):
    return jax.shard_map(
        per_device,
        mesh=mesh,
        in_specs=(P(("row", "col"), None), P(("col", "row"), None)),
        out_specs=(P(("row", "col"), None), P(("col", "row"), None), P()),
        check_vma=False,
    )
```

```python
import functools
import math

import jax
import jax.numpy as jnp
import numpy as np
from jax import lax
from jax.experimental import pallas as pl
from jax.experimental.pallas import tpu as pltpu
from jax.sharding import PartitionSpec as P

PIECE = 128
PART = 2 * PIECE
WIDTH = 1280
RING = 4
PART_AT = ((2, 0), (2, 1), (1, 1), (3, 1), (0, 1), (0, 0), (1, 0), (3, 0))
PARTS = len(PART_AT)
FAR = 2
ROWS, COLS = 8, 16
IMG = PARTS * PART
TXT = PARTS * PIECE
FAR_IMG, FAR_TXT = FAR * PART, FAR * PIECE
NEAR_IMG, NEAR_TXT = IMG - FAR_IMG, TXT - FAR_TXT
CORE, TXT_AT, MATCH_AT = 40, 32, 16
TAIL = 16
PRODUCT_FLOPS = 5 * 10**10

SHIFT = 22.0
LIFT = 70.0
FLOOR = math.exp(-62.0)
LOG2E = math.log2(math.e)

VM = pl.BlockSpec(memory_space=pltpu.VMEM)
SM = pl.BlockSpec(memory_space=pltpu.SMEM)
PARAMS = pltpu.CompilerParams(vmem_limit_bytes=8 * 1024 * 1024)
F32, BF = jnp.float32, jnp.bfloat16
NT = (((1,), (1,)), ((), ()))
NN = (((1,), (0,)), ((), ()))
TN = (((0,), (0,)), ((), ()))
AXES = ("row", "col")


def dot(a, b, dims):
    return lax.dot_general(a, b, dims, preferred_element_type=F32)


def device(yl, z, x, yh, k):
    return (yl * 4 + z) * COLS + (x * 2 + yh) * 2 + k


def places():
    return [
        (yl, z, x, yh, k)
        for yl in range(2) for z in range(RING) for x in range(RING) for yh in range(2) for k in range(2)
    ]


def neighbour(y, k):
    return y ^ 1 if k == 0 else (y + (1 if y % 2 else 3)) % RING


def group(value, d, side):
    pairs = []
    for yl, z, x, yh, k in places():
        y = yh * 2 + yl
        y = neighbour(y, k) if side else y
        target = device(y % 2, (z + d * k) % RING, (x + d * (1 - k)) % RING, y // 2, k)
        pairs.append((device(yl, z, x, yh, k), target))
    return lax.ppermute(value, AXES, pairs)


def ring(value, d):
    return group(value, d, 0)


def flip(value):
    return group(value, 0, 1)


def group_sum(value):
    value = value + ring(value, 1) + ring(value, 2) + ring(value, 3)
    return value + flip(value)


def swap(value):
    return lax.ppermute(value, AXES, [
        (device(yl, z, x, yh, k), device(yl, z, x, yh, 1 - k)) for yl, z, x, yh, k in places()
    ])


def device_table():
    table = np.zeros((ROWS * COLS, 41), np.int32)
    for yl, z, x, yh, k in places():
        y = yh * 2 + yl
        img, match, txt, owned = [], [], [], []
        for d, side in PART_AT:
            zt, yt = (z + d) % RING, neighbour(y, 1) if side else y
            txt.append(zt * 2 + (yt + 1) % 2)
            owner = device(yt % 2, zt, x, yt // 2, k)
            owned.append(owner % COLS * ROWS + owner // COLS)
        for d, side in PART_AT:
            xi, yi = (x + d) % RING, neighbour(y, 0) if side else y
            for h in range(2):
                img.append((xi * 2 + yi % 2) * 2 + h)
                piece = device(yi % 2, z, xi, yi // 2, h)
                match.append(owned.index(piece) if piece in owned else -1)
        table[device(yl, z, x, yh, k)] = img + match + txt + [k]
    return table


def cost(flops, bytes_accessed):
    return pl.CostEstimate(flops=flops, bytes_accessed=bytes_accessed, transcendentals=0)


def diagonal():
    shape = (PIECE, PIECE)
    return lax.broadcasted_iota(jnp.int32, shape, 0) == lax.broadcasted_iota(jnp.int32, shape, 1)


def unit_kernel(image_ref, text_ref, keep_ref, send_ref):
    core = lax.axis_index("col") % 2

    def unit(src):
        x = src[...]
        return (x / jnp.sqrt(jnp.sum(x * x, axis=1, keepdims=True) + 1e-06)).astype(BF)

    image, text = unit(image_ref), unit(text_ref)

    @pl.when(core == 0)
    def _():
        keep_ref[...] = image
        send_ref[...] = text

    @pl.when(core == 1)
    def _():
        keep_ref[...] = text
        send_ref[...] = image


def unit_pair(image, text):
    shape = jax.ShapeDtypeStruct((PIECE, WIDTH), BF)
    return pl.pallas_call(
        unit_kernel, out_shape=(shape, shape), in_specs=[VM, VM], out_specs=(VM, VM),
        compiler_params=PARAMS, name="unit_rows",
    )(image, text)


def place_parts(core, here, there, img, txt):
    @pl.when(core == 0)
    def _():
        for m, (mine, other) in enumerate(zip(here, there)):
            img[m * PART:(m + 1) * PART, :] = mine[...]
            txt[m * PIECE:(m + 1) * PIECE, :] = other[:PIECE, :]

    @pl.when(core == 1)
    def _():
        for m, (mine, other) in enumerate(zip(here, there)):
            img[m * PART:(m + 1) * PART, :] = other[...]
            txt[m * PIECE:(m + 1) * PIECE, :] = mine[PIECE:, :]


def score_tiles(tiles, img, txt, held, racc, cacc):
    def epilogue(t):
        row, rows, col, h_out, h_row, h_col = tiles[t]
        cols = slice(col, col + 256)
        total = jnp.zeros((8, 256), F32)
        for p in range(0, rows, PIECE):
            d = held[t % 2][p:p + PIECE, :]
            h = jnp.exp2(d * (50.0 * LOG2E) - (0.5 * SHIFT * LOG2E))
            h_out[h_row + p:h_row + p + PIECE, h_col:h_col + 256] = h
            q = h * h
            racc[row + p:row + p + PIECE, :] += q[:, :PIECE] + q[:, PIECE:]
            total += jnp.sum(q.reshape(16, 8, 256), axis=0)
        cacc[:, cols] += total

    for t, (row, rows, col, *_) in enumerate(tiles):
        held[t % 2][:rows, :] = dot(img[row:row + rows, :], txt[col:col + 256, :], NT)
        if t:
            epilogue(t - 1)
    epilogue(len(tiles) - 1)


def near_kernel(ids, *refs):
    count = PARTS - FAR
    here, there = refs[:count], refs[count:2 * count]
    h_out, img, txt, racc, cacc, even, odd = refs[2 * count:]
    place_parts(ids[CORE], here, there, img, txt)
    racc[...] = jnp.zeros_like(racc)
    cacc[...] = jnp.zeros_like(cacc)
    half = NEAR_IMG // 2
    tiles = [(r, half, c, h_out, r, c) for c in range(0, NEAR_TXT, 256) for r in (0, half)]
    score_tiles(tiles, img, txt, (even, odd), racc, cacc)


def near_scores(ids, here, there):
    return list(pl.pallas_call(
        near_kernel,
        out_shape=(
            jax.ShapeDtypeStruct((NEAR_IMG, NEAR_TXT), F32),
            jax.ShapeDtypeStruct((NEAR_IMG, WIDTH), BF),
            jax.ShapeDtypeStruct((NEAR_TXT, WIDTH), BF),
            jax.ShapeDtypeStruct((NEAR_IMG, PIECE), F32),
            jax.ShapeDtypeStruct((8, NEAR_TXT), F32),
        ),
        in_specs=[SM] + [VM] * (2 * len(here)),
        out_specs=(VM,) * 5,
        scratch_shapes=[pltpu.VMEM((NEAR_IMG // 2, 256), F32)] * 2,
        compiler_params=PARAMS,
        cost_estimate=cost(1, 1),
        name="near_scores",
    )(ids, *here, *there))


def far_kernel(ids, left, right, there_left, there_right, near, near_img, near_txt, near_racc,
               near_cacc, h_rows, h_cols, img, txt, keep, send, even, odd, racc, cacc, rs, cs, dg):
    core = ids[CORE]

    def place(halves, text):
        for i in range(FAR):
            for k, half in enumerate(halves):
                at = i * PART + k * PIECE
                img[at:at + PIECE, :] = half[i * PIECE:(i + 1) * PIECE, :]
        txt[:FAR_TXT, :] = text[...]

    pl.when(core == 0)(lambda: place((left, right), there_left))
    pl.when(core == 1)(lambda: place((there_left, there_right), right))
    img[FAR_IMG:, :] = near_img[...]
    txt[FAR_TXT:, :] = near_txt[...]
    racc[:FAR_IMG, :] = jnp.zeros((FAR_IMG, PIECE), F32)
    racc[FAR_IMG:, :] = near_racc[...]
    cacc[:, :FAR_TXT] = jnp.zeros((8, FAR_TXT), F32)
    cacc[:, FAR_TXT:] = near_cacc[...]
    for ref in (rs, cs, dg, keep, send):
        ref[...] = jnp.zeros_like(ref)
    half = NEAR_IMG // 2
    tiles = [(FAR_IMG + r, half, 0, h_cols, r, 0) for r in (0, half)]
    tiles += [(0, FAR_IMG, c, h_rows, 0, c) for c in range(0, TXT, 256)]
    score_tiles(tiles, img, txt, (even, odd), racc, cacc)

    lowest = jnp.full((1, PIECE), jnp.inf, F32)
    for p in range(COLS):
        part = jnp.sum(racc[p * PIECE:(p + 1) * PIECE, :].T, axis=0, keepdims=True)
        rs[0, pl.ds(ids[p], 1), :] = part
        lowest = jnp.minimum(lowest, part)
    total = jnp.sum(cacc[...], axis=0, keepdims=True)
    for m in range(PARTS):
        part = total[:, m * PIECE:(m + 1) * PIECE]
        cs[0, pl.ds(ids[TXT_AT + m], 1), :] = part
        lowest = jnp.minimum(lowest, part)

    def half_of(p, m):
        at = p * PIECE if p < 2 * FAR else (p - 2 * FAR) * PIECE
        if p < 2 * FAR:
            return h_rows[at:at + PIECE, m * PIECE:(m + 1) * PIECE]
        if m < FAR:
            return h_cols[at:at + PIECE, m * PIECE:(m + 1) * PIECE]
        return near[at:at + PIECE, (m - FAR) * PIECE:(m - FAR + 1) * PIECE]

    @pl.when(jnp.min(lowest) < FLOOR)
    def _():
        for p in range(COLS):
            part = jnp.zeros((PIECE, PIECE), F32)
            for m in range(PARTS):
                g = half_of(p, m) * math.exp(0.5 * (SHIFT + LIFT))
                part += g * g
                cs[1, pl.ds(ids[TXT_AT + m], 1), :] += jnp.sum(g * g, axis=0, keepdims=True)
            rs[1, pl.ds(ids[p], 1), :] = jnp.sum(part.T, axis=0, keepdims=True)

    for p in range(COLS):
        match = ids[MATCH_AT + p]

        @pl.when(match >= 0)
        def _():
            other = txt[pl.ds(pl.multiple_of(match * PIECE, PIECE), PIECE), :]
            s = 100.0 * dot(img[p * PIECE:(p + 1) * PIECE, :], other, NT)
            dg[...] += jnp.sum(jnp.where(diagonal(), s, 0.0).reshape(16, 8, PIECE), axis=0)

    @pl.when(core == 0)
    def _():
        keep[0:2] = rs[...]
        keep[2, 0:8] = dg[...]
        send[0:2, 0:8] = cs[...]

    @pl.when(core == 1)
    def _():
        send[0:2] = rs[...]
        send[2, 0:8] = dg[...]
        keep[0:2, 8:16] = cs[...]


def far_scores(ids, here, there, near):
    sums = jax.ShapeDtypeStruct((3, COLS, PIECE), F32)
    return pl.pallas_call(
        far_kernel,
        out_shape=(
            jax.ShapeDtypeStruct((FAR_IMG, TXT), F32),
            jax.ShapeDtypeStruct((NEAR_IMG, FAR_TXT), F32),
            jax.ShapeDtypeStruct((IMG, WIDTH), BF),
            jax.ShapeDtypeStruct((TXT, WIDTH), BF),
            sums, sums,
        ),
        in_specs=[SM] + [VM] * 9,
        out_specs=(VM,) * 6,
        scratch_shapes=[
            pltpu.VMEM((NEAR_IMG // 2, 256), F32),
            pltpu.VMEM((NEAR_IMG // 2, 256), F32),
            pltpu.VMEM((IMG, PIECE), F32),
            pltpu.VMEM((8, TXT), F32),
            pltpu.VMEM((2, COLS, PIECE), F32),
            pltpu.VMEM((2, ROWS, PIECE), F32),
            pltpu.VMEM((8, PIECE), F32),
        ],
        compiler_params=PARAMS,
        cost_estimate=cost(2 * (IMG * TXT - NEAR_IMG * NEAR_TXT) * WIDTH, 16 << 20),
        name="far_scores",
    )(ids, *here, *there, *near)


def lse_of(sums):
    return jnp.where(sums[0] >= FLOOR, SHIFT + jnp.log(sums[0]), jnp.log(sums[1]) - LIFT)


def row_col_factors(core, own, far, a_s, b_s):
    scale = math.sqrt(0.5)
    factors = [scale * jnp.exp(0.5 * (SHIFT - lse_of(v))) for v in (own, far)]
    a_s[...] = jnp.where(core == 0, factors[0], factors[1])
    b_s[...] = jnp.where(core == 0, factors[1][:8], factors[0][8:])


def weights_block(ids, half, w, row, col, a_s, b_s, p0, p1, m0, m1):
    b = [b_s[pl.ds(ids[TXT_AT + m], 1), :] for m in range(m0, m1)]

    @pl.loop(p0, p1)
    def _(p):
        rows = pl.ds(pl.multiple_of((p - p0) * PIECE, PIECE), PIECE)
        to = pl.ds(pl.multiple_of((p - p0) * PIECE + row, PIECE), PIECE)
        a = jnp.broadcast_to(a_s[pl.ds(ids[p], 1), :], (PIECE, PIECE)).T
        for m in range(m1 - m0):
            h = half[rows, m * PIECE:(m + 1) * PIECE]
            v, t = h * a, h * b[m]
            w[to, col + m * PIECE:col + (m + 1) * PIECE] = (v * v + t * t).astype(BF)
        match = ids[MATCH_AT + p]

        @pl.when((match >= m0) & (match < m1))
        def _():
            at = pl.multiple_of((match - m0) * PIECE, PIECE)
            h = half[rows, pl.ds(at, PIECE)]
            v, t = h * a, h * b_s[pl.ds(ids[TXT_AT + match], 1), :]
            cols = pl.ds(pl.multiple_of(at + col, PIECE), PIECE)
            w[to, cols] = (v * v + t * t - diagonal().astype(F32)).astype(BF)


def product_kernel(kept_here, core, w_rows, w_lanes, img, txt, out):
    def image_side():
        w, where = w_rows
        for n in range(WIDTH // 256):
            cols = slice(n * 256, n * 256 + 256)
            out[:, cols] = dot(w[where, :], txt[:, cols], NN).astype(BF)

    def text_side():
        at, pad = (PIECE, 0) if kept_here else (0, PIECE)
        w, where = w_lanes
        d = dot(w[:, where], img[...], TN).astype(BF)
        for i in range(d.shape[0] // PIECE):
            out[i * PART + at:i * PART + at + PIECE, :] = d[i * PIECE:(i + 1) * PIECE]
            out[i * PART + pad:i * PART + pad + PIECE, :] = jnp.zeros((PIECE, WIDTH), BF)

    pl.when(core == (0 if kept_here else 1))(image_side)
    pl.when(core == (1 if kept_here else 0))(text_side)


def parts_of(w, start, end):
    return (w, slice(start * PART, end * PART)), (w, slice(start * PIECE, end * PIECE))


FACTORS = [pltpu.VMEM((COLS, PIECE), F32), pltpu.VMEM((ROWS, PIECE), F32)]


def far_products(ids, own, far, h_rows, h_cols, img, txt):
    def kernel(ids, own, far, h_rows, h_cols, img, txt, w_rows, w_lanes, out, a_s, b_s):
        row_col_factors(ids[CORE], own, far, a_s, b_s)
        weights_block(ids, h_rows, w_rows, 0, 0, a_s, b_s, 0, 2 * FAR, 0, PARTS)
        weights_block(ids, h_cols, w_lanes, FAR_IMG, 0, a_s, b_s, 2 * FAR, COLS, 0, FAR)
        w_lanes[:FAR_IMG, :] = w_rows[:, :FAR_TXT]
        product_kernel(
            False, ids[CORE], (w_rows, slice(None)), (w_lanes, slice(None)), img, txt, out
        )

    return pl.pallas_call(
        kernel,
        out_shape=(
            jax.ShapeDtypeStruct((FAR_IMG, TXT), BF),
            jax.ShapeDtypeStruct((IMG, FAR_TXT), BF),
            jax.ShapeDtypeStruct((FAR * PART, WIDTH), BF),
        ),
        in_specs=[SM] + [VM] * 6,
        out_specs=(VM,) * 3,
        scratch_shapes=FACTORS,
        compiler_params=PARAMS,
        cost_estimate=cost(PRODUCT_FLOPS, 1),
        name="far_products",
    )(ids, own, far, h_rows, h_cols, img, txt)


def near_products(token, ids, own, far, near, w_rows, w_lanes, img, txt):
    def kernel(token, ids, own, far, near, w_rows, w_lanes, img, txt, w, s0, s1, out, a_s, b_s,
               sent):
        row_col_factors(ids[CORE], own, far, a_s, b_s)
        w[:FAR_IMG, :] = w_rows[...]
        w[FAR_IMG:, :FAR_TXT] = w_lanes[FAR_IMG:, :]
        weights_block(ids, near, w, FAR_IMG, FAR_TXT, a_s, b_s, 2 * FAR, COLS, FAR, PARTS)
        parts = parts_of(w, FAR, FAR + 2)
        product_kernel(False, ids[CORE], *parts, img, txt, sent)
        s0[...] = sent[:PART, :]
        s1[...] = sent[PART:, :]
        product_kernel(True, ids[CORE], *parts, img, txt, out)

    part = jax.ShapeDtypeStruct((PART, WIDTH), BF)
    return pl.pallas_call(
        kernel,
        out_shape=(
            jax.ShapeDtypeStruct((IMG, TXT), BF),
            part, part,
            jax.ShapeDtypeStruct((2 * PART, WIDTH), BF),
        ),
        in_specs=[VM, SM] + [VM] * 7,
        out_specs=(VM,) * 4,
        scratch_shapes=[*FACTORS, pltpu.VMEM((2 * PART, WIDTH), BF)],
        compiler_params=PARAMS,
        cost_estimate=cost(PRODUCT_FLOPS, 1),
        name="near_products",
    )(token, ids, own, far, near, w_rows, w_lanes, img, txt)


def kept_far(ids, w_rows, w_lanes, img, txt, sums):
    def kernel(ids, w_rows, w_lanes, img, txt, sums, out, tail, lse_out):
        terms = lse_of(sums[...])
        terms = terms[:8] + terms[8:]
        terms = terms - jnp.where(ids[CORE] == 0, 0.0, 2.0) * sums[2, :8]
        lse_out[...] = terms
        write_tail(tail, 0, terms)
        product_kernel(
            True, ids[CORE], (w_rows, slice(None)), (w_lanes, slice(None)), img, txt, out
        )

    return pl.pallas_call(
        kernel,
        out_shape=(
            jax.ShapeDtypeStruct((FAR * PART, WIDTH), BF),
            jax.ShapeDtypeStruct((TAIL, WIDTH), BF),
            jax.ShapeDtypeStruct((8, PIECE), F32),
        ),
        in_specs=[SM] + [VM] * 5,
        out_specs=(VM,) * 3,
        compiler_params=PARAMS,
        cost_estimate=cost(PRODUCT_FLOPS, 1),
        name="far_kept",
    )(ids, w_rows, w_lanes, img, txt, sums)


def products(start, end, kept_here, tokens, ids, w, img, txt, flops=PRODUCT_FLOPS):
    def kernel(ids, img, txt, w, *refs):
        product_kernel(kept_here, ids[CORE], *parts_of(w, start, end), img, txt, refs[-1])

    return pl.pallas_call(
        kernel,
        out_shape=jax.ShapeDtypeStruct(((end - start) * PART, WIDTH), BF),
        in_specs=[SM] + [VM] * (3 + len(tokens)),
        out_specs=VM,
        compiler_params=PARAMS,
        cost_estimate=cost(flops, 1),
        name="products_kept" if kept_here else "products_sent",
    )(ids, img, txt, w, *tokens)


def read_tail(ref, at):
    rows = ref[at:at + TAIL, :3 * PIECE].astype(F32)[:8]
    return sum(rows[:, i * PIECE:(i + 1) * PIECE] for i in range(3))


def write_tail(ref, at, terms):
    ref[at:at + TAIL, :] = jnp.zeros((TAIL, WIDTH), BF)
    pad = jnp.zeros((TAIL - 8, PIECE), F32)
    for i in range(3):
        piece = terms.astype(BF).astype(F32)
        ref[at:at + TAIL, i * PIECE:(i + 1) * PIECE] = jnp.concatenate([piece, pad]).astype(BF)
        terms = terms - piece


def far_sum_kernel(kept, sent, tail, far0, far1):
    for i, far in enumerate((far0, far1)):
        rows = slice(i * PART, (i + 1) * PART)
        far[:PART, :] = (kept[rows, :].astype(F32) + sent[rows, :].astype(F32)).astype(BF)
        far[PART:, :] = tail[...]


def near_sum_kernel(kept, sent0, sent1, through0, through1, near, back):
    near[:PART, :] = (kept[:PART, :].astype(F32) + sent0[...].astype(F32)).astype(BF)
    near[PART:, :] = through0[PART:, :]
    total = kept[PART:, :].astype(F32) + sent1[...].astype(F32)
    back[...] = (total + through1[:PART, :].astype(F32)).astype(BF)


def across_kernel(kept, sent, right, left, through0, through1, lse, first, second, lse_out):
    total = kept[:PART, :].astype(F32) + sent[:PART, :].astype(F32)
    total = (total + right[:PART, :].astype(F32) + left[...].astype(F32)).astype(BF)
    first[...] = total[:PIECE]
    second[:PIECE, :] = total[PIECE:]
    terms = lse[...]
    for ref in (through0, through1, right):
        terms = terms + read_tail(ref, PART)
    lse_out[...] = terms
    write_tail(second, PIECE, terms)


def sum_kernel(ids, kept, sent, right, left, back0, back1, lse, keep, send, lse_out):
    core = ids[CORE]
    total = kept[PART:2 * PART, :].astype(F32) + sent[PART:2 * PART, :].astype(F32)
    total = total + right[...].astype(F32) + left[...].astype(F32)
    back = (back0[...].astype(F32), back1[:PIECE, :].astype(F32))
    terms = lse[...] + read_tail(back1, PIECE)
    lse_out[...] = terms
    write_tail(send, PIECE, terms)

    @pl.when(core == 0)
    def _():
        keep[...] = total[:PIECE] + back[0]
        send[:PIECE, :] = (total[PIECE:] + back[1]).astype(BF)

    @pl.when(core == 1)
    def _():
        keep[...] = total[PIECE:] + back[1]
        send[:PIECE, :] = (total[:PIECE] + back[0]).astype(BF)


def grad_kernel(ids, image, text, keep, got, lse, image_out, text_out, loss_out):
    core = ids[CORE]

    def grad(values, total, out):
        x = values[...]
        norm = jnp.sqrt(jnp.sum(x * x, axis=1, keepdims=True) + 1e-06)
        unit = x / norm
        g = total[:PIECE, :].astype(F32)
        out[...] = (g - unit * jnp.sum(unit * g, axis=1, keepdims=True)) / norm

    @pl.when(core == 0)
    def _():
        grad(image, keep, image_out)
        grad(text, got, text_out)

    @pl.when(core == 1)
    def _():
        grad(image, got, image_out)
        grad(text, keep, text_out)

    terms = lse[...] + read_tail(got, PIECE)
    total = jnp.sum(jnp.sum(terms, axis=0, keepdims=True), axis=1, keepdims=True)
    loss_out[...] = total * (1.0 / (2.0 * ROWS * COLS * PIECE))


def per_device(image_embeds, text_embeds):
    here = lax.axis_index("row") * COLS + lax.axis_index("col")
    first = lax.axis_index("col") % 2 == 0

    keep, send = unit_pair(image_embeds, text_embeds)
    got = swap(send)
    here, keep = lax.optimization_barrier((here, keep))
    ids = lax.dynamic_index_in_dim(jnp.asarray(device_table()), here, keepdims=False)
    own = jnp.concatenate([jnp.where(first, keep, got), jnp.where(first, got, keep)])
    own, ids = lax.optimization_barrier((own, ids))

    other = flip(own)
    left0, right0 = ring(own, 1), ring(own, 3)
    left1, right1 = ring(other, 1), ring(other, 3)
    far_left = ring(jnp.concatenate([left0[:PIECE], left1[:PIECE]]), 1)
    far_right = ring(jnp.concatenate([right0[PIECE:], right1[PIECE:]]), 3)
    mine = [right1, left1, other, own, right0, left0]
    late, _ = lax.optimization_barrier((own, other))
    theirs = [swap(late if v is own else v) for v in mine]
    near = near_scores(ids, mine, theirs)
    far_right, near[0] = lax.optimization_barrier((far_right, near[0]))
    there_right = swap(far_right)
    far_left, there_right = lax.optimization_barrier((far_left, there_right))
    h_rows, h_cols, img, txt, keep, send = far_scores(
        ids, (far_left, far_right), (swap(far_left), there_right), near
    )
    sums = keep + swap(send)
    sums = group_sum(sums)
    theirs = swap(sums)

    def add(*v):
        return functools.reduce(lambda a, b: a + b, [u.astype(F32) for u in v]).astype(BF)

    def part(value, i):
        return value[i * PART:(i + 1) * PART]

    def mark(done):
        return swap(done[:16, :PIECE])

    w_rows, w_lanes, sent = far_products(ids, sums, theirs, h_rows, h_cols, img, txt)
    sent = swap(sent)
    kept, tail, lse = kept_far(ids, w_rows, w_lanes, img, txt, theirs)
    tailed = jax.ShapeDtypeStruct((PART + TAIL, WIDTH), BF)
    lane = jax.ShapeDtypeStruct((8, PIECE), F32)
    far0, far1 = pl.pallas_call(
        far_sum_kernel, out_shape=(tailed, tailed), in_specs=[VM] * 3,
        out_specs=(VM, VM), compiler_params=PARAMS, name="far_sums",
    )(kept, sent, tail)
    through0, through1 = ring(far0, 1), ring(far1, 3)

    w, s0, s1, kept = near_products(
        mark(far0), ids, sums, theirs, near[0], w_rows, w_lanes, img, txt
    )
    near1, back1 = pl.pallas_call(
        near_sum_kernel, out_shape=(tailed, jax.ShapeDtypeStruct((PART, WIDTH), BF)),
        in_specs=[VM] * 5, out_specs=(VM, VM), compiler_params=PARAMS, name="near_sums",
    )(kept, swap(s0), swap(s1), through0, through1)
    right1, left1 = ring(near1, 1), ring(back1, 3)

    token = mark(back1)
    sent_on = swap(products(4, 8, False, (token,), ids, w, img, txt))
    kept = products(4, 8, True, (token,), ids, w, img, txt)
    near0 = add(part(kept, 2), part(sent_on, 2), part(through0, 0))
    back0 = add(part(kept, 3), part(sent_on, 3))
    near0, back0, kept, sent_on = lax.optimization_barrier((near0, back0, kept, sent_on))
    right0, left0 = ring(near0, 1), ring(back0, 3)
    shape = jax.ShapeDtypeStruct((PIECE, WIDTH), F32)
    last0, last1, lse = pl.pallas_call(
        across_kernel,
        out_shape=(
            jax.ShapeDtypeStruct((PIECE, WIDTH), BF),
            jax.ShapeDtypeStruct((PIECE + TAIL, WIDTH), BF),
            lane,
        ),
        in_specs=[VM] * 7, out_specs=(VM, VM, VM),
        compiler_params=PARAMS, name="across_sums",
    )(kept, sent_on, right1, left1, through0, through1, lse)
    backs = flip(last0), flip(last1)
    keep, send, lse = pl.pallas_call(
        sum_kernel,
        out_shape=(shape, jax.ShapeDtypeStruct((PIECE + TAIL, WIDTH), BF), lane),
        in_specs=[SM] + [VM] * 7, out_specs=(VM, VM, VM),
        compiler_params=PARAMS, name="own_sums",
    )(ids, kept, sent_on, right0, left0, *backs, lse)
    image_grad, text_grad, loss = pl.pallas_call(
        grad_kernel,
        out_shape=(shape, shape, jax.ShapeDtypeStruct((1, 1), F32)),
        in_specs=[SM] + [VM] * 5, out_specs=(VM, VM, VM),
        compiler_params=PARAMS, name="grad_rows",
    )(ids, image_embeds, text_embeds, keep, swap(send), lse)
    loss = loss[0, 0]
    return (image_grad, text_grad, loss)


def solution(mesh):
    return jax.shard_map(
        per_device,
        mesh=mesh,
        in_specs=(P(("row", "col"), None), P(("col", "row"), None)),
        out_specs=(P(("row", "col"), None), P(("col", "row"), None), P()),
        check_vma=False,
    )
```

```python
import functools
import math

import jax
import jax.numpy as jnp
import numpy as np
from jax import lax
from jax.experimental import pallas as pl
from jax.experimental.pallas import tpu as pltpu
from jax.sharding import PartitionSpec as P

PIECE = 128
PART = 2 * PIECE
WIDTH = 1280
RING = 4
PART_AT = ((2, 0), (2, 1), (1, 1), (3, 1), (0, 1), (0, 0), (1, 0), (3, 0))
PARTS = len(PART_AT)
FAR = 2
ROWS, COLS = 8, 16
IMG = PARTS * PART
TXT = PARTS * PIECE
FAR_IMG, FAR_TXT = FAR * PART, FAR * PIECE
NEAR_IMG, NEAR_TXT = IMG - FAR_IMG, TXT - FAR_TXT
CORE, TXT_AT, MATCH_AT = 40, 32, 16
TAIL = 16
PRODUCT_FLOPS = 5 * 10**10

SHIFT = 22.0
LIFT = 70.0
FLOOR = math.exp(-62.0)
LOG2E = math.log2(math.e)

VM = pl.BlockSpec(memory_space=pltpu.VMEM)
SM = pl.BlockSpec(memory_space=pltpu.SMEM)
PARAMS = pltpu.CompilerParams(vmem_limit_bytes=8 * 1024 * 1024)
F32, BF = jnp.float32, jnp.bfloat16
NT = (((1,), (1,)), ((), ()))
NN = (((1,), (0,)), ((), ()))
TN = (((0,), (0,)), ((), ()))
AXES = ("row", "col")


def dot(a, b, dims):
    return lax.dot_general(a, b, dims, preferred_element_type=F32)


def device(yl, z, x, yh, k):
    return (yl * 4 + z) * COLS + (x * 2 + yh) * 2 + k


def places():
    return [
        (yl, z, x, yh, k)
        for yl in range(2) for z in range(RING) for x in range(RING) for yh in range(2) for k in range(2)
    ]


def neighbour(y, k):
    return y ^ 1 if k == 0 else (y + (1 if y % 2 else 3)) % RING


def group(value, d, side):
    pairs = []
    for yl, z, x, yh, k in places():
        y = yh * 2 + yl
        y = neighbour(y, k) if side else y
        target = device(y % 2, (z + d * k) % RING, (x + d * (1 - k)) % RING, y // 2, k)
        pairs.append((device(yl, z, x, yh, k), target))
    return lax.ppermute(value, AXES, pairs)


def ring(value, d):
    return group(value, d, 0)


def flip(value):
    return group(value, 0, 1)


def group_sum(value):
    value = value + ring(value, 1) + ring(value, 2) + ring(value, 3)
    return value + flip(value)


def swap(value):
    return lax.ppermute(value, AXES, [
        (device(yl, z, x, yh, k), device(yl, z, x, yh, 1 - k)) for yl, z, x, yh, k in places()
    ])


def device_table():
    table = np.zeros((ROWS * COLS, 41), np.int32)
    for yl, z, x, yh, k in places():
        y = yh * 2 + yl
        img, match, txt, owned = [], [], [], []
        for d, side in PART_AT:
            zt, yt = (z + d) % RING, neighbour(y, 1) if side else y
            txt.append(zt * 2 + (yt + 1) % 2)
            owner = device(yt % 2, zt, x, yt // 2, k)
            owned.append(owner % COLS * ROWS + owner // COLS)
        for d, side in PART_AT:
            xi, yi = (x + d) % RING, neighbour(y, 0) if side else y
            for h in range(2):
                img.append((xi * 2 + yi % 2) * 2 + h)
                piece = device(yi % 2, z, xi, yi // 2, h)
                match.append(owned.index(piece) if piece in owned else -1)
        table[device(yl, z, x, yh, k)] = img + match + txt + [k]
    return table


def cost(flops, bytes_accessed):
    return pl.CostEstimate(flops=flops, bytes_accessed=bytes_accessed, transcendentals=0)


def diagonal():
    shape = (PIECE, PIECE)
    return lax.broadcasted_iota(jnp.int32, shape, 0) == lax.broadcasted_iota(jnp.int32, shape, 1)


def unit_kernel(image_ref, text_ref, keep_ref, send_ref):
    core = lax.axis_index("col") % 2

    def unit(src):
        x = src[...]
        return (x / jnp.sqrt(jnp.sum(x * x, axis=1, keepdims=True) + 1e-06)).astype(BF)

    image, text = unit(image_ref), unit(text_ref)

    @pl.when(core == 0)
    def _():
        keep_ref[...] = image
        send_ref[...] = text

    @pl.when(core == 1)
    def _():
        keep_ref[...] = text
        send_ref[...] = image


def unit_pair(image, text):
    shape = jax.ShapeDtypeStruct((PIECE, WIDTH), BF)
    return pl.pallas_call(
        unit_kernel, out_shape=(shape, shape), in_specs=[VM, VM], out_specs=(VM, VM),
        compiler_params=PARAMS, name="unit_rows",
    )(image, text)


def place_parts(core, here, there, img, txt):
    @pl.when(core == 0)
    def _():
        for m, (mine, other) in enumerate(zip(here, there)):
            img[m * PART:(m + 1) * PART, :] = mine[...]
            txt[m * PIECE:(m + 1) * PIECE, :] = other[:PIECE, :]

    @pl.when(core == 1)
    def _():
        for m, (mine, other) in enumerate(zip(here, there)):
            img[m * PART:(m + 1) * PART, :] = other[...]
            txt[m * PIECE:(m + 1) * PIECE, :] = mine[PIECE:, :]


def score_tiles(tiles, img, txt, held, racc, cacc):
    def epilogue(t):
        row, rows, col, h_out, h_row, h_col = tiles[t]
        cols = slice(col, col + 256)
        total = jnp.zeros((8, 256), F32)
        for p in range(0, rows, PIECE):
            d = held[t % 2][p:p + PIECE, :]
            h = jnp.exp2(d * (50.0 * LOG2E) - (0.5 * SHIFT * LOG2E))
            h_out[h_row + p:h_row + p + PIECE, h_col:h_col + 256] = h
            q = h * h
            racc[row + p:row + p + PIECE, :] += q[:, :PIECE] + q[:, PIECE:]
            total += jnp.sum(q.reshape(16, 8, 256), axis=0)
        cacc[:, cols] += total

    for t, (row, rows, col, *_) in enumerate(tiles):
        held[t % 2][:rows, :] = dot(img[row:row + rows, :], txt[col:col + 256, :], NT)
        if t:
            epilogue(t - 1)
    epilogue(len(tiles) - 1)


def near_kernel(ids, *refs):
    count = PARTS - FAR
    here, there = refs[:count], refs[count:2 * count]
    h_out, img, txt, racc, cacc, even, odd = refs[2 * count:]
    place_parts(ids[CORE], here, there, img, txt)
    racc[...] = jnp.zeros_like(racc)
    cacc[...] = jnp.zeros_like(cacc)
    half = NEAR_IMG // 2
    tiles = [(r, half, c, h_out, r, c) for c in range(0, NEAR_TXT, 256) for r in (0, half)]
    score_tiles(tiles, img, txt, (even, odd), racc, cacc)


def near_scores(ids, here, there):
    return list(pl.pallas_call(
        near_kernel,
        out_shape=(
            jax.ShapeDtypeStruct((NEAR_IMG, NEAR_TXT), F32),
            jax.ShapeDtypeStruct((NEAR_IMG, WIDTH), BF),
            jax.ShapeDtypeStruct((NEAR_TXT, WIDTH), BF),
            jax.ShapeDtypeStruct((NEAR_IMG, PIECE), F32),
            jax.ShapeDtypeStruct((8, NEAR_TXT), F32),
        ),
        in_specs=[SM] + [VM] * (2 * len(here)),
        out_specs=(VM,) * 5,
        scratch_shapes=[pltpu.VMEM((NEAR_IMG // 2, 256), F32)] * 2,
        compiler_params=PARAMS,
        cost_estimate=cost(1, 1),
        name="near_scores",
    )(ids, *here, *there))


def far_kernel(ids, left, right, there_left, there_right, near, near_img, near_txt, near_racc,
               near_cacc, h_rows, h_cols, img, txt, keep, send, even, odd, racc, cacc, rs, cs, dg):
    core = ids[CORE]

    def place(halves, text):
        for i in range(FAR):
            for k, half in enumerate(halves):
                at = i * PART + k * PIECE
                img[at:at + PIECE, :] = half[i * PIECE:(i + 1) * PIECE, :]
        txt[:FAR_TXT, :] = text[...]

    pl.when(core == 0)(lambda: place((left, right), there_left))
    pl.when(core == 1)(lambda: place((there_left, there_right), right))
    img[FAR_IMG:, :] = near_img[...]
    txt[FAR_TXT:, :] = near_txt[...]
    racc[:FAR_IMG, :] = jnp.zeros((FAR_IMG, PIECE), F32)
    racc[FAR_IMG:, :] = near_racc[...]
    cacc[:, :FAR_TXT] = jnp.zeros((8, FAR_TXT), F32)
    cacc[:, FAR_TXT:] = near_cacc[...]
    for ref in (rs, cs, dg, keep, send):
        ref[...] = jnp.zeros_like(ref)
    half = NEAR_IMG // 2
    tiles = [(FAR_IMG + r, half, 0, h_cols, r, 0) for r in (0, half)]
    tiles += [(0, FAR_IMG, c, h_rows, 0, c) for c in range(0, TXT, 256)]
    score_tiles(tiles, img, txt, (even, odd), racc, cacc)

    lowest = jnp.full((1, PIECE), jnp.inf, F32)
    for p in range(COLS):
        part = jnp.sum(racc[p * PIECE:(p + 1) * PIECE, :].T, axis=0, keepdims=True)
        rs[0, pl.ds(ids[p], 1), :] = part
        lowest = jnp.minimum(lowest, part)
    total = jnp.sum(cacc[...], axis=0, keepdims=True)
    for m in range(PARTS):
        part = total[:, m * PIECE:(m + 1) * PIECE]
        cs[0, pl.ds(ids[TXT_AT + m], 1), :] = part
        lowest = jnp.minimum(lowest, part)

    def half_of(p, m):
        at = p * PIECE if p < 2 * FAR else (p - 2 * FAR) * PIECE
        if p < 2 * FAR:
            return h_rows[at:at + PIECE, m * PIECE:(m + 1) * PIECE]
        if m < FAR:
            return h_cols[at:at + PIECE, m * PIECE:(m + 1) * PIECE]
        return near[at:at + PIECE, (m - FAR) * PIECE:(m - FAR + 1) * PIECE]

    @pl.when(jnp.min(lowest) < FLOOR)
    def _():
        for p in range(COLS):
            part = jnp.zeros((PIECE, PIECE), F32)
            for m in range(PARTS):
                g = half_of(p, m) * math.exp(0.5 * (SHIFT + LIFT))
                part += g * g
                cs[1, pl.ds(ids[TXT_AT + m], 1), :] += jnp.sum(g * g, axis=0, keepdims=True)
            rs[1, pl.ds(ids[p], 1), :] = jnp.sum(part.T, axis=0, keepdims=True)

    for p in range(COLS):
        match = ids[MATCH_AT + p]

        @pl.when(match >= 0)
        def _():
            other = txt[pl.ds(pl.multiple_of(match * PIECE, PIECE), PIECE), :]
            s = 100.0 * dot(img[p * PIECE:(p + 1) * PIECE, :], other, NT)
            dg[...] += jnp.sum(jnp.where(diagonal(), s, 0.0).reshape(16, 8, PIECE), axis=0)

    @pl.when(core == 0)
    def _():
        keep[0:2] = rs[...]
        keep[2, 0:8] = dg[...]
        send[0:2, 0:8] = cs[...]

    @pl.when(core == 1)
    def _():
        send[0:2] = rs[...]
        send[2, 0:8] = dg[...]
        keep[0:2, 8:16] = cs[...]


def far_scores(ids, here, there, near):
    sums = jax.ShapeDtypeStruct((3, COLS, PIECE), F32)
    return pl.pallas_call(
        far_kernel,
        out_shape=(
            jax.ShapeDtypeStruct((FAR_IMG, TXT), F32),
            jax.ShapeDtypeStruct((NEAR_IMG, FAR_TXT), F32),
            jax.ShapeDtypeStruct((IMG, WIDTH), BF),
            jax.ShapeDtypeStruct((TXT, WIDTH), BF),
            sums, sums,
        ),
        in_specs=[SM] + [VM] * 9,
        out_specs=(VM,) * 6,
        scratch_shapes=[
            pltpu.VMEM((NEAR_IMG // 2, 256), F32),
            pltpu.VMEM((NEAR_IMG // 2, 256), F32),
            pltpu.VMEM((IMG, PIECE), F32),
            pltpu.VMEM((8, TXT), F32),
            pltpu.VMEM((2, COLS, PIECE), F32),
            pltpu.VMEM((2, ROWS, PIECE), F32),
            pltpu.VMEM((8, PIECE), F32),
        ],
        compiler_params=PARAMS,
        cost_estimate=cost(2 * (IMG * TXT - NEAR_IMG * NEAR_TXT) * WIDTH, 16 << 20),
        name="far_scores",
    )(ids, *here, *there, *near)


def lse_of(sums):
    return jnp.where(sums[0] >= FLOOR, SHIFT + jnp.log(sums[0]), jnp.log(sums[1]) - LIFT)


def row_col_factors(core, own, far, a_s, b_s):
    scale = math.sqrt(0.5)
    factors = [scale * jnp.exp(0.5 * (SHIFT - lse_of(v))) for v in (own, far)]
    a_s[...] = jnp.where(core == 0, factors[0], factors[1])
    b_s[...] = jnp.where(core == 0, factors[1][:8], factors[0][8:])


def weights_block(ids, half, w, row, col, a_s, b_s, p0, p1, m0, m1):
    b = [b_s[pl.ds(ids[TXT_AT + m], 1), :] for m in range(m0, m1)]

    @pl.loop(p0, p1)
    def _(p):
        rows = pl.ds(pl.multiple_of((p - p0) * PIECE, PIECE), PIECE)
        to = pl.ds(pl.multiple_of((p - p0) * PIECE + row, PIECE), PIECE)
        a = jnp.broadcast_to(a_s[pl.ds(ids[p], 1), :], (PIECE, PIECE)).T
        for m in range(m1 - m0):
            h = half[rows, m * PIECE:(m + 1) * PIECE]
            v, t = h * a, h * b[m]
            w[to, col + m * PIECE:col + (m + 1) * PIECE] = (v * v + t * t).astype(BF)
        match = ids[MATCH_AT + p]

        @pl.when((match >= m0) & (match < m1))
        def _():
            at = pl.multiple_of((match - m0) * PIECE, PIECE)
            h = half[rows, pl.ds(at, PIECE)]
            v, t = h * a, h * b_s[pl.ds(ids[TXT_AT + match], 1), :]
            cols = pl.ds(pl.multiple_of(at + col, PIECE), PIECE)
            w[to, cols] = (v * v + t * t - diagonal().astype(F32)).astype(BF)


def product_kernel(kept_here, core, w_rows, w_lanes, img, txt, out):
    def image_side():
        w, where = w_rows
        for n in range(WIDTH // 256):
            cols = slice(n * 256, n * 256 + 256)
            out[:, cols] = dot(w[where, :], txt[:, cols], NN).astype(BF)

    def text_side():
        at, pad = (PIECE, 0) if kept_here else (0, PIECE)
        w, where = w_lanes
        d = dot(w[:, where], img[...], TN).astype(BF)
        for i in range(d.shape[0] // PIECE):
            out[i * PART + at:i * PART + at + PIECE, :] = d[i * PIECE:(i + 1) * PIECE]
            out[i * PART + pad:i * PART + pad + PIECE, :] = jnp.zeros((PIECE, WIDTH), BF)

    pl.when(core == (0 if kept_here else 1))(image_side)
    pl.when(core == (1 if kept_here else 0))(text_side)


def parts_of(w, start, end):
    return (w, slice(start * PART, end * PART)), (w, slice(start * PIECE, end * PIECE))


FACTORS = [pltpu.VMEM((COLS, PIECE), F32), pltpu.VMEM((ROWS, PIECE), F32)]


def far_products(ids, own, far, h_rows, h_cols, img, txt):
    def kernel(ids, own, far, h_rows, h_cols, img, txt, w_rows, w_lanes, out, a_s, b_s):
        row_col_factors(ids[CORE], own, far, a_s, b_s)
        weights_block(ids, h_rows, w_rows, 0, 0, a_s, b_s, 0, 2 * FAR, 0, PARTS)
        weights_block(ids, h_cols, w_lanes, FAR_IMG, 0, a_s, b_s, 2 * FAR, COLS, 0, FAR)
        w_lanes[:FAR_IMG, :] = w_rows[:, :FAR_TXT]
        product_kernel(
            False, ids[CORE], (w_rows, slice(None)), (w_lanes, slice(None)), img, txt, out
        )

    return pl.pallas_call(
        kernel,
        out_shape=(
            jax.ShapeDtypeStruct((FAR_IMG, TXT), BF),
            jax.ShapeDtypeStruct((IMG, FAR_TXT), BF),
            jax.ShapeDtypeStruct((FAR * PART, WIDTH), BF),
        ),
        in_specs=[SM] + [VM] * 6,
        out_specs=(VM,) * 3,
        scratch_shapes=FACTORS,
        compiler_params=PARAMS,
        cost_estimate=cost(PRODUCT_FLOPS, 1),
        name="far_products",
    )(ids, own, far, h_rows, h_cols, img, txt)


def near_products(token, ids, own, far, near, w_rows, w_lanes, img, txt):
    def kernel(token, ids, own, far, near, w_rows, w_lanes, img, txt, w, s0, s1, out, a_s, b_s,
               sent):
        row_col_factors(ids[CORE], own, far, a_s, b_s)
        w[:FAR_IMG, :] = w_rows[...]
        w[FAR_IMG:, :FAR_TXT] = w_lanes[FAR_IMG:, :]
        weights_block(ids, near, w, FAR_IMG, FAR_TXT, a_s, b_s, 2 * FAR, COLS, FAR, PARTS)
        parts = parts_of(w, FAR, FAR + 2)
        product_kernel(False, ids[CORE], *parts, img, txt, sent)
        s0[...] = sent[:PART, :]
        s1[...] = sent[PART:, :]
        product_kernel(True, ids[CORE], *parts, img, txt, out)

    part = jax.ShapeDtypeStruct((PART, WIDTH), BF)
    return pl.pallas_call(
        kernel,
        out_shape=(
            jax.ShapeDtypeStruct((IMG, TXT), BF),
            part, part,
            jax.ShapeDtypeStruct((2 * PART, WIDTH), BF),
        ),
        in_specs=[VM, SM] + [VM] * 7,
        out_specs=(VM,) * 4,
        scratch_shapes=[*FACTORS, pltpu.VMEM((2 * PART, WIDTH), BF)],
        compiler_params=PARAMS,
        cost_estimate=cost(PRODUCT_FLOPS, 1),
        name="near_products",
    )(token, ids, own, far, near, w_rows, w_lanes, img, txt)


def kept_far(ids, w_rows, w_lanes, img, txt, sums):
    def kernel(ids, w_rows, w_lanes, img, txt, sums, out, tail, lse_out):
        terms = lse_of(sums[...])
        terms = terms[:8] + terms[8:]
        terms = terms - jnp.where(ids[CORE] == 0, 0.0, 2.0) * sums[2, :8]
        lse_out[...] = terms
        write_tail(tail, 0, terms)
        product_kernel(
            True, ids[CORE], (w_rows, slice(None)), (w_lanes, slice(None)), img, txt, out
        )

    return pl.pallas_call(
        kernel,
        out_shape=(
            jax.ShapeDtypeStruct((FAR * PART, WIDTH), BF),
            jax.ShapeDtypeStruct((TAIL, WIDTH), BF),
            jax.ShapeDtypeStruct((8, PIECE), F32),
        ),
        in_specs=[SM] + [VM] * 5,
        out_specs=(VM,) * 3,
        compiler_params=PARAMS,
        cost_estimate=cost(PRODUCT_FLOPS, 1),
        name="far_kept",
    )(ids, w_rows, w_lanes, img, txt, sums)


def last_sent(token, ids, w, img, txt):
    def kernel(ids, img, txt, w, token, first, second, out):
        product_kernel(False, ids[CORE], *parts_of(w, 4, 8), img, txt, out)
        first[...] = out[:2 * PART, :]
        second[...] = out[2 * PART:, :]

    half = jax.ShapeDtypeStruct((2 * PART, WIDTH), BF)
    return pl.pallas_call(
        kernel,
        out_shape=(half, half),
        in_specs=[SM] + [VM] * 4,
        out_specs=(VM, VM),
        scratch_shapes=[pltpu.VMEM((4 * PART, WIDTH), BF)],
        compiler_params=PARAMS,
        cost_estimate=cost(PRODUCT_FLOPS, 1),
        name="last_sent",
    )(ids, img, txt, w, token)


def last_kept(token, ids, w, img, txt):
    def kernel(ids, img, txt, w, token, out):
        product_kernel(True, ids[CORE], *parts_of(w, 4, 8), img, txt, out)

    return pl.pallas_call(
        kernel,
        out_shape=jax.ShapeDtypeStruct((4 * PART, WIDTH), BF),
        in_specs=[SM] + [VM] * 4,
        out_specs=VM,
        compiler_params=PARAMS,
        cost_estimate=cost(PRODUCT_FLOPS, 1),
        name="last_kept",
    )(ids, img, txt, w, token)


def read_tail(ref, at):
    rows = ref[at:at + TAIL, :3 * PIECE].astype(F32)[:8]
    return sum(rows[:, i * PIECE:(i + 1) * PIECE] for i in range(3))


def write_tail(ref, at, terms):
    ref[at:at + TAIL, :] = jnp.zeros((TAIL, WIDTH), BF)
    pad = jnp.zeros((TAIL - 8, PIECE), F32)
    for i in range(3):
        piece = terms.astype(BF).astype(F32)
        ref[at:at + TAIL, i * PIECE:(i + 1) * PIECE] = jnp.concatenate([piece, pad]).astype(BF)
        terms = terms - piece


def far_sum_kernel(kept, sent, tail, far0, far1):
    for i, far in enumerate((far0, far1)):
        rows = slice(i * PART, (i + 1) * PART)
        far[:PART, :] = (kept[rows, :].astype(F32) + sent[rows, :].astype(F32)).astype(BF)
        far[PART:, :] = tail[...]


def near_sum_kernel(kept, sent0, sent1, through0, through1, near, back):
    near[:PART, :] = (kept[:PART, :].astype(F32) + sent0[...].astype(F32)).astype(BF)
    near[PART:, :] = through0[PART:, :]
    total = kept[PART:, :].astype(F32) + sent1[...].astype(F32)
    back[...] = (total + through1[:PART, :].astype(F32)).astype(BF)


def across_kernel(kept, sent, right, left, through0, through1, lse, first, second, lse_out):
    total = kept[:PART, :].astype(F32) + sent[:PART, :].astype(F32)
    total = (total + right[:PART, :].astype(F32) + left[...].astype(F32)).astype(BF)
    first[...] = total[:PIECE]
    second[:PIECE, :] = total[PIECE:]
    terms = lse[...]
    for ref in (through0, through1, right):
        terms = terms + read_tail(ref, PART)
    lse_out[...] = terms
    write_tail(second, PIECE, terms)


def sum_kernel(ids, kept, sent, right, left, back0, back1, lse, keep, send, lse_out):
    core = ids[CORE]
    total = kept[PART:2 * PART, :].astype(F32) + sent[PART:2 * PART, :].astype(F32)
    total = total + right[...].astype(F32) + left[...].astype(F32)
    back = (back0[...].astype(F32), back1[:PIECE, :].astype(F32))
    terms = lse[...] + read_tail(back1, PIECE)
    lse_out[...] = terms
    write_tail(send, PIECE, terms)

    @pl.when(core == 0)
    def _():
        keep[...] = total[:PIECE] + back[0]
        send[:PIECE, :] = (total[PIECE:] + back[1]).astype(BF)

    @pl.when(core == 1)
    def _():
        keep[...] = total[PIECE:] + back[1]
        send[:PIECE, :] = (total[:PIECE] + back[0]).astype(BF)


def gradient(values, total):
    x = values[...]
    norm = jnp.sqrt(jnp.sum(x * x, axis=1, keepdims=True) + 1e-06)
    unit = x / norm
    return (total - unit * jnp.sum(unit * total, axis=1, keepdims=True)) / norm


def kept_grad_kernel(ids, image, text, keep, out):
    total = keep[...]

    @pl.when(ids[CORE] == 0)
    def _():
        out[...] = gradient(image, total)

    @pl.when(ids[CORE] == 1)
    def _():
        out[...] = gradient(text, total)


def grad_kernel(ids, image, text, kept, got, lse, image_out, text_out, loss_out, other, sems):
    def put(own_out, other_out, values):
        first = pltpu.make_async_copy(kept, own_out, sems.at[0])
        first.start()
        other[...] = gradient(values, got[:PIECE, :].astype(F32))
        second = pltpu.make_async_copy(other, other_out, sems.at[1])
        second.start()
        first.wait()
        second.wait()

    pl.when(ids[CORE] == 0)(lambda: put(image_out, text_out, text))
    pl.when(ids[CORE] == 1)(lambda: put(text_out, image_out, image))
    terms = lse[...] + read_tail(got, PIECE)
    total = jnp.sum(jnp.sum(terms, axis=0, keepdims=True), axis=1, keepdims=True)
    loss_out[...] = total * (1.0 / (2.0 * ROWS * COLS * PIECE))


def per_device(image_embeds, text_embeds):
    here = lax.axis_index("row") * COLS + lax.axis_index("col")
    first = lax.axis_index("col") % 2 == 0

    keep, send = unit_pair(image_embeds, text_embeds)
    got = swap(send)
    here, keep = lax.optimization_barrier((here, keep))
    ids = lax.dynamic_index_in_dim(jnp.asarray(device_table()), here, keepdims=False)
    own = jnp.concatenate([jnp.where(first, keep, got), jnp.where(first, got, keep)])
    own, ids = lax.optimization_barrier((own, ids))

    other = flip(own)
    left0, right0 = ring(own, 1), ring(own, 3)
    left1, right1 = ring(other, 1), ring(other, 3)
    far_left = ring(jnp.concatenate([left0[:PIECE], left1[:PIECE]]), 1)
    far_right = ring(jnp.concatenate([right0[PIECE:], right1[PIECE:]]), 3)
    mine = [right1, left1, other, own, right0, left0]
    late, _ = lax.optimization_barrier((own, other))
    theirs = [swap(late if v is own else v) for v in mine]
    near = near_scores(ids, mine, theirs)
    far_right, near[0] = lax.optimization_barrier((far_right, near[0]))
    there_right = swap(far_right)
    far_left, there_right = lax.optimization_barrier((far_left, there_right))
    h_rows, h_cols, img, txt, keep, send = far_scores(
        ids, (far_left, far_right), (swap(far_left), there_right), near
    )
    sums = keep + swap(send)
    sums = group_sum(sums)
    theirs = swap(sums)

    def add(*v):
        return functools.reduce(lambda a, b: a + b, [u.astype(F32) for u in v]).astype(BF)

    def part(value, i):
        return value[i * PART:(i + 1) * PART]

    def mark(done):
        return swap(done[:16, :PIECE])

    w_rows, w_lanes, sent = far_products(ids, sums, theirs, h_rows, h_cols, img, txt)
    sent = swap(sent)
    kept, tail, lse = kept_far(ids, w_rows, w_lanes, img, txt, theirs)
    tailed = jax.ShapeDtypeStruct((PART + TAIL, WIDTH), BF)
    lane = jax.ShapeDtypeStruct((8, PIECE), F32)
    far0, far1 = pl.pallas_call(
        far_sum_kernel, out_shape=(tailed, tailed), in_specs=[VM] * 3,
        out_specs=(VM, VM), compiler_params=PARAMS, name="far_sums",
    )(kept, sent, tail)
    through0, through1 = ring(far0, 1), ring(far1, 3)

    w, s0, s1, kept = near_products(
        mark(far0), ids, sums, theirs, near[0], w_rows, w_lanes, img, txt
    )
    near1, back1 = pl.pallas_call(
        near_sum_kernel, out_shape=(tailed, jax.ShapeDtypeStruct((PART, WIDTH), BF)),
        in_specs=[VM] * 5, out_specs=(VM, VM), compiler_params=PARAMS, name="near_sums",
    )(kept, swap(s0), swap(s1), through0, through1)
    right1, left1 = ring(near1, 1), ring(back1, 3)

    token = mark(back1)
    sent_own, sent_near = last_sent(token, ids, w, img, txt)
    sent_near, sent_own = swap(sent_near), swap(sent_own)
    kept = last_kept(token, ids, w, img, txt)
    near0 = add(part(kept, 2), part(sent_near, 0), part(through0, 0))
    back0 = add(part(kept, 3), part(sent_near, 1))
    near0, back0, kept = lax.optimization_barrier((near0, back0, kept))
    right0, left0 = ring(near0, 1), ring(back0, 3)
    shape = jax.ShapeDtypeStruct((PIECE, WIDTH), F32)
    last0, last1, lse = pl.pallas_call(
        across_kernel,
        out_shape=(
            jax.ShapeDtypeStruct((PIECE, WIDTH), BF),
            jax.ShapeDtypeStruct((PIECE + TAIL, WIDTH), BF),
            lane,
        ),
        in_specs=[VM] * 7, out_specs=(VM, VM, VM),
        compiler_params=PARAMS, name="across_sums",
    )(kept, sent_own, right1, left1, through0, through1, lse)
    backs = flip(last0), flip(last1)
    keep, send, lse = pl.pallas_call(
        sum_kernel,
        out_shape=(shape, jax.ShapeDtypeStruct((PIECE + TAIL, WIDTH), BF), lane),
        in_specs=[SM] + [VM] * 7, out_specs=(VM, VM, VM),
        compiler_params=PARAMS, name="own_sums",
    )(ids, kept, sent_own, right0, left0, *backs, lse)
    kept = pl.pallas_call(
        kept_grad_kernel, out_shape=shape, in_specs=[SM] + [VM] * 3, out_specs=VM,
        compiler_params=PARAMS, name="kept_grad",
    )(ids, image_embeds, text_embeds, keep)
    anywhere = pl.BlockSpec(memory_space=pl.ANY)
    image_grad, text_grad, loss = pl.pallas_call(
        grad_kernel,
        out_shape=(shape, shape, jax.ShapeDtypeStruct((1, 1), F32)),
        in_specs=[SM] + [VM] * 5, out_specs=(anywhere, anywhere, VM),
        scratch_shapes=[pltpu.VMEM((PIECE, WIDTH), F32), pltpu.SemaphoreType.DMA((2,))],
        compiler_params=PARAMS, name="grad_rows",
    )(ids, image_embeds, text_embeds, kept, swap(send), lse)
    loss = loss[0, 0]
    return (image_grad, text_grad, loss)


def solution(mesh):
    return jax.shard_map(
        per_device,
        mesh=mesh,
        in_specs=(P(("row", "col"), None), P(("col", "row"), None)),
        out_specs=(P(("row", "col"), None), P(("col", "row"), None), P()),
        check_vma=False,
    )
```

```python
import functools
import math

import jax
import jax.numpy as jnp
import numpy as np
from jax import lax
from jax.experimental import pallas as pl
from jax.experimental.pallas import tpu as pltpu
from jax.sharding import PartitionSpec as P

PIECE = 128
PART = 2 * PIECE
WIDTH = 1280
RING = 4
PART_AT = ((2, 0), (2, 1), (1, 1), (3, 1), (0, 1), (0, 0), (1, 0), (3, 0))
PARTS = len(PART_AT)
FAR = 2
ROWS, COLS = 8, 16
IMG = PARTS * PART
TXT = PARTS * PIECE
FAR_IMG, FAR_TXT = FAR * PART, FAR * PIECE
NEAR_IMG, NEAR_TXT = IMG - FAR_IMG, TXT - FAR_TXT
CORE, TXT_AT, MATCH_AT = 40, 32, 16
TAIL = 16
PRODUCT_FLOPS = 5 * 10**10

SHIFT = 22.0
LIFT = 70.0
FLOOR = math.exp(-62.0)
LOG2E = math.log2(math.e)

VM = pl.BlockSpec(memory_space=pltpu.VMEM)
SM = pl.BlockSpec(memory_space=pltpu.SMEM)
PARAMS = pltpu.CompilerParams(vmem_limit_bytes=8 * 1024 * 1024)
F32, BF = jnp.float32, jnp.bfloat16
NT = (((1,), (1,)), ((), ()))
NN = (((1,), (0,)), ((), ()))
TN = (((0,), (0,)), ((), ()))
AXES = ("row", "col")


def dot(a, b, dims):
    return lax.dot_general(a, b, dims, preferred_element_type=F32)


def device(yl, z, x, yh, k):
    return (yl * 4 + z) * COLS + (x * 2 + yh) * 2 + k


def places():
    return [
        (yl, z, x, yh, k)
        for yl in range(2) for z in range(RING) for x in range(RING) for yh in range(2) for k in range(2)
    ]


def neighbour(y, k):
    return y ^ 1 if k == 0 else (y + (1 if y % 2 else 3)) % RING


def group(value, d, side):
    pairs = []
    for yl, z, x, yh, k in places():
        y = yh * 2 + yl
        y = neighbour(y, k) if side else y
        target = device(y % 2, (z + d * k) % RING, (x + d * (1 - k)) % RING, y // 2, k)
        pairs.append((device(yl, z, x, yh, k), target))
    return lax.ppermute(value, AXES, pairs)


def ring(value, d):
    return group(value, d, 0)


def flip(value):
    return group(value, 0, 1)


def group_sum(value):
    value = value + ring(value, 1) + ring(value, 2) + ring(value, 3)
    return value + flip(value)


def swap(value):
    return lax.ppermute(value, AXES, [
        (device(yl, z, x, yh, k), device(yl, z, x, yh, 1 - k)) for yl, z, x, yh, k in places()
    ])


def device_table():
    table = np.zeros((ROWS * COLS, 41), np.int32)
    for yl, z, x, yh, k in places():
        y = yh * 2 + yl
        img, match, txt, owned = [], [], [], []
        for d, side in PART_AT:
            zt, yt = (z + d) % RING, neighbour(y, 1) if side else y
            txt.append(zt * 2 + (yt + 1) % 2)
            owner = device(yt % 2, zt, x, yt // 2, k)
            owned.append(owner % COLS * ROWS + owner // COLS)
        for d, side in PART_AT:
            xi, yi = (x + d) % RING, neighbour(y, 0) if side else y
            for h in range(2):
                img.append((xi * 2 + yi % 2) * 2 + h)
                piece = device(yi % 2, z, xi, yi // 2, h)
                match.append(owned.index(piece) if piece in owned else -1)
        table[device(yl, z, x, yh, k)] = img + match + txt + [k]
    return table


def cost(flops, bytes_accessed):
    return pl.CostEstimate(flops=flops, bytes_accessed=bytes_accessed, transcendentals=0)


def diagonal():
    shape = (PIECE, PIECE)
    return lax.broadcasted_iota(jnp.int32, shape, 0) == lax.broadcasted_iota(jnp.int32, shape, 1)


def unit_kernel(image_ref, text_ref, keep_ref, send_ref):
    core = lax.axis_index("col") % 2

    def unit(src):
        x = src[...]
        return (x / jnp.sqrt(jnp.sum(x * x, axis=1, keepdims=True) + 1e-06)).astype(BF)

    image, text = unit(image_ref), unit(text_ref)

    @pl.when(core == 0)
    def _():
        keep_ref[...] = image
        send_ref[...] = text

    @pl.when(core == 1)
    def _():
        keep_ref[...] = text
        send_ref[...] = image


def unit_pair(image, text):
    shape = jax.ShapeDtypeStruct((PIECE, WIDTH), BF)
    return pl.pallas_call(
        unit_kernel, out_shape=(shape, shape), in_specs=[VM, VM], out_specs=(VM, VM),
        compiler_params=PARAMS, name="unit_rows",
    )(image, text)


def place_parts(core, here, there, img, txt):
    @pl.when(core == 0)
    def _():
        for m, (mine, other) in enumerate(zip(here, there)):
            img[m * PART:(m + 1) * PART, :] = mine[...]
            txt[m * PIECE:(m + 1) * PIECE, :] = other[:PIECE, :]

    @pl.when(core == 1)
    def _():
        for m, (mine, other) in enumerate(zip(here, there)):
            img[m * PART:(m + 1) * PART, :] = other[...]
            txt[m * PIECE:(m + 1) * PIECE, :] = mine[PIECE:, :]


def score_tiles(tiles, img, txt, held, racc, cacc):
    def epilogue(t):
        row, rows, col, h_out, h_row, h_col = tiles[t]
        cols = slice(col, col + 256)
        total = jnp.zeros((8, 256), F32)
        for p in range(0, rows, PIECE):
            d = held[t % 2][p:p + PIECE, :]
            h = jnp.exp2(d * (50.0 * LOG2E) - (0.5 * SHIFT * LOG2E))
            h_out[h_row + p:h_row + p + PIECE, h_col:h_col + 256] = h
            q = h * h
            racc[row + p:row + p + PIECE, :] += q[:, :PIECE] + q[:, PIECE:]
            total += jnp.sum(q.reshape(16, 8, 256), axis=0)
        cacc[:, cols] += total

    for t, (row, rows, col, *_) in enumerate(tiles):
        held[t % 2][:rows, :] = dot(img[row:row + rows, :], txt[col:col + 256, :], NT)
        if t:
            epilogue(t - 1)
    epilogue(len(tiles) - 1)


def near_kernel(ids, *refs):
    count = PARTS - FAR
    here, there = refs[:count], refs[count:2 * count]
    h_out, img, txt, racc, cacc, even, odd = refs[2 * count:]
    place_parts(ids[CORE], here, there, img, txt)
    racc[...] = jnp.zeros_like(racc)
    cacc[...] = jnp.zeros_like(cacc)
    half = NEAR_IMG // 2
    tiles = [(r, half, c, h_out, r, c) for c in range(0, NEAR_TXT, 256) for r in (0, half)]
    score_tiles(tiles, img, txt, (even, odd), racc, cacc)


def near_scores(ids, here, there):
    return list(pl.pallas_call(
        near_kernel,
        out_shape=(
            jax.ShapeDtypeStruct((NEAR_IMG, NEAR_TXT), F32),
            jax.ShapeDtypeStruct((NEAR_IMG, WIDTH), BF),
            jax.ShapeDtypeStruct((NEAR_TXT, WIDTH), BF),
            jax.ShapeDtypeStruct((NEAR_IMG, PIECE), F32),
            jax.ShapeDtypeStruct((8, NEAR_TXT), F32),
        ),
        in_specs=[SM] + [VM] * (2 * len(here)),
        out_specs=(VM,) * 5,
        scratch_shapes=[pltpu.VMEM((NEAR_IMG // 2, 256), F32)] * 2,
        compiler_params=PARAMS,
        cost_estimate=cost(1, 1),
        name="near_scores",
    )(ids, *here, *there))


def far_kernel(ids, left, right, there_left, there_right, near, near_img, near_txt, near_racc,
               near_cacc, h_rows, h_cols, img, txt, keep, send, even, odd, racc, cacc, rs, cs, dg):
    core = ids[CORE]

    def place(halves, text):
        for i in range(FAR):
            for k, half in enumerate(halves):
                at = i * PART + k * PIECE
                img[at:at + PIECE, :] = half[i * PIECE:(i + 1) * PIECE, :]
        txt[:FAR_TXT, :] = text[...]

    pl.when(core == 0)(lambda: place((left, right), there_left))
    pl.when(core == 1)(lambda: place((there_left, there_right), right))
    img[FAR_IMG:, :] = near_img[...]
    txt[FAR_TXT:, :] = near_txt[...]
    racc[:FAR_IMG, :] = jnp.zeros((FAR_IMG, PIECE), F32)
    racc[FAR_IMG:, :] = near_racc[...]
    cacc[:, :FAR_TXT] = jnp.zeros((8, FAR_TXT), F32)
    cacc[:, FAR_TXT:] = near_cacc[...]
    for ref in (rs, cs, dg, keep, send):
        ref[...] = jnp.zeros_like(ref)
    half = NEAR_IMG // 2
    tiles = [(FAR_IMG + r, half, 0, h_cols, r, 0) for r in (0, half)]
    tiles += [(0, FAR_IMG, c, h_rows, 0, c) for c in range(0, TXT, 256)]
    score_tiles(tiles, img, txt, (even, odd), racc, cacc)

    lowest = jnp.full((1, PIECE), jnp.inf, F32)
    for p in range(COLS):
        part = jnp.sum(racc[p * PIECE:(p + 1) * PIECE, :].T, axis=0, keepdims=True)
        rs[0, pl.ds(ids[p], 1), :] = part
        lowest = jnp.minimum(lowest, part)
    total = jnp.sum(cacc[...], axis=0, keepdims=True)
    for m in range(PARTS):
        part = total[:, m * PIECE:(m + 1) * PIECE]
        cs[0, pl.ds(ids[TXT_AT + m], 1), :] = part
        lowest = jnp.minimum(lowest, part)

    def half_of(p, m):
        at = p * PIECE if p < 2 * FAR else (p - 2 * FAR) * PIECE
        if p < 2 * FAR:
            return h_rows[at:at + PIECE, m * PIECE:(m + 1) * PIECE]
        if m < FAR:
            return h_cols[at:at + PIECE, m * PIECE:(m + 1) * PIECE]
        return near[at:at + PIECE, (m - FAR) * PIECE:(m - FAR + 1) * PIECE]

    @pl.when(jnp.min(lowest) < FLOOR)
    def _():
        for p in range(COLS):
            part = jnp.zeros((PIECE, PIECE), F32)
            for m in range(PARTS):
                g = half_of(p, m) * math.exp(0.5 * (SHIFT + LIFT))
                part += g * g
                cs[1, pl.ds(ids[TXT_AT + m], 1), :] += jnp.sum(g * g, axis=0, keepdims=True)
            rs[1, pl.ds(ids[p], 1), :] = jnp.sum(part.T, axis=0, keepdims=True)

    for p in range(COLS):
        match = ids[MATCH_AT + p]

        @pl.when(match >= 0)
        def _():
            other = txt[pl.ds(pl.multiple_of(match * PIECE, PIECE), PIECE), :]
            s = 100.0 * dot(img[p * PIECE:(p + 1) * PIECE, :], other, NT)
            dg[...] += jnp.sum(jnp.where(diagonal(), s, 0.0).reshape(16, 8, PIECE), axis=0)

    @pl.when(core == 0)
    def _():
        keep[0:2] = rs[...]
        keep[2, 0:8] = dg[...]
        send[0:2, 0:8] = cs[...]

    @pl.when(core == 1)
    def _():
        send[0:2] = rs[...]
        send[2, 0:8] = dg[...]
        keep[0:2, 8:16] = cs[...]


def far_scores(ids, here, there, near):
    sums = jax.ShapeDtypeStruct((3, COLS, PIECE), F32)
    return pl.pallas_call(
        far_kernel,
        out_shape=(
            jax.ShapeDtypeStruct((FAR_IMG, TXT), F32),
            jax.ShapeDtypeStruct((NEAR_IMG, FAR_TXT), F32),
            jax.ShapeDtypeStruct((IMG, WIDTH), BF),
            jax.ShapeDtypeStruct((TXT, WIDTH), BF),
            sums, sums,
        ),
        in_specs=[SM] + [VM] * 9,
        out_specs=(VM,) * 6,
        scratch_shapes=[
            pltpu.VMEM((NEAR_IMG // 2, 256), F32),
            pltpu.VMEM((NEAR_IMG // 2, 256), F32),
            pltpu.VMEM((IMG, PIECE), F32),
            pltpu.VMEM((8, TXT), F32),
            pltpu.VMEM((2, COLS, PIECE), F32),
            pltpu.VMEM((2, ROWS, PIECE), F32),
            pltpu.VMEM((8, PIECE), F32),
        ],
        compiler_params=PARAMS,
        cost_estimate=cost(2 * (IMG * TXT - NEAR_IMG * NEAR_TXT) * WIDTH, 16 << 20),
        name="far_scores",
    )(ids, *here, *there, *near)


def lse_of(sums):
    return jnp.where(sums[0] >= FLOOR, SHIFT + jnp.log(sums[0]), jnp.log(sums[1]) - LIFT)


def row_col_factors(core, own, far, a_s, b_s):
    scale = math.sqrt(0.5)
    factors = [scale * jnp.exp(0.5 * (SHIFT - lse_of(v))) for v in (own, far)]
    a_s[...] = jnp.where(core == 0, factors[0], factors[1])
    b_s[...] = jnp.where(core == 0, factors[1][:8], factors[0][8:])


def weights_block(ids, half, w, row, col, a_s, b_s, p0, p1, m0, m1):
    b = [b_s[pl.ds(ids[TXT_AT + m], 1), :] for m in range(m0, m1)]

    @pl.loop(p0, p1)
    def _(p):
        rows = pl.ds(pl.multiple_of((p - p0) * PIECE, PIECE), PIECE)
        to = pl.ds(pl.multiple_of((p - p0) * PIECE + row, PIECE), PIECE)
        a = jnp.broadcast_to(a_s[pl.ds(ids[p], 1), :], (PIECE, PIECE)).T
        for m in range(m1 - m0):
            h = half[rows, m * PIECE:(m + 1) * PIECE]
            v, t = h * a, h * b[m]
            w[to, col + m * PIECE:col + (m + 1) * PIECE] = (v * v + t * t).astype(BF)
        match = ids[MATCH_AT + p]

        @pl.when((match >= m0) & (match < m1))
        def _():
            at = pl.multiple_of((match - m0) * PIECE, PIECE)
            h = half[rows, pl.ds(at, PIECE)]
            v, t = h * a, h * b_s[pl.ds(ids[TXT_AT + match], 1), :]
            cols = pl.ds(pl.multiple_of(at + col, PIECE), PIECE)
            w[to, cols] = (v * v + t * t - diagonal().astype(F32)).astype(BF)


def product_kernel(kept_here, core, w_rows, w_lanes, img, txt, out):
    def image_side():
        w, where = w_rows
        for n in range(WIDTH // 256):
            cols = slice(n * 256, n * 256 + 256)
            out[:, cols] = dot(w[where, :], txt[:, cols], NN).astype(BF)

    def text_side():
        at, pad = (PIECE, 0) if kept_here else (0, PIECE)
        w, where = w_lanes
        d = dot(w[:, where], img[...], TN).astype(BF)
        for i in range(d.shape[0] // PIECE):
            out[i * PART + at:i * PART + at + PIECE, :] = d[i * PIECE:(i + 1) * PIECE]
            out[i * PART + pad:i * PART + pad + PIECE, :] = jnp.zeros((PIECE, WIDTH), BF)

    pl.when(core == (0 if kept_here else 1))(image_side)
    pl.when(core == (1 if kept_here else 0))(text_side)


def parts_of(w, start, end):
    return (w, slice(start * PART, end * PART)), (w, slice(start * PIECE, end * PIECE))


FACTORS = [pltpu.VMEM((COLS, PIECE), F32), pltpu.VMEM((ROWS, PIECE), F32)]


def far_products(ids, own, far, h_rows, h_cols, img, txt):
    def kernel(ids, own, far, h_rows, h_cols, img, txt, w_rows, w_lanes, out, a_s, b_s):
        row_col_factors(ids[CORE], own, far, a_s, b_s)
        weights_block(ids, h_rows, w_rows, 0, 0, a_s, b_s, 0, 2 * FAR, 0, PARTS)
        weights_block(ids, h_cols, w_lanes, FAR_IMG, 0, a_s, b_s, 2 * FAR, COLS, 0, FAR)
        w_lanes[:FAR_IMG, :] = w_rows[:, :FAR_TXT]
        product_kernel(
            False, ids[CORE], (w_rows, slice(None)), (w_lanes, slice(None)), img, txt, out
        )

    return pl.pallas_call(
        kernel,
        out_shape=(
            jax.ShapeDtypeStruct((FAR_IMG, TXT), BF),
            jax.ShapeDtypeStruct((IMG, FAR_TXT), BF),
            jax.ShapeDtypeStruct((FAR * PART, WIDTH), BF),
        ),
        in_specs=[SM] + [VM] * 6,
        out_specs=(VM,) * 3,
        scratch_shapes=FACTORS,
        compiler_params=PARAMS,
        cost_estimate=cost(PRODUCT_FLOPS, 1),
        name="far_products",
    )(ids, own, far, h_rows, h_cols, img, txt)


def near_products(token, ids, own, far, near, w_rows, w_lanes, img, txt):
    def kernel(token, ids, own, far, near, w_rows, w_lanes, img, txt, w, s0, s1, a_s, b_s, sent):
        row_col_factors(ids[CORE], own, far, a_s, b_s)
        w[:FAR_IMG, :] = w_rows[...]
        w[FAR_IMG:, :FAR_TXT] = w_lanes[FAR_IMG:, :]
        weights_block(ids, near, w, FAR_IMG, FAR_TXT, a_s, b_s, 2 * FAR, COLS, FAR, PARTS)
        parts = parts_of(w, FAR, FAR + 2)
        product_kernel(False, ids[CORE], *parts, img, txt, sent)
        s0[...] = sent[:PART, :]
        s1[...] = sent[PART:, :]

    part = jax.ShapeDtypeStruct((PART, WIDTH), BF)
    return pl.pallas_call(
        kernel,
        out_shape=(
            jax.ShapeDtypeStruct((IMG, TXT), BF),
            part, part,
        ),
        in_specs=[VM, SM] + [VM] * 7,
        out_specs=(VM,) * 3,
        scratch_shapes=[*FACTORS, pltpu.VMEM((2 * PART, WIDTH), BF)],
        compiler_params=PARAMS,
        cost_estimate=cost(PRODUCT_FLOPS, 1),
        name="near_products",
    )(token, ids, own, far, near, w_rows, w_lanes, img, txt)


def kept_far(ids, w_rows, w_lanes, img, txt, sums):
    def kernel(ids, w_rows, w_lanes, img, txt, sums, out, tail, lse_out):
        terms = lse_of(sums[...])
        terms = terms[:8] + terms[8:]
        terms = terms - jnp.where(ids[CORE] == 0, 0.0, 2.0) * sums[2, :8]
        lse_out[...] = terms
        write_tail(tail, 0, terms)
        product_kernel(
            True, ids[CORE], (w_rows, slice(None)), (w_lanes, slice(None)), img, txt, out
        )

    return pl.pallas_call(
        kernel,
        out_shape=(
            jax.ShapeDtypeStruct((FAR * PART, WIDTH), BF),
            jax.ShapeDtypeStruct((TAIL, WIDTH), BF),
            jax.ShapeDtypeStruct((8, PIECE), F32),
        ),
        in_specs=[SM] + [VM] * 5,
        out_specs=(VM,) * 3,
        compiler_params=PARAMS,
        cost_estimate=cost(PRODUCT_FLOPS, 1),
        name="far_kept",
    )(ids, w_rows, w_lanes, img, txt, sums)


def last_sent(token, ids, w, img, txt):
    def kernel(ids, img, txt, w, token, first, second, out):
        product_kernel(False, ids[CORE], *parts_of(w, 4, 8), img, txt, out)
        first[...] = out[:2 * PART, :]
        second[...] = out[2 * PART:, :]

    half = jax.ShapeDtypeStruct((2 * PART, WIDTH), BF)
    return pl.pallas_call(
        kernel,
        out_shape=(half, half),
        in_specs=[SM] + [VM] * 4,
        out_specs=(VM, VM),
        scratch_shapes=[pltpu.VMEM((4 * PART, WIDTH), BF)],
        compiler_params=PARAMS,
        cost_estimate=cost(PRODUCT_FLOPS, 1),
        name="last_sent",
    )(ids, img, txt, w, token)


def kept_products(start, end, tokens, flops, ids, w, img, txt):
    def kernel(ids, img, txt, w, *refs):
        product_kernel(True, ids[CORE], *parts_of(w, start, end), img, txt, refs[-1])

    return pl.pallas_call(
        kernel,
        out_shape=jax.ShapeDtypeStruct(((end - start) * PART, WIDTH), BF),
        in_specs=[SM] + [VM] * (3 + len(tokens)),
        out_specs=VM,
        compiler_params=PARAMS,
        cost_estimate=cost(flops, 1),
        name="products_kept",
    )(ids, img, txt, w, *tokens)


def read_tail(ref, at):
    rows = ref[at:at + TAIL, :3 * PIECE].astype(F32)[:8]
    return sum(rows[:, i * PIECE:(i + 1) * PIECE] for i in range(3))


def write_tail(ref, at, terms):
    ref[at:at + TAIL, :] = jnp.zeros((TAIL, WIDTH), BF)
    pad = jnp.zeros((TAIL - 8, PIECE), F32)
    for i in range(3):
        piece = terms.astype(BF).astype(F32)
        ref[at:at + TAIL, i * PIECE:(i + 1) * PIECE] = jnp.concatenate([piece, pad]).astype(BF)
        terms = terms - piece


def far_sum_kernel(kept, sent, tail, far0, far1):
    for i, far in enumerate((far0, far1)):
        rows = slice(i * PART, (i + 1) * PART)
        far[:PART, :] = (kept[rows, :].astype(F32) + sent[rows, :].astype(F32)).astype(BF)
        far[PART:, :] = tail[...]


def near_sum_kernel(kept, sent0, sent1, through0, through1, near, back):
    near[:PART, :] = (kept[:PART, :].astype(F32) + sent0[...].astype(F32)).astype(BF)
    near[PART:, :] = through0[PART:, :]
    total = kept[PART:, :].astype(F32) + sent1[...].astype(F32)
    back[...] = (total + through1[:PART, :].astype(F32)).astype(BF)


def across_kernel(kept, sent, right, left, through0, through1, lse, first, second, lse_out):
    total = kept[:PART, :].astype(F32) + sent[:PART, :].astype(F32)
    total = (total + right[:PART, :].astype(F32) + left[...].astype(F32)).astype(BF)
    first[...] = total[:PIECE]
    second[:PIECE, :] = total[PIECE:]
    terms = lse[...]
    for ref in (through0, through1, right):
        terms = terms + read_tail(ref, PART)
    lse_out[...] = terms
    write_tail(second, PIECE, terms)


def sum_kernel(ids, kept, sent, right, left, back0, back1, lse, keep, send, lse_out):
    core = ids[CORE]
    total = kept[PART:2 * PART, :].astype(F32) + sent[PART:2 * PART, :].astype(F32)
    total = total + right[...].astype(F32) + left[...].astype(F32)
    back = (back0[...].astype(F32), back1[:PIECE, :].astype(F32))
    terms = lse[...] + read_tail(back1, PIECE)
    lse_out[...] = terms
    write_tail(send, PIECE, terms)

    @pl.when(core == 0)
    def _():
        keep[...] = total[:PIECE] + back[0]
        send[:PIECE, :] = (total[PIECE:] + back[1]).astype(BF)

    @pl.when(core == 1)
    def _():
        keep[...] = total[PIECE:] + back[1]
        send[:PIECE, :] = (total[:PIECE] + back[0]).astype(BF)


def gradient(x, total):
    norm = jnp.sqrt(jnp.sum(x * x, axis=1, keepdims=True) + 1e-06)
    unit = x / norm
    return (total - unit * jnp.sum(unit * total, axis=1, keepdims=True)) / norm


def kept_grad_kernel(ids, image, text, keep, out):
    total = keep[...]

    @pl.when(ids[CORE] == 0)
    def _():
        out[...] = gradient(image[...], total)

    @pl.when(ids[CORE] == 1)
    def _():
        out[...] = gradient(text[...], total)


def grad_kernel(ids, image, text, kept, got, lse, image_out, text_out, loss_out, other, sems):
    pieces = [pl.ds(i * 32, 32) for i in range(PIECE // 32)]

    def put(own_out, other_out, values):
        copies = [
            pltpu.make_async_copy(kept.at[rows], own_out.at[rows], sems.at[i])
            for i, rows in enumerate(pieces)
        ]
        for c in copies:
            c.start()
        for i, rows in enumerate(pieces):
            other[rows, :] = gradient(values[rows, :], got[rows, :].astype(F32))
            out = pltpu.make_async_copy(
                other.at[rows], other_out.at[rows], sems.at[len(pieces) + i]
            )
            out.start()
            copies.append(out)
        for c in copies:
            c.wait()

    terms = lse[...] + read_tail(got, PIECE)
    total = jnp.sum(jnp.sum(terms, axis=0, keepdims=True), axis=1, keepdims=True)
    loss_out[...] = total * (1.0 / (2.0 * ROWS * COLS * PIECE))
    pl.when(ids[CORE] == 0)(lambda: put(image_out, text_out, text))
    pl.when(ids[CORE] == 1)(lambda: put(text_out, image_out, image))


def per_device(image_embeds, text_embeds):
    here = lax.axis_index("row") * COLS + lax.axis_index("col")
    first = lax.axis_index("col") % 2 == 0

    keep, send = unit_pair(image_embeds, text_embeds)
    got = swap(send)
    here, keep = lax.optimization_barrier((here, keep))
    ids = lax.dynamic_index_in_dim(jnp.asarray(device_table()), here, keepdims=False)
    own = jnp.concatenate([jnp.where(first, keep, got), jnp.where(first, got, keep)])
    own, ids = lax.optimization_barrier((own, ids))

    other = flip(own)
    left0, right0 = ring(own, 1), ring(own, 3)
    left1, right1 = ring(other, 1), ring(other, 3)
    far_left = ring(jnp.concatenate([left0[:PIECE], left1[:PIECE]]), 1)
    far_right = ring(jnp.concatenate([right0[PIECE:], right1[PIECE:]]), 3)
    mine = [right1, left1, other, own, right0, left0]
    late, _ = lax.optimization_barrier((own, other))
    theirs = [swap(late if v is own else v) for v in mine]
    near = near_scores(ids, mine, theirs)
    far_right, near[0] = lax.optimization_barrier((far_right, near[0]))
    there_right = swap(far_right)
    far_left, there_right = lax.optimization_barrier((far_left, there_right))
    h_rows, h_cols, img, txt, keep, send = far_scores(
        ids, (far_left, far_right), (swap(far_left), there_right), near
    )
    sums = keep + swap(send)
    sums = group_sum(sums)
    theirs = swap(sums)

    def add(*v):
        return functools.reduce(lambda a, b: a + b, [u.astype(F32) for u in v]).astype(BF)

    def part(value, i):
        return value[i * PART:(i + 1) * PART]

    def mark(done):
        return swap(done[:16, :PIECE])

    w_rows, w_lanes, sent = far_products(ids, sums, theirs, h_rows, h_cols, img, txt)
    sent = swap(sent)
    kept, tail, lse = kept_far(ids, w_rows, w_lanes, img, txt, theirs)
    tailed = jax.ShapeDtypeStruct((PART + TAIL, WIDTH), BF)
    lane = jax.ShapeDtypeStruct((8, PIECE), F32)
    far0, far1 = pl.pallas_call(
        far_sum_kernel, out_shape=(tailed, tailed), in_specs=[VM] * 3,
        out_specs=(VM, VM), compiler_params=PARAMS, name="far_sums",
    )(kept, sent, tail)
    through0, through1 = ring(far0, 1), ring(far1, 3)

    w, s0, s1 = near_products(
        mark(far0), ids, sums, theirs, near[0], w_rows, w_lanes, img, txt
    )
    kept = kept_products(FAR, 4, (), 1, ids, w, img, txt)
    near1, back1 = pl.pallas_call(
        near_sum_kernel, out_shape=(tailed, jax.ShapeDtypeStruct((PART, WIDTH), BF)),
        in_specs=[VM] * 5, out_specs=(VM, VM), compiler_params=PARAMS, name="near_sums",
    )(kept, swap(s0), swap(s1), through0, through1)
    right1, left1 = ring(near1, 1), ring(back1, 3)

    token = mark(back1)
    sent_own, sent_near = last_sent(token, ids, w, img, txt)
    sent_near, sent_own = swap(sent_near), swap(sent_own)
    kept = kept_products(4, 8, (token,), PRODUCT_FLOPS, ids, w, img, txt)
    near0 = add(part(kept, 2), part(sent_near, 0), part(through0, 0))
    back0 = add(part(kept, 3), part(sent_near, 1))
    near0, back0, kept = lax.optimization_barrier((near0, back0, kept))
    right0, left0 = ring(near0, 1), ring(back0, 3)
    shape = jax.ShapeDtypeStruct((PIECE, WIDTH), F32)
    last0, last1, lse = pl.pallas_call(
        across_kernel,
        out_shape=(
            jax.ShapeDtypeStruct((PIECE, WIDTH), BF),
            jax.ShapeDtypeStruct((PIECE + TAIL, WIDTH), BF),
            lane,
        ),
        in_specs=[VM] * 7, out_specs=(VM, VM, VM),
        compiler_params=PARAMS, name="across_sums",
    )(kept, sent_own, right1, left1, through0, through1, lse)
    backs = flip(last0), flip(last1)
    keep, send, lse = pl.pallas_call(
        sum_kernel,
        out_shape=(shape, jax.ShapeDtypeStruct((PIECE + TAIL, WIDTH), BF), lane),
        in_specs=[SM] + [VM] * 7, out_specs=(VM, VM, VM),
        compiler_params=PARAMS, name="own_sums",
    )(ids, kept, sent_own, right0, left0, *backs, lse)
    kept = pl.pallas_call(
        kept_grad_kernel, out_shape=shape, in_specs=[SM] + [VM] * 3, out_specs=VM,
        compiler_params=PARAMS, name="kept_grad",
    )(ids, image_embeds, text_embeds, keep)
    anywhere = pl.BlockSpec(memory_space=pl.ANY)
    image_grad, text_grad, loss = pl.pallas_call(
        grad_kernel,
        out_shape=(shape, shape, jax.ShapeDtypeStruct((1, 1), F32)),
        in_specs=[SM] + [VM] * 5, out_specs=(anywhere, anywhere, VM),
        scratch_shapes=[pltpu.VMEM((PIECE, WIDTH), F32), pltpu.SemaphoreType.DMA((8,))],
        compiler_params=PARAMS, name="grad_rows",
    )(ids, image_embeds, text_embeds, kept, swap(send), lse)
    loss = loss[0, 0]
    return (image_grad, text_grad, loss)


def solution(mesh):
    return jax.shard_map(
        per_device,
        mesh=mesh,
        in_specs=(P(("row", "col"), None), P(("col", "row"), None)),
        out_specs=(P(("row", "col"), None), P(("col", "row"), None), P()),
        check_vma=False,
    )
```

```python
import functools
import math

import jax
import jax.numpy as jnp
import numpy as np
from jax import lax
from jax.experimental import pallas as pl
from jax.experimental.pallas import tpu as pltpu
from jax.sharding import PartitionSpec as P

PIECE = 128
PART = 2 * PIECE
WIDTH = 1280
RING = 4
PART_AT = ((2, 0), (2, 1), (1, 1), (3, 1), (0, 1), (0, 0), (1, 0), (3, 0))
PARTS = len(PART_AT)
FAR = 2
ROWS, COLS = 8, 16
IMG = PARTS * PART
TXT = PARTS * PIECE
FAR_IMG, FAR_TXT = FAR * PART, FAR * PIECE
NEAR_IMG, NEAR_TXT = IMG - FAR_IMG, TXT - FAR_TXT
CORE, TXT_AT, MATCH_AT = 40, 32, 16
TAIL = 16
PRODUCT_FLOPS = 5 * 10**10

SHIFT = 22.0
LIFT = 70.0
FLOOR = math.exp(-62.0)
LOG2E = math.log2(math.e)

VM = pl.BlockSpec(memory_space=pltpu.VMEM)
SM = pl.BlockSpec(memory_space=pltpu.SMEM)
PARAMS = pltpu.CompilerParams(vmem_limit_bytes=8 * 1024 * 1024)
F32, BF = jnp.float32, jnp.bfloat16
NT = (((1,), (1,)), ((), ()))
NN = (((1,), (0,)), ((), ()))
TN = (((0,), (0,)), ((), ()))
AXES = ("row", "col")


def dot(a, b, dims):
    return lax.dot_general(a, b, dims, preferred_element_type=F32)


def device(yl, z, x, yh, k):
    return (yl * 4 + z) * COLS + (x * 2 + yh) * 2 + k


def places():
    return [
        (yl, z, x, yh, k)
        for yl in range(2) for z in range(RING) for x in range(RING) for yh in range(2) for k in range(2)
    ]


def neighbour(y, k):
    return y ^ 1 if k == 0 else (y + (1 if y % 2 else 3)) % RING


def group(value, d, side):
    pairs = []
    for yl, z, x, yh, k in places():
        y = yh * 2 + yl
        y = neighbour(y, k) if side else y
        target = device(y % 2, (z + d * k) % RING, (x + d * (1 - k)) % RING, y // 2, k)
        pairs.append((device(yl, z, x, yh, k), target))
    return lax.ppermute(value, AXES, pairs)


def ring(value, d):
    return group(value, d, 0)


def flip(value):
    return group(value, 0, 1)


def group_sum(value):
    value = value + ring(value, 1) + ring(value, 2) + ring(value, 3)
    return value + flip(value)


def swap(value):
    return lax.ppermute(value, AXES, [
        (device(yl, z, x, yh, k), device(yl, z, x, yh, 1 - k)) for yl, z, x, yh, k in places()
    ])


def device_table():
    table = np.zeros((ROWS * COLS, 41), np.int32)
    for yl, z, x, yh, k in places():
        y = yh * 2 + yl
        img, match, txt, owned = [], [], [], []
        for d, side in PART_AT:
            zt, yt = (z + d) % RING, neighbour(y, 1) if side else y
            txt.append(zt * 2 + (yt + 1) % 2)
            owner = device(yt % 2, zt, x, yt // 2, k)
            owned.append(owner % COLS * ROWS + owner // COLS)
        for d, side in PART_AT:
            xi, yi = (x + d) % RING, neighbour(y, 0) if side else y
            for h in range(2):
                img.append((xi * 2 + yi % 2) * 2 + h)
                piece = device(yi % 2, z, xi, yi // 2, h)
                match.append(owned.index(piece) if piece in owned else -1)
        table[device(yl, z, x, yh, k)] = img + match + txt + [k]
    return table


def cost(flops, bytes_accessed):
    return pl.CostEstimate(flops=flops, bytes_accessed=bytes_accessed, transcendentals=0)


def diagonal():
    shape = (PIECE, PIECE)
    return lax.broadcasted_iota(jnp.int32, shape, 0) == lax.broadcasted_iota(jnp.int32, shape, 1)


def unit_kernel(image_ref, text_ref, keep_ref, send_ref):
    core = lax.axis_index("col") % 2

    def unit(src):
        x = src[...]
        return (x / jnp.sqrt(jnp.sum(x * x, axis=1, keepdims=True) + 1e-06)).astype(BF)

    image, text = unit(image_ref), unit(text_ref)

    @pl.when(core == 0)
    def _():
        keep_ref[...] = image
        send_ref[...] = text

    @pl.when(core == 1)
    def _():
        keep_ref[...] = text
        send_ref[...] = image


def unit_pair(image, text):
    shape = jax.ShapeDtypeStruct((PIECE, WIDTH), BF)
    return pl.pallas_call(
        unit_kernel, out_shape=(shape, shape), in_specs=[VM, VM], out_specs=(VM, VM),
        compiler_params=PARAMS, name="unit_rows",
    )(image, text)


def place_parts(core, here, there, img, txt):
    @pl.when(core == 0)
    def _():
        for m, (mine, other) in enumerate(zip(here, there)):
            img[m * PART:(m + 1) * PART, :] = mine[...]
            txt[m * PIECE:(m + 1) * PIECE, :] = other[:PIECE, :]

    @pl.when(core == 1)
    def _():
        for m, (mine, other) in enumerate(zip(here, there)):
            img[m * PART:(m + 1) * PART, :] = other[...]
            txt[m * PIECE:(m + 1) * PIECE, :] = mine[PIECE:, :]


def score_tiles(tiles, img, txt, held, racc, cacc):
    def epilogue(t):
        row, rows, col, h_out, h_row, h_col = tiles[t]
        cols = slice(col, col + 256)
        total = jnp.zeros((8, 256), F32)
        for p in range(0, rows, PIECE):
            d = held[t % 2][p:p + PIECE, :]
            h = jnp.exp2(d * (50.0 * LOG2E) - (0.5 * SHIFT * LOG2E))
            h_out[h_row + p:h_row + p + PIECE, h_col:h_col + 256] = h
            q = h * h
            racc[row + p:row + p + PIECE, :] += q[:, :PIECE] + q[:, PIECE:]
            total += jnp.sum(q.reshape(16, 8, 256), axis=0)
        cacc[:, cols] += total

    for t, (row, rows, col, *_) in enumerate(tiles):
        held[t % 2][:rows, :] = dot(img[row:row + rows, :], txt[col:col + 256, :], NT)
        if t:
            epilogue(t - 1)
    epilogue(len(tiles) - 1)


def near_kernel(ids, *refs):
    count = PARTS - FAR
    here, there = refs[:count], refs[count:2 * count]
    h_out, img, txt, racc, cacc, even, odd = refs[2 * count:]
    place_parts(ids[CORE], here, there, img, txt)
    racc[...] = jnp.zeros_like(racc)
    cacc[...] = jnp.zeros_like(cacc)
    half = NEAR_IMG // 2
    tiles = [(r, half, c, h_out, r, c) for c in range(0, NEAR_TXT, 256) for r in (0, half)]
    score_tiles(tiles, img, txt, (even, odd), racc, cacc)


def near_scores(ids, here, there):
    return list(pl.pallas_call(
        near_kernel,
        out_shape=(
            jax.ShapeDtypeStruct((NEAR_IMG, NEAR_TXT), F32),
            jax.ShapeDtypeStruct((NEAR_IMG, WIDTH), BF),
            jax.ShapeDtypeStruct((NEAR_TXT, WIDTH), BF),
            jax.ShapeDtypeStruct((NEAR_IMG, PIECE), F32),
            jax.ShapeDtypeStruct((8, NEAR_TXT), F32),
        ),
        in_specs=[SM] + [VM] * (2 * len(here)),
        out_specs=(VM,) * 5,
        scratch_shapes=[pltpu.VMEM((NEAR_IMG // 2, 256), F32)] * 2,
        compiler_params=PARAMS,
        cost_estimate=cost(1, 1),
        name="near_scores",
    )(ids, *here, *there))


def far_kernel(ids, left, right, there_left, there_right, near, near_img, near_txt, near_racc,
               near_cacc, h_rows, h_cols, img, txt, keep, send, even, odd, racc, cacc, rs, cs, dg):
    core = ids[CORE]

    def place(halves, text):
        for i in range(FAR):
            for k, half in enumerate(halves):
                at = i * PART + k * PIECE
                img[at:at + PIECE, :] = half[i * PIECE:(i + 1) * PIECE, :]
        txt[:FAR_TXT, :] = text[...]

    pl.when(core == 0)(lambda: place((left, right), there_left))
    pl.when(core == 1)(lambda: place((there_left, there_right), right))
    img[FAR_IMG:, :] = near_img[...]
    txt[FAR_TXT:, :] = near_txt[...]
    racc[:FAR_IMG, :] = jnp.zeros((FAR_IMG, PIECE), F32)
    racc[FAR_IMG:, :] = near_racc[...]
    cacc[:, :FAR_TXT] = jnp.zeros((8, FAR_TXT), F32)
    cacc[:, FAR_TXT:] = near_cacc[...]
    for ref in (rs, cs, dg, keep, send):
        ref[...] = jnp.zeros_like(ref)
    half = NEAR_IMG // 2
    tiles = [(FAR_IMG + r, half, 0, h_cols, r, 0) for r in (0, half)]
    tiles += [(0, FAR_IMG, c, h_rows, 0, c) for c in range(0, TXT, 256)]
    score_tiles(tiles, img, txt, (even, odd), racc, cacc)

    lowest = jnp.full((1, PIECE), jnp.inf, F32)
    for p in range(COLS):
        part = jnp.sum(racc[p * PIECE:(p + 1) * PIECE, :].T, axis=0, keepdims=True)
        rs[0, pl.ds(ids[p], 1), :] = part
        lowest = jnp.minimum(lowest, part)
    total = jnp.sum(cacc[...], axis=0, keepdims=True)
    for m in range(PARTS):
        part = total[:, m * PIECE:(m + 1) * PIECE]
        cs[0, pl.ds(ids[TXT_AT + m], 1), :] = part
        lowest = jnp.minimum(lowest, part)

    def half_of(p, m):
        at = p * PIECE if p < 2 * FAR else (p - 2 * FAR) * PIECE
        if p < 2 * FAR:
            return h_rows[at:at + PIECE, m * PIECE:(m + 1) * PIECE]
        if m < FAR:
            return h_cols[at:at + PIECE, m * PIECE:(m + 1) * PIECE]
        return near[at:at + PIECE, (m - FAR) * PIECE:(m - FAR + 1) * PIECE]

    @pl.when(jnp.min(lowest) < FLOOR)
    def _():
        for p in range(COLS):
            part = jnp.zeros((PIECE, PIECE), F32)
            for m in range(PARTS):
                g = half_of(p, m) * math.exp(0.5 * (SHIFT + LIFT))
                part += g * g
                cs[1, pl.ds(ids[TXT_AT + m], 1), :] += jnp.sum(g * g, axis=0, keepdims=True)
            rs[1, pl.ds(ids[p], 1), :] = jnp.sum(part.T, axis=0, keepdims=True)

    for p in range(COLS):
        match = ids[MATCH_AT + p]

        @pl.when(match >= 0)
        def _():
            other = txt[pl.ds(pl.multiple_of(match * PIECE, PIECE), PIECE), :]
            s = 100.0 * dot(img[p * PIECE:(p + 1) * PIECE, :], other, NT)
            dg[...] += jnp.sum(jnp.where(diagonal(), s, 0.0).reshape(16, 8, PIECE), axis=0)

    @pl.when(core == 0)
    def _():
        keep[0:2] = rs[...]
        keep[2, 0:8] = dg[...]
        send[0:2, 0:8] = cs[...]

    @pl.when(core == 1)
    def _():
        send[0:2] = rs[...]
        send[2, 0:8] = dg[...]
        keep[0:2, 8:16] = cs[...]


def far_scores(ids, here, there, near):
    sums = jax.ShapeDtypeStruct((3, COLS, PIECE), F32)
    return pl.pallas_call(
        far_kernel,
        out_shape=(
            jax.ShapeDtypeStruct((FAR_IMG, TXT), F32),
            jax.ShapeDtypeStruct((NEAR_IMG, FAR_TXT), F32),
            jax.ShapeDtypeStruct((IMG, WIDTH), BF),
            jax.ShapeDtypeStruct((TXT, WIDTH), BF),
            sums, sums,
        ),
        in_specs=[SM] + [VM] * 9,
        out_specs=(VM,) * 6,
        scratch_shapes=[
            pltpu.VMEM((NEAR_IMG // 2, 256), F32),
            pltpu.VMEM((NEAR_IMG // 2, 256), F32),
            pltpu.VMEM((IMG, PIECE), F32),
            pltpu.VMEM((8, TXT), F32),
            pltpu.VMEM((2, COLS, PIECE), F32),
            pltpu.VMEM((2, ROWS, PIECE), F32),
            pltpu.VMEM((8, PIECE), F32),
        ],
        compiler_params=PARAMS,
        cost_estimate=cost(2 * (IMG * TXT - NEAR_IMG * NEAR_TXT) * WIDTH, 16 << 20),
        name="far_scores",
    )(ids, *here, *there, *near)


def lse_of(sums):
    return jnp.where(sums[0] >= FLOOR, SHIFT + jnp.log(sums[0]), jnp.log(sums[1]) - LIFT)


def row_col_factors(core, own, far, a_s, b_s):
    scale = math.sqrt(0.5)
    factors = [scale * jnp.exp(0.5 * (SHIFT - lse_of(v))) for v in (own, far)]
    a_s[...] = jnp.where(core == 0, factors[0], factors[1])
    b_s[...] = jnp.where(core == 0, factors[1][:8], factors[0][8:])


def weights_block(ids, half, w, row, col, a_s, b_s, p0, p1, m0, m1):
    b = [b_s[pl.ds(ids[TXT_AT + m], 1), :] for m in range(m0, m1)]

    @pl.loop(p0, p1, unroll=4)
    def _(p):
        rows = pl.ds(pl.multiple_of((p - p0) * PIECE, PIECE), PIECE)
        to = pl.ds(pl.multiple_of((p - p0) * PIECE + row, PIECE), PIECE)
        a = jnp.broadcast_to(a_s[pl.ds(ids[p], 1), :], (PIECE, PIECE)).T
        for m in range(m1 - m0):
            h = half[rows, m * PIECE:(m + 1) * PIECE]
            v, t = h * a, h * b[m]
            w[to, col + m * PIECE:col + (m + 1) * PIECE] = (v * v + t * t).astype(BF)
        match = ids[MATCH_AT + p]

        @pl.when((match >= m0) & (match < m1))
        def _():
            at = pl.multiple_of((match - m0) * PIECE, PIECE)
            h = half[rows, pl.ds(at, PIECE)]
            v, t = h * a, h * b_s[pl.ds(ids[TXT_AT + match], 1), :]
            cols = pl.ds(pl.multiple_of(at + col, PIECE), PIECE)
            w[to, cols] = (v * v + t * t - diagonal().astype(F32)).astype(BF)


def product_kernel(kept_here, core, w_rows, w_lanes, img, txt, out):
    def image_side():
        w, where = w_rows
        for n in range(WIDTH // 256):
            cols = slice(n * 256, n * 256 + 256)
            out[:, cols] = dot(w[where, :], txt[:, cols], NN).astype(BF)

    def text_side():
        at, pad = (PIECE, 0) if kept_here else (0, PIECE)
        w, where = w_lanes
        d = dot(w[:, where], img[...], TN).astype(BF)
        for i in range(d.shape[0] // PIECE):
            out[i * PART + at:i * PART + at + PIECE, :] = d[i * PIECE:(i + 1) * PIECE]
            out[i * PART + pad:i * PART + pad + PIECE, :] = jnp.zeros((PIECE, WIDTH), BF)

    pl.when(core == (0 if kept_here else 1))(image_side)
    pl.when(core == (1 if kept_here else 0))(text_side)


def parts_of(w, start, end):
    return (w, slice(start * PART, end * PART)), (w, slice(start * PIECE, end * PIECE))


FACTORS = [pltpu.VMEM((COLS, PIECE), F32), pltpu.VMEM((ROWS, PIECE), F32)]


def far_products(ids, own, far, h_rows, h_cols, img, txt):
    def kernel(ids, own, far, h_rows, h_cols, img, txt, w_rows, w_lanes, out, a_s, b_s):
        row_col_factors(ids[CORE], own, far, a_s, b_s)
        weights_block(ids, h_rows, w_rows, 0, 0, a_s, b_s, 0, 2 * FAR, 0, PARTS)
        weights_block(ids, h_cols, w_lanes, FAR_IMG, 0, a_s, b_s, 2 * FAR, COLS, 0, FAR)
        w_lanes[:FAR_IMG, :] = w_rows[:, :FAR_TXT]
        product_kernel(
            False, ids[CORE], (w_rows, slice(None)), (w_lanes, slice(None)), img, txt, out
        )

    return pl.pallas_call(
        kernel,
        out_shape=(
            jax.ShapeDtypeStruct((FAR_IMG, TXT), BF),
            jax.ShapeDtypeStruct((IMG, FAR_TXT), BF),
            jax.ShapeDtypeStruct((FAR * PART, WIDTH), BF),
        ),
        in_specs=[SM] + [VM] * 6,
        out_specs=(VM,) * 3,
        scratch_shapes=FACTORS,
        compiler_params=PARAMS,
        cost_estimate=cost(PRODUCT_FLOPS, 1),
        name="far_products",
    )(ids, own, far, h_rows, h_cols, img, txt)


def near_products(token, ids, own, far, near, w_rows, w_lanes, img, txt):
    def kernel(token, ids, own, far, near, w_rows, w_lanes, img, txt, w, s0, s1, a_s, b_s, sent):
        row_col_factors(ids[CORE], own, far, a_s, b_s)
        w[:FAR_IMG, :] = w_rows[...]
        w[FAR_IMG:, :FAR_TXT] = w_lanes[FAR_IMG:, :]
        weights_block(ids, near, w, FAR_IMG, FAR_TXT, a_s, b_s, 2 * FAR, COLS, FAR, PARTS)
        parts = parts_of(w, FAR, FAR + 2)
        product_kernel(False, ids[CORE], *parts, img, txt, sent)
        s0[...] = sent[:PART, :]
        s1[...] = sent[PART:, :]

    part = jax.ShapeDtypeStruct((PART, WIDTH), BF)
    return pl.pallas_call(
        kernel,
        out_shape=(
            jax.ShapeDtypeStruct((IMG, TXT), BF),
            part, part,
        ),
        in_specs=[VM, SM] + [VM] * 7,
        out_specs=(VM,) * 3,
        scratch_shapes=[*FACTORS, pltpu.VMEM((2 * PART, WIDTH), BF)],
        compiler_params=PARAMS,
        cost_estimate=cost(PRODUCT_FLOPS, 1),
        name="near_products",
    )(token, ids, own, far, near, w_rows, w_lanes, img, txt)


def kept_far(ids, w_rows, w_lanes, img, txt, sums):
    def kernel(ids, w_rows, w_lanes, img, txt, sums, out, tail, lse_out):
        terms = lse_of(sums[...])
        terms = terms[:8] + terms[8:]
        terms = terms - jnp.where(ids[CORE] == 0, 0.0, 2.0) * sums[2, :8]
        lse_out[...] = terms
        write_tail(tail, 0, terms)
        product_kernel(
            True, ids[CORE], (w_rows, slice(None)), (w_lanes, slice(None)), img, txt, out
        )

    return pl.pallas_call(
        kernel,
        out_shape=(
            jax.ShapeDtypeStruct((FAR * PART, WIDTH), BF),
            jax.ShapeDtypeStruct((TAIL, WIDTH), BF),
            jax.ShapeDtypeStruct((8, PIECE), F32),
        ),
        in_specs=[SM] + [VM] * 5,
        out_specs=(VM,) * 3,
        compiler_params=PARAMS,
        cost_estimate=cost(PRODUCT_FLOPS, 1),
        name="far_kept",
    )(ids, w_rows, w_lanes, img, txt, sums)


def last_sent(token, ids, w, img, txt):
    def kernel(ids, img, txt, w, token, first, second, out):
        product_kernel(False, ids[CORE], *parts_of(w, 4, 8), img, txt, out)
        first[...] = out[:2 * PART, :]
        second[...] = out[2 * PART:, :]

    half = jax.ShapeDtypeStruct((2 * PART, WIDTH), BF)
    return pl.pallas_call(
        kernel,
        out_shape=(half, half),
        in_specs=[SM] + [VM] * 4,
        out_specs=(VM, VM),
        scratch_shapes=[pltpu.VMEM((4 * PART, WIDTH), BF)],
        compiler_params=PARAMS,
        cost_estimate=cost(PRODUCT_FLOPS, 1),
        name="last_sent",
    )(ids, img, txt, w, token)


def kept_products(start, end, tokens, flops, ids, w, img, txt):
    def kernel(ids, img, txt, w, *refs):
        product_kernel(True, ids[CORE], *parts_of(w, start, end), img, txt, refs[-1])

    return pl.pallas_call(
        kernel,
        out_shape=jax.ShapeDtypeStruct(((end - start) * PART, WIDTH), BF),
        in_specs=[SM] + [VM] * (3 + len(tokens)),
        out_specs=VM,
        compiler_params=PARAMS,
        cost_estimate=cost(flops, 1),
        name="products_kept",
    )(ids, img, txt, w, *tokens)


def read_tail(ref, at):
    rows = ref[at:at + TAIL, :3 * PIECE].astype(F32)[:8]
    return sum(rows[:, i * PIECE:(i + 1) * PIECE] for i in range(3))


def write_tail(ref, at, terms):
    ref[at:at + TAIL, :] = jnp.zeros((TAIL, WIDTH), BF)
    pad = jnp.zeros((TAIL - 8, PIECE), F32)
    for i in range(3):
        piece = terms.astype(BF).astype(F32)
        ref[at:at + TAIL, i * PIECE:(i + 1) * PIECE] = jnp.concatenate([piece, pad]).astype(BF)
        terms = terms - piece


def far_sum_kernel(kept, sent, tail, far0, far1):
    for i, far in enumerate((far0, far1)):
        rows = slice(i * PART, (i + 1) * PART)
        far[:PART, :] = (kept[rows, :].astype(F32) + sent[rows, :].astype(F32)).astype(BF)
        far[PART:, :] = tail[...]


def near_sum_kernel(kept, sent0, sent1, through0, through1, near, back):
    near[:PART, :] = (kept[:PART, :].astype(F32) + sent0[...].astype(F32)).astype(BF)
    near[PART:, :] = through0[PART:, :]
    total = kept[PART:, :].astype(F32) + sent1[...].astype(F32)
    back[...] = (total + through1[:PART, :].astype(F32)).astype(BF)


def across_kernel(kept, sent, right, left, through0, through1, lse, first, second, lse_out):
    total = kept[:PART, :].astype(F32) + sent[:PART, :].astype(F32)
    total = (total + right[:PART, :].astype(F32) + left[...].astype(F32)).astype(BF)
    first[...] = total[:PIECE]
    second[:PIECE, :] = total[PIECE:]
    terms = lse[...]
    for ref in (through0, through1, right):
        terms = terms + read_tail(ref, PART)
    lse_out[...] = terms
    write_tail(second, PIECE, terms)


def sum_kernel(ids, kept, sent, right, left, back0, back1, lse, keep, send, lse_out):
    core = ids[CORE]
    total = kept[PART:2 * PART, :].astype(F32) + sent[PART:2 * PART, :].astype(F32)
    total = total + right[...].astype(F32) + left[...].astype(F32)
    back = (back0[...].astype(F32), back1[:PIECE, :].astype(F32))
    terms = lse[...] + read_tail(back1, PIECE)
    lse_out[...] = terms
    write_tail(send, PIECE, terms)

    @pl.when(core == 0)
    def _():
        keep[...] = total[:PIECE] + back[0]
        send[:PIECE, :] = (total[PIECE:] + back[1]).astype(BF)

    @pl.when(core == 1)
    def _():
        keep[...] = total[PIECE:] + back[1]
        send[:PIECE, :] = (total[:PIECE] + back[0]).astype(BF)


def gradient(x, total):
    norm = jnp.sqrt(jnp.sum(x * x, axis=1, keepdims=True) + 1e-06)
    unit = x / norm
    return (total - unit * jnp.sum(unit * total, axis=1, keepdims=True)) / norm


def kept_grad_kernel(ids, image, text, keep, out):
    total = keep[...]

    @pl.when(ids[CORE] == 0)
    def _():
        out[...] = gradient(image[...], total)

    @pl.when(ids[CORE] == 1)
    def _():
        out[...] = gradient(text[...], total)


def grad_kernel(ids, image, text, kept, got, lse, image_out, text_out, loss_out, other, sems):
    pieces = [pl.ds(i * 32, 32) for i in range(PIECE // 32)]

    def put(own_out, other_out, values):
        copies = [
            pltpu.make_async_copy(kept.at[rows], own_out.at[rows], sems.at[i])
            for i, rows in enumerate(pieces)
        ]
        for c in copies:
            c.start()
        for i, rows in enumerate(pieces):
            other[rows, :] = gradient(values[rows, :], got[rows, :].astype(F32))
            out = pltpu.make_async_copy(
                other.at[rows], other_out.at[rows], sems.at[len(pieces) + i]
            )
            out.start()
            copies.append(out)
        for c in copies:
            c.wait()

    terms = lse[...] + read_tail(got, PIECE)
    total = jnp.sum(jnp.sum(terms, axis=0, keepdims=True), axis=1, keepdims=True)
    loss_out[...] = total * (1.0 / (2.0 * ROWS * COLS * PIECE))
    pl.when(ids[CORE] == 0)(lambda: put(image_out, text_out, text))
    pl.when(ids[CORE] == 1)(lambda: put(text_out, image_out, image))


def per_device(image_embeds, text_embeds):
    here = lax.axis_index("row") * COLS + lax.axis_index("col")
    first = lax.axis_index("col") % 2 == 0

    keep, send = unit_pair(image_embeds, text_embeds)
    got = swap(send)
    here, keep = lax.optimization_barrier((here, keep))
    ids = lax.dynamic_index_in_dim(jnp.asarray(device_table()), here, keepdims=False)
    own = jnp.concatenate([jnp.where(first, keep, got), jnp.where(first, got, keep)])
    own, ids = lax.optimization_barrier((own, ids))

    other = flip(own)
    left0, right0 = ring(own, 1), ring(own, 3)
    left1, right1 = ring(other, 1), ring(other, 3)
    far_left = ring(jnp.concatenate([left0[:PIECE], left1[:PIECE]]), 1)
    far_right = ring(jnp.concatenate([right0[PIECE:], right1[PIECE:]]), 3)
    mine = [right1, left1, other, own, right0, left0]
    late, _ = lax.optimization_barrier((own, other))
    theirs = [swap(late if v is own else v) for v in mine]
    near = near_scores(ids, mine, theirs)
    far_right, near[0] = lax.optimization_barrier((far_right, near[0]))
    there_right = swap(far_right)
    far_left, there_right = lax.optimization_barrier((far_left, there_right))
    h_rows, h_cols, img, txt, keep, send = far_scores(
        ids, (far_left, far_right), (swap(far_left), there_right), near
    )
    sums = keep + swap(send)
    sums = group_sum(sums)
    theirs = swap(sums)

    def add(*v):
        return functools.reduce(lambda a, b: a + b, [u.astype(F32) for u in v]).astype(BF)

    def part(value, i):
        return value[i * PART:(i + 1) * PART]

    def mark(done):
        return swap(done[:16, :PIECE])

    w_rows, w_lanes, sent = far_products(ids, sums, theirs, h_rows, h_cols, img, txt)
    sent = swap(sent)
    kept, tail, lse = kept_far(ids, w_rows, w_lanes, img, txt, theirs)
    tailed = jax.ShapeDtypeStruct((PART + TAIL, WIDTH), BF)
    lane = jax.ShapeDtypeStruct((8, PIECE), F32)
    far0, far1 = pl.pallas_call(
        far_sum_kernel, out_shape=(tailed, tailed), in_specs=[VM] * 3,
        out_specs=(VM, VM), compiler_params=PARAMS, name="far_sums",
    )(kept, sent, tail)
    through0, through1 = ring(far0, 1), ring(far1, 3)

    w, s0, s1 = near_products(
        mark(far0), ids, sums, theirs, near[0], w_rows, w_lanes, img, txt
    )
    kept = kept_products(FAR, 4, (), 1, ids, w, img, txt)
    near1, back1 = pl.pallas_call(
        near_sum_kernel, out_shape=(tailed, jax.ShapeDtypeStruct((PART, WIDTH), BF)),
        in_specs=[VM] * 5, out_specs=(VM, VM), compiler_params=PARAMS, name="near_sums",
    )(kept, swap(s0), swap(s1), through0, through1)
    right1, left1 = ring(near1, 1), ring(back1, 3)

    token = mark(back1)
    sent_own, sent_near = last_sent(token, ids, w, img, txt)
    sent_near, sent_own = swap(sent_near), swap(sent_own)
    kept = kept_products(4, 8, (token,), PRODUCT_FLOPS, ids, w, img, txt)
    near0 = add(part(kept, 2), part(sent_near, 0), part(through0, 0))
    back0 = add(part(kept, 3), part(sent_near, 1))
    near0, back0, kept = lax.optimization_barrier((near0, back0, kept))
    right0, left0 = ring(near0, 1), ring(back0, 3)
    shape = jax.ShapeDtypeStruct((PIECE, WIDTH), F32)
    last0, last1, lse = pl.pallas_call(
        across_kernel,
        out_shape=(
            jax.ShapeDtypeStruct((PIECE, WIDTH), BF),
            jax.ShapeDtypeStruct((PIECE + TAIL, WIDTH), BF),
            lane,
        ),
        in_specs=[VM] * 7, out_specs=(VM, VM, VM),
        compiler_params=PARAMS, name="across_sums",
    )(kept, sent_own, right1, left1, through0, through1, lse)
    backs = flip(last0), flip(last1)
    keep, send, lse = pl.pallas_call(
        sum_kernel,
        out_shape=(shape, jax.ShapeDtypeStruct((PIECE + TAIL, WIDTH), BF), lane),
        in_specs=[SM] + [VM] * 7, out_specs=(VM, VM, VM),
        compiler_params=PARAMS, name="own_sums",
    )(ids, kept, sent_own, right0, left0, *backs, lse)
    kept = pl.pallas_call(
        kept_grad_kernel, out_shape=shape, in_specs=[SM] + [VM] * 3, out_specs=VM,
        compiler_params=PARAMS, name="kept_grad",
    )(ids, image_embeds, text_embeds, keep)
    anywhere = pl.BlockSpec(memory_space=pl.ANY)
    image_grad, text_grad, loss = pl.pallas_call(
        grad_kernel,
        out_shape=(shape, shape, jax.ShapeDtypeStruct((1, 1), F32)),
        in_specs=[SM] + [VM] * 5, out_specs=(anywhere, anywhere, VM),
        scratch_shapes=[pltpu.VMEM((PIECE, WIDTH), F32), pltpu.SemaphoreType.DMA((8,))],
        compiler_params=PARAMS, name="grad_rows",
    )(ids, image_embeds, text_embeds, kept, swap(send), lse)
    loss = loss[0, 0]
    return (image_grad, text_grad, loss)


def solution(mesh):
    return jax.shard_map(
        per_device,
        mesh=mesh,
        in_specs=(P(("row", "col"), None), P(("col", "row"), None)),
        out_specs=(P(("row", "col"), None), P(("col", "row"), None), P()),
        check_vma=False,
    )
```

```python
import functools
import math

import jax
import jax.numpy as jnp
import numpy as np
from jax import lax
from jax.experimental import pallas as pl
from jax.experimental.pallas import tpu as pltpu
from jax.sharding import PartitionSpec as P

PIECE = 128
PART = 2 * PIECE
WIDTH = 1280
RING = 4
PART_AT = ((2, 0), (2, 1), (1, 1), (3, 1), (0, 1), (0, 0), (1, 0), (3, 0))
PARTS = len(PART_AT)
FAR = 2
ROWS, COLS = 8, 16
IMG = PARTS * PART
TXT = PARTS * PIECE
FAR_IMG, FAR_TXT = FAR * PART, FAR * PIECE
NEAR_IMG, NEAR_TXT = IMG - FAR_IMG, TXT - FAR_TXT
CORE, TXT_AT, MATCH_AT = 40, 32, 16
TAIL = 16
PRODUCT_FLOPS = 5 * 10**10

SHIFT = 22.0
LIFT = 70.0
FLOOR = math.exp(-62.0)
LOG2E = math.log2(math.e)

VM = pl.BlockSpec(memory_space=pltpu.VMEM)
SM = pl.BlockSpec(memory_space=pltpu.SMEM)
PARAMS = pltpu.CompilerParams(vmem_limit_bytes=8 * 1024 * 1024)
F32, BF = jnp.float32, jnp.bfloat16
NT = (((1,), (1,)), ((), ()))
NN = (((1,), (0,)), ((), ()))
TN = (((0,), (0,)), ((), ()))
AXES = ("row", "col")


def dot(a, b, dims):
    return lax.dot_general(a, b, dims, preferred_element_type=F32)


def device(yl, z, x, yh, k):
    return (yl * 4 + z) * COLS + (x * 2 + yh) * 2 + k


def places():
    return [
        (yl, z, x, yh, k)
        for yl in range(2) for z in range(RING) for x in range(RING) for yh in range(2) for k in range(2)
    ]


def neighbour(y, k):
    return y ^ 1 if k == 0 else (y + (1 if y % 2 else 3)) % RING


def group(value, d, side):
    pairs = []
    for yl, z, x, yh, k in places():
        y = yh * 2 + yl
        y = neighbour(y, k) if side else y
        target = device(y % 2, (z + d * k) % RING, (x + d * (1 - k)) % RING, y // 2, k)
        pairs.append((device(yl, z, x, yh, k), target))
    return lax.ppermute(value, AXES, pairs)


def ring(value, d):
    return group(value, d, 0)


def flip(value):
    return group(value, 0, 1)


def group_sum(value):
    value = value + ring(value, 1) + ring(value, 2) + ring(value, 3)
    return value + flip(value)


def swap(value):
    return lax.ppermute(value, AXES, [
        (device(yl, z, x, yh, k), device(yl, z, x, yh, 1 - k)) for yl, z, x, yh, k in places()
    ])


def device_table():
    table = np.zeros((ROWS * COLS, 41), np.int32)
    for yl, z, x, yh, k in places():
        y = yh * 2 + yl
        img, match, txt, owned = [], [], [], []
        for d, side in PART_AT:
            zt, yt = (z + d) % RING, neighbour(y, 1) if side else y
            txt.append(zt * 2 + (yt + 1) % 2)
            owner = device(yt % 2, zt, x, yt // 2, k)
            owned.append(owner % COLS * ROWS + owner // COLS)
        for d, side in PART_AT:
            xi, yi = (x + d) % RING, neighbour(y, 0) if side else y
            for h in range(2):
                img.append((xi * 2 + yi % 2) * 2 + h)
                piece = device(yi % 2, z, xi, yi // 2, h)
                match.append(owned.index(piece) if piece in owned else -1)
        table[device(yl, z, x, yh, k)] = img + match + txt + [k]
    return table


def cost(flops, bytes_accessed):
    return pl.CostEstimate(flops=flops, bytes_accessed=bytes_accessed, transcendentals=0)


def diagonal():
    shape = (PIECE, PIECE)
    return lax.broadcasted_iota(jnp.int32, shape, 0) == lax.broadcasted_iota(jnp.int32, shape, 1)


def unit_kernel(image_ref, text_ref, keep_ref, send_ref):
    core = lax.axis_index("col") % 2

    def unit(src):
        x = src[...]
        return (x / jnp.sqrt(jnp.sum(x * x, axis=1, keepdims=True) + 1e-06)).astype(BF)

    image, text = unit(image_ref), unit(text_ref)

    @pl.when(core == 0)
    def _():
        keep_ref[...] = image
        send_ref[...] = text

    @pl.when(core == 1)
    def _():
        keep_ref[...] = text
        send_ref[...] = image


def unit_pair(image, text):
    shape = jax.ShapeDtypeStruct((PIECE, WIDTH), BF)
    return pl.pallas_call(
        unit_kernel, out_shape=(shape, shape), in_specs=[VM, VM], out_specs=(VM, VM),
        compiler_params=PARAMS, name="unit_rows",
    )(image, text)


def place_parts(core, here, there, img, txt):
    @pl.when(core == 0)
    def _():
        for m, (mine, other) in enumerate(zip(here, there)):
            img[m * PART:(m + 1) * PART, :] = mine[...]
            txt[m * PIECE:(m + 1) * PIECE, :] = other[:PIECE, :]

    @pl.when(core == 1)
    def _():
        for m, (mine, other) in enumerate(zip(here, there)):
            img[m * PART:(m + 1) * PART, :] = other[...]
            txt[m * PIECE:(m + 1) * PIECE, :] = mine[PIECE:, :]


def score_tiles(tiles, img, txt, held, racc, cacc):
    def epilogue(t):
        row, rows, col, h_out, h_row, h_col = tiles[t]
        cols = slice(col, col + 256)
        total = jnp.zeros((8, 256), F32)
        for p in range(0, rows, PIECE):
            d = held[t % 2][p:p + PIECE, :]
            h = jnp.exp2(d * (50.0 * LOG2E) - (0.5 * SHIFT * LOG2E))
            h_out[h_row + p:h_row + p + PIECE, h_col:h_col + 256] = h
            q = h * h
            racc[row + p:row + p + PIECE, :] += q[:, :PIECE] + q[:, PIECE:]
            total += jnp.sum(q.reshape(16, 8, 256), axis=0)
        cacc[:, cols] += total

    for t, (row, rows, col, *_) in enumerate(tiles):
        held[t % 2][:rows, :] = dot(img[row:row + rows, :], txt[col:col + 256, :], NT)
        if t:
            epilogue(t - 1)
    epilogue(len(tiles) - 1)


def near_kernel(ids, *refs):
    count = PARTS - FAR
    here, there = refs[:count], refs[count:2 * count]
    h_out, img, txt, racc, cacc, even, odd = refs[2 * count:]
    place_parts(ids[CORE], here, there, img, txt)
    racc[...] = jnp.zeros_like(racc)
    cacc[...] = jnp.zeros_like(cacc)
    half = NEAR_IMG // 2
    tiles = [(r, half, c, h_out, r, c) for c in range(0, NEAR_TXT, 256) for r in (0, half)]
    score_tiles(tiles, img, txt, (even, odd), racc, cacc)


def near_scores(ids, here, there):
    return list(pl.pallas_call(
        near_kernel,
        out_shape=(
            jax.ShapeDtypeStruct((NEAR_IMG, NEAR_TXT), F32),
            jax.ShapeDtypeStruct((NEAR_IMG, WIDTH), BF),
            jax.ShapeDtypeStruct((NEAR_TXT, WIDTH), BF),
            jax.ShapeDtypeStruct((NEAR_IMG, PIECE), F32),
            jax.ShapeDtypeStruct((8, NEAR_TXT), F32),
        ),
        in_specs=[SM] + [VM] * (2 * len(here)),
        out_specs=(VM,) * 5,
        scratch_shapes=[pltpu.VMEM((NEAR_IMG // 2, 256), F32)] * 2,
        compiler_params=PARAMS,
        cost_estimate=cost(1, 1),
        name="near_scores",
    )(ids, *here, *there))


def far_kernel(ids, left, right, there_left, there_right, near, near_img, near_txt, near_racc,
               near_cacc, h_rows, h_cols, img, txt, keep, send, even, odd, racc, cacc, rs, cs, dg):
    core = ids[CORE]

    def place(halves, text):
        for i in range(FAR):
            for k, half in enumerate(halves):
                at = i * PART + k * PIECE
                img[at:at + PIECE, :] = half[i * PIECE:(i + 1) * PIECE, :]
        txt[:FAR_TXT, :] = text[...]

    pl.when(core == 0)(lambda: place((left, right), there_left))
    pl.when(core == 1)(lambda: place((there_left, there_right), right))
    img[FAR_IMG:, :] = near_img[...]
    txt[FAR_TXT:, :] = near_txt[...]
    racc[:FAR_IMG, :] = jnp.zeros((FAR_IMG, PIECE), F32)
    racc[FAR_IMG:, :] = near_racc[...]
    cacc[:, :FAR_TXT] = jnp.zeros((8, FAR_TXT), F32)
    cacc[:, FAR_TXT:] = near_cacc[...]
    for ref in (rs, cs, dg, keep, send):
        ref[...] = jnp.zeros_like(ref)
    half = NEAR_IMG // 2
    tiles = [(FAR_IMG + r, half, 0, h_cols, r, 0) for r in (0, half)]
    tiles += [(0, FAR_IMG, c, h_rows, 0, c) for c in range(0, TXT, 256)]
    score_tiles(tiles, img, txt, (even, odd), racc, cacc)

    lowest = jnp.full((1, PIECE), jnp.inf, F32)
    for p in range(COLS):
        part = jnp.sum(racc[p * PIECE:(p + 1) * PIECE, :].T, axis=0, keepdims=True)
        rs[0, pl.ds(ids[p], 1), :] = part
        lowest = jnp.minimum(lowest, part)
    total = jnp.sum(cacc[...], axis=0, keepdims=True)
    for m in range(PARTS):
        part = total[:, m * PIECE:(m + 1) * PIECE]
        cs[0, pl.ds(ids[TXT_AT + m], 1), :] = part
        lowest = jnp.minimum(lowest, part)

    def half_of(p, m):
        at = p * PIECE if p < 2 * FAR else (p - 2 * FAR) * PIECE
        if p < 2 * FAR:
            return h_rows[at:at + PIECE, m * PIECE:(m + 1) * PIECE]
        if m < FAR:
            return h_cols[at:at + PIECE, m * PIECE:(m + 1) * PIECE]
        return near[at:at + PIECE, (m - FAR) * PIECE:(m - FAR + 1) * PIECE]

    @pl.when(jnp.min(lowest) < FLOOR)
    def _():
        for p in range(COLS):
            part = jnp.zeros((PIECE, PIECE), F32)
            for m in range(PARTS):
                g = half_of(p, m) * math.exp(0.5 * (SHIFT + LIFT))
                part += g * g
                cs[1, pl.ds(ids[TXT_AT + m], 1), :] += jnp.sum(g * g, axis=0, keepdims=True)
            rs[1, pl.ds(ids[p], 1), :] = jnp.sum(part.T, axis=0, keepdims=True)

    for p in range(COLS):
        match = ids[MATCH_AT + p]

        @pl.when(match >= 0)
        def _():
            other = txt[pl.ds(pl.multiple_of(match * PIECE, PIECE), PIECE), :]
            s = 100.0 * dot(img[p * PIECE:(p + 1) * PIECE, :], other, NT)
            dg[...] += jnp.sum(jnp.where(diagonal(), s, 0.0).reshape(16, 8, PIECE), axis=0)

    @pl.when(core == 0)
    def _():
        keep[0:2] = rs[...]
        keep[2, 0:8] = dg[...]
        send[0:2, 0:8] = cs[...]

    @pl.when(core == 1)
    def _():
        send[0:2] = rs[...]
        send[2, 0:8] = dg[...]
        keep[0:2, 8:16] = cs[...]


def far_scores(ids, here, there, near):
    sums = jax.ShapeDtypeStruct((3, COLS, PIECE), F32)
    return pl.pallas_call(
        far_kernel,
        out_shape=(
            jax.ShapeDtypeStruct((FAR_IMG, TXT), F32),
            jax.ShapeDtypeStruct((NEAR_IMG, FAR_TXT), F32),
            jax.ShapeDtypeStruct((IMG, WIDTH), BF),
            jax.ShapeDtypeStruct((TXT, WIDTH), BF),
            sums, sums,
        ),
        in_specs=[SM] + [VM] * 9,
        out_specs=(VM,) * 6,
        scratch_shapes=[
            pltpu.VMEM((NEAR_IMG // 2, 256), F32),
            pltpu.VMEM((NEAR_IMG // 2, 256), F32),
            pltpu.VMEM((IMG, PIECE), F32),
            pltpu.VMEM((8, TXT), F32),
            pltpu.VMEM((2, COLS, PIECE), F32),
            pltpu.VMEM((2, ROWS, PIECE), F32),
            pltpu.VMEM((8, PIECE), F32),
        ],
        compiler_params=PARAMS,
        cost_estimate=cost(2 * (IMG * TXT - NEAR_IMG * NEAR_TXT) * WIDTH, 16 << 20),
        name="far_scores",
    )(ids, *here, *there, *near)


def lse_of(sums):
    return jnp.where(sums[0] >= FLOOR, SHIFT + jnp.log(sums[0]), jnp.log(sums[1]) - LIFT)


def row_col_factors(core, own, far, a_s, b_s):
    scale = math.sqrt(0.5)
    factors = [scale * jnp.exp(0.5 * (SHIFT - lse_of(v))) for v in (own, far)]
    a_s[...] = jnp.where(core == 0, factors[0], factors[1])
    b_s[...] = jnp.where(core == 0, factors[1][:8], factors[0][8:])


def weights_block(ids, half, w, row, col, a_s, b_s, p0, p1, m0, m1):
    b = [b_s[pl.ds(ids[TXT_AT + m], 1), :] for m in range(m0, m1)]

    @pl.loop(p0, p1)
    def _(p):
        rows = pl.ds(pl.multiple_of((p - p0) * PIECE, PIECE), PIECE)
        to = pl.ds(pl.multiple_of((p - p0) * PIECE + row, PIECE), PIECE)
        a = jnp.broadcast_to(a_s[pl.ds(ids[p], 1), :], (PIECE, PIECE)).T
        for m in range(m1 - m0):
            h = half[rows, m * PIECE:(m + 1) * PIECE]
            v, t = h * a, h * b[m]
            w[to, col + m * PIECE:col + (m + 1) * PIECE] = (v * v + t * t).astype(BF)
        match = ids[MATCH_AT + p]

        @pl.when((match >= m0) & (match < m1))
        def _():
            at = pl.multiple_of((match - m0) * PIECE, PIECE)
            h = half[rows, pl.ds(at, PIECE)]
            v, t = h * a, h * b_s[pl.ds(ids[TXT_AT + match], 1), :]
            cols = pl.ds(pl.multiple_of(at + col, PIECE), PIECE)
            w[to, cols] = (v * v + t * t - diagonal().astype(F32)).astype(BF)


def product_kernel(kept_here, core, w_rows, w_lanes, img, txt, out):
    def image_side():
        w, where = w_rows
        for n in range(WIDTH // 256):
            cols = slice(n * 256, n * 256 + 256)
            out[:, cols] = dot(w[where, :], txt[:, cols], NN).astype(BF)

    def text_side():
        at, pad = (PIECE, 0) if kept_here else (0, PIECE)
        w, where = w_lanes
        d = dot(w[:, where], img[...], TN).astype(BF)
        for i in range(d.shape[0] // PIECE):
            out[i * PART + at:i * PART + at + PIECE, :] = d[i * PIECE:(i + 1) * PIECE]
            out[i * PART + pad:i * PART + pad + PIECE, :] = jnp.zeros((PIECE, WIDTH), BF)

    pl.when(core == (0 if kept_here else 1))(image_side)
    pl.when(core == (1 if kept_here else 0))(text_side)


def parts_of(w, start, end):
    return (w, slice(start * PART, end * PART)), (w, slice(start * PIECE, end * PIECE))


FACTORS = [pltpu.VMEM((COLS, PIECE), F32), pltpu.VMEM((ROWS, PIECE), F32)]


def far_products(ids, own, far, h_rows, h_cols, img, txt):
    def kernel(ids, own, far, h_rows, h_cols, img, txt, w_rows, w_lanes, out, a_s, b_s):
        row_col_factors(ids[CORE], own, far, a_s, b_s)
        weights_block(ids, h_rows, w_rows, 0, 0, a_s, b_s, 0, 2 * FAR, 0, PARTS)
        weights_block(ids, h_cols, w_lanes, FAR_IMG, 0, a_s, b_s, 2 * FAR, COLS, 0, FAR)
        w_lanes[:FAR_IMG, :] = w_rows[:, :FAR_TXT]
        product_kernel(
            False, ids[CORE], (w_rows, slice(None)), (w_lanes, slice(None)), img, txt, out
        )

    return pl.pallas_call(
        kernel,
        out_shape=(
            jax.ShapeDtypeStruct((FAR_IMG, TXT), BF),
            jax.ShapeDtypeStruct((IMG, FAR_TXT), BF),
            jax.ShapeDtypeStruct((FAR * PART, WIDTH), BF),
        ),
        in_specs=[SM] + [VM] * 6,
        out_specs=(VM,) * 3,
        scratch_shapes=FACTORS,
        compiler_params=PARAMS,
        cost_estimate=cost(PRODUCT_FLOPS, 1),
        name="far_products",
    )(ids, own, far, h_rows, h_cols, img, txt)


def near_products(token, ids, own, far, near, w_rows, w_lanes, img, txt):
    def kernel(token, ids, own, far, near, w_rows, w_lanes, img, txt, w, s0, s1, out, a_s, b_s,
               sent):
        row_col_factors(ids[CORE], own, far, a_s, b_s)
        w[:FAR_IMG, :] = w_rows[...]
        w[FAR_IMG:, :FAR_TXT] = w_lanes[FAR_IMG:, :]
        weights_block(ids, near, w, FAR_IMG, FAR_TXT, a_s, b_s, 2 * FAR, COLS, FAR, PARTS)
        parts = parts_of(w, FAR, FAR + 2)
        product_kernel(False, ids[CORE], *parts, img, txt, sent)
        s0[...] = sent[:PART, :]
        s1[...] = sent[PART:, :]
        product_kernel(True, ids[CORE], *parts, img, txt, out)

    part = jax.ShapeDtypeStruct((PART, WIDTH), BF)
    return pl.pallas_call(
        kernel,
        out_shape=(
            jax.ShapeDtypeStruct((IMG, TXT), BF),
            part, part,
            jax.ShapeDtypeStruct((2 * PART, WIDTH), BF),
        ),
        in_specs=[VM, SM] + [VM] * 7,
        out_specs=(VM,) * 4,
        scratch_shapes=[*FACTORS, pltpu.VMEM((2 * PART, WIDTH), BF)],
        compiler_params=PARAMS,
        cost_estimate=cost(PRODUCT_FLOPS, 1),
        name="near_products",
    )(token, ids, own, far, near, w_rows, w_lanes, img, txt)


def kept_far(ids, w_rows, w_lanes, img, txt, sums):
    def kernel(ids, w_rows, w_lanes, img, txt, sums, out, tail, lse_out):
        terms = lse_of(sums[...])
        terms = terms[:8] + terms[8:]
        terms = terms - jnp.where(ids[CORE] == 0, 0.0, 2.0) * sums[2, :8]
        lse_out[...] = terms
        write_tail(tail, 0, terms)
        product_kernel(
            True, ids[CORE], (w_rows, slice(None)), (w_lanes, slice(None)), img, txt, out
        )

    return pl.pallas_call(
        kernel,
        out_shape=(
            jax.ShapeDtypeStruct((FAR * PART, WIDTH), BF),
            jax.ShapeDtypeStruct((TAIL, WIDTH), BF),
            jax.ShapeDtypeStruct((8, PIECE), F32),
        ),
        in_specs=[SM] + [VM] * 5,
        out_specs=(VM,) * 3,
        compiler_params=PARAMS,
        cost_estimate=cost(PRODUCT_FLOPS, 1),
        name="far_kept",
    )(ids, w_rows, w_lanes, img, txt, sums)


def products(start, end, kept_here, tokens, ids, w, img, txt, flops=PRODUCT_FLOPS):
    def kernel(ids, img, txt, w, *refs):
        product_kernel(kept_here, ids[CORE], *parts_of(w, start, end), img, txt, refs[-1])

    return pl.pallas_call(
        kernel,
        out_shape=jax.ShapeDtypeStruct(((end - start) * PART, WIDTH), BF),
        in_specs=[SM] + [VM] * (3 + len(tokens)),
        out_specs=VM,
        compiler_params=PARAMS,
        cost_estimate=cost(flops, 1),
        name="products_kept" if kept_here else "products_sent",
    )(ids, img, txt, w, *tokens)


def read_tail(ref, at):
    rows = ref[at:at + TAIL, :3 * PIECE].astype(F32)[:8]
    return sum(rows[:, i * PIECE:(i + 1) * PIECE] for i in range(3))


def write_tail(ref, at, terms):
    ref[at:at + TAIL, :] = jnp.zeros((TAIL, WIDTH), BF)
    pad = jnp.zeros((TAIL - 8, PIECE), F32)
    for i in range(3):
        piece = terms.astype(BF).astype(F32)
        ref[at:at + TAIL, i * PIECE:(i + 1) * PIECE] = jnp.concatenate([piece, pad]).astype(BF)
        terms = terms - piece


def far_sum_kernel(kept, sent, tail, far0, far1):
    for i, far in enumerate((far0, far1)):
        rows = slice(i * PART, (i + 1) * PART)
        far[:PART, :] = (kept[rows, :].astype(F32) + sent[rows, :].astype(F32)).astype(BF)
        far[PART:, :] = tail[...]


def near_sum_kernel(kept, sent0, sent1, through0, through1, near, back):
    near[:PART, :] = (kept[:PART, :].astype(F32) + sent0[...].astype(F32)).astype(BF)
    near[PART:, :] = through0[PART:, :]
    total = kept[PART:, :].astype(F32) + sent1[...].astype(F32)
    back[...] = (total + through1[:PART, :].astype(F32)).astype(BF)


def across_kernel(kept, sent, right, left, through0, through1, lse, first, second, lse_out):
    total = kept[:PART, :].astype(F32) + sent[:PART, :].astype(F32)
    total = (total + right[:PART, :].astype(F32) + left[...].astype(F32)).astype(BF)
    first[...] = total[:PIECE]
    second[:PIECE, :] = total[PIECE:]
    terms = lse[...]
    for ref in (through0, through1, right):
        terms = terms + read_tail(ref, PART)
    lse_out[...] = terms
    write_tail(second, PIECE, terms)


def sum_kernel(ids, kept, sent, right, left, back0, back1, lse, token, keep, send, lse_out):
    core = ids[CORE]
    total = kept[PART:2 * PART, :].astype(F32) + sent[PART:2 * PART, :].astype(F32)
    total = total + right[...].astype(F32) + left[...].astype(F32)
    back = (back0[...].astype(F32), back1[:PIECE, :].astype(F32))
    terms = lse[...] + read_tail(back1, PIECE)
    lse_out[...] = terms
    write_tail(send, PIECE, terms)

    @pl.when(core == 0)
    def _():
        keep[...] = total[:PIECE] + back[0]
        send[:PIECE, :] = (total[PIECE:] + back[1]).astype(BF)

    @pl.when(core == 1)
    def _():
        keep[...] = total[PIECE:] + back[1]
        send[:PIECE, :] = (total[:PIECE] + back[0]).astype(BF)


def grad_kernel(ids, image, text, keep, got, lse, image_out, text_out, loss_out):
    core = ids[CORE]

    def grad(values, total, out):
        x = values[...]
        norm = jnp.sqrt(jnp.sum(x * x, axis=1, keepdims=True) + 1e-06)
        unit = x / norm
        g = total[:PIECE, :].astype(F32)
        out[...] = (g - unit * jnp.sum(unit * g, axis=1, keepdims=True)) / norm

    @pl.when(core == 0)
    def _():
        grad(image, keep, image_out)
        grad(text, got, text_out)

    @pl.when(core == 1)
    def _():
        grad(image, got, image_out)
        grad(text, keep, text_out)

    terms = lse[...] + read_tail(got, PIECE)
    total = jnp.sum(jnp.sum(terms, axis=0, keepdims=True), axis=1, keepdims=True)
    loss_out[...] = total * (1.0 / (2.0 * ROWS * COLS * PIECE))


def per_device(image_embeds, text_embeds):
    here = lax.axis_index("row") * COLS + lax.axis_index("col")
    first = lax.axis_index("col") % 2 == 0

    keep, send = unit_pair(image_embeds, text_embeds)
    got = swap(send)
    here, keep = lax.optimization_barrier((here, keep))
    ids = lax.dynamic_index_in_dim(jnp.asarray(device_table()), here, keepdims=False)
    own = jnp.concatenate([jnp.where(first, keep, got), jnp.where(first, got, keep)])
    own, ids = lax.optimization_barrier((own, ids))

    other = flip(own)
    left0, right0 = ring(own, 1), ring(own, 3)
    left1, right1 = ring(other, 1), ring(other, 3)
    far_left = ring(jnp.concatenate([left0[:PIECE], left1[:PIECE]]), 1)
    far_right = ring(jnp.concatenate([right0[PIECE:], right1[PIECE:]]), 3)
    mine = [right1, left1, other, own, right0, left0]
    late, _ = lax.optimization_barrier((own, other))
    theirs = [swap(late if v is own else v) for v in mine]
    near = near_scores(ids, mine, theirs)
    far_right, near[0] = lax.optimization_barrier((far_right, near[0]))
    there_right = swap(far_right)
    far_left, there_right = lax.optimization_barrier((far_left, there_right))
    h_rows, h_cols, img, txt, keep, send = far_scores(
        ids, (far_left, far_right), (swap(far_left), there_right), near
    )
    sums = keep + swap(send)
    sums = group_sum(sums)
    theirs = swap(sums)

    def add(*v):
        return functools.reduce(lambda a, b: a + b, [u.astype(F32) for u in v]).astype(BF)

    def part(value, i):
        return value[i * PART:(i + 1) * PART]

    def mark(done):
        return swap(done[:16, :PIECE])

    w_rows, w_lanes, sent = far_products(ids, sums, theirs, h_rows, h_cols, img, txt)
    sent = swap(sent)
    kept, tail, lse = kept_far(ids, w_rows, w_lanes, img, txt, theirs)
    tailed = jax.ShapeDtypeStruct((PART + TAIL, WIDTH), BF)
    lane = jax.ShapeDtypeStruct((8, PIECE), F32)
    far0, far1 = pl.pallas_call(
        far_sum_kernel, out_shape=(tailed, tailed), in_specs=[VM] * 3,
        out_specs=(VM, VM), compiler_params=PARAMS, name="far_sums",
    )(kept, sent, tail)
    through0, through1 = ring(far0, 1), ring(far1, 3)

    w, s0, s1, kept = near_products(
        mark(far0), ids, sums, theirs, near[0], w_rows, w_lanes, img, txt
    )
    near1, back1 = pl.pallas_call(
        near_sum_kernel, out_shape=(tailed, jax.ShapeDtypeStruct((PART, WIDTH), BF)),
        in_specs=[VM] * 5, out_specs=(VM, VM), compiler_params=PARAMS, name="near_sums",
    )(kept, swap(s0), swap(s1), through0, through1)
    right1, left1 = ring(near1, 1), ring(back1, 3)

    token = mark(back1)
    sent_on = swap(products(4, 8, False, (token,), ids, w, img, txt))
    kept = products(4, 8, True, (token,), ids, w, img, txt)
    near0 = add(part(kept, 2), part(sent_on, 2), part(through0, 0))
    back0 = add(part(kept, 3), part(sent_on, 3))
    near0, back0, kept, sent_on = lax.optimization_barrier((near0, back0, kept, sent_on))
    right0 = ring(near0, 1)
    shape = jax.ShapeDtypeStruct((PIECE, WIDTH), F32)
    last0, last1, lse = pl.pallas_call(
        across_kernel,
        out_shape=(
            jax.ShapeDtypeStruct((PIECE, WIDTH), BF),
            jax.ShapeDtypeStruct((PIECE + TAIL, WIDTH), BF),
            lane,
        ),
        in_specs=[VM] * 7, out_specs=(VM, VM, VM),
        compiler_params=PARAMS, name="across_sums",
    )(kept, sent_on, right1, left1, through0, through1, lse)
    backs = flip(last0), flip(last1)
    back0, token = lax.optimization_barrier((back0, mark(last0)))
    left0 = ring(back0, 3)
    keep, send, lse = pl.pallas_call(
        sum_kernel,
        out_shape=(shape, jax.ShapeDtypeStruct((PIECE + TAIL, WIDTH), BF), lane),
        in_specs=[SM] + [VM] * 8, out_specs=(VM, VM, VM),
        compiler_params=PARAMS, name="own_sums",
    )(ids, kept, sent_on, right0, left0, *backs, lse, token)
    image_grad, text_grad, loss = pl.pallas_call(
        grad_kernel,
        out_shape=(shape, shape, jax.ShapeDtypeStruct((1, 1), F32)),
        in_specs=[SM] + [VM] * 5, out_specs=(VM, VM, VM),
        compiler_params=PARAMS, name="grad_rows",
    )(ids, image_embeds, text_embeds, keep, swap(send), lse)
    loss = loss[0, 0]
    return (image_grad, text_grad, loss)


def solution(mesh):
    return jax.shard_map(
        per_device,
        mesh=mesh,
        in_specs=(P(("row", "col"), None), P(("col", "row"), None)),
        out_specs=(P(("row", "col"), None), P(("col", "row"), None), P()),
        check_vma=False,
    )
```
